512 devices in a mesh: seq: 128 (over z, y, core), ch: 4 (over x).
Axes of the slice: x: 4, y: 4, z: 16, core: 2. Of those that a mesh axis runs over, the one named last changes fastest.
Arguments:
- q_stream: bfloat16 [16384, 4096], P('seq', 'ch'), may hold values from -6 to 6
- k_stream: bfloat16 [16384, 4096], P('seq', 'ch'), may hold values from -6 to 6
- v_stream: bfloat16 [16384, 4096], P('seq', 'ch'), may hold values from -6 to 6
- short_filter: float32 [3, 3, 4096], P(None, None, 'ch'), may hold values from -4 to 4
- rates: float32 [16, 4096], P(None, 'ch'), may hold values from 6.1035155e-07 to 0.03
- residues: float32 [16, 4096], P(None, 'ch'), may hold values from -3 to 3
- skip: float32 [4096], P('ch'), may hold values from -3 to 3
- prior_state: float32 [16, 4096], P(None, 'ch'), may hold values from -5 to 5
- out_weight: bfloat16 [4096, 4096], P('ch', 'seq'), may hold values from -0.375 to 0.375
- residual: bfloat16 [16384, 4096], P('seq', 'ch'), may hold values from -24 to 24
- norm_gain: float32 [4096], P('ch'), may hold values from 0.5 to 1.5
Outputs:
- hidden_out: bfloat16 [16384, 4096], P('seq', 'ch')
- normed: bfloat16 [16384, 4096], P('seq', 'ch')
The draws below stay inside these ranges and needn't reach their ends.
All inputs are finite; a program needn't handle non-finite values.
Results may differ from the reference program's by a relative error of at most 0.005.
Values may be sent and summed in bfloat16 or wider, within the bound.
A program may use at most 128 MiB of HBM per device.

```python
import math
import jax
import jax.numpy as jnp
from jax import lax

D = 4096
MODES = 16
TAPS = 3
TOKENS = 16384


def draw_residual(key, part):
    key = jax.random.fold_in(key, 11)
    first_key, second_key = jax.random.split(key)
    columns = jnp.arange(D, dtype=jnp.float32)
    scales = (0.5 + columns / D) * jnp.exp(jax.random.uniform(first_key, (D,), jnp.float32, -1.15, 1.15))
    base = jnp.clip(jax.random.normal(second_key, (TOKENS, D), jnp.float32), -5.0, 5.0)
    return (base * scales[None, :]).astype(jnp.bfloat16)


def strengthened(array, own_key, source, target, shards_of, factor):
    owner, partner = [(jnp.arange(array.shape[dim]) // (array.shape[dim] // shards_of)).reshape([-1 if axis == dim else 1 for axis in range(array.ndim)]) for dim in (source, target)]
    chosen = jax.random.permutation(own_key, shards_of)[partner]
    strong = (owner == chosen) | (owner == (partner + shards_of // 2) % shards_of)
    return jnp.where(strong, factor * array, array)


def block_scale(own_key, extent, cuts, low, high):
    loudness = 1.0
    for axis_at, parts in cuts:
        steps = jax.random.uniform(jax.random.fold_in(jax.random.fold_in(own_key, 6), axis_at), (parts,), jnp.float32, low / len(cuts), high / len(cuts))
        loudness = loudness * jnp.repeat(jnp.exp(steps), extent[axis_at] // parts).reshape((-1,) + (1,) * (len(extent) - 1 - axis_at))
    return loudness


def bell_draw(stream_key, extent, spread, reach, pieces=(), held_as=jnp.bfloat16):
    values = spread * jax.random.normal(stream_key, extent, jnp.float32)
    if pieces:
        values = values * block_scale(stream_key, extent, pieces, -0.22, 0.18)
    return jnp.clip(values, -reach, reach).astype(held_as)


def gaussian_with(key, extent, scale, limit, cuts, heavy, held_as=jnp.bfloat16):
    array = scale * jax.random.normal(key, extent, jnp.float32)
    if cuts:
        array = array * block_scale(key, extent, cuts, -0.22, 0.18)
    return jnp.clip(strengthened(array, jax.random.fold_in(key, 3), *heavy), -limit, limit).astype(held_as)


def setup_inputs(seed: int = 0) -> dict:
    arg_keys = jax.random.split(jax.random.key(seed), 12)
    q_stream = bell_draw(arg_keys[0], (TOKENS, D), 1.0, 6.0, ((0, 128), (1, 4)))
    k_stream = bell_draw(arg_keys[1], (TOKENS, D), 1.0, 6.0, ((0, 128), (1, 4)))
    v_stream = bell_draw(arg_keys[2], (TOKENS, D), 1.0, 6.0, ((0, 128), (1, 4)))
    short_filter = bell_draw(arg_keys[3], (3, TAPS, D), 0.6, 4.0, ((2, 4),), jnp.float32)
    rates = jnp.clip(jnp.exp(math.log(0.03) - 10.8026728 * jax.random.uniform(arg_keys[4], (MODES, D), jnp.float32) ** block_scale(arg_keys[4], (MODES, D), ((1, 4),), -0.2, 0.2)), 6.103515488575795e-07, 0.03)
    residues = bell_draw(arg_keys[5], (MODES, D), 0.35, 3.0, ((1, 4),), jnp.float32)
    skip = bell_draw(arg_keys[6], (D,), 0.5, 3.0, ((0, 4),), jnp.float32)
    prior_state = bell_draw(arg_keys[7], (MODES, D), 1.0, 5.0, ((1, 4),), jnp.float32)
    out_weight = gaussian_with(arg_keys[8], (D, D), D ** -0.5, 0.375, ((0, 4), (1, 128)), (0, 1, 128, 5.5))
    residual = draw_residual(jax.random.fold_in(arg_keys[11], 71), 0)
    norm_gain = jnp.clip(1.0 + 0.1 * jax.random.normal(arg_keys[10], (D,), jnp.float32), 0.5, 1.5)
    return dict(q_stream=q_stream, k_stream=k_stream, v_stream=v_stream, short_filter=short_filter, rates=rates, residues=residues, skip=skip, prior_state=prior_state, out_weight=out_weight, residual=residual, norm_gain=norm_gain)


def featurize(stream, tap_table):
    values = stream.astype(jnp.float32)
    padded = jnp.pad(values, ((TAPS - 1, 0), (0, 0)))
    result = jnp.zeros_like(values)
    for offset in range(TAPS):
        result = result + tap_table[offset][None, :] * padded[TAPS - 1 - offset:TAPS - 1 - offset + TOKENS]
    return result

def reference(q_stream, k_stream, v_stream, short_filter, rates, residues, skip, prior_state, out_weight, residual, norm_gain):
    feat_q = featurize(q_stream, short_filter[0])
    feat_k = featurize(k_stream, short_filter[1])
    feat_v = featurize(v_stream, short_filter[2])
    gated = feat_k * feat_v
    pole_value = jnp.exp(-rates)
    inflow = jnp.sqrt(-jnp.expm1(-2.0 * rates))

    def advance(carried, gated_row):
        carried = pole_value * carried + inflow * gated_row[None, :]
        return (carried, lax.optimization_barrier(jnp.sum(residues * carried, axis=0)))
    _, filtered = lax.scan(advance, prior_state.astype(jnp.float32), gated)
    mixer_out = (feat_q * (filtered + skip[None, :] * gated)).astype(jnp.bfloat16)
    summed = jnp.dot(mixer_out, out_weight, preferred_element_type=jnp.float32) + residual.astype(jnp.float32)
    mean_square = lax.optimization_barrier(jnp.mean(summed * summed, axis=1, keepdims=True))
    normed = (summed * lax.rsqrt(mean_square + 1e-05) * norm_gain[None, :]).astype(jnp.bfloat16)
    return (summed.astype(jnp.bfloat16), normed)
```

```python
import functools

import jax
import jax.numpy as jnp
from jax import lax
from jax.experimental import pallas as pl
from jax.experimental.pallas import tpu as pltpu
from jax.sharding import PartitionSpec as P

MESH = pl.DeviceIdType.MESH
F32 = jnp.float32
BF16 = jnp.bfloat16
NX, NY, NZ, NH = 4, 4, 16, 2
NJ = NY * NH
ROWS = 128
CHANS = 1024
LANES = 128
SUBS = 8
MODES = 16
BAND = CHANS // NX


def one_minus_exp(x):
    series = jnp.full_like(x, 1.0 / 8.0)
    for n in (7.0, 6.0, 5.0, 4.0, 3.0, 2.0):
        series = (1.0 - x * series) * (1.0 / n)
    return jnp.where(x < 0.25, x * (1.0 - x * series), 1.0 - jnp.exp(-x))


def kernel(
    q_ref, k_ref, v_ref, taps_ref, rates_ref, residues_ref, skip_ref, prior_ref, weight_ref, residual_ref, gain_ref,
    hidden_ref, normed_ref,
    streams, halo, gated, featq, filt, tap_rows, rate_rows, res_rows, prior_rows, pole_rows, inres_rows, inflow_rows,
    ends, plane_in, line_in, line_out, back_out, carry,
    weights, acts, far_out, far_in, near_out, near_in, near_part, own_part, back_rows, final_in, summed, stat_out, stat_in,
    halo_s, halo_r, s1_s, s1_r, s2_s, s2_r, s3_s, s3_r, ring_s, ring_r, sib_s, sib_r,
    act_s, act_r, fwd_s, fwd_r, far_s, far_r, near_s, near_r, fin_s, fin_r, stat_s, stat_r,
):
    seq, x = lax.axis_index("seq"), lax.axis_index("ch")
    z, j = seq // NJ, seq % NJ
    y, h = j // NH, j % NH

    def device(z_, j_, x_):
        return (z_ * NJ + j_, x_)

    def remote(src, dst, send, recv, target):
        return pltpu.make_async_remote_copy(
            src_ref=src, dst_ref=dst, send_sem=send, recv_sem=recv, device_id=target, device_id_type=MESH
        )

    def row(t):
        return pl.ds(pl.multiple_of(t * SUBS, SUBS), SUBS)

    barrier = pltpu.get_barrier_semaphore()

    def greet(target):
        pl.semaphore_signal(barrier, inc=1, device_id=target, device_id_type=MESH)

    @pl.loop(1, NJ)
    def _(d):
        greet(device(z, (j + d) % NJ, x))

    @pl.loop(1, NZ)
    def _(d):
        greet(device((z + d) % NZ, j, x))

    @pl.loop(1, NX)
    def _(d):
        greet(device(z, j, (x + d) % NX))

    has_next, has_prev = seq < NZ * NJ - 1, seq > 0
    first_j, last_j = j == 0, j == NJ - 1

    @pl.when(last_j)
    def _():
        greet(device((z + 1) % NZ, 0, x))

    @pl.when(first_j)
    def _():
        greet(device((z + NZ - 1) % NZ, NJ - 1, x))

    for stream, ref in enumerate((q_ref, k_ref, v_ref)):
        for part in range(SUBS):
            streams[stream, pl.ds(part, ROWS, stride=SUBS), :] = ref[:, part * LANES : (part + 1) * LANES].astype(F32)
    weights[row_block(z, h), :] = weight_ref[...]

    peers = NJ + NZ + NX - 3
    edge = jnp.logical_or(first_j, last_j)

    @pl.when(edge)
    def _():
        pl.semaphore_wait(barrier, peers + 1)

    @pl.when(jnp.logical_not(edge))
    def _():
        pl.semaphore_wait(barrier, peers)

    last = (ROWS - 2) * SUBS
    halo_copy = remote(
        streams.at[:, pl.ds(last, 2 * SUBS), :], halo, halo_s, halo_r, ((seq + 1) % (NZ * NJ), x)
    )

    @pl.when(has_next)
    def _():
        halo_copy.start()

    direction = 1 - 2 * h
    sibling = device(z, y * NH + 1 - h, x)
    ring_to = device((z + direction + NZ) % NZ, j, x)

    def ring_shard(step, part):
        return weights.at[row_block((z - direction * step + 2 * NZ) % NZ, (h + part) % 2), :]

    def ring_copy(step, part):
        shard = ring_shard(step, part)
        return remote(shard, shard, ring_s.at[2 * step + part], ring_r.at[2 * step + part], ring_to)

    def sib_copy(step, part):
        shard = ring_shard(step, part)
        return remote(shard, shard, sib_s.at[2 * step + part], sib_r.at[2 * step + part], sibling)

    upward = h == 0

    def ring_step(step):
        for part in range(2):
            if step == 0:
                if part == 0:
                    sib_copy(0, 0).start()
                    ring_copy(0, 0).start()
                else:
                    sib_copy(0, 0).wait_recv()
                    ring_copy(0, 1).start()
                continue
            if step < 8:
                ring_copy(step - 1, part).wait_recv()
                if step < 7:
                    ring_copy(step, part).start()
                else:
                    pl.when(upward)(ring_copy(step, part).start)
                sib_copy(step, part).start()
            else:

                @pl.when(upward)
                def _():
                    ring_copy(step - 1, part).wait_recv()
                    sib_copy(step, part).start()

    ring_step(0)

    for part in range(SUBS):
        cut = slice(part * LANES, (part + 1) * LANES)
        to = pl.ds(part, MODES, stride=SUBS)
        rate_rows[to, :] = rates_ref[:, cut]
        res_rows[to, :] = residues_ref[:, cut]
        prior_rows[to, :] = prior_ref[:, cut]
        for stream in range(3):
            for tap in range(3):
                n = (3 * stream + tap) * SUBS + part
                tap_rows[n : n + 1, :] = taps_ref[stream, tap : tap + 1, cut]
    rates = rate_rows[...]
    inflow = jnp.sqrt(one_minus_exp(2.0 * rates))
    pole_rows[...] = jnp.exp(-rates)
    inflow_rows[...] = inflow
    inres_rows[...] = res_rows[...] * inflow

    def modes_of(ref):
        return [ref[m * SUBS : (m + 1) * SUBS, :] for m in range(MODES)]

    taps = [tap_rows[n * SUBS : (n + 1) * SUBS, :] for n in range(9)]
    poles = modes_of(pole_rows)
    skip = skip_ref[...]

    def feature(stream, now, back1, back2):
        return taps[3 * stream] * now + taps[3 * stream + 1] * back1 + taps[3 * stream + 2] * back2

    def features(t, history):
        later, feats = [], []
        for stream, (back1, back2) in enumerate(history):
            now = streams[stream, row(t), :]
            feats.append(feature(stream, now, back1, back2))
            later.append((now, back1))
        gated_now = feats[1] * feats[2]
        gated[row(t), :] = gated_now
        featq[row(t), :] = feats[0]
        return gated_now, tuple(later)

    def advance(states, value):
        return tuple(pole * state + value for pole, state in zip(poles, states))

    history = tuple((streams[s, SUBS : 2 * SUBS, :], streams[s, 0:SUBS, :]) for s in range(3))
    states = tuple(jnp.zeros((SUBS, LANES), F32) for _ in range(MODES))

    def scan_step(t, carried):
        states, history = carried
        value, history = features(t, history)
        return advance(states, value), history

    states, history = lax.fori_loop(2, ROWS, scan_step, (states, history), unroll=6)

    @pl.when(has_prev)
    def _():
        halo_copy.wait_recv()

    @pl.when(jnp.logical_not(has_prev))
    def _():
        halo[...] = jnp.zeros_like(halo)

    history = tuple((halo[s, SUBS : 2 * SUBS, :], halo[s, 0:SUBS, :]) for s in range(3))
    first, history = features(0, history)
    second, history = features(1, history)
    for m in range(MODES):
        at = slice(m * SUBS, (m + 1) * SUBS)
        late = jnp.exp(-(ROWS - 2.0) * rate_rows[at, :])
        ends[at, :] = inflow_rows[at, :] * (states[m] + late * (poles[m] * first + second))

    pair = 2 * SUBS

    def pair_rows(n):
        return pl.ds(pl.multiple_of(n * pair, pair), pair)

    def to_owner(d):
        to = (j + d) % NJ
        return remote(ends.at[pair_rows(to), :], plane_in.at[j], s1_s.at[d], s1_r.at[d], device(z, to, x))

    def along_line(d):
        return remote(line_out, line_in.at[z], s2_s.at[d], s2_r.at[d], device((z + d) % NZ, j, x))

    def from_owner(d):
        to = (j + d) % NJ
        return remote(back_out.at[to], carry.at[pair_rows(j), :], s3_s.at[d], s3_r.at[d], device(z, to, x))

    @pl.loop(1, NJ)
    def _(d):
        to_owner(d).start()

    plane_in[j] = ends[pair_rows(j), :]
    ring_step(1)

    inres = modes_of(inres_rows)

    def output_step(t, states):
        value = gated[row(t), :]
        states = advance(states, value)
        terms = [r * s for r, s in zip(inres, states)] + [skip * value]
        filt[row(t), :] = tree_sum(terms)
        return states

    states = tuple(jnp.zeros((SUBS, LANES), F32) for _ in range(MODES))
    states = lax.fori_loop(0, 64, output_step, states, unroll=4)

    @pl.loop(1, NJ)
    def _(d):
        to_owner(d).wait_recv()

    my_rates = rate_rows[pair_rows(j), :]
    block_decay = jnp.exp(-float(ROWS) * my_rates)
    plane_decay = jnp.exp(-float(ROWS * NJ) * my_rates)
    total = plane_in[0]
    for i in range(1, NJ):
        total = block_decay * total + plane_in[i]
    line_out[...] = total

    @pl.loop(1, NZ - z)
    def _(d):
        along_line(d).start()

    ring_step(2)
    lax.fori_loop(64, ROWS, output_step, states, unroll=4)
    ring_step(3)

    @pl.loop(1, z + 1)
    def _(d):
        along_line(d).wait_recv()

    incoming = lax.fori_loop(0, z, lambda i, s: plane_decay * s + line_in[i], prior_rows[pair_rows(j), :])
    for i in range(NJ):
        back_out[i] = incoming
        incoming = block_decay * incoming + plane_in[i]

    @pl.loop(1, NJ)
    def _(d):
        from_owner(d).start()

    carry[pair_rows(j), :] = back_out[j]
    ring_step(4)

    @pl.loop(1, NJ)
    def _(d):
        from_owner(d).wait_recv()

    half = ROWS // 2
    up = device(z, ((y + 1) % NY) * NH + h, x)
    down = device(z, ((y + 3) % NY) * NH + h, x)
    across = device(z, ((y + 2) % NY) * NH + h, x)

    def act_copy(part, side):
        cut = pl.ds(part * half, half)
        n = 2 * part + side
        return remote(acts.at[0, cut, :], acts.at[1 + side, cut, :], act_s.at[n], act_r.at[n], (up, down)[side])

    def fwd_copy(part):
        cut = pl.ds(part * half, half)
        return remote(acts.at[1 + part, cut, :], acts.at[3, cut, :], fwd_s.at[part], fwd_r.at[part], (up, down)[part])

    def carried_step(t, waves):
        waves = tuple(pole * wave for pole, wave in zip(poles, waves))
        filt[row(t), :] = featq[row(t), :] * (filt[row(t), :] + tree_sum(list(waves)))
        return waves

    waves = tuple(res_rows[m * SUBS : (m + 1) * SUBS, :] * carry[m * SUBS : (m + 1) * SUBS, :] for m in range(MODES))
    for part in range(2):
        waves = lax.fori_loop(part * half, (part + 1) * half, carried_step, waves, unroll=4)
        for sub in range(SUBS):
            from_rows = pl.ds(part * half * SUBS + sub, half, stride=SUBS)
            acts[0, part * half : (part + 1) * half, sub * LANES : (sub + 1) * LANES] = filt[from_rows, :].astype(BF16)
        act_copy(part, 0).start()
        act_copy(part, 1).start()

    for step in range(5, 9):
        ring_step(step)
    for step in range(8):
        for part in range(2):
            if step == 0 and part == 0:
                continue
            if step > 0:
                sib_copy(step, part).wait_recv()

    @pl.when(jnp.logical_not(upward))
    def _():
        for part in range(2):
            sib_copy(8, part).wait_recv()

    right, left = device(z, j, (x + 1) % NX), device(z, j, (x + 3) % NX)
    sides = (right, left)

    def product(block, dx):
        band = weights[pl.ds(pl.multiple_of(((x + dx) % NX) * BAND, BAND), BAND), :]
        return lax.dot_general(acts[block], band, (((1,), (1,)), ((), ())), preferred_element_type=F32)

    def far_copy(block, side):
        n = 2 * block + side
        return remote(far_out.at[n], far_in.at[n], far_s.at[n], far_r.at[n], sides[side])

    def near_copy(block, side):
        n = 2 * block + side
        return remote(near_out.at[n], near_in.at[n], near_s.at[n], near_r.at[n], sides[side])

    def begin(block):
        far = product(block, 2).astype(BF16)
        for side in range(2):
            far_out[2 * block + side] = far[:, side * LANES : (side + 1) * LANES]
            far_copy(block, side).start()
        near_part[2 * (block % 2)] = product(block, 1)
        near_part[2 * (block % 2) + 1] = product(block, 3)
        own_part[block] = product(block, 0)

    def middle(block):
        for side in range(2):
            n = 2 * block + side
            cut = slice(side * LANES, (side + 1) * LANES)
            rest = slice((1 - side) * LANES, (2 - side) * LANES)
            far_copy(block, side).wait_recv()
            part = near_part.at[2 * (block % 2) + side]
            near_out[n, :, cut] = (part[:, cut] + far_in[n].astype(F32)).astype(BF16)
            near_out[n, :, rest] = part[:, rest].astype(BF16)
            near_copy(block, side).start()

    def fin_copy(block):
        to = (None, down, up, across)[block]
        return remote(back_rows.at[block - 1], final_in.at[y], fin_s.at[block - 1], fin_r.at[block - 1], to)

    def finish(block):
        for side in range(2):
            near_copy(block, side).wait_recv()
        value = own_part[block] + near_in[2 * block].astype(F32) + near_in[2 * block + 1].astype(F32)
        if block == 0:
            final_in[y] = value.astype(BF16)
        else:
            back_rows[block - 1] = value.astype(BF16)
            fin_copy(block).start()

    begin(0)
    for part in range(2):
        act_copy(part, part).wait_recv()
        fwd_copy(part).start()
    act_copy(1, 0).wait_recv()
    act_copy(0, 1).wait_recv()
    begin(1)
    middle(0)
    begin(2)
    middle(1)
    finish(0)
    for part in range(2):
        fwd_copy(part).wait_recv()
    begin(3)
    middle(2)
    finish(1)
    middle(3)
    finish(2)
    finish(3)
    for block in range(1, 4):
        fin_copy(block).wait_recv()

    low = lax.broadcasted_iota(jnp.int32, (ROWS, LANES), 1) < LANES // 2
    squares = jnp.zeros((ROWS, LANES), F32)
    for tile in range(SUBS):
        cut = slice(tile * LANES, (tile + 1) * LANES)
        group, odd = tile // 4, (tile // 2) % 2
        from_cut = slice(group * LANES, (group + 1) * LANES)
        even_y = final_in[2 * (tile % 2), :, from_cut].astype(F32)
        odd_y = final_in[2 * (tile % 2) + 1, :, from_cut].astype(F32)
        if odd:
            even_y = pltpu.roll(even_y, LANES // 2, 1)
        else:
            odd_y = pltpu.roll(odd_y, LANES // 2, 1)
        value = residual_ref[:, cut].astype(F32) + jnp.where(low, even_y, odd_y)
        summed[:, cut] = value
        hidden_ref[:, cut] = value.astype(BF16)
        squares = squares + value * value
    mine = jnp.sum(squares.T, axis=0, keepdims=True)
    stat_out[...] = jnp.broadcast_to(mine, (SUBS, LANES))

    def stat_copy(d):
        return remote(stat_out, stat_in.at[d - 1], stat_s.at[d - 1], stat_r.at[d - 1], device(z, j, (x + d) % NX))

    for d in range(1, NX):
        stat_copy(d).start()
    for d in range(1, NX):
        stat_copy(d).wait_recv()
    total = stat_out[...] + stat_in[0] + stat_in[1] + stat_in[2]
    scale = lax.rsqrt(total * (1.0 / (NX * CHANS)) + 1e-05)
    scale = jnp.broadcast_to(scale[0:1, :], (ROWS, LANES)).T
    for tile in range(SUBS):
        cut = slice(tile * LANES, (tile + 1) * LANES)
        normed_ref[:, cut] = (summed[:, cut] * scale * gain_ref[tile : tile + 1, :]).astype(BF16)

    pl.when(has_next)(halo_copy.wait_send)

    @pl.loop(1, NJ)
    def _(d):
        to_owner(d).wait_send()
        from_owner(d).wait_send()

    @pl.loop(1, NZ - z)
    def _(d):
        along_line(d).wait_send()

    for part in range(2):
        for step in range(7):
            ring_copy(step, part).wait_send()
        pl.when(upward)(ring_copy(7, part).wait_send)
        for step in range(8):
            if step > 0 or part == 0:
                sib_copy(step, part).wait_send()
        pl.when(upward)(sib_copy(8, part).wait_send)
        for side in range(2):
            act_copy(part, side).wait_send()
        fwd_copy(part).wait_send()
    for block in range(4):
        for side in range(2):
            far_copy(block, side).wait_send()
            near_copy(block, side).wait_send()
    for block in range(1, 4):
        fin_copy(block).wait_send()
    for d in range(1, NX):
        stat_copy(d).wait_send()


def row_block(z, h):
    return pl.ds(pl.multiple_of(z * 64 + h * 32, 32), 32)


def tree_sum(terms):
    while len(terms) > 1:
        rest = [terms[-1]] if len(terms) % 2 else []
        terms = [a + b for a, b in zip(terms[0::2], terms[1::2])] + rest
    return terms[0]


def local(
    q_stream, k_stream, v_stream, short_filter, rates, residues, skip, prior_state, out_weight, residual, norm_gain
):
    vmem = pl.BlockSpec(memory_space=pltpu.VMEM)
    dma = pltpu.SemaphoreType.DMA
    wide = (ROWS * SUBS, LANES)
    params = (MODES * SUBS, LANES)
    pair = (2 * SUBS, LANES)
    scratch = [
        pltpu.VMEM((3,) + wide, F32),
        pltpu.VMEM((3, 2 * SUBS, LANES), F32),
        pltpu.VMEM(wide, F32),
        pltpu.VMEM(wide, F32),
        pltpu.VMEM(wide, F32),
        pltpu.VMEM((9 * SUBS, LANES), F32),
        pltpu.VMEM(params, F32),
        pltpu.VMEM(params, F32),
        pltpu.VMEM(params, F32),
        pltpu.VMEM(params, F32),
        pltpu.VMEM(params, F32),
        pltpu.VMEM(params, F32),
        pltpu.VMEM(params, F32),
        pltpu.VMEM((NJ,) + pair, F32),
        pltpu.VMEM((NZ,) + pair, F32),
        pltpu.VMEM(pair, F32),
        pltpu.VMEM((NJ,) + pair, F32),
        pltpu.VMEM(params, F32),
        pltpu.VMEM((CHANS, CHANS), BF16),
        pltpu.VMEM((NY, ROWS, CHANS), BF16),
        pltpu.VMEM((8, ROWS, LANES), BF16),
        pltpu.VMEM((8, ROWS, LANES), BF16),
        pltpu.VMEM((8, ROWS, BAND), BF16),
        pltpu.VMEM((8, ROWS, BAND), BF16),
        pltpu.VMEM((4, ROWS, BAND), F32),
        pltpu.VMEM((NY, ROWS, BAND), F32),
        pltpu.VMEM((NY - 1, ROWS, BAND), BF16),
        pltpu.VMEM((NY, ROWS, BAND), BF16),
        pltpu.VMEM((ROWS, CHANS), F32),
        pltpu.VMEM((SUBS, LANES), F32),
        pltpu.VMEM((NX - 1, SUBS, LANES), F32),
    ]
    sems = []
    for count in (0, NJ, NZ, NJ, 16, 18, 4, 2, 8, 8, NY - 1, NX - 1):
        sems += [dma(()), dma(())] if count == 0 else [dma((count,)), dma((count,))]
    return pl.pallas_call(
        kernel,
        out_shape=(jax.ShapeDtypeStruct((ROWS, CHANS), BF16), jax.ShapeDtypeStruct((ROWS, CHANS), BF16)),
        in_specs=[vmem] * 11,
        out_specs=(vmem, vmem),
        scratch_shapes=scratch + sems,
        compiler_params=pltpu.CompilerParams(
            collective_id=0, has_side_effects=True, vmem_limit_bytes=40 * 1024 * 1024
        ),
        name="mixer",
    )(
        q_stream, k_stream, v_stream, short_filter, rates, residues, skip.reshape(SUBS, LANES), prior_state,
        out_weight.T, residual, norm_gain.reshape(SUBS, LANES),
    )


def solution(mesh):
    placed = (
        P("seq", "ch"),
        P("seq", "ch"),
        P("seq", "ch"),
        P(None, None, "ch"),
        P(None, "ch"),
        P(None, "ch"),
        P("ch"),
        P(None, "ch"),
        P("ch", "seq"),
        P("seq", "ch"),
        P("ch"),
    )
    return jax.shard_map(
        local,
        mesh=mesh,
        in_specs=placed,
        out_specs=(P("seq", "ch"), P("seq", "ch")),
        check_vma=False,
    )
```

```python
import functools

import jax
import jax.numpy as jnp
from jax import lax
from jax.experimental import pallas as pl
from jax.experimental.pallas import tpu as pltpu
from jax.sharding import PartitionSpec as P

MESH = pl.DeviceIdType.MESH
F32 = jnp.float32
BF16 = jnp.bfloat16
NX, NY, NZ, NH = 4, 4, 16, 2
NJ = NY * NH
ROWS = 128
CHANS = 1024
LANES = 128
SUBS = 8
MODES = 16
BAND = CHANS // NX


def one_minus_exp(x):
    series = jnp.full_like(x, 1.0 / 8.0)
    for n in (7.0, 6.0, 5.0, 4.0, 3.0, 2.0):
        series = (1.0 - x * series) * (1.0 / n)
    return jnp.where(x < 0.25, x * (1.0 - x * series), 1.0 - jnp.exp(-x))


def kernel(
    q_hbm, k_hbm, v_hbm, taps_hbm, rates_hbm, residues_hbm, skip_hbm, prior_hbm, weight_hbm, residual_hbm, gain_hbm,
    hidden_ref, normed_ref,
    q_ref, k_ref, v_ref, taps_ref, rates_ref, residues_ref, skip_ref, prior_ref, residual_ref, gain_ref,
    streams, halo, gated, featq, filt, tap_rows, rate_rows, res_rows, prior_rows, pole_rows, inres_rows, inflow_rows,
    ends, plane_in, line_in, line_out, back_out, carry,
    weights, acts, far_out, far_in, near_out, near_in, near_part, own_part, back_rows, final_in, summed, stat_out, stat_in,
    input_s, halo_s, halo_r, s1_s, s1_r, s2_s, s2_r, s3_s, s3_r, ring_s, ring_r, sib_s, sib_r,
    act_s, act_r, fwd_s, fwd_r, far_s, far_r, near_s, near_r, fin_s, fin_r, stat_s, stat_r,
):
    seq, x = lax.axis_index("seq"), lax.axis_index("ch")
    z, j = seq // NJ, seq % NJ
    y, h = j // NH, j % NH

    def device(z_, j_, x_):
        return (z_ * NJ + j_, x_)

    def remote(src, dst, send, recv, target):
        return pltpu.make_async_remote_copy(
            src_ref=src, dst_ref=dst, send_sem=send, recv_sem=recv, device_id=target, device_id_type=MESH
        )

    def row(t):
        return pl.ds(pl.multiple_of(t * SUBS, SUBS), SUBS)

    own_weights = weights.at[row_block(z, h), :]
    inputs = [
        pltpu.make_async_copy(src, dst, input_s.at[n])
        for n, (src, dst) in enumerate((
            (k_hbm, k_ref), (v_hbm, v_ref), (q_hbm, q_ref), (weight_hbm, own_weights), (rates_hbm, rates_ref),
            (taps_hbm, taps_ref), (residues_hbm, residues_ref), (prior_hbm, prior_ref), (skip_hbm, skip_ref),
            (residual_hbm, residual_ref), (gain_hbm, gain_ref),
        ))
    ]
    for copy in inputs:
        copy.start()

    barrier = pltpu.get_barrier_semaphore()

    def greet(target):
        pl.semaphore_signal(barrier, inc=1, device_id=target, device_id_type=MESH)

    @pl.loop(1, NJ)
    def _(d):
        greet(device(z, (j + d) % NJ, x))

    @pl.loop(1, NZ)
    def _(d):
        greet(device((z + d) % NZ, j, x))

    @pl.loop(1, NX)
    def _(d):
        greet(device(z, j, (x + d) % NX))

    has_next, has_prev = seq < NZ * NJ - 1, seq > 0
    first_j, last_j = j == 0, j == NJ - 1

    @pl.when(last_j)
    def _():
        greet(device((z + 1) % NZ, 0, x))

    @pl.when(first_j)
    def _():
        greet(device((z + NZ - 1) % NZ, NJ - 1, x))

    peers = NJ + NZ + NX - 3
    edge = jnp.logical_or(first_j, last_j)

    @pl.when(edge)
    def _():
        pl.semaphore_wait(barrier, peers + 1)

    @pl.when(jnp.logical_not(edge))
    def _():
        pl.semaphore_wait(barrier, peers)

    direction = 1 - 2 * h
    sibling = device(z, y * NH + 1 - h, x)
    ring_to = device((z + direction + NZ) % NZ, j, x)

    def ring_shard(step, part):
        return weights.at[row_block((z - direction * step + 2 * NZ) % NZ, (h + part) % 2), :]

    def ring_copy(step, part):
        shard = ring_shard(step, part)
        src = weight_hbm if (step, part) == (0, 0) else shard
        return remote(src, shard, ring_s.at[2 * step + part], ring_r.at[2 * step + part], ring_to)

    def sib_copy(step, part):
        shard = ring_shard(step, part)
        src = weight_hbm if step == 0 else shard
        return remote(src, shard, sib_s.at[2 * step + part], sib_r.at[2 * step + part], sibling)

    upward = h == 0

    def ring_step(step):
        for part in range(2):
            if step < 8:
                ring_copy(step - 1, part).wait_recv()
                if step < 7:
                    ring_copy(step, part).start()
                else:
                    pl.when(upward)(ring_copy(step, part).start)
                sib_copy(step, part).start()
            else:

                @pl.when(upward)
                def _():
                    ring_copy(step - 1, part).wait_recv()
                    sib_copy(step, part).start()

    ring_copy(0, 0).start()
    sib_copy(0, 0).start()

    def convert(stream, ref, begin, end):
        for part in range(SUBS):
            to = pl.ds(begin * SUBS + part, end - begin, stride=SUBS)
            streams[stream, to, :] = ref[begin:end, part * LANES : (part + 1) * LANES].astype(F32)

    for n in range(3):
        inputs[n].wait()
    for stream, ref in enumerate((q_ref, k_ref, v_ref)):
        convert(stream, ref, ROWS - 16, ROWS)
    last = (ROWS - 2) * SUBS
    halo_copy = remote(
        streams.at[:, pl.ds(last, 2 * SUBS), :], halo, halo_s, halo_r, ((seq + 1) % (NZ * NJ), x)
    )
    pl.when(has_next)(halo_copy.start)
    convert(1, k_ref, 0, ROWS - 16)
    sib_copy(0, 0).wait_recv()
    ring_copy(0, 1).start()
    convert(2, v_ref, 0, ROWS - 16)
    for n in range(3, len(inputs)):
        inputs[n].wait()

    for part in range(SUBS):
        cut = slice(part * LANES, (part + 1) * LANES)
        to = pl.ds(part, MODES, stride=SUBS)
        rate_rows[to, :] = rates_ref[:, cut]
        res_rows[to, :] = residues_ref[:, cut]
        prior_rows[to, :] = prior_ref[:, cut]
        for stream in range(3):
            for tap in range(3):
                n = (3 * stream + tap) * SUBS + part
                tap_rows[n : n + 1, :] = taps_ref[stream, tap : tap + 1, cut]
    rates = rate_rows[...]
    inflow = jnp.sqrt(one_minus_exp(2.0 * rates))
    pole_rows[...] = jnp.exp(-rates)
    inflow_rows[...] = inflow
    inres_rows[...] = res_rows[...] * inflow

    def modes_of(ref):
        return [ref[m * SUBS : (m + 1) * SUBS, :] for m in range(MODES)]

    taps = [tap_rows[n * SUBS : (n + 1) * SUBS, :] for n in range(9)]
    poles = modes_of(pole_rows)
    skip = skip_ref[...]

    def feature(stream, now, back1, back2):
        return taps[3 * stream] * now + taps[3 * stream + 1] * back1 + taps[3 * stream + 2] * back2

    def gate(t, history):
        later, feats = [], []
        for stream, (back1, back2) in zip((1, 2), history):
            now = streams[stream, row(t), :]
            feats.append(feature(stream, now, back1, back2))
            later.append((now, back1))
        value = feats[0] * feats[1]
        gated[row(t), :] = value
        return value, tuple(later)

    def advance(states, value):
        return tuple(pole * state + value for pole, state in zip(poles, states))

    ring_step(1)

    history = tuple((streams[s, SUBS : 2 * SUBS, :], streams[s, 0:SUBS, :]) for s in (1, 2))
    states = tuple(jnp.zeros((SUBS, LANES), F32) for _ in range(MODES))

    def scan_step(t, carried):
        states, history = carried
        value, history = gate(t, history)
        return advance(states, value), history

    scan = lax.fori_loop(2, 65, scan_step, (states, history), unroll=7)
    ring_step(2)
    states, history = lax.fori_loop(65, ROWS, scan_step, scan, unroll=7)

    @pl.when(has_prev)
    def _():
        halo_copy.wait_recv()

    @pl.when(jnp.logical_not(has_prev))
    def _():
        halo[...] = jnp.zeros_like(halo)

    def halo_rows(s):
        return halo[s, SUBS : 2 * SUBS, :], halo[s, 0:SUBS, :]

    first, history = gate(0, (halo_rows(1), halo_rows(2)))
    second, history = gate(1, history)
    for m in range(MODES):
        at = slice(m * SUBS, (m + 1) * SUBS)
        late = jnp.exp(-(ROWS - 2.0) * rate_rows[at, :])
        ends[at, :] = inflow_rows[at, :] * (states[m] + late * (poles[m] * first + second))

    pair = 2 * SUBS

    def pair_rows(n):
        return pl.ds(pl.multiple_of(n * pair, pair), pair)

    def to_owner(d):
        to = (j + d) % NJ
        return remote(ends.at[pair_rows(to), :], plane_in.at[j], s1_s.at[d], s1_r.at[d], device(z, to, x))

    def along_line(d):
        return remote(line_out, line_in.at[z], s2_s.at[d], s2_r.at[d], device((z + d) % NZ, j, x))

    def from_owner(d):
        to = (j + d) % NJ
        return remote(back_out.at[to], carry.at[pair_rows(j), :], s3_s.at[d], s3_r.at[d], device(z, to, x))

    @pl.loop(1, NJ)
    def _(d):
        to_owner(d).start()

    plane_in[j] = ends[pair_rows(j), :]
    ring_step(3)

    inres = modes_of(inres_rows)

    def output_step(t, carried):
        states, (back1, back2) = carried
        now = streams[0, row(t), :]
        featq[row(t), :] = feature(0, now, back1, back2)
        value = gated[row(t), :]
        states = advance(states, value)
        terms = [r * s for r, s in zip(inres, states)] + [skip * value]
        filt[row(t), :] = tree_sum(terms)
        return states, (now, back1)

    convert(0, q_ref, 0, ROWS - 16)
    states = tuple(jnp.zeros((SUBS, LANES), F32) for _ in range(MODES))
    outputs = lax.fori_loop(0, 64, output_step, (states, halo_rows(0)), unroll=4)

    @pl.loop(1, NJ)
    def _(d):
        to_owner(d).wait_recv()

    my_rates = rate_rows[pair_rows(j), :]
    block_decay = jnp.exp(-float(ROWS) * my_rates)
    plane_decay = jnp.exp(-float(ROWS * NJ) * my_rates)
    total = plane_in[0]
    for i in range(1, NJ):
        total = block_decay * total + plane_in[i]
    line_out[...] = total

    @pl.loop(1, NZ - z)
    def _(d):
        along_line(d).start()

    ring_step(4)
    lax.fori_loop(64, ROWS, output_step, outputs, unroll=4)
    ring_step(5)

    @pl.loop(1, z + 1)
    def _(d):
        along_line(d).wait_recv()

    incoming = lax.fori_loop(0, z, lambda i, s: plane_decay * s + line_in[i], prior_rows[pair_rows(j), :])
    for i in range(NJ):
        back_out[i] = incoming
        incoming = block_decay * incoming + plane_in[i]

    @pl.loop(1, NJ)
    def _(d):
        from_owner(d).start()

    carry[pair_rows(j), :] = back_out[j]
    ring_step(6)

    @pl.loop(1, NJ)
    def _(d):
        from_owner(d).wait_recv()

    half = ROWS // 2
    up = device(z, ((y + 1) % NY) * NH + h, x)
    down = device(z, ((y + 3) % NY) * NH + h, x)
    across = device(z, ((y + 2) % NY) * NH + h, x)

    def act_copy(part, side):
        cut = pl.ds(part * half, half)
        n = 2 * part + side
        return remote(acts.at[0, cut, :], acts.at[1 + side, cut, :], act_s.at[n], act_r.at[n], (up, down)[side])

    def fwd_copy(part):
        cut = pl.ds(part * half, half)
        return remote(acts.at[1 + part, cut, :], acts.at[3, cut, :], fwd_s.at[part], fwd_r.at[part], (up, down)[part])

    def carried_step(t, waves):
        waves = tuple(pole * wave for pole, wave in zip(poles, waves))
        filt[row(t), :] = featq[row(t), :] * (filt[row(t), :] + tree_sum(list(waves)))
        return waves

    waves = tuple(res_rows[m * SUBS : (m + 1) * SUBS, :] * carry[m * SUBS : (m + 1) * SUBS, :] for m in range(MODES))
    for part in range(2):
        waves = lax.fori_loop(part * half, (part + 1) * half, carried_step, waves, unroll=4)
        for sub in range(SUBS):
            from_rows = pl.ds(part * half * SUBS + sub, half, stride=SUBS)
            acts[0, part * half : (part + 1) * half, sub * LANES : (sub + 1) * LANES] = filt[from_rows, :].astype(BF16)
        act_copy(part, 0).start()
        act_copy(part, 1).start()
        ring_step(7 + part)

    for step in range(8):
        for part in range(2):
            if step == 0 and part == 0:
                continue
            if step > 0:
                sib_copy(step, part).wait_recv()

    @pl.when(jnp.logical_not(upward))
    def _():
        for part in range(2):
            sib_copy(8, part).wait_recv()

    right, left = device(z, j, (x + 1) % NX), device(z, j, (x + 3) % NX)
    sides = (right, left)

    def product(block, dx):
        band = weights[pl.ds(pl.multiple_of(((x + dx) % NX) * BAND, BAND), BAND), :]
        return lax.dot_general(acts[block], band, (((1,), (1,)), ((), ())), preferred_element_type=F32)

    def far_copy(block, side):
        n = 2 * block + side
        return remote(far_out.at[n], far_in.at[n], far_s.at[n], far_r.at[n], sides[side])

    def near_copy(block, side):
        n = 2 * block + side
        return remote(near_out.at[n], near_in.at[n], near_s.at[n], near_r.at[n], sides[side])

    def begin(block):
        far = product(block, 2).astype(BF16)
        for side in range(2):
            far_out[2 * block + side] = far[:, side * LANES : (side + 1) * LANES]
            far_copy(block, side).start()
        near_part[2 * (block % 2)] = product(block, 1)
        near_part[2 * (block % 2) + 1] = product(block, 3)
        own_part[block] = product(block, 0)

    def middle(block):
        for side in range(2):
            n = 2 * block + side
            cut = slice(side * LANES, (side + 1) * LANES)
            rest = slice((1 - side) * LANES, (2 - side) * LANES)
            far_copy(block, side).wait_recv()
            part = near_part.at[2 * (block % 2) + side]
            near_out[n, :, cut] = (part[:, cut] + far_in[n].astype(F32)).astype(BF16)
            near_out[n, :, rest] = part[:, rest].astype(BF16)
            near_copy(block, side).start()

    def fin_copy(block):
        to = (None, down, up, across)[block]
        return remote(back_rows.at[block - 1], final_in.at[y], fin_s.at[block - 1], fin_r.at[block - 1], to)

    def finish(block):
        for side in range(2):
            near_copy(block, side).wait_recv()
        value = own_part[block] + near_in[2 * block].astype(F32) + near_in[2 * block + 1].astype(F32)
        if block == 0:
            final_in[y] = value.astype(BF16)
        else:
            back_rows[block - 1] = value.astype(BF16)
            fin_copy(block).start()

    begin(0)
    for part in range(2):
        act_copy(part, part).wait_recv()
        fwd_copy(part).start()
    act_copy(1, 0).wait_recv()
    act_copy(0, 1).wait_recv()
    begin(1)
    middle(0)
    begin(2)
    middle(1)
    finish(0)
    for part in range(2):
        fwd_copy(part).wait_recv()
    begin(3)
    middle(2)
    finish(1)
    middle(3)
    finish(2)
    finish(3)
    for block in range(1, 4):
        fin_copy(block).wait_recv()

    low = lax.broadcasted_iota(jnp.int32, (ROWS, LANES), 1) < LANES // 2
    squares = jnp.zeros((ROWS, LANES), F32)
    for tile in range(SUBS):
        cut = slice(tile * LANES, (tile + 1) * LANES)
        group, odd = tile // 4, (tile // 2) % 2
        from_cut = slice(group * LANES, (group + 1) * LANES)
        even_y = final_in[2 * (tile % 2), :, from_cut].astype(F32)
        odd_y = final_in[2 * (tile % 2) + 1, :, from_cut].astype(F32)
        if odd:
            even_y = pltpu.roll(even_y, LANES // 2, 1)
        else:
            odd_y = pltpu.roll(odd_y, LANES // 2, 1)
        value = residual_ref[:, cut].astype(F32) + jnp.where(low, even_y, odd_y)
        summed[:, cut] = value
        hidden_ref[:, cut] = value.astype(BF16)
        squares = squares + value * value
    mine = jnp.sum(squares.T, axis=0, keepdims=True)
    stat_out[...] = jnp.broadcast_to(mine, (SUBS, LANES))

    def stat_copy(d):
        return remote(stat_out, stat_in.at[d - 1], stat_s.at[d - 1], stat_r.at[d - 1], device(z, j, (x + d) % NX))

    for d in range(1, NX):
        stat_copy(d).start()
    for d in range(1, NX):
        stat_copy(d).wait_recv()
    total = stat_out[...] + stat_in[0] + stat_in[1] + stat_in[2]
    scale = lax.rsqrt(total * (1.0 / (NX * CHANS)) + 1e-05)
    scale = jnp.broadcast_to(scale[0:1, :], (ROWS, LANES)).T
    for tile in range(SUBS):
        cut = slice(tile * LANES, (tile + 1) * LANES)
        normed_ref[:, cut] = (summed[:, cut] * scale * gain_ref[tile : tile + 1, :]).astype(BF16)

    pl.when(has_next)(halo_copy.wait_send)

    @pl.loop(1, NJ)
    def _(d):
        to_owner(d).wait_send()
        from_owner(d).wait_send()

    @pl.loop(1, NZ - z)
    def _(d):
        along_line(d).wait_send()

    for part in range(2):
        for step in range(7):
            ring_copy(step, part).wait_send()
        pl.when(upward)(ring_copy(7, part).wait_send)
        for step in range(8):
            if step > 0 or part == 0:
                sib_copy(step, part).wait_send()
        pl.when(upward)(sib_copy(8, part).wait_send)
        for side in range(2):
            act_copy(part, side).wait_send()
        fwd_copy(part).wait_send()
    for block in range(4):
        for side in range(2):
            far_copy(block, side).wait_send()
            near_copy(block, side).wait_send()
    for block in range(1, 4):
        fin_copy(block).wait_send()
    for d in range(1, NX):
        stat_copy(d).wait_send()


def row_block(z, h):
    return pl.ds(pl.multiple_of(z * 64 + h * 32, 32), 32)


def tree_sum(terms):
    while len(terms) > 1:
        rest = [terms[-1]] if len(terms) % 2 else []
        terms = [a + b for a, b in zip(terms[0::2], terms[1::2])] + rest
    return terms[0]


def local(
    q_stream, k_stream, v_stream, short_filter, rates, residues, skip, prior_state, out_weight, residual, norm_gain
):
    vmem = pl.BlockSpec(memory_space=pltpu.VMEM)
    hbm = pl.BlockSpec(memory_space=pltpu.HBM)
    dma = pltpu.SemaphoreType.DMA
    wide = (ROWS * SUBS, LANES)
    params = (MODES * SUBS, LANES)
    pair = (2 * SUBS, LANES)
    rows = (ROWS, CHANS)
    scratch = [
        pltpu.VMEM(rows, BF16),
        pltpu.VMEM(rows, BF16),
        pltpu.VMEM(rows, BF16),
        pltpu.VMEM(short_filter.shape, F32),
        pltpu.VMEM((MODES, CHANS), F32),
        pltpu.VMEM((MODES, CHANS), F32),
        pltpu.VMEM((SUBS, LANES), F32),
        pltpu.VMEM((MODES, CHANS), F32),
        pltpu.VMEM(rows, BF16),
        pltpu.VMEM((SUBS, LANES), F32),
        pltpu.VMEM((3,) + wide, F32),
        pltpu.VMEM((3, 2 * SUBS, LANES), F32),
        pltpu.VMEM(wide, F32),
        pltpu.VMEM(wide, F32),
        pltpu.VMEM(wide, F32),
        pltpu.VMEM((9 * SUBS, LANES), F32),
        pltpu.VMEM(params, F32),
        pltpu.VMEM(params, F32),
        pltpu.VMEM(params, F32),
        pltpu.VMEM(params, F32),
        pltpu.VMEM(params, F32),
        pltpu.VMEM(params, F32),
        pltpu.VMEM(params, F32),
        pltpu.VMEM((NJ,) + pair, F32),
        pltpu.VMEM((NZ,) + pair, F32),
        pltpu.VMEM(pair, F32),
        pltpu.VMEM((NJ,) + pair, F32),
        pltpu.VMEM(params, F32),
        pltpu.VMEM((CHANS, CHANS), BF16),
        pltpu.VMEM((NY, ROWS, CHANS), BF16),
        pltpu.VMEM((8, ROWS, LANES), BF16),
        pltpu.VMEM((8, ROWS, LANES), BF16),
        pltpu.VMEM((8, ROWS, BAND), BF16),
        pltpu.VMEM((8, ROWS, BAND), BF16),
        pltpu.VMEM((4, ROWS, BAND), F32),
        pltpu.VMEM((NY, ROWS, BAND), F32),
        pltpu.VMEM((NY - 1, ROWS, BAND), BF16),
        pltpu.VMEM((NY, ROWS, BAND), BF16),
        pltpu.VMEM((ROWS, CHANS), F32),
        pltpu.VMEM((SUBS, LANES), F32),
        pltpu.VMEM((NX - 1, SUBS, LANES), F32),
    ]
    sems = [dma((11,))]
    for count in (0, NJ, NZ, NJ, 16, 18, 4, 2, 8, 8, NY - 1, NX - 1):
        sems += [dma(()), dma(())] if count == 0 else [dma((count,)), dma((count,))]
    return pl.pallas_call(
        kernel,
        out_shape=(jax.ShapeDtypeStruct((ROWS, CHANS), BF16), jax.ShapeDtypeStruct((ROWS, CHANS), BF16)),
        in_specs=[hbm] * 11,
        out_specs=(vmem, vmem),
        scratch_shapes=scratch + sems,
        compiler_params=pltpu.CompilerParams(
            collective_id=0, has_side_effects=True, vmem_limit_bytes=63 * 1024 * 1024
        ),
        name="mixer",
    )(
        q_stream, k_stream, v_stream, short_filter, rates, residues, skip.reshape(SUBS, LANES), prior_state,
        out_weight.T, residual, norm_gain.reshape(SUBS, LANES),
    )


def solution(mesh):
    placed = (
        P("seq", "ch"),
        P("seq", "ch"),
        P("seq", "ch"),
        P(None, None, "ch"),
        P(None, "ch"),
        P(None, "ch"),
        P("ch"),
        P(None, "ch"),
        P("ch", "seq"),
        P("seq", "ch"),
        P("ch"),
    )
    return jax.shard_map(
        local,
        mesh=mesh,
        in_specs=placed,
        out_specs=(P("seq", "ch"), P("seq", "ch")),
        check_vma=False,
    )
```

```python
import functools

import jax
import jax.numpy as jnp
from jax import lax
from jax.experimental import pallas as pl
from jax.experimental.pallas import tpu as pltpu
from jax.sharding import PartitionSpec as P

MESH = pl.DeviceIdType.MESH
F32 = jnp.float32
BF16 = jnp.bfloat16
NX, NY, NZ, NH = 4, 4, 16, 2
NJ = NY * NH
ROWS = 128
CHANS = 1024
LANES = 128
SUBS = 8
MODES = 16
BAND = CHANS // NX


def one_minus_exp(x):
    series = jnp.full_like(x, 1.0 / 8.0)
    for n in (7.0, 6.0, 5.0, 4.0, 3.0, 2.0):
        series = (1.0 - x * series) * (1.0 / n)
    return jnp.where(x < 0.25, x * (1.0 - x * series), 1.0 - jnp.exp(-x))


def kernel(
    q_hbm, k_hbm, v_hbm, taps_hbm, rates_hbm, residues_hbm, skip_hbm, prior_hbm, weight_hbm, residual_hbm, gain_hbm,
    hidden_ref, normed_ref,
    q_ref, k_ref, v_ref, taps_ref, rates_ref, residues_ref, skip_ref, prior_ref, residual_ref, gain_ref,
    streams, halo, gated, featq, filt, tap_rows, rate_rows, res_rows, prior_rows, pole_rows, inres_rows, inflow_rows,
    ends, plane_in, line_in, line_out, back_out, carry,
    weights, acts, far_out, far_in, near_out, near_in, parts, back_rows, final_in, summed, stat_out, stat_in,
    input_s, halo_s, halo_r, s1_s, s1_r, s2_s, s2_r, s3_s, s3_r, ring_s, ring_r, sib_s, sib_r,
    act_s, act_r, fwd_s, fwd_r, far_s, far_r, near_s, near_r, fin_s, fin_r, stat_s, stat_r,
):
    seq, x = lax.axis_index("seq"), lax.axis_index("ch")
    z, j = seq // NJ, seq % NJ
    y, h = j // NH, j % NH

    def device(z_, j_, x_):
        return (z_ * NJ + j_, x_)

    def remote(src, dst, send, recv, target):
        return pltpu.make_async_remote_copy(
            src_ref=src, dst_ref=dst, send_sem=send, recv_sem=recv, device_id=target, device_id_type=MESH
        )

    def row(t):
        return pl.ds(pl.multiple_of(t * SUBS, SUBS), SUBS)

    own_weights = weights.at[row_block(z, h), :]
    inputs = [
        pltpu.make_async_copy(src, dst, input_s.at[n])
        for n, (src, dst) in enumerate((
            (k_hbm, k_ref), (v_hbm, v_ref), (q_hbm, q_ref), (weight_hbm, own_weights), (rates_hbm, rates_ref),
            (taps_hbm, taps_ref), (residues_hbm, residues_ref), (prior_hbm, prior_ref), (skip_hbm, skip_ref),
            (residual_hbm, residual_ref), (gain_hbm, gain_ref),
        ))
    ]
    for copy in inputs:
        copy.start()

    barrier = pltpu.get_barrier_semaphore()

    def greet(target):
        pl.semaphore_signal(barrier, inc=1, device_id=target, device_id_type=MESH)

    @pl.loop(1, NJ)
    def _(d):
        greet(device(z, (j + d) % NJ, x))

    @pl.loop(1, NZ)
    def _(d):
        greet(device((z + d) % NZ, j, x))

    @pl.loop(1, NX)
    def _(d):
        greet(device(z, j, (x + d) % NX))

    has_next, has_prev = seq < NZ * NJ - 1, seq > 0
    first_j, last_j = j == 0, j == NJ - 1

    @pl.when(last_j)
    def _():
        greet(device((z + 1) % NZ, 0, x))

    @pl.when(first_j)
    def _():
        greet(device((z + NZ - 1) % NZ, NJ - 1, x))

    peers = NJ + NZ + NX - 3
    edge = jnp.logical_or(first_j, last_j)

    @pl.when(edge)
    def _():
        pl.semaphore_wait(barrier, peers + 1)

    @pl.when(jnp.logical_not(edge))
    def _():
        pl.semaphore_wait(barrier, peers)

    direction = 1 - 2 * h
    sibling = device(z, y * NH + 1 - h, x)
    ring_to = device((z + direction + NZ) % NZ, j, x)

    def ring_shard(step, part):
        return weights.at[row_block((z - direction * step + 2 * NZ) % NZ, (h + part) % 2), :]

    def ring_copy(step, part):
        shard = ring_shard(step, part)
        src = weight_hbm if (step, part) == (0, 0) else shard
        return remote(src, shard, ring_s.at[2 * step + part], ring_r.at[2 * step + part], ring_to)

    def sib_copy(step, part):
        shard = ring_shard(step, part)
        src = weight_hbm if step == 0 else shard
        return remote(src, shard, sib_s.at[2 * step + part], sib_r.at[2 * step + part], sibling)

    upward = h == 0

    def ring_step(step):
        for part in range(2):
            if step < 8:
                ring_copy(step - 1, part).wait_recv()
                if step < 7:
                    ring_copy(step, part).start()
                else:
                    pl.when(upward)(ring_copy(step, part).start)
                sib_copy(step, part).start()
            else:

                @pl.when(upward)
                def _():
                    ring_copy(step - 1, part).wait_recv()
                    sib_copy(step, part).start()

    ring_copy(0, 0).start()
    sib_copy(0, 0).start()

    def convert(stream, ref, begin, end):
        for part in range(SUBS):
            to = pl.ds(begin * SUBS + part, end - begin, stride=SUBS)
            streams[stream, to, :] = ref[begin:end, part * LANES : (part + 1) * LANES].astype(F32)

    for n in range(3):
        inputs[n].wait()
    for stream, ref in enumerate((q_ref, k_ref, v_ref)):
        convert(stream, ref, ROWS - 16, ROWS)
    last = (ROWS - 2) * SUBS
    halo_copy = remote(
        streams.at[:, pl.ds(last, 2 * SUBS), :], halo, halo_s, halo_r, ((seq + 1) % (NZ * NJ), x)
    )
    pl.when(has_next)(halo_copy.start)
    convert(1, k_ref, 0, ROWS - 16)
    sib_copy(0, 0).wait_recv()
    ring_copy(0, 1).start()
    convert(2, v_ref, 0, ROWS - 16)
    for n in range(3, len(inputs)):
        inputs[n].wait()

    for part in range(SUBS):
        cut = slice(part * LANES, (part + 1) * LANES)
        to = pl.ds(part, MODES, stride=SUBS)
        rate_rows[to, :] = rates_ref[:, cut]
        res_rows[to, :] = residues_ref[:, cut]
        prior_rows[to, :] = prior_ref[:, cut]
        for stream in range(3):
            for tap in range(3):
                n = (3 * stream + tap) * SUBS + part
                tap_rows[n : n + 1, :] = taps_ref[stream, tap : tap + 1, cut]
    rates = rate_rows[...]
    inflow = jnp.sqrt(one_minus_exp(2.0 * rates))
    pole_rows[...] = jnp.exp(-rates)
    inflow_rows[...] = inflow
    inres_rows[...] = res_rows[...] * inflow

    def modes_of(ref):
        return [ref[m * SUBS : (m + 1) * SUBS, :] for m in range(MODES)]

    taps = [tap_rows[n * SUBS : (n + 1) * SUBS, :] for n in range(9)]
    poles = modes_of(pole_rows)
    skip = skip_ref[...]

    def feature(stream, now, back1, back2):
        return taps[3 * stream] * now + taps[3 * stream + 1] * back1 + taps[3 * stream + 2] * back2

    def gate(t, history):
        later, feats = [], []
        for stream, (back1, back2) in zip((1, 2), history):
            now = streams[stream, row(t), :]
            feats.append(feature(stream, now, back1, back2))
            later.append((now, back1))
        value = feats[0] * feats[1]
        gated[row(t), :] = value
        return value, tuple(later)

    def advance(states, value):
        return tuple(pole * state + value for pole, state in zip(poles, states))

    ring_step(1)

    history = tuple((streams[s, SUBS : 2 * SUBS, :], streams[s, 0:SUBS, :]) for s in (1, 2))
    states = tuple(jnp.zeros((SUBS, LANES), F32) for _ in range(MODES))

    def scan_step(t, carried):
        states, history = carried
        value, history = gate(t, history)
        return advance(states, value), history

    scan = lax.fori_loop(2, 65, scan_step, (states, history), unroll=7)
    ring_step(2)
    states, history = lax.fori_loop(65, ROWS, scan_step, scan, unroll=7)

    @pl.when(has_prev)
    def _():
        halo_copy.wait_recv()

    @pl.when(jnp.logical_not(has_prev))
    def _():
        halo[...] = jnp.zeros_like(halo)

    def halo_rows(s):
        return halo[s, SUBS : 2 * SUBS, :], halo[s, 0:SUBS, :]

    first, history = gate(0, (halo_rows(1), halo_rows(2)))
    second, history = gate(1, history)
    for m in range(MODES):
        at = slice(m * SUBS, (m + 1) * SUBS)
        late = jnp.exp(-(ROWS - 2.0) * rate_rows[at, :])
        ends[at, :] = inflow_rows[at, :] * (states[m] + late * (poles[m] * first + second))

    pair = 2 * SUBS

    def pair_rows(n):
        return pl.ds(pl.multiple_of(n * pair, pair), pair)

    def to_owner(d):
        to = (j + d) % NJ
        return remote(ends.at[pair_rows(to), :], plane_in.at[j], s1_s.at[d], s1_r.at[d], device(z, to, x))

    def along_line(d):
        return remote(line_out, line_in.at[z], s2_s.at[d], s2_r.at[d], device((z + d) % NZ, j, x))

    def from_owner(d):
        to = (j + d) % NJ
        return remote(back_out.at[to], carry.at[pair_rows(j), :], s3_s.at[d], s3_r.at[d], device(z, to, x))

    @pl.loop(1, NJ)
    def _(d):
        to_owner(d).start()

    plane_in[j] = ends[pair_rows(j), :]
    ring_step(3)

    inres = modes_of(inres_rows)

    def output_step(t, carried):
        states, (back1, back2) = carried
        now = streams[0, row(t), :]
        featq[row(t), :] = feature(0, now, back1, back2)
        value = gated[row(t), :]
        states = advance(states, value)
        terms = [r * s for r, s in zip(inres, states)] + [skip * value]
        filt[row(t), :] = tree_sum(terms)
        return states, (now, back1)

    convert(0, q_ref, 0, ROWS - 16)
    states = tuple(jnp.zeros((SUBS, LANES), F32) for _ in range(MODES))
    outputs = lax.fori_loop(0, 64, output_step, (states, halo_rows(0)), unroll=4)

    @pl.loop(1, NJ)
    def _(d):
        to_owner(d).wait_recv()

    my_rates = rate_rows[pair_rows(j), :]
    block_decay = jnp.exp(-float(ROWS) * my_rates)
    plane_decay = jnp.exp(-float(ROWS * NJ) * my_rates)
    total = plane_in[0]
    for i in range(1, NJ):
        total = block_decay * total + plane_in[i]
    line_out[...] = total

    @pl.loop(1, NZ - z)
    def _(d):
        along_line(d).start()

    ring_step(4)
    lax.fori_loop(64, ROWS, output_step, outputs, unroll=4)
    ring_step(5)

    @pl.loop(1, z + 1)
    def _(d):
        along_line(d).wait_recv()

    incoming = lax.fori_loop(0, z, lambda i, s: plane_decay * s + line_in[i], prior_rows[pair_rows(j), :])
    for i in range(NJ):
        back_out[i] = incoming
        incoming = block_decay * incoming + plane_in[i]

    @pl.loop(1, NJ)
    def _(d):
        from_owner(d).start()

    carry[pair_rows(j), :] = back_out[j]
    ring_step(6)

    @pl.loop(1, NJ)
    def _(d):
        from_owner(d).wait_recv()

    half = ROWS // 2
    up = device(z, ((y + 1) % NY) * NH + h, x)
    down = device(z, ((y + 3) % NY) * NH + h, x)
    across = device(z, ((y + 2) % NY) * NH + h, x)

    def act_copy(part, side):
        cut = pl.ds(part * half, half)
        n = 2 * part + side
        return remote(acts.at[0, cut, :], acts.at[1 + side, cut, :], act_s.at[n], act_r.at[n], (up, down)[side])

    def fwd_copy(part):
        cut = pl.ds(part * half, half)
        return remote(acts.at[1 + part, cut, :], acts.at[3, cut, :], fwd_s.at[part], fwd_r.at[part], (up, down)[part])

    def carried_step(t, waves):
        waves = tuple(pole * wave for pole, wave in zip(poles, waves))
        filt[row(t), :] = featq[row(t), :] * (filt[row(t), :] + tree_sum(list(waves)))
        return waves

    waves = tuple(res_rows[m * SUBS : (m + 1) * SUBS, :] * carry[m * SUBS : (m + 1) * SUBS, :] for m in range(MODES))
    for part in range(2):
        waves = lax.fori_loop(part * half, (part + 1) * half, carried_step, waves, unroll=4)
        for sub in range(SUBS):
            from_rows = pl.ds(part * half * SUBS + sub, half, stride=SUBS)
            acts[0, part * half : (part + 1) * half, sub * LANES : (sub + 1) * LANES] = filt[from_rows, :].astype(BF16)
        act_copy(part, 0).start()
        act_copy(part, 1).start()
        ring_step(7 + part)

    for step in range(8):
        for part in range(2):
            if step == 0 and part == 0:
                continue
            if step > 0:
                sib_copy(step, part).wait_recv()

    @pl.when(jnp.logical_not(upward))
    def _():
        for part in range(2):
            sib_copy(8, part).wait_recv()

    right, left = device(z, j, (x + 1) % NX), device(z, j, (x + 3) % NX)
    sides = (right, left)

    def band(dx):
        return pl.ds(pl.multiple_of(((x + dx) % NX) * BAND, BAND), BAND)

    def far_copy(block, side):
        n = 2 * block + side
        return remote(far_out.at[n], far_in.at[n], far_s.at[n], far_r.at[n], sides[side])

    def near_copy(block, side):
        n = 2 * block + side
        return remote(near_out.at[n], near_in.at[n], near_s.at[n], near_r.at[n], sides[side])

    def begin(block):
        parts[block] = lax.dot_general(
            weights[...], acts[block], (((1,), (1,)), ((), ())), preferred_element_type=F32
        )
        far = parts[block, band(2), :].astype(BF16)
        for side in range(2):
            far_out[2 * block + side] = far[side * LANES : (side + 1) * LANES, :]
            far_copy(block, side).start()

    def middle(block):
        for side in range(2):
            n = 2 * block + side
            part = parts[block, band((1, 3)[side]), :]
            cut = slice(side * LANES, (side + 1) * LANES)
            rest = slice((1 - side) * LANES, (2 - side) * LANES)
            far_copy(block, side).wait_recv()
            near_out[n, cut, :] = (part[cut, :] + far_in[n].astype(F32)).astype(BF16)
            near_out[n, rest, :] = part[rest, :].astype(BF16)
            near_copy(block, side).start()

    def fin_copy(block):
        to = (None, down, up, across)[block]
        return remote(back_rows.at[block - 1], final_in.at[y], fin_s.at[block - 1], fin_r.at[block - 1], to)

    def finish(block):
        for side in range(2):
            near_copy(block, side).wait_recv()
        value = parts[block, band(0), :] + near_in[2 * block].astype(F32) + near_in[2 * block + 1].astype(F32)
        if block == 0:
            final_in[y] = value.astype(BF16)
        else:
            back_rows[block - 1] = value.astype(BF16)
            fin_copy(block).start()

    begin(0)
    for part in range(2):
        act_copy(part, part).wait_recv()
        fwd_copy(part).start()
    act_copy(1, 0).wait_recv()
    act_copy(0, 1).wait_recv()
    begin(1)
    middle(0)
    begin(2)
    middle(1)
    finish(0)
    for part in range(2):
        fwd_copy(part).wait_recv()
    begin(3)
    middle(2)
    finish(1)
    middle(3)
    finish(2)
    finish(3)
    for block in range(1, 4):
        fin_copy(block).wait_recv()

    squares = jnp.zeros((ROWS, LANES), F32)
    for tile in range(SUBS):
        cut = slice(tile * LANES, (tile + 1) * LANES)
        from_rows = slice((tile // 2) * 64, (tile // 2) * 64 + 64)
        mixed = [final_in[2 * (tile % 2) + odd, from_rows, :].astype(F32) for odd in range(2)]
        value = residual_ref[:, cut].astype(F32) + jnp.concatenate(mixed, axis=0).T
        summed[:, cut] = value
        hidden_ref[:, cut] = value.astype(BF16)
        squares = squares + value * value
    mine = jnp.sum(squares.T, axis=0, keepdims=True)
    stat_out[...] = jnp.broadcast_to(mine, (SUBS, LANES))

    def stat_copy(d):
        return remote(stat_out, stat_in.at[d - 1], stat_s.at[d - 1], stat_r.at[d - 1], device(z, j, (x + d) % NX))

    for d in range(1, NX):
        stat_copy(d).start()
    for d in range(1, NX):
        stat_copy(d).wait_recv()
    total = stat_out[...] + stat_in[0] + stat_in[1] + stat_in[2]
    scale = lax.rsqrt(total * (1.0 / (NX * CHANS)) + 1e-05)
    scale = jnp.broadcast_to(scale[0:1, :], (ROWS, LANES)).T
    for tile in range(SUBS):
        cut = slice(tile * LANES, (tile + 1) * LANES)
        normed_ref[:, cut] = (summed[:, cut] * scale * gain_ref[tile : tile + 1, :]).astype(BF16)

    pl.when(has_next)(halo_copy.wait_send)

    @pl.loop(1, NJ)
    def _(d):
        to_owner(d).wait_send()
        from_owner(d).wait_send()

    @pl.loop(1, NZ - z)
    def _(d):
        along_line(d).wait_send()

    for part in range(2):
        for step in range(7):
            ring_copy(step, part).wait_send()
        pl.when(upward)(ring_copy(7, part).wait_send)
        for step in range(8):
            if step > 0 or part == 0:
                sib_copy(step, part).wait_send()
        pl.when(upward)(sib_copy(8, part).wait_send)
        for side in range(2):
            act_copy(part, side).wait_send()
        fwd_copy(part).wait_send()
    for block in range(4):
        for side in range(2):
            far_copy(block, side).wait_send()
            near_copy(block, side).wait_send()
    for block in range(1, 4):
        fin_copy(block).wait_send()
    for d in range(1, NX):
        stat_copy(d).wait_send()


def row_block(z, h):
    return pl.ds(pl.multiple_of(z * 64 + h * 32, 32), 32)


def tree_sum(terms):
    while len(terms) > 1:
        rest = [terms[-1]] if len(terms) % 2 else []
        terms = [a + b for a, b in zip(terms[0::2], terms[1::2])] + rest
    return terms[0]


def local(
    q_stream, k_stream, v_stream, short_filter, rates, residues, skip, prior_state, out_weight, residual, norm_gain
):
    vmem = pl.BlockSpec(memory_space=pltpu.VMEM)
    hbm = pl.BlockSpec(memory_space=pltpu.HBM)
    dma = pltpu.SemaphoreType.DMA
    wide = (ROWS * SUBS, LANES)
    params = (MODES * SUBS, LANES)
    pair = (2 * SUBS, LANES)
    rows = (ROWS, CHANS)
    scratch = [
        pltpu.VMEM(rows, BF16),
        pltpu.VMEM(rows, BF16),
        pltpu.VMEM(rows, BF16),
        pltpu.VMEM(short_filter.shape, F32),
        pltpu.VMEM((MODES, CHANS), F32),
        pltpu.VMEM((MODES, CHANS), F32),
        pltpu.VMEM((SUBS, LANES), F32),
        pltpu.VMEM((MODES, CHANS), F32),
        pltpu.VMEM(rows, BF16),
        pltpu.VMEM((SUBS, LANES), F32),
        pltpu.VMEM((3,) + wide, F32),
        pltpu.VMEM((3, 2 * SUBS, LANES), F32),
        pltpu.VMEM(wide, F32),
        pltpu.VMEM(wide, F32),
        pltpu.VMEM(wide, F32),
        pltpu.VMEM((9 * SUBS, LANES), F32),
        pltpu.VMEM(params, F32),
        pltpu.VMEM(params, F32),
        pltpu.VMEM(params, F32),
        pltpu.VMEM(params, F32),
        pltpu.VMEM(params, F32),
        pltpu.VMEM(params, F32),
        pltpu.VMEM(params, F32),
        pltpu.VMEM((NJ,) + pair, F32),
        pltpu.VMEM((NZ,) + pair, F32),
        pltpu.VMEM(pair, F32),
        pltpu.VMEM((NJ,) + pair, F32),
        pltpu.VMEM(params, F32),
        pltpu.VMEM((CHANS, CHANS), BF16),
        pltpu.VMEM((NY, ROWS, CHANS), BF16),
        pltpu.VMEM((8, ROWS, LANES), BF16),
        pltpu.VMEM((8, ROWS, LANES), BF16),
        pltpu.VMEM((8, BAND, ROWS), BF16),
        pltpu.VMEM((8, BAND, ROWS), BF16),
        pltpu.VMEM((NY, CHANS, ROWS), F32),
        pltpu.VMEM((NY - 1, BAND, ROWS), BF16),
        pltpu.VMEM((NY, BAND, ROWS), BF16),
        pltpu.VMEM((ROWS, CHANS), F32),
        pltpu.VMEM((SUBS, LANES), F32),
        pltpu.VMEM((NX - 1, SUBS, LANES), F32),
    ]
    sems = [dma((11,))]
    for count in (0, NJ, NZ, NJ, 16, 18, 4, 2, 8, 8, NY - 1, NX - 1):
        sems += [dma(()), dma(())] if count == 0 else [dma((count,)), dma((count,))]
    return pl.pallas_call(
        kernel,
        out_shape=(jax.ShapeDtypeStruct((ROWS, CHANS), BF16), jax.ShapeDtypeStruct((ROWS, CHANS), BF16)),
        in_specs=[hbm] * 11,
        out_specs=(vmem, vmem),
        scratch_shapes=scratch + sems,
        compiler_params=pltpu.CompilerParams(
            collective_id=0, has_side_effects=True, vmem_limit_bytes=63 * 1024 * 1024
        ),
        name="mixer",
    )(
        q_stream, k_stream, v_stream, short_filter, rates, residues, skip.reshape(SUBS, LANES), prior_state,
        out_weight.T, residual, norm_gain.reshape(SUBS, LANES),
    )


def solution(mesh):
    placed = (
        P("seq", "ch"),
        P("seq", "ch"),
        P("seq", "ch"),
        P(None, None, "ch"),
        P(None, "ch"),
        P(None, "ch"),
        P("ch"),
        P(None, "ch"),
        P("ch", "seq"),
        P("seq", "ch"),
        P("ch"),
    )
    return jax.shard_map(
        local,
        mesh=mesh,
        in_specs=placed,
        out_specs=(P("seq", "ch"), P("seq", "ch")),
        check_vma=False,
    )
```

```python
import functools

import jax
import jax.numpy as jnp
from jax import lax
from jax.experimental import pallas as pl
from jax.experimental.pallas import tpu as pltpu
from jax.sharding import PartitionSpec as P

MESH = pl.DeviceIdType.MESH
F32 = jnp.float32
BF16 = jnp.bfloat16
NX, NY, NZ, NH = 4, 4, 16, 2
NJ = NY * NH
ROWS = 128
CHANS = 1024
LANES = 128
SUBS = 8
MODES = 16
BAND = CHANS // NX


def one_minus_exp(x):
    series = jnp.full_like(x, 1.0 / 8.0)
    for n in (7.0, 6.0, 5.0, 4.0, 3.0, 2.0):
        series = (1.0 - x * series) * (1.0 / n)
    return jnp.where(x < 0.25, x * (1.0 - x * series), 1.0 - jnp.exp(-x))


def kernel(
    q_hbm, k_hbm, v_hbm, taps_hbm, rates_hbm, residues_hbm, skip_hbm, prior_hbm, weight_hbm, residual_hbm, gain_hbm,
    hidden_ref, normed_ref,
    q_ref, k_ref, v_ref, taps_ref, rates_ref, residues_ref, skip_ref, prior_ref, residual_ref, gain_ref,
    streams, halo, gated, featq, filt, tap_rows, rate_rows, res_rows, prior_rows, pole_rows, inres_rows, inflow_rows,
    ends, plane_in, line_in, line_out, back_out, carry,
    weights, acts, far_out, far_in, near_out, near_in, parts, back_rows, final_in, summed, stat_out, stat_in,
    input_s, halo_s, halo_r, s1_s, s1_r, s2_s, s2_r, s3_s, s3_r, ring_s, ring_r, sib_s, sib_r,
    act_s, act_r, fwd_s, fwd_r, far_s, far_r, near_s, near_r, fin_s, fin_r, stat_s, stat_r,
):
    seq, x = lax.axis_index("seq"), lax.axis_index("ch")
    z, j = lax.div(seq, NJ), lax.rem(seq, NJ)
    y, h = lax.div(j, NH), lax.rem(j, NH)

    def device(z_, j_, x_):
        return (z_ * NJ + j_, x_)

    def remote(src, dst, send, recv, target):
        return pltpu.make_async_remote_copy(
            src_ref=src, dst_ref=dst, send_sem=send, recv_sem=recv, device_id=target, device_id_type=MESH
        )

    def row(t):
        return pl.ds(pl.multiple_of(t * SUBS, SUBS), SUBS)

    own_weights = weights.at[shard_rows(0, h), :]
    inputs = [
        pltpu.make_async_copy(src, dst, input_s.at[n])
        for n, (src, dst) in enumerate((
            (k_hbm, k_ref), (v_hbm, v_ref), (q_hbm, q_ref), (weight_hbm, own_weights), (rates_hbm, rates_ref),
            (taps_hbm, taps_ref), (residues_hbm, residues_ref), (prior_hbm, prior_ref), (skip_hbm, skip_ref),
            (residual_hbm, residual_ref), (gain_hbm, gain_ref),
        ))
    ]
    for copy in inputs:
        copy.start()

    barrier = pltpu.get_barrier_semaphore()

    def greet(target):
        pl.semaphore_signal(barrier, inc=1, device_id=target, device_id_type=MESH)

    @pl.loop(1, NJ)
    def _(d):
        greet(device(z, lax.rem(j + d, NJ), x))

    @pl.loop(1, NZ)
    def _(d):
        greet(device(lax.rem(z + d, NZ), j, x))

    @pl.loop(1, NX)
    def _(d):
        greet(device(z, j, lax.rem(x + d, NX)))

    has_next, has_prev = seq < NZ * NJ - 1, seq > 0
    first_j, last_j = j == 0, j == NJ - 1

    @pl.when(last_j)
    def _():
        greet(device(lax.rem(z + 1, NZ), 0, x))

    @pl.when(first_j)
    def _():
        greet(device(lax.rem(z + NZ - 1, NZ), NJ - 1, x))

    peers = NJ + NZ + NX - 3
    edge = jnp.logical_or(first_j, last_j)

    @pl.when(edge)
    def _():
        pl.semaphore_wait(barrier, peers + 1)

    @pl.when(jnp.logical_not(edge))
    def _():
        pl.semaphore_wait(barrier, peers)

    direction = 1 - 2 * h
    sibling = device(z, y * NH + 1 - h, x)
    ring_to = device(lax.rem(z + direction + NZ, NZ), j, x)

    def slot(step):
        return step if step == 0 else (1 - h) * (NZ - step) + h * step

    def ring_copy(step, part):
        rows = part + h - 2 * part * h
        src = weight_hbm if (step, part) == (0, 0) else weights.at[shard_rows(slot(step), rows), :]
        n = 2 * step + part
        return remote(src, weights.at[shard_rows(slot(step + 1), rows), :], ring_s.at[n], ring_r.at[n], ring_to)

    def sib_copy(step):
        if step == 0:
            return remote(weight_hbm, own_weights, sib_s.at[0], sib_r.at[0], sibling)
        both = weights.at[pl.ds(pl.multiple_of(slot(step) * 64, 64), 64), :]
        return remote(both, both, sib_s.at[step], sib_r.at[step], sibling)

    upward = h == 0

    def ring_step(step):
        if step < 8:
            for part in range(2):
                ring_copy(step - 1, part).wait_recv()
                if step < 7:
                    ring_copy(step, part).start()
                else:
                    pl.when(upward)(ring_copy(step, part).start)
            sib_copy(step).start()
        else:

            @pl.when(upward)
            def _():
                ring_copy(7, 0).wait_recv()
                ring_copy(7, 1).wait_recv()
                sib_copy(8).start()

    ring_copy(0, 0).start()
    sib_copy(0).start()

    def convert(stream, ref, begin, end):
        for part in range(SUBS):
            to = pl.ds(begin * SUBS + part, end - begin, stride=SUBS)
            streams[stream, to, :] = ref[begin:end, part * LANES : (part + 1) * LANES].astype(F32)

    for n in range(3):
        inputs[n].wait()
    for stream, ref in enumerate((q_ref, k_ref, v_ref)):
        convert(stream, ref, ROWS - 16, ROWS)
    last = (ROWS - 2) * SUBS
    halo_copy = remote(
        streams.at[:, pl.ds(last, 2 * SUBS), :], halo, halo_s, halo_r, (lax.rem(seq + 1, NZ * NJ), x)
    )
    pl.when(has_next)(halo_copy.start)
    convert(1, k_ref, 0, ROWS - 16)
    sib_copy(0).wait_recv()
    ring_copy(0, 1).start()
    convert(2, v_ref, 0, ROWS - 16)
    for n in range(3, len(inputs)):
        inputs[n].wait()

    for part in range(SUBS):
        cut = slice(part * LANES, (part + 1) * LANES)
        to = pl.ds(part, MODES, stride=SUBS)
        rate_rows[to, :] = rates_ref[:, cut]
        res_rows[to, :] = residues_ref[:, cut]
        prior_rows[to, :] = prior_ref[:, cut]
        for stream in range(3):
            for tap in range(3):
                n = (3 * stream + tap) * SUBS + part
                tap_rows[n : n + 1, :] = taps_ref[stream, tap : tap + 1, cut]
    rates = rate_rows[...]
    inflow = jnp.sqrt(one_minus_exp(2.0 * rates))
    pole_rows[...] = jnp.exp(-rates)
    inflow_rows[...] = inflow
    inres_rows[...] = res_rows[...] * inflow

    def modes_of(ref):
        return [ref[m * SUBS : (m + 1) * SUBS, :] for m in range(MODES)]

    taps = [tap_rows[n * SUBS : (n + 1) * SUBS, :] for n in range(9)]
    poles = modes_of(pole_rows)
    skip = skip_ref[...]

    def feature(stream, now, back1, back2):
        return taps[3 * stream] * now + taps[3 * stream + 1] * back1 + taps[3 * stream + 2] * back2

    def gate(t, history):
        later, feats = [], []
        for stream, (back1, back2) in zip((1, 2), history):
            now = streams[stream, row(t), :]
            feats.append(feature(stream, now, back1, back2))
            later.append((now, back1))
        value = feats[0] * feats[1]
        gated[row(t), :] = value
        return value, tuple(later)

    def steps(begin, end, step, carried):
        def eight(block, carried):
            for t in range(8):
                carried = step(block * 8 + t, carried)
            return carried

        return lax.fori_loop(begin // 8, end // 8, eight, carried)

    def advance(states, value):
        return tuple(pole * state + value for pole, state in zip(poles, states))

    ring_step(1)

    history = tuple((streams[s, SUBS : 2 * SUBS, :], streams[s, 0:SUBS, :]) for s in (1, 2))
    states = tuple(jnp.zeros((SUBS, LANES), F32) for _ in range(MODES))

    def scan_step(t, carried):
        states, history = carried
        value, history = gate(t, history)
        return advance(states, value), history

    scan = (states, history)
    for t in range(2, 8):
        scan = scan_step(t, scan)
    states, history = steps(8, ROWS, scan_step, scan)

    @pl.when(has_prev)
    def _():
        halo_copy.wait_recv()

    @pl.when(jnp.logical_not(has_prev))
    def _():
        halo[...] = jnp.zeros_like(halo)

    def halo_rows(s):
        return halo[s, SUBS : 2 * SUBS, :], halo[s, 0:SUBS, :]

    first, history = gate(0, (halo_rows(1), halo_rows(2)))
    second, history = gate(1, history)
    for m in range(MODES):
        at = slice(m * SUBS, (m + 1) * SUBS)
        late = jnp.exp(-(ROWS - 2.0) * rate_rows[at, :])
        ends[at, :] = inflow_rows[at, :] * (states[m] + late * (poles[m] * first + second))

    pair = 2 * SUBS

    def pair_rows(n):
        return pl.ds(pl.multiple_of(n * pair, pair), pair)

    def to_owner(d):
        to = lax.rem(j + d, NJ)
        return remote(ends.at[pair_rows(to), :], plane_in.at[j], s1_s.at[d], s1_r.at[d], device(z, to, x))

    def along_line(d):
        return remote(line_out, line_in.at[z], s2_s.at[d], s2_r.at[d], device(lax.rem(z + d, NZ), j, x))

    def from_owner(d):
        to = lax.rem(j + d, NJ)
        return remote(back_out.at[to], carry.at[pair_rows(j), :], s3_s.at[d], s3_r.at[d], device(z, to, x))

    @pl.loop(1, NJ)
    def _(d):
        to_owner(d).start()

    plane_in[j] = ends[pair_rows(j), :]
    ring_step(2)

    inres = modes_of(inres_rows)

    def output_step(t, carried):
        states, (back1, back2) = carried
        now = streams[0, row(t), :]
        featq[row(t), :] = feature(0, now, back1, back2)
        value = gated[row(t), :]
        states = advance(states, value)
        terms = [r * s for r, s in zip(inres, states)] + [skip * value]
        filt[row(t), :] = tree_sum(terms)
        return states, (now, back1)

    convert(0, q_ref, 0, ROWS - 16)
    states = tuple(jnp.zeros((SUBS, LANES), F32) for _ in range(MODES))
    outputs = steps(0, 64, output_step, (states, halo_rows(0)))
    ring_step(3)

    @pl.loop(1, NJ)
    def _(d):
        to_owner(d).wait_recv()

    my_rates = rate_rows[pair_rows(j), :]
    block_decay = jnp.exp(-float(ROWS) * my_rates)
    plane_decay = jnp.exp(-float(ROWS * NJ) * my_rates)
    total = plane_in[0]
    for i in range(1, NJ):
        total = block_decay * total + plane_in[i]
    line_out[...] = total

    @pl.loop(1, NZ - z)
    def _(d):
        along_line(d).start()

    ring_step(4)
    steps(64, ROWS, output_step, outputs)
    ring_step(5)

    @pl.loop(1, z + 1)
    def _(d):
        along_line(d).wait_recv()

    incoming = lax.fori_loop(0, z, lambda i, s: plane_decay * s + line_in[i], prior_rows[pair_rows(j), :])
    for i in range(NJ):
        back_out[i] = incoming
        incoming = block_decay * incoming + plane_in[i]

    @pl.loop(1, NJ)
    def _(d):
        from_owner(d).start()

    carry[pair_rows(j), :] = back_out[j]
    ring_step(6)

    @pl.loop(1, NJ)
    def _(d):
        from_owner(d).wait_recv()

    half = ROWS // 2
    up = device(z, lax.rem(y + 1, NY) * NH + h, x)
    down = device(z, lax.rem(y + 3, NY) * NH + h, x)
    across = device(z, lax.rem(y + 2, NY) * NH + h, x)

    def act_copy(part, side):
        cut = pl.ds(part * half, half)
        n = 2 * part + side
        return remote(acts.at[0, cut, :], acts.at[1 + side, cut, :], act_s.at[n], act_r.at[n], (up, down)[side])

    def fwd_copy(part):
        cut = pl.ds(part * half, half)
        return remote(acts.at[1 + part, cut, :], acts.at[3, cut, :], fwd_s.at[part], fwd_r.at[part], (up, down)[part])

    def carried_step(t, waves):
        waves = tuple(pole * wave for pole, wave in zip(poles, waves))
        filt[row(t), :] = featq[row(t), :] * (filt[row(t), :] + tree_sum(list(waves)))
        return waves

    waves = tuple(res_rows[m * SUBS : (m + 1) * SUBS, :] * carry[m * SUBS : (m + 1) * SUBS, :] for m in range(MODES))
    for part in range(2):
        waves = steps(part * half, (part + 1) * half, carried_step, waves)
        for sub in range(SUBS):
            from_rows = pl.ds(part * half * SUBS + sub, half, stride=SUBS)
            acts[0, part * half : (part + 1) * half, sub * LANES : (sub + 1) * LANES] = filt[from_rows, :].astype(BF16)
        act_copy(part, 0).start()
        act_copy(part, 1).start()

    ring_step(7)
    ring_step(8)
    for step in range(1, 8):
        sib_copy(step).wait_recv()
    pl.when(jnp.logical_not(upward))(sib_copy(8).wait_recv)

    right, left = device(z, j, lax.rem(x + 1, NX)), device(z, j, lax.rem(x + 3, NX))
    sides = (right, left)

    def band(block, dx):
        first = lax.rem(x + dx, NX) * 4 + NZ - z
        chunks = [pl.ds(pl.multiple_of(lax.rem(first + i, NZ) * 64, 64), 64) for i in range(4)]
        return [parts[block, chunk, :] for chunk in chunks]

    def far_copy(block, side):
        n = 2 * block + side
        return remote(far_out.at[n], far_in.at[n], far_s.at[n], far_r.at[n], sides[side])

    def near_copy(block, side):
        n = 2 * block + side
        return remote(near_out.at[n], near_in.at[n], near_s.at[n], near_r.at[n], sides[side])

    def begin(block):
        parts[block] = lax.dot_general(
            weights[...], acts[block], (((1,), (1,)), ((), ())), preferred_element_type=F32
        )
        far = band(block, 2)
        for side in range(2):
            for i in range(2):
                far_out[2 * block + side, 64 * i : 64 * i + 64, :] = far[2 * side + i].astype(BF16)
            far_copy(block, side).start()

    def middle(block):
        for side in range(2):
            n = 2 * block + side
            part = band(block, (1, 3)[side])
            far_copy(block, side).wait_recv()
            for i in range(4):
                value = part[i]
                if i // 2 == side:
                    value = value + far_in[n, 64 * (i % 2) : 64 * (i % 2) + 64, :].astype(F32)
                near_out[n, 64 * i : 64 * i + 64, :] = value.astype(BF16)
            near_copy(block, side).start()

    def fin_copy(block):
        to = (None, down, up, across)[block]
        return remote(back_rows.at[block - 1], final_in.at[y], fin_s.at[block - 1], fin_r.at[block - 1], to)

    def finish(block):
        for side in range(2):
            near_copy(block, side).wait_recv()
        value = jnp.concatenate(band(block, 0), axis=0) + near_in[2 * block].astype(F32) + near_in[2 * block + 1].astype(F32)
        if block == 0:
            final_in[y] = value.astype(BF16)
        else:
            back_rows[block - 1] = value.astype(BF16)
            fin_copy(block).start()

    begin(0)
    for part in range(2):
        act_copy(part, part).wait_recv()
        fwd_copy(part).start()
    act_copy(1, 0).wait_recv()
    act_copy(0, 1).wait_recv()
    begin(1)
    middle(0)
    begin(2)
    middle(1)
    finish(0)
    for part in range(2):
        fwd_copy(part).wait_recv()
    begin(3)
    middle(2)
    finish(1)
    middle(3)
    finish(2)
    finish(3)
    for block in range(1, 4):
        fin_copy(block).wait_recv()

    squares = jnp.zeros((ROWS, LANES), F32)
    for tile in range(SUBS):
        cut = slice(tile * LANES, (tile + 1) * LANES)
        from_rows = slice((tile // 2) * 64, (tile // 2) * 64 + 64)
        mixed = [final_in[2 * (tile % 2) + odd, from_rows, :].astype(F32) for odd in range(2)]
        value = residual_ref[:, cut].astype(F32) + jnp.concatenate(mixed, axis=0).T
        summed[:, cut] = value
        hidden_ref[:, cut] = value.astype(BF16)
        squares = squares + value * value
    mine = jnp.sum(squares.T, axis=0, keepdims=True)
    stat_out[...] = jnp.broadcast_to(mine, (SUBS, LANES))

    def stat_copy(d):
        return remote(stat_out, stat_in.at[d - 1], stat_s.at[d - 1], stat_r.at[d - 1], device(z, j, lax.rem(x + d, NX)))

    for d in range(1, NX):
        stat_copy(d).start()
    for d in range(1, NX):
        stat_copy(d).wait_recv()
    total = stat_out[...] + stat_in[0] + stat_in[1] + stat_in[2]
    scale = lax.rsqrt(total * (1.0 / (NX * CHANS)) + 1e-05)
    scale = jnp.broadcast_to(scale[0:1, :], (ROWS, LANES)).T
    for tile in range(SUBS):
        cut = slice(tile * LANES, (tile + 1) * LANES)
        normed_ref[:, cut] = (summed[:, cut] * scale * gain_ref[tile : tile + 1, :]).astype(BF16)

    pl.when(has_next)(halo_copy.wait_send)

    @pl.loop(1, NJ)
    def _(d):
        to_owner(d).wait_send()
        from_owner(d).wait_send()

    @pl.loop(1, NZ - z)
    def _(d):
        along_line(d).wait_send()

    for step in range(8):
        sib_copy(step).wait_send()
    pl.when(upward)(sib_copy(8).wait_send)
    for part in range(2):
        for step in range(7):
            ring_copy(step, part).wait_send()
        pl.when(upward)(ring_copy(7, part).wait_send)
        for side in range(2):
            act_copy(part, side).wait_send()
        fwd_copy(part).wait_send()
    for block in range(4):
        for side in range(2):
            far_copy(block, side).wait_send()
            near_copy(block, side).wait_send()
    for block in range(1, 4):
        fin_copy(block).wait_send()
    for d in range(1, NX):
        stat_copy(d).wait_send()


def shard_rows(slot, h):
    return pl.ds(pl.multiple_of(slot * 64 + h * 32, 32), 32)


def tree_sum(terms):
    while len(terms) > 1:
        rest = [terms[-1]] if len(terms) % 2 else []
        terms = [a + b for a, b in zip(terms[0::2], terms[1::2])] + rest
    return terms[0]


def local(
    q_stream, k_stream, v_stream, short_filter, rates, residues, skip, prior_state, out_weight, residual, norm_gain
):
    vmem = pl.BlockSpec(memory_space=pltpu.VMEM)
    hbm = pl.BlockSpec(memory_space=pltpu.HBM)
    dma = pltpu.SemaphoreType.DMA
    wide = (ROWS * SUBS, LANES)
    params = (MODES * SUBS, LANES)
    pair = (2 * SUBS, LANES)
    rows = (ROWS, CHANS)
    scratch = [
        pltpu.VMEM(rows, BF16),
        pltpu.VMEM(rows, BF16),
        pltpu.VMEM(rows, BF16),
        pltpu.VMEM(short_filter.shape, F32),
        pltpu.VMEM((MODES, CHANS), F32),
        pltpu.VMEM((MODES, CHANS), F32),
        pltpu.VMEM((SUBS, LANES), F32),
        pltpu.VMEM((MODES, CHANS), F32),
        pltpu.VMEM(rows, BF16),
        pltpu.VMEM((SUBS, LANES), F32),
        pltpu.VMEM((3,) + wide, F32),
        pltpu.VMEM((3, 2 * SUBS, LANES), F32),
        pltpu.VMEM(wide, F32),
        pltpu.VMEM(wide, F32),
        pltpu.VMEM(wide, F32),
        pltpu.VMEM((9 * SUBS, LANES), F32),
        pltpu.VMEM(params, F32),
        pltpu.VMEM(params, F32),
        pltpu.VMEM(params, F32),
        pltpu.VMEM(params, F32),
        pltpu.VMEM(params, F32),
        pltpu.VMEM(params, F32),
        pltpu.VMEM(params, F32),
        pltpu.VMEM((NJ,) + pair, F32),
        pltpu.VMEM((NZ,) + pair, F32),
        pltpu.VMEM(pair, F32),
        pltpu.VMEM((NJ,) + pair, F32),
        pltpu.VMEM(params, F32),
        pltpu.VMEM((CHANS, CHANS), BF16),
        pltpu.VMEM((NY, ROWS, CHANS), BF16),
        pltpu.VMEM((8, ROWS, LANES), BF16),
        pltpu.VMEM((8, ROWS, LANES), BF16),
        pltpu.VMEM((8, BAND, ROWS), BF16),
        pltpu.VMEM((8, BAND, ROWS), BF16),
        pltpu.VMEM((NY, CHANS, ROWS), F32),
        pltpu.VMEM((NY - 1, BAND, ROWS), BF16),
        pltpu.VMEM((NY, BAND, ROWS), BF16),
        pltpu.VMEM((ROWS, CHANS), F32),
        pltpu.VMEM((SUBS, LANES), F32),
        pltpu.VMEM((NX - 1, SUBS, LANES), F32),
    ]
    sems = [dma((11,))]
    for count in (0, NJ, NZ, NJ, 16, 9, 4, 2, 8, 8, NY - 1, NX - 1):
        sems += [dma(()), dma(())] if count == 0 else [dma((count,)), dma((count,))]
    return pl.pallas_call(
        kernel,
        out_shape=(jax.ShapeDtypeStruct((ROWS, CHANS), BF16), jax.ShapeDtypeStruct((ROWS, CHANS), BF16)),
        in_specs=[hbm] * 11,
        out_specs=(vmem, vmem),
        scratch_shapes=scratch + sems,
        compiler_params=pltpu.CompilerParams(
            collective_id=0, has_side_effects=True, vmem_limit_bytes=63 * 1024 * 1024
        ),
        name="mixer",
    )(
        q_stream, k_stream, v_stream, short_filter, rates, residues, skip.reshape(SUBS, LANES), prior_state,
        out_weight.T, residual, norm_gain.reshape(SUBS, LANES),
    )


def solution(mesh):
    placed = (
        P("seq", "ch"),
        P("seq", "ch"),
        P("seq", "ch"),
        P(None, None, "ch"),
        P(None, "ch"),
        P(None, "ch"),
        P("ch"),
        P(None, "ch"),
        P("ch", "seq"),
        P("seq", "ch"),
        P("ch"),
    )
    return jax.shard_map(
        local,
        mesh=mesh,
        in_specs=placed,
        out_specs=(P("seq", "ch"), P("seq", "ch")),
        check_vma=False,
    )
```

```python
import functools

import jax
import jax.numpy as jnp
from jax import lax
from jax.experimental import pallas as pl
from jax.experimental.pallas import tpu as pltpu
from jax.sharding import PartitionSpec as P

MESH = pl.DeviceIdType.MESH
F32 = jnp.float32
BF16 = jnp.bfloat16
NX, NY, NZ, NH = 4, 4, 16, 2
NJ = NY * NH
ROWS = 128
CHANS = 1024
LANES = 128
SUBS = 8
MODES = 16
BAND = CHANS // NX


def one_minus_exp(x):
    series = jnp.full_like(x, 1.0 / 8.0)
    for n in (7.0, 6.0, 5.0, 4.0, 3.0, 2.0):
        series = (1.0 - x * series) * (1.0 / n)
    return jnp.where(x < 0.25, x * (1.0 - x * series), 1.0 - jnp.exp(-x))


def kernel(
    q_hbm, k_hbm, v_hbm, taps_hbm, rates_hbm, residues_hbm, skip_hbm, prior_hbm, weight_hbm, residual_hbm, gain_hbm,
    hidden_ref, normed_ref,
    q_ref, k_ref, v_ref, taps_ref, rates_ref, residues_ref, skip_ref, prior_ref, residual_ref, gain_ref,
    streams, halo, gated, featq, filt, tap_rows, rate_rows, res_rows, prior_rows, pole_rows, inres_rows, inflow_rows,
    ends, plane_in, line_in, line_out, back_out, carry,
    weights, acts, far_out, far_in, near_out, near_in, parts, back_rows, final_in, summed, stat_out, stat_in,
    input_s, halo_s, halo_r, s1_s, s1_r, s2_s, s2_r, s3_s, s3_r, ring_s, ring_r, sib_s, sib_r,
    act_s, act_r, fwd_s, fwd_r, far_s, far_r, near_s, near_r, fin_s, fin_r, stat_s, stat_r,
):
    seq, x = lax.axis_index("seq"), lax.axis_index("ch")
    z, j = lax.div(seq, NJ), lax.rem(seq, NJ)
    y, h = lax.div(j, NH), lax.rem(j, NH)

    def device(z_, j_, x_):
        return (z_ * NJ + j_, x_)

    def remote(src, dst, send, recv, target):
        return pltpu.make_async_remote_copy(
            src_ref=src, dst_ref=dst, send_sem=send, recv_sem=recv, device_id=target, device_id_type=MESH
        )

    def row(t):
        return pl.ds(pl.multiple_of(t * SUBS, SUBS), SUBS)

    own_weights = weights.at[shard_rows(0, h), :]
    inputs = [
        pltpu.make_async_copy(src, dst, input_s.at[n])
        for n, (src, dst) in enumerate((
            (k_hbm, k_ref), (v_hbm, v_ref), (q_hbm, q_ref), (weight_hbm, own_weights), (rates_hbm, rates_ref),
            (taps_hbm, taps_ref), (residues_hbm, residues_ref), (prior_hbm, prior_ref), (skip_hbm, skip_ref),
            (residual_hbm, residual_ref), (gain_hbm, gain_ref),
        ))
    ]
    for copy in inputs:
        copy.start()

    barrier = pltpu.get_barrier_semaphore()

    def greet(target):
        pl.semaphore_signal(barrier, inc=1, device_id=target, device_id_type=MESH)

    @pl.loop(1, NJ)
    def _(d):
        greet(device(z, lax.rem(j + d, NJ), x))

    @pl.loop(1, NZ)
    def _(d):
        greet(device(lax.rem(z + d, NZ), j, x))

    @pl.loop(1, NX)
    def _(d):
        greet(device(z, j, lax.rem(x + d, NX)))

    has_next, has_prev = seq < NZ * NJ - 1, seq > 0
    first_j, last_j = j == 0, j == NJ - 1

    @pl.when(last_j)
    def _():
        greet(device(lax.rem(z + 1, NZ), 0, x))

    @pl.when(first_j)
    def _():
        greet(device(lax.rem(z + NZ - 1, NZ), NJ - 1, x))

    peers = NJ + NZ + NX - 3
    edge = jnp.logical_or(first_j, last_j)

    @pl.when(edge)
    def _():
        pl.semaphore_wait(barrier, peers + 1)

    @pl.when(jnp.logical_not(edge))
    def _():
        pl.semaphore_wait(barrier, peers)

    direction = 1 - 2 * h
    sibling = device(z, y * NH + 1 - h, x)
    ring_to = [None] + [device(lax.rem(z + direction * d + NZ, NZ), j, x) for d in (1, 2)]

    def slot(far):
        return far if far == 0 else (1 - h) * (NZ - far) + h * far

    def ring_copy(far, part=None):
        hops = 2 - far % 2
        if far > 2:
            rows = [pl.ds(pl.multiple_of(slot(f) * 64, 64), 64) for f in (far - hops, far)]
            src, n = weights.at[rows[0], :], 2 * far
        else:
            shard = part + h - 2 * part * h
            rows = [shard_rows(slot(f), shard) for f in (0, far)]
            src, n = (weight_hbm if part == 0 else weights.at[rows[0], :]), 2 * far + part
        return remote(src, weights.at[rows[1], :], ring_s.at[n], ring_r.at[n], ring_to[hops])

    def sib_copy(step, count=2):
        if step == 0:
            return remote(weight_hbm, own_weights, sib_s.at[0], sib_r.at[0], sibling)
        first = (1 - h) * (NZ - 2 * step) + h * (2 * step - 1)
        both = weights.at[pl.ds(pl.multiple_of(first * 64, 64), 64 * count), :]
        return remote(both, both, sib_s.at[step], sib_r.at[step], sibling)

    upward = h == 0

    def arrived(far):
        if far > 2:
            ring_copy(far).wait_recv()
        else:
            ring_copy(far, 0).wait_recv()
            ring_copy(far, 1).wait_recv()

    def ring_step(step):
        far = 2 * step
        if step < 4:
            arrived(far)
            if step < 3:
                ring_copy(far + 2).start()
            else:
                pl.when(upward)(ring_copy(8).start)
            ring_copy(far + 1).start()
            arrived(far - 1)
            sib_copy(step).start()
        else:
            arrived(7)

            @pl.when(upward)
            def _():
                arrived(8)
                sib_copy(4).start()

            pl.when(jnp.logical_not(upward))(sib_copy(4, 1).start)

    ring_copy(2, 0).start()
    sib_copy(0).start()
    ring_copy(1, 0).start()

    def convert(stream, ref, begin, end):
        for part in range(SUBS):
            to = pl.ds(begin * SUBS + part, end - begin, stride=SUBS)
            streams[stream, to, :] = ref[begin:end, part * LANES : (part + 1) * LANES].astype(F32)

    for n in range(3):
        inputs[n].wait()
    for stream, ref in enumerate((q_ref, k_ref, v_ref)):
        convert(stream, ref, ROWS - 16, ROWS)
    last = (ROWS - 2) * SUBS
    halo_copy = remote(
        streams.at[:, pl.ds(last, 2 * SUBS), :], halo, halo_s, halo_r, (lax.rem(seq + 1, NZ * NJ), x)
    )
    pl.when(has_next)(halo_copy.start)
    convert(1, k_ref, 0, ROWS - 16)
    sib_copy(0).wait_recv()
    ring_copy(2, 1).start()
    ring_copy(1, 1).start()
    convert(2, v_ref, 0, ROWS - 16)
    for n in range(3, len(inputs)):
        inputs[n].wait()

    for part in range(SUBS):
        cut = slice(part * LANES, (part + 1) * LANES)
        to = pl.ds(part, MODES, stride=SUBS)
        rate_rows[to, :] = rates_ref[:, cut]
        res_rows[to, :] = residues_ref[:, cut]
        prior_rows[to, :] = prior_ref[:, cut]
        for stream in range(3):
            for tap in range(3):
                n = (3 * stream + tap) * SUBS + part
                tap_rows[n : n + 1, :] = taps_ref[stream, tap : tap + 1, cut]
    rates = rate_rows[...]
    inflow = jnp.sqrt(one_minus_exp(2.0 * rates))
    pole_rows[...] = jnp.exp(-rates)
    inflow_rows[...] = inflow
    inres_rows[...] = res_rows[...] * inflow

    def modes_of(ref):
        return [ref[m * SUBS : (m + 1) * SUBS, :] for m in range(MODES)]

    taps = [tap_rows[n * SUBS : (n + 1) * SUBS, :] for n in range(9)]
    poles = modes_of(pole_rows)
    skip = skip_ref[...]

    def feature(stream, now, back1, back2):
        return taps[3 * stream] * now + taps[3 * stream + 1] * back1 + taps[3 * stream + 2] * back2

    def gate(t, history):
        later, feats = [], []
        for stream, (back1, back2) in zip((1, 2), history):
            now = streams[stream, row(t), :]
            feats.append(feature(stream, now, back1, back2))
            later.append((now, back1))
        value = feats[0] * feats[1]
        gated[row(t), :] = value
        return value, tuple(later)

    def steps(begin, end, step, carried):
        def eight(block, carried):
            for t in range(8):
                carried = step(block * 8 + t, carried)
            return carried

        return lax.fori_loop(begin // 8, end // 8, eight, carried)

    def advance(states, value):
        return tuple(pole * state + value for pole, state in zip(poles, states))

    history = tuple((streams[s, SUBS : 2 * SUBS, :], streams[s, 0:SUBS, :]) for s in (1, 2))
    states = tuple(jnp.zeros((SUBS, LANES), F32) for _ in range(MODES))

    def scan_step(t, carried):
        states, history = carried
        value, history = gate(t, history)
        return advance(states, value), history

    scan = (states, history)
    for t in range(2, 8):
        scan = scan_step(t, scan)
    states, history = steps(8, ROWS, scan_step, scan)

    @pl.when(has_prev)
    def _():
        halo_copy.wait_recv()

    @pl.when(jnp.logical_not(has_prev))
    def _():
        halo[...] = jnp.zeros_like(halo)

    def halo_rows(s):
        return halo[s, SUBS : 2 * SUBS, :], halo[s, 0:SUBS, :]

    first, history = gate(0, (halo_rows(1), halo_rows(2)))
    second, history = gate(1, history)
    for m in range(MODES):
        at = slice(m * SUBS, (m + 1) * SUBS)
        late = jnp.exp(-(ROWS - 2.0) * rate_rows[at, :])
        ends[at, :] = inflow_rows[at, :] * (states[m] + late * (poles[m] * first + second))

    pair = 2 * SUBS

    def pair_rows(n):
        return pl.ds(pl.multiple_of(n * pair, pair), pair)

    def to_owner(d):
        to = lax.rem(j + d, NJ)
        return remote(ends.at[pair_rows(to), :], plane_in.at[j], s1_s.at[d], s1_r.at[d], device(z, to, x))

    def along_line(d):
        return remote(line_out, line_in.at[z], s2_s.at[d], s2_r.at[d], device(lax.rem(z + d, NZ), j, x))

    def from_owner(d):
        to = lax.rem(j + d, NJ)
        return remote(back_out.at[to], carry.at[pair_rows(j), :], s3_s.at[d], s3_r.at[d], device(z, to, x))

    @pl.loop(1, NJ)
    def _(d):
        to_owner(d).start()

    plane_in[j] = ends[pair_rows(j), :]
    ring_step(1)

    inres = modes_of(inres_rows)

    def output_step(t, carried):
        states, (back1, back2) = carried
        now = streams[0, row(t), :]
        featq[row(t), :] = feature(0, now, back1, back2)
        value = gated[row(t), :]
        states = advance(states, value)
        terms = [r * s for r, s in zip(inres, states)] + [skip * value]
        filt[row(t), :] = tree_sum(terms)
        return states, (now, back1)

    convert(0, q_ref, 0, ROWS - 16)
    states = tuple(jnp.zeros((SUBS, LANES), F32) for _ in range(MODES))
    outputs = steps(0, 64, output_step, (states, halo_rows(0)))

    @pl.loop(1, NJ)
    def _(d):
        to_owner(d).wait_recv()

    my_rates = rate_rows[pair_rows(j), :]
    block_decay = jnp.exp(-float(ROWS) * my_rates)
    plane_decay = jnp.exp(-float(ROWS * NJ) * my_rates)
    total = plane_in[0]
    for i in range(1, NJ):
        total = block_decay * total + plane_in[i]
    line_out[...] = total

    @pl.loop(1, NZ - z)
    def _(d):
        along_line(d).start()

    ring_step(2)
    steps(64, ROWS, output_step, outputs)

    @pl.loop(1, z + 1)
    def _(d):
        along_line(d).wait_recv()

    incoming = lax.fori_loop(0, z, lambda i, s: plane_decay * s + line_in[i], prior_rows[pair_rows(j), :])
    for i in range(NJ):
        back_out[i] = incoming
        incoming = block_decay * incoming + plane_in[i]

    @pl.loop(1, NJ)
    def _(d):
        from_owner(d).start()

    carry[pair_rows(j), :] = back_out[j]
    ring_step(3)

    @pl.loop(1, NJ)
    def _(d):
        from_owner(d).wait_recv()

    half = ROWS // 2
    up = device(z, lax.rem(y + 1, NY) * NH + h, x)
    down = device(z, lax.rem(y + 3, NY) * NH + h, x)
    across = device(z, lax.rem(y + 2, NY) * NH + h, x)

    def act_copy(part, side):
        cut = pl.ds(part * half, half)
        n = 2 * part + side
        return remote(acts.at[0, cut, :], acts.at[1 + side, cut, :], act_s.at[n], act_r.at[n], (up, down)[side])

    def fwd_copy(part):
        cut = pl.ds(part * half, half)
        return remote(acts.at[1 + part, cut, :], acts.at[3, cut, :], fwd_s.at[part], fwd_r.at[part], (up, down)[part])

    def carried_step(t, waves):
        waves = tuple(pole * wave for pole, wave in zip(poles, waves))
        filt[row(t), :] = featq[row(t), :] * (filt[row(t), :] + tree_sum(list(waves)))
        return waves

    waves = tuple(res_rows[m * SUBS : (m + 1) * SUBS, :] * carry[m * SUBS : (m + 1) * SUBS, :] for m in range(MODES))
    for part in range(2):
        waves = steps(part * half, (part + 1) * half, carried_step, waves)
        for sub in range(SUBS):
            from_rows = pl.ds(part * half * SUBS + sub, half, stride=SUBS)
            acts[0, part * half : (part + 1) * half, sub * LANES : (sub + 1) * LANES] = filt[from_rows, :].astype(BF16)
        act_copy(part, 0).start()
        act_copy(part, 1).start()

    ring_step(4)
    for step in range(1, 4):
        sib_copy(step).wait_recv()
    pl.when(upward)(sib_copy(4, 1).wait_recv)
    pl.when(jnp.logical_not(upward))(sib_copy(4).wait_recv)

    right, left = device(z, j, lax.rem(x + 1, NX)), device(z, j, lax.rem(x + 3, NX))
    sides = (right, left)

    def band(block, dx):
        first = lax.rem(x + dx, NX) * 4 + NZ - z
        chunks = [pl.ds(pl.multiple_of(lax.rem(first + i, NZ) * 64, 64), 64) for i in range(4)]
        return [parts[block, chunk, :] for chunk in chunks]

    def far_copy(block, side):
        n = 2 * block + side
        return remote(far_out.at[n], far_in.at[n], far_s.at[n], far_r.at[n], sides[side])

    def near_copy(block, side):
        n = 2 * block + side
        return remote(near_out.at[n], near_in.at[n], near_s.at[n], near_r.at[n], sides[side])

    def begin(block):
        parts[block] = lax.dot_general(
            weights[...], acts[block], (((1,), (1,)), ((), ())), preferred_element_type=F32
        )
        far = band(block, 2)
        for side in range(2):
            for i in range(2):
                far_out[2 * block + side, 64 * i : 64 * i + 64, :] = far[2 * side + i].astype(BF16)
            far_copy(block, side).start()

    def middle(block):
        for side in range(2):
            n = 2 * block + side
            part = band(block, (1, 3)[side])
            far_copy(block, side).wait_recv()
            for i in range(4):
                value = part[i]
                if i // 2 == side:
                    value = value + far_in[n, 64 * (i % 2) : 64 * (i % 2) + 64, :].astype(F32)
                near_out[n, 64 * i : 64 * i + 64, :] = value.astype(BF16)
            near_copy(block, side).start()

    def fin_copy(block):
        to = (None, down, up, across)[block]
        return remote(back_rows.at[block - 1], final_in.at[y], fin_s.at[block - 1], fin_r.at[block - 1], to)

    def finish(block):
        for side in range(2):
            near_copy(block, side).wait_recv()
        value = jnp.concatenate(band(block, 0), axis=0) + near_in[2 * block].astype(F32) + near_in[2 * block + 1].astype(F32)
        if block == 0:
            final_in[y] = value.astype(BF16)
        else:
            back_rows[block - 1] = value.astype(BF16)
            fin_copy(block).start()

    begin(0)
    for part in range(2):
        act_copy(part, part).wait_recv()
        fwd_copy(part).start()
    act_copy(1, 0).wait_recv()
    act_copy(0, 1).wait_recv()
    begin(1)
    middle(0)
    begin(2)
    middle(1)
    finish(0)
    for part in range(2):
        fwd_copy(part).wait_recv()
    begin(3)
    middle(2)
    finish(1)
    middle(3)
    finish(2)
    finish(3)
    for block in range(1, 4):
        fin_copy(block).wait_recv()

    squares = jnp.zeros((ROWS, LANES), F32)
    for tile in range(SUBS):
        cut = slice(tile * LANES, (tile + 1) * LANES)
        from_rows = slice((tile // 2) * 64, (tile // 2) * 64 + 64)
        mixed = [final_in[2 * (tile % 2) + odd, from_rows, :].astype(F32) for odd in range(2)]
        value = residual_ref[:, cut].astype(F32) + jnp.concatenate(mixed, axis=0).T
        summed[:, cut] = value
        hidden_ref[:, cut] = value.astype(BF16)
        squares = squares + value * value
    mine = jnp.sum(squares.T, axis=0, keepdims=True)
    stat_out[...] = jnp.broadcast_to(mine, (SUBS, LANES))

    def stat_copy(d):
        return remote(stat_out, stat_in.at[d - 1], stat_s.at[d - 1], stat_r.at[d - 1], device(z, j, lax.rem(x + d, NX)))

    for d in range(1, NX):
        stat_copy(d).start()
    for d in range(1, NX):
        stat_copy(d).wait_recv()
    total = stat_out[...] + stat_in[0] + stat_in[1] + stat_in[2]
    scale = lax.rsqrt(total * (1.0 / (NX * CHANS)) + 1e-05)
    scale = jnp.broadcast_to(scale[0:1, :], (ROWS, LANES)).T
    for tile in range(SUBS):
        cut = slice(tile * LANES, (tile + 1) * LANES)
        normed_ref[:, cut] = (summed[:, cut] * scale * gain_ref[tile : tile + 1, :]).astype(BF16)

    pl.when(has_next)(halo_copy.wait_send)

    @pl.loop(1, NJ)
    def _(d):
        to_owner(d).wait_send()
        from_owner(d).wait_send()

    @pl.loop(1, NZ - z)
    def _(d):
        along_line(d).wait_send()

    for step in range(4):
        sib_copy(step).wait_send()
    pl.when(upward)(sib_copy(4).wait_send)
    pl.when(jnp.logical_not(upward))(sib_copy(4, 1).wait_send)
    for far in range(3, 8):
        ring_copy(far).wait_send()
    pl.when(upward)(ring_copy(8).wait_send)
    for part in range(2):
        ring_copy(1, part).wait_send()
        ring_copy(2, part).wait_send()
        for side in range(2):
            act_copy(part, side).wait_send()
        fwd_copy(part).wait_send()
    for block in range(4):
        for side in range(2):
            far_copy(block, side).wait_send()
            near_copy(block, side).wait_send()
    for block in range(1, 4):
        fin_copy(block).wait_send()
    for d in range(1, NX):
        stat_copy(d).wait_send()


def shard_rows(slot, h):
    return pl.ds(pl.multiple_of(slot * 64 + h * 32, 32), 32)


def tree_sum(terms):
    while len(terms) > 1:
        rest = [terms[-1]] if len(terms) % 2 else []
        terms = [a + b for a, b in zip(terms[0::2], terms[1::2])] + rest
    return terms[0]


def local(
    q_stream, k_stream, v_stream, short_filter, rates, residues, skip, prior_state, out_weight, residual, norm_gain
):
    vmem = pl.BlockSpec(memory_space=pltpu.VMEM)
    hbm = pl.BlockSpec(memory_space=pltpu.HBM)
    dma = pltpu.SemaphoreType.DMA
    wide = (ROWS * SUBS, LANES)
    params = (MODES * SUBS, LANES)
    pair = (2 * SUBS, LANES)
    rows = (ROWS, CHANS)
    scratch = [
        pltpu.VMEM(rows, BF16),
        pltpu.VMEM(rows, BF16),
        pltpu.VMEM(rows, BF16),
        pltpu.VMEM(short_filter.shape, F32),
        pltpu.VMEM((MODES, CHANS), F32),
        pltpu.VMEM((MODES, CHANS), F32),
        pltpu.VMEM((SUBS, LANES), F32),
        pltpu.VMEM((MODES, CHANS), F32),
        pltpu.VMEM(rows, BF16),
        pltpu.VMEM((SUBS, LANES), F32),
        pltpu.VMEM((3,) + wide, F32),
        pltpu.VMEM((3, 2 * SUBS, LANES), F32),
        pltpu.VMEM(wide, F32),
        pltpu.VMEM(wide, F32),
        pltpu.VMEM(wide, F32),
        pltpu.VMEM((9 * SUBS, LANES), F32),
        pltpu.VMEM(params, F32),
        pltpu.VMEM(params, F32),
        pltpu.VMEM(params, F32),
        pltpu.VMEM(params, F32),
        pltpu.VMEM(params, F32),
        pltpu.VMEM(params, F32),
        pltpu.VMEM(params, F32),
        pltpu.VMEM((NJ,) + pair, F32),
        pltpu.VMEM((NZ,) + pair, F32),
        pltpu.VMEM(pair, F32),
        pltpu.VMEM((NJ,) + pair, F32),
        pltpu.VMEM(params, F32),
        pltpu.VMEM((CHANS, CHANS), BF16),
        pltpu.VMEM((NY, ROWS, CHANS), BF16),
        pltpu.VMEM((8, ROWS, LANES), BF16),
        pltpu.VMEM((8, ROWS, LANES), BF16),
        pltpu.VMEM((8, BAND, ROWS), BF16),
        pltpu.VMEM((8, BAND, ROWS), BF16),
        pltpu.VMEM((NY, CHANS, ROWS), F32),
        pltpu.VMEM((NY - 1, BAND, ROWS), BF16),
        pltpu.VMEM((NY, BAND, ROWS), BF16),
        pltpu.VMEM((ROWS, CHANS), F32),
        pltpu.VMEM((SUBS, LANES), F32),
        pltpu.VMEM((NX - 1, SUBS, LANES), F32),
    ]
    sems = [dma((11,))]
    for count in (0, NJ, NZ, NJ, 18, 5, 4, 2, 8, 8, NY - 1, NX - 1):
        sems += [dma(()), dma(())] if count == 0 else [dma((count,)), dma((count,))]
    return pl.pallas_call(
        kernel,
        out_shape=(jax.ShapeDtypeStruct((ROWS, CHANS), BF16), jax.ShapeDtypeStruct((ROWS, CHANS), BF16)),
        in_specs=[hbm] * 11,
        out_specs=(vmem, vmem),
        scratch_shapes=scratch + sems,
        compiler_params=pltpu.CompilerParams(
            collective_id=0, has_side_effects=True, vmem_limit_bytes=63 * 1024 * 1024
        ),
        name="mixer",
    )(
        q_stream, k_stream, v_stream, short_filter, rates, residues, skip.reshape(SUBS, LANES), prior_state,
        out_weight.T, residual, norm_gain.reshape(SUBS, LANES),
    )


def solution(mesh):
    placed = (
        P("seq", "ch"),
        P("seq", "ch"),
        P("seq", "ch"),
        P(None, None, "ch"),
        P(None, "ch"),
        P(None, "ch"),
        P("ch"),
        P(None, "ch"),
        P("ch", "seq"),
        P("seq", "ch"),
        P("ch"),
    )
    return jax.shard_map(
        local,
        mesh=mesh,
        in_specs=placed,
        out_specs=(P("seq", "ch"), P("seq", "ch")),
        check_vma=False,
    )
```

```python
import functools

import jax
import jax.numpy as jnp
from jax import lax
from jax.experimental import pallas as pl
from jax.experimental.pallas import tpu as pltpu
from jax.sharding import PartitionSpec as P

MESH = pl.DeviceIdType.MESH
F32 = jnp.float32
BF16 = jnp.bfloat16
NX, NY, NZ, NH = 4, 4, 16, 2
NJ = NY * NH
ROWS = 128
CHANS = 1024
LANES = 128
SUBS = 8
MODES = 16
BAND = CHANS // NX


def one_minus_exp(x):
    series = jnp.full_like(x, 1.0 / 8.0)
    for n in (7.0, 6.0, 5.0, 4.0, 3.0, 2.0):
        series = (1.0 - x * series) * (1.0 / n)
    return jnp.where(x < 0.25, x * (1.0 - x * series), 1.0 - jnp.exp(-x))


def kernel(
    q_hbm, k_hbm, v_hbm, taps_hbm, rates_hbm, residues_hbm, skip_hbm, prior_hbm, weight_hbm, residual_hbm, gain_hbm,
    hidden_ref, normed_ref,
    q_ref, k_ref, v_ref, taps_ref, rates_ref, residues_ref, skip_ref, prior_ref, residual_ref, gain_ref,
    streams, halo, gated, featq, filt, tap_rows, rate_rows, res_rows, prior_rows, pole_rows, inres_rows, inflow_rows,
    ends, plane_in, line_in, line_out, back_out, carry,
    weights, acts, far_out, far_in, near_out, near_in, parts, back_rows, final_in, summed, stat_out, stat_in,
    input_s, halo_s, halo_r, s1_s, s1_r, s2_s, s2_r, s3_s, s3_r, ring_s, ring_r, sib_s, sib_r,
    act_s, act_r, fwd_s, fwd_r, far_s, far_r, near_s, near_r, fin_s, fin_r, stat_s, stat_r,
):
    seq, x = lax.axis_index("seq"), lax.axis_index("ch")
    z, j = lax.div(seq, NJ), lax.rem(seq, NJ)
    y, h = lax.div(j, NH), lax.rem(j, NH)

    def device(z_, j_, x_):
        return (z_ * NJ + j_, x_)

    def remote(src, dst, send, recv, target):
        return pltpu.make_async_remote_copy(
            src_ref=src, dst_ref=dst, send_sem=send, recv_sem=recv, device_id=target, device_id_type=MESH
        )

    def row(t):
        return pl.ds(pl.multiple_of(t * SUBS, SUBS), SUBS)

    own_weights = weights.at[shard_rows(0, h), :]
    inputs = [
        pltpu.make_async_copy(src, dst, input_s.at[n])
        for n, (src, dst) in enumerate((
            (k_hbm, k_ref), (v_hbm, v_ref), (q_hbm, q_ref), (weight_hbm, own_weights), (rates_hbm, rates_ref),
            (taps_hbm, taps_ref), (residues_hbm, residues_ref), (prior_hbm, prior_ref), (skip_hbm, skip_ref),
            (residual_hbm, residual_ref), (gain_hbm, gain_ref),
        ))
    ]
    for copy in inputs:
        copy.start()

    barrier = pltpu.get_barrier_semaphore()

    def greet(target):
        pl.semaphore_signal(barrier, inc=1, device_id=target, device_id_type=MESH)

    @pl.loop(1, NJ)
    def _(d):
        greet(device(z, lax.rem(j + d, NJ), x))

    @pl.loop(1, NZ)
    def _(d):
        greet(device(lax.rem(z + d, NZ), j, x))

    @pl.loop(1, NX)
    def _(d):
        greet(device(z, j, lax.rem(x + d, NX)))

    has_next, has_prev = seq < NZ * NJ - 1, seq > 0
    first_j, last_j = j == 0, j == NJ - 1

    @pl.when(last_j)
    def _():
        greet(device(lax.rem(z + 1, NZ), 0, x))

    @pl.when(first_j)
    def _():
        greet(device(lax.rem(z + NZ - 1, NZ), NJ - 1, x))

    peers = NJ + NZ + NX - 3
    edge = jnp.logical_or(first_j, last_j)

    @pl.when(edge)
    def _():
        pl.semaphore_wait(barrier, peers + 1)

    @pl.when(jnp.logical_not(edge))
    def _():
        pl.semaphore_wait(barrier, peers)

    direction = 1 - 2 * h
    sibling = device(z, y * NH + 1 - h, x)
    ring_to = [None] + [device(lax.rem(z + direction * d + NZ, NZ), j, x) for d in (1, 2)]

    def slot(far):
        return far if far == 0 else (1 - h) * (NZ - far) + h * far

    def ring_copy(far, part=None):
        hops = 2 - far % 2
        if far > 2:
            rows = [pl.ds(pl.multiple_of(slot(f) * 64, 64), 64) for f in (far - hops, far)]
            src, n = weights.at[rows[0], :], 2 * far
        else:
            shard = part + h - 2 * part * h
            rows = [shard_rows(slot(f), shard) for f in (0, far)]
            src, n = (weight_hbm if part == 0 else weights.at[rows[0], :]), 2 * far + part
        return remote(src, weights.at[rows[1], :], ring_s.at[n], ring_r.at[n], ring_to[hops])

    def sib_copy(step, count=2):
        if step == 0:
            return remote(weight_hbm, own_weights, sib_s.at[0], sib_r.at[0], sibling)
        first = (1 - h) * (NZ - 2 * step) + h * (2 * step - 1)
        both = weights.at[pl.ds(pl.multiple_of(first * 64, 64), 64 * count), :]
        return remote(both, both, sib_s.at[step], sib_r.at[step], sibling)

    upward = h == 0

    def arrived(far):
        if far > 2:
            ring_copy(far).wait_recv()
        else:
            ring_copy(far, 0).wait_recv()
            ring_copy(far, 1).wait_recv()

    def ring_step(step):
        far = 2 * step
        if step < 4:
            arrived(far)
            if step < 3:
                ring_copy(far + 2).start()
            else:
                pl.when(upward)(ring_copy(8).start)
            ring_copy(far + 1).start()
            arrived(far - 1)
            sib_copy(step).start()
        else:
            arrived(7)

            @pl.when(upward)
            def _():
                arrived(8)
                sib_copy(4).start()

            pl.when(jnp.logical_not(upward))(sib_copy(4, 1).start)

    ring_copy(2, 0).start()
    sib_copy(0).start()
    ring_copy(1, 0).start()

    def convert(stream, ref, begin, end):
        for part in range(SUBS):
            to = pl.ds(begin * SUBS + part, end - begin, stride=SUBS)
            streams[stream, to, :] = ref[begin:end, part * LANES : (part + 1) * LANES].astype(F32)

    for n in range(3):
        inputs[n].wait()
    for stream, ref in enumerate((q_ref, k_ref, v_ref)):
        convert(stream, ref, ROWS - 16, ROWS)
    last = (ROWS - 2) * SUBS
    halo_copy = remote(
        streams.at[:, pl.ds(last, 2 * SUBS), :], halo, halo_s, halo_r, (lax.rem(seq + 1, NZ * NJ), x)
    )
    pl.when(has_next)(halo_copy.start)
    convert(1, k_ref, 0, ROWS - 16)
    sib_copy(0).wait_recv()
    ring_copy(2, 1).start()
    ring_copy(1, 1).start()
    convert(2, v_ref, 0, ROWS - 16)
    for n in range(3, len(inputs)):
        inputs[n].wait()

    for part in range(SUBS):
        cut = slice(part * LANES, (part + 1) * LANES)
        to = pl.ds(part, MODES, stride=SUBS)
        rate_rows[to, :] = rates_ref[:, cut]
        res_rows[to, :] = residues_ref[:, cut]
        prior_rows[to, :] = prior_ref[:, cut]
        for stream in range(3):
            for tap in range(3):
                n = (3 * stream + tap) * SUBS + part
                tap_rows[n : n + 1, :] = taps_ref[stream, tap : tap + 1, cut]
    rates = rate_rows[...]
    inflow = jnp.sqrt(one_minus_exp(2.0 * rates))
    pole_rows[...] = jnp.exp(-rates)
    inflow_rows[...] = inflow
    inres_rows[...] = res_rows[...] * inflow

    def modes_of(ref):
        return [ref[m * SUBS : (m + 1) * SUBS, :] for m in range(MODES)]

    taps = [tap_rows[n * SUBS : (n + 1) * SUBS, :] for n in range(9)]
    poles = modes_of(pole_rows)
    skip = skip_ref[...]

    def feature(stream, now, back1, back2):
        return taps[3 * stream] * now + taps[3 * stream + 1] * back1 + taps[3 * stream + 2] * back2

    def gate(t, history):
        later, feats = [], []
        for stream, (back1, back2) in zip((1, 2), history):
            now = streams[stream, row(t), :]
            feats.append(feature(stream, now, back1, back2))
            later.append((now, back1))
        value = feats[0] * feats[1]
        gated[row(t), :] = value
        return value, tuple(later)

    def steps(begin, end, step, carried):
        def eight(block, carried):
            for t in range(8):
                carried = step(block * 8 + t, carried)
            return carried

        return lax.fori_loop(begin // 8, end // 8, eight, carried)

    def advance(states, value):
        return tuple(pole * state + value for pole, state in zip(poles, states))

    history = tuple((streams[s, SUBS : 2 * SUBS, :], streams[s, 0:SUBS, :]) for s in (1, 2))
    states = tuple(jnp.zeros((SUBS, LANES), F32) for _ in range(MODES))

    def scan_step(t, carried):
        states, history = carried
        value, history = gate(t, history)
        return advance(states, value), history

    scan = (states, history)
    for t in range(2, 8):
        scan = scan_step(t, scan)
    states, history = steps(8, ROWS, scan_step, scan)

    @pl.when(has_prev)
    def _():
        halo_copy.wait_recv()

    @pl.when(jnp.logical_not(has_prev))
    def _():
        halo[...] = jnp.zeros_like(halo)

    def halo_rows(s):
        return halo[s, SUBS : 2 * SUBS, :], halo[s, 0:SUBS, :]

    first, history = gate(0, (halo_rows(1), halo_rows(2)))
    second, history = gate(1, history)
    for m in range(MODES):
        at = slice(m * SUBS, (m + 1) * SUBS)
        late = jnp.exp(-(ROWS - 2.0) * rate_rows[at, :])
        ends[at, :] = inflow_rows[at, :] * (states[m] + late * (poles[m] * first + second))

    pair = 2 * SUBS

    def pair_rows(n):
        return pl.ds(pl.multiple_of(n * pair, pair), pair)

    def to_owner(d):
        to = lax.rem(j + d, NJ)
        return remote(ends.at[pair_rows(to), :], plane_in.at[j], s1_s.at[d], s1_r.at[d], device(z, to, x))

    def along_line(d):
        return remote(line_out, line_in.at[z], s2_s.at[d], s2_r.at[d], device(lax.rem(z + d, NZ), j, x))

    def from_owner(d):
        to = lax.rem(j + d, NJ)
        return remote(back_out.at[to], carry.at[pair_rows(j), :], s3_s.at[d], s3_r.at[d], device(z, to, x))

    @pl.loop(1, NJ)
    def _(d):
        to_owner(d).start()

    plane_in[j] = ends[pair_rows(j), :]
    ring_step(1)

    inres = modes_of(inres_rows)

    def output_step(t, carried):
        states, (back1, back2) = carried
        now = streams[0, row(t), :]
        featq[row(t), :] = feature(0, now, back1, back2)
        value = gated[row(t), :]
        states = advance(states, value)
        terms = [r * s for r, s in zip(inres, states)] + [skip * value]
        filt[row(t), :] = tree_sum(terms)
        return states, (now, back1)

    convert(0, q_ref, 0, ROWS - 16)
    states = tuple(jnp.zeros((SUBS, LANES), F32) for _ in range(MODES))
    outputs = steps(0, 64, output_step, (states, halo_rows(0)))

    @pl.loop(1, NJ)
    def _(d):
        to_owner(d).wait_recv()

    my_rates = rate_rows[pair_rows(j), :]
    block_decay = jnp.exp(-float(ROWS) * my_rates)
    plane_decay = jnp.exp(-float(ROWS * NJ) * my_rates)
    total = plane_in[0]
    for i in range(1, NJ):
        total = block_decay * total + plane_in[i]
    line_out[...] = total

    @pl.loop(1, NZ - z)
    def _(d):
        along_line(d).start()

    steps(64, ROWS, output_step, outputs)

    @pl.loop(1, z + 1)
    def _(d):
        along_line(d).wait_recv()

    incoming = lax.fori_loop(0, z, lambda i, s: plane_decay * s + line_in[i], prior_rows[pair_rows(j), :])
    for i in range(NJ):
        back_out[i] = incoming
        incoming = block_decay * incoming + plane_in[i]

    @pl.loop(1, NJ)
    def _(d):
        from_owner(d).start()

    carry[pair_rows(j), :] = back_out[j]
    ring_step(2)

    @pl.loop(1, NJ)
    def _(d):
        from_owner(d).wait_recv()

    half = ROWS // 2
    up = device(z, lax.rem(y + 1, NY) * NH + h, x)
    down = device(z, lax.rem(y + 3, NY) * NH + h, x)
    across = device(z, lax.rem(y + 2, NY) * NH + h, x)

    def act_copy(part, side):
        cut = pl.ds(part * half, half)
        n = 2 * part + side
        return remote(acts.at[0, cut, :], acts.at[1 + side, cut, :], act_s.at[n], act_r.at[n], (up, down)[side])

    def fwd_copy(part):
        cut = pl.ds(part * half, half)
        return remote(acts.at[1 + part, cut, :], acts.at[3, cut, :], fwd_s.at[part], fwd_r.at[part], (up, down)[part])

    def carried_step(t, waves):
        waves = tuple(pole * wave for pole, wave in zip(poles, waves))
        filt[row(t), :] = featq[row(t), :] * (filt[row(t), :] + tree_sum(list(waves)))
        return waves

    waves = tuple(res_rows[m * SUBS : (m + 1) * SUBS, :] * carry[m * SUBS : (m + 1) * SUBS, :] for m in range(MODES))
    for part in range(2):
        waves = steps(part * half, (part + 1) * half, carried_step, waves)
        for sub in range(SUBS):
            from_rows = pl.ds(part * half * SUBS + sub, half, stride=SUBS)
            acts[0, part * half : (part + 1) * half, sub * LANES : (sub + 1) * LANES] = filt[from_rows, :].astype(BF16)
        act_copy(part, 0).start()
        act_copy(part, 1).start()

    ring_step(3)
    for part in range(2):
        act_copy(part, part).wait_recv()
        fwd_copy(part).start()
    ring_step(4)
    for step in range(1, 4):
        sib_copy(step).wait_recv()
    pl.when(upward)(sib_copy(4, 1).wait_recv)
    pl.when(jnp.logical_not(upward))(sib_copy(4).wait_recv)

    right, left = device(z, j, lax.rem(x + 1, NX)), device(z, j, lax.rem(x + 3, NX))
    sides = (right, left)

    def band(block, dx):
        first = lax.rem(x + dx, NX) * 4 + NZ - z
        chunks = [pl.ds(pl.multiple_of(lax.rem(first + i, NZ) * 64, 64), 64) for i in range(4)]
        return [parts[block, chunk, :] for chunk in chunks]

    def far_copy(block, side):
        n = 2 * block + side
        return remote(far_out.at[n], far_in.at[n], far_s.at[n], far_r.at[n], sides[side])

    def near_copy(block, side):
        n = 2 * block + side
        return remote(near_out.at[n], near_in.at[n], near_s.at[n], near_r.at[n], sides[side])

    def begin(block):
        parts[block] = lax.dot_general(
            weights[...], acts[block], (((1,), (1,)), ((), ())), preferred_element_type=F32
        )
        far = band(block, 2)
        for side in range(2):
            for i in range(2):
                far_out[2 * block + side, 64 * i : 64 * i + 64, :] = far[2 * side + i].astype(BF16)
            far_copy(block, side).start()

    def middle(block):
        for side in range(2):
            n = 2 * block + side
            part = band(block, (1, 3)[side])
            far_copy(block, side).wait_recv()
            for i in range(4):
                value = part[i]
                if i // 2 == side:
                    value = value + far_in[n, 64 * (i % 2) : 64 * (i % 2) + 64, :].astype(F32)
                near_out[n, 64 * i : 64 * i + 64, :] = value.astype(BF16)
            near_copy(block, side).start()

    def fin_copy(block):
        to = (None, down, up, across)[block]
        return remote(back_rows.at[block - 1], final_in.at[y], fin_s.at[block - 1], fin_r.at[block - 1], to)

    def finish(block):
        for side in range(2):
            near_copy(block, side).wait_recv()
        value = jnp.concatenate(band(block, 0), axis=0) + near_in[2 * block].astype(F32) + near_in[2 * block + 1].astype(F32)
        if block == 0:
            final_in[y] = value.astype(BF16)
        else:
            back_rows[block - 1] = value.astype(BF16)
            fin_copy(block).start()

    begin(0)
    act_copy(1, 0).wait_recv()
    act_copy(0, 1).wait_recv()
    begin(1)
    middle(0)
    begin(2)
    middle(1)
    finish(0)
    for part in range(2):
        fwd_copy(part).wait_recv()
    begin(3)
    middle(2)
    finish(1)
    middle(3)
    finish(2)
    finish(3)
    for block in range(1, 4):
        fin_copy(block).wait_recv()

    squares = jnp.zeros((ROWS, LANES), F32)
    for tile in range(SUBS):
        cut = slice(tile * LANES, (tile + 1) * LANES)
        from_rows = slice((tile // 2) * 64, (tile // 2) * 64 + 64)
        mixed = [final_in[2 * (tile % 2) + odd, from_rows, :].astype(F32) for odd in range(2)]
        value = residual_ref[:, cut].astype(F32) + jnp.concatenate(mixed, axis=0).T
        summed[:, cut] = value
        hidden_ref[:, cut] = value.astype(BF16)
        squares = squares + value * value
    mine = jnp.sum(squares.T, axis=0, keepdims=True)
    stat_out[...] = jnp.broadcast_to(mine, (SUBS, LANES))

    def stat_copy(d):
        return remote(stat_out, stat_in.at[d - 1], stat_s.at[d - 1], stat_r.at[d - 1], device(z, j, lax.rem(x + d, NX)))

    for d in range(1, NX):
        stat_copy(d).start()
    for d in range(1, NX):
        stat_copy(d).wait_recv()
    total = stat_out[...] + stat_in[0] + stat_in[1] + stat_in[2]
    scale = lax.rsqrt(total * (1.0 / (NX * CHANS)) + 1e-05)
    scale = jnp.broadcast_to(scale[0:1, :], (ROWS, LANES)).T
    for tile in range(SUBS):
        cut = slice(tile * LANES, (tile + 1) * LANES)
        normed_ref[:, cut] = (summed[:, cut] * scale * gain_ref[tile : tile + 1, :]).astype(BF16)

    pl.when(has_next)(halo_copy.wait_send)

    @pl.loop(1, NJ)
    def _(d):
        to_owner(d).wait_send()
        from_owner(d).wait_send()

    @pl.loop(1, NZ - z)
    def _(d):
        along_line(d).wait_send()

    for step in range(4):
        sib_copy(step).wait_send()
    pl.when(upward)(sib_copy(4).wait_send)
    pl.when(jnp.logical_not(upward))(sib_copy(4, 1).wait_send)
    for far in range(3, 8):
        ring_copy(far).wait_send()
    pl.when(upward)(ring_copy(8).wait_send)
    for part in range(2):
        ring_copy(1, part).wait_send()
        ring_copy(2, part).wait_send()
        for side in range(2):
            act_copy(part, side).wait_send()
        fwd_copy(part).wait_send()
    for block in range(4):
        for side in range(2):
            far_copy(block, side).wait_send()
            near_copy(block, side).wait_send()
    for block in range(1, 4):
        fin_copy(block).wait_send()
    for d in range(1, NX):
        stat_copy(d).wait_send()


def shard_rows(slot, h):
    return pl.ds(pl.multiple_of(slot * 64 + h * 32, 32), 32)


def tree_sum(terms):
    while len(terms) > 1:
        rest = [terms[-1]] if len(terms) % 2 else []
        terms = [a + b for a, b in zip(terms[0::2], terms[1::2])] + rest
    return terms[0]


def local(
    q_stream, k_stream, v_stream, short_filter, rates, residues, skip, prior_state, out_weight, residual, norm_gain
):
    vmem = pl.BlockSpec(memory_space=pltpu.VMEM)
    hbm = pl.BlockSpec(memory_space=pltpu.HBM)
    dma = pltpu.SemaphoreType.DMA
    wide = (ROWS * SUBS, LANES)
    params = (MODES * SUBS, LANES)
    pair = (2 * SUBS, LANES)
    rows = (ROWS, CHANS)
    scratch = [
        pltpu.VMEM(rows, BF16),
        pltpu.VMEM(rows, BF16),
        pltpu.VMEM(rows, BF16),
        pltpu.VMEM(short_filter.shape, F32),
        pltpu.VMEM((MODES, CHANS), F32),
        pltpu.VMEM((MODES, CHANS), F32),
        pltpu.VMEM((SUBS, LANES), F32),
        pltpu.VMEM((MODES, CHANS), F32),
        pltpu.VMEM(rows, BF16),
        pltpu.VMEM((SUBS, LANES), F32),
        pltpu.VMEM((3,) + wide, F32),
        pltpu.VMEM((3, 2 * SUBS, LANES), F32),
        pltpu.VMEM(wide, F32),
        pltpu.VMEM(wide, F32),
        pltpu.VMEM(wide, F32),
        pltpu.VMEM((9 * SUBS, LANES), F32),
        pltpu.VMEM(params, F32),
        pltpu.VMEM(params, F32),
        pltpu.VMEM(params, F32),
        pltpu.VMEM(params, F32),
        pltpu.VMEM(params, F32),
        pltpu.VMEM(params, F32),
        pltpu.VMEM(params, F32),
        pltpu.VMEM((NJ,) + pair, F32),
        pltpu.VMEM((NZ,) + pair, F32),
        pltpu.VMEM(pair, F32),
        pltpu.VMEM((NJ,) + pair, F32),
        pltpu.VMEM(params, F32),
        pltpu.VMEM((CHANS, CHANS), BF16),
        pltpu.VMEM((NY, ROWS, CHANS), BF16),
        pltpu.VMEM((8, ROWS, LANES), BF16),
        pltpu.VMEM((8, ROWS, LANES), BF16),
        pltpu.VMEM((8, BAND, ROWS), BF16),
        pltpu.VMEM((8, BAND, ROWS), BF16),
        pltpu.VMEM((NY, CHANS, ROWS), F32),
        pltpu.VMEM((NY - 1, BAND, ROWS), BF16),
        pltpu.VMEM((NY, BAND, ROWS), BF16),
        pltpu.VMEM((ROWS, CHANS), F32),
        pltpu.VMEM((SUBS, LANES), F32),
        pltpu.VMEM((NX - 1, SUBS, LANES), F32),
    ]
    sems = [dma((11,))]
    for count in (0, NJ, NZ, NJ, 18, 5, 4, 2, 8, 8, NY - 1, NX - 1):
        sems += [dma(()), dma(())] if count == 0 else [dma((count,)), dma((count,))]
    return pl.pallas_call(
        kernel,
        out_shape=(jax.ShapeDtypeStruct((ROWS, CHANS), BF16), jax.ShapeDtypeStruct((ROWS, CHANS), BF16)),
        in_specs=[hbm] * 11,
        out_specs=(vmem, vmem),
        scratch_shapes=scratch + sems,
        compiler_params=pltpu.CompilerParams(
            collective_id=0, has_side_effects=True, vmem_limit_bytes=63 * 1024 * 1024
        ),
        name="mixer",
    )(
        q_stream, k_stream, v_stream, short_filter, rates, residues, skip.reshape(SUBS, LANES), prior_state,
        out_weight.T, residual, norm_gain.reshape(SUBS, LANES),
    )


def solution(mesh):
    placed = (
        P("seq", "ch"),
        P("seq", "ch"),
        P("seq", "ch"),
        P(None, None, "ch"),
        P(None, "ch"),
        P(None, "ch"),
        P("ch"),
        P(None, "ch"),
        P("ch", "seq"),
        P("seq", "ch"),
        P("ch"),
    )
    return jax.shard_map(
        local,
        mesh=mesh,
        in_specs=placed,
        out_specs=(P("seq", "ch"), P("seq", "ch")),
        check_vma=False,
    )
```

```python
import functools

import jax
import jax.numpy as jnp
from jax import lax
from jax.experimental import pallas as pl
from jax.experimental.pallas import tpu as pltpu
from jax.sharding import PartitionSpec as P

MESH = pl.DeviceIdType.MESH
F32 = jnp.float32
BF16 = jnp.bfloat16
NX, NY, NZ, NH = 4, 4, 16, 2
NJ = NY * NH
ROWS = 128
CHANS = 1024
LANES = 128
SUBS = 8
MODES = 16
BAND = CHANS // NX


def one_minus_exp(x):
    series = jnp.full_like(x, 1.0 / 8.0)
    for n in (7.0, 6.0, 5.0, 4.0, 3.0, 2.0):
        series = (1.0 - x * series) * (1.0 / n)
    return jnp.where(x < 0.25, x * (1.0 - x * series), 1.0 - jnp.exp(-x))


def kernel(
    q_hbm, k_hbm, v_hbm, taps_hbm, rates_hbm, residues_hbm, skip_hbm, prior_hbm, weight_hbm, residual_hbm, gain_hbm,
    hidden_ref, normed_ref,
    q_ref, k_ref, v_ref, taps_ref, rates_ref, residues_ref, skip_ref, prior_ref, residual_ref, gain_ref,
    streams, halo, gated, featq, filt, tap_rows, rate_rows, res_rows, prior_rows, pole_rows, inres_rows, inflow_rows,
    ends, plane_in, line_in, line_out, back_out, carry,
    weights, acts, far_out, far_in, near_out, near_in, direct_out, direct_in, parts, back_rows, final_in,
    res_out, res_in, summed, stat_out, stat_in,
    input_s, halo_s, halo_r, s1_s, s1_r, s2_s, s2_r, s3_s, s3_r, ring_s, ring_r, sib_s, sib_r,
    act_s, act_r, fwd_s, fwd_r, far_s, far_r, near_s, near_r, direct_s, direct_r,
    fin_s, fin_r, res_s, res_r, stat_s, stat_r,
):
    seq, x = lax.axis_index("seq"), lax.axis_index("ch")
    z, j = lax.div(seq, NJ), lax.rem(seq, NJ)
    y, h = lax.div(j, NH), lax.rem(j, NH)

    def device(z_, j_, x_):
        return (z_ * NJ + j_, x_)

    def remote(src, dst, send, recv, target):
        return pltpu.make_async_remote_copy(
            src_ref=src, dst_ref=dst, send_sem=send, recv_sem=recv, device_id=target, device_id_type=MESH
        )

    def row(t):
        return pl.ds(pl.multiple_of(t * SUBS, SUBS), SUBS)

    own_weights = weights.at[shard_rows(0, h), :]
    inputs = [
        pltpu.make_async_copy(src, dst, input_s.at[n])
        for n, (src, dst) in enumerate((
            (k_hbm, k_ref), (v_hbm, v_ref), (q_hbm, q_ref), (weight_hbm, own_weights), (rates_hbm, rates_ref),
            (taps_hbm, taps_ref), (residues_hbm, residues_ref), (prior_hbm, prior_ref), (skip_hbm, skip_ref),
            (residual_hbm, residual_ref), (gain_hbm, gain_ref),
        ))
    ]
    for copy in inputs:
        copy.start()

    barrier = pltpu.get_barrier_semaphore()

    def greet(target):
        pl.semaphore_signal(barrier, inc=1, device_id=target, device_id_type=MESH)

    @pl.loop(1, NJ)
    def _(d):
        greet(device(z, lax.rem(j + d, NJ), x))

    @pl.loop(1, NZ)
    def _(d):
        greet(device(lax.rem(z + d, NZ), j, x))

    @pl.loop(1, NX)
    def _(d):
        greet(device(z, j, lax.rem(x + d, NX)))

    has_next, has_prev = seq < NZ * NJ - 1, seq > 0
    first_j, last_j = j == 0, j == NJ - 1

    @pl.when(last_j)
    def _():
        greet(device(lax.rem(z + 1, NZ), 0, x))

    @pl.when(first_j)
    def _():
        greet(device(lax.rem(z + NZ - 1, NZ), NJ - 1, x))

    @pl.loop(1, 3)
    def _(d):
        greet(device(lax.rem(z + d, NZ), y * NH + 1 - h, x))
        greet(device(lax.rem(z + NZ - d, NZ), y * NH + 1 - h, x))

    @pl.loop(1, NX)
    def _(d):
        @pl.loop(1, NY)
        def _(e):
            greet(device(z, lax.rem(y + e, NY) * NH + h, lax.rem(x + d, NX)))

    peers = NJ + NZ + NX - 3 + 4 + (NX - 1) * (NY - 1)
    edge = jnp.logical_or(first_j, last_j)

    @pl.when(edge)
    def _():
        pl.semaphore_wait(barrier, peers + 1)

    @pl.when(jnp.logical_not(edge))
    def _():
        pl.semaphore_wait(barrier, peers)

    direction = 1 - 2 * h
    sibling = device(z, y * NH + 1 - h, x)
    ring_to = [None] + [device(lax.rem(z + direction * d + NZ, NZ), j, x) for d in (1, 2)]
    other_to = [None] + [device(lax.rem(z + direction * d + NZ, NZ), y * NH + 1 - h, x) for d in (1, 2)]

    def slot(far):
        return far if far == 0 else (1 - h) * (NZ - far) + h * far

    def ring_copy(far, part=None, other=False):
        hops = 2 - far % 2
        if far > 2:
            rows = [pl.ds(pl.multiple_of(slot(f) * 64, 64), 64) for f in (far - hops, far)]
            src, n = weights.at[rows[0], :], 2 * far
        else:
            shard = part + h - 2 * part * h
            rows = [shard_rows(slot(f), shard) for f in (0, far)]
            src, n = (weight_hbm if part == 0 else weights.at[rows[0], :]), 2 * far + part
        if other:
            return remote(src, weights.at[rows[1], :], ring_s.at[n + 1], ring_r.at[n + 1], other_to[hops])
        return remote(src, weights.at[rows[1], :], ring_s.at[n], ring_r.at[n], ring_to[hops])

    def sib_copy(step):
        if step == 0:
            return remote(weight_hbm, own_weights, sib_s.at[0], sib_r.at[0], sibling)
        first = (1 - h) * (NZ - 2 * step) + h * (2 * step - 1)
        both = weights.at[pl.ds(pl.multiple_of(first * 64, 64), 128), :]
        return remote(both, both, sib_s.at[step], sib_r.at[step], sibling)

    upward = h == 0

    def arrived(far):
        if far > 2:
            ring_copy(far).wait_recv()
        else:
            ring_copy(far, 0).wait_recv()
            ring_copy(far, 1).wait_recv()

    def ring_step(step):
        far = 2 * step
        if step < 4:
            arrived(far)
            if step < 3:
                ring_copy(far + 2).start()
                ring_copy(far + 1).start()
            else:

                @pl.when(upward)
                def _():
                    ring_copy(8).start()
                    ring_copy(8, other=True).start()

                ring_copy(7).start()
                ring_copy(7, other=True).start()
            arrived(far - 1)
            sib_copy(step).start()
        else:
            arrived(7)
            ring_copy(7, other=True).wait_recv()

            @pl.when(upward)
            def _():
                arrived(8)

            @pl.when(jnp.logical_not(upward))
            def _():
                ring_copy(8, other=True).wait_recv()

    ring_copy(2, 0).start()
    sib_copy(0).start()
    ring_copy(1, 0).start()

    def convert(stream, ref, begin, end):
        for part in range(SUBS):
            to = pl.ds(begin * SUBS + part, end - begin, stride=SUBS)
            streams[stream, to, :] = ref[begin:end, part * LANES : (part + 1) * LANES].astype(F32)

    for n in range(3):
        inputs[n].wait()
    for stream, ref in enumerate((q_ref, k_ref, v_ref)):
        convert(stream, ref, ROWS - 16, ROWS)
    last = (ROWS - 2) * SUBS
    halo_copy = remote(
        streams.at[:, pl.ds(last, 2 * SUBS), :], halo, halo_s, halo_r, (lax.rem(seq + 1, NZ * NJ), x)
    )
    pl.when(has_next)(halo_copy.start)
    convert(1, k_ref, 0, ROWS - 16)
    sib_copy(0).wait_recv()
    ring_copy(2, 1).start()
    ring_copy(1, 1).start()
    convert(2, v_ref, 0, ROWS - 16)
    for n in range(3, len(inputs)):
        inputs[n].wait()

    for part in range(SUBS):
        cut = slice(part * LANES, (part + 1) * LANES)
        to = pl.ds(part, MODES, stride=SUBS)
        rate_rows[to, :] = rates_ref[:, cut]
        res_rows[to, :] = residues_ref[:, cut]
        prior_rows[to, :] = prior_ref[:, cut]
        for stream in range(3):
            for tap in range(3):
                n = (3 * stream + tap) * SUBS + part
                tap_rows[n : n + 1, :] = taps_ref[stream, tap : tap + 1, cut]
    rates = rate_rows[...]
    inflow = jnp.sqrt(one_minus_exp(2.0 * rates))
    pole_rows[...] = jnp.exp(-rates)
    inflow_rows[...] = inflow
    inres_rows[...] = res_rows[...] * inflow

    def modes_of(ref):
        return [ref[m * SUBS : (m + 1) * SUBS, :] for m in range(MODES)]

    taps = [tap_rows[n * SUBS : (n + 1) * SUBS, :] for n in range(9)]
    poles = modes_of(pole_rows)
    skip = skip_ref[...]

    def feature(stream, now, back1, back2):
        return taps[3 * stream] * now + taps[3 * stream + 1] * back1 + taps[3 * stream + 2] * back2

    def gate(t, history):
        later, feats = [], []
        for stream, (back1, back2) in zip((1, 2), history):
            now = streams[stream, row(t), :]
            feats.append(feature(stream, now, back1, back2))
            later.append((now, back1))
        value = feats[0] * feats[1]
        gated[row(t), :] = value
        return value, tuple(later)

    def steps(begin, end, step, carried):
        def eight(block, carried):
            for t in range(8):
                carried = step(block * 8 + t, carried)
            return carried

        return lax.fori_loop(begin // 8, end // 8, eight, carried)

    def advance(states, value):
        return tuple(pole * state + value for pole, state in zip(poles, states))

    history = tuple((streams[s, SUBS : 2 * SUBS, :], streams[s, 0:SUBS, :]) for s in (1, 2))
    states = tuple(jnp.zeros((SUBS, LANES), F32) for _ in range(MODES))

    def scan_step(t, carried):
        states, history = carried
        value, history = gate(t, history)
        return advance(states, value), history

    scan = (states, history)
    for t in range(2, 8):
        scan = scan_step(t, scan)
    states, history = steps(8, ROWS, scan_step, scan)

    @pl.when(has_prev)
    def _():
        halo_copy.wait_recv()

    @pl.when(jnp.logical_not(has_prev))
    def _():
        halo[...] = jnp.zeros_like(halo)

    def halo_rows(s):
        return halo[s, SUBS : 2 * SUBS, :], halo[s, 0:SUBS, :]

    first, history = gate(0, (halo_rows(1), halo_rows(2)))
    second, history = gate(1, history)
    for m in range(MODES):
        at = slice(m * SUBS, (m + 1) * SUBS)
        late = jnp.exp(-(ROWS - 2.0) * rate_rows[at, :])
        ends[at, :] = inflow_rows[at, :] * (states[m] + late * (poles[m] * first + second))

    pair = 2 * SUBS

    def pair_rows(n):
        return pl.ds(pl.multiple_of(n * pair, pair), pair)

    def to_owner(d):
        to = lax.rem(j + d, NJ)
        return remote(ends.at[pair_rows(to), :], plane_in.at[j], s1_s.at[d], s1_r.at[d], device(z, to, x))

    def along_line(d):
        return remote(line_out, line_in.at[z], s2_s.at[d], s2_r.at[d], device(lax.rem(z + d, NZ), j, x))

    def from_owner(d):
        to = lax.rem(j + d, NJ)
        return remote(back_out.at[to], carry.at[pair_rows(j), :], s3_s.at[d], s3_r.at[d], device(z, to, x))

    @pl.loop(1, NJ)
    def _(d):
        to_owner(d).start()

    plane_in[j] = ends[pair_rows(j), :]
    ring_step(1)

    inres = modes_of(inres_rows)

    def output_step(t, carried):
        states, (back1, back2) = carried
        now = streams[0, row(t), :]
        featq[row(t), :] = feature(0, now, back1, back2)
        value = gated[row(t), :]
        states = advance(states, value)
        terms = [r * s for r, s in zip(inres, states)] + [skip * value]
        filt[row(t), :] = tree_sum(terms)
        return states, (now, back1)

    for tile in range(SUBS):
        turned = residual_ref[:, tile * LANES : (tile + 1) * LANES].astype(F32).T.astype(BF16)
        to_rows = slice((tile // 2) * 64, (tile // 2) * 64 + 64)
        for odd in range(2):
            res_out[2 * (tile % 2) + odd, to_rows, :] = turned[64 * odd : 64 * odd + 64, :]

    def beside(block, dx=0):
        return device(z, lax.rem(y + (0, 3, 1, 2)[block], NY) * NH + h, x if dx == 0 else lax.rem(x + dx, NX))

    def res_copy(block):
        ahead = (0, 1, 3, 2)[block]
        to = lax.rem(y + ahead, NY)
        n = block - 1
        return remote(res_out.at[to], res_in.at[n], res_s.at[n], res_r.at[n], device(z, to * NH + h, x))

    for block in range(1, 4):
        res_copy(block).start()

    convert(0, q_ref, 0, ROWS - 16)
    states = tuple(jnp.zeros((SUBS, LANES), F32) for _ in range(MODES))
    outputs = steps(0, 64, output_step, (states, halo_rows(0)))

    @pl.loop(1, NJ)
    def _(d):
        to_owner(d).wait_recv()

    my_rates = rate_rows[pair_rows(j), :]
    block_decay = jnp.exp(-float(ROWS) * my_rates)
    plane_decay = jnp.exp(-float(ROWS * NJ) * my_rates)
    total = plane_in[0]
    for i in range(1, NJ):
        total = block_decay * total + plane_in[i]
    line_out[...] = total

    @pl.loop(1, NZ - z)
    def _(d):
        along_line(d).start()

    ring_step(2)
    steps(64, ROWS, output_step, outputs)

    @pl.loop(1, z + 1)
    def _(d):
        along_line(d).wait_recv()

    incoming = lax.fori_loop(0, z, lambda i, s: plane_decay * s + line_in[i], prior_rows[pair_rows(j), :])
    for i in range(NJ):
        back_out[i] = incoming
        incoming = block_decay * incoming + plane_in[i]

    @pl.loop(1, NJ)
    def _(d):
        from_owner(d).start()

    carry[pair_rows(j), :] = back_out[j]
    ring_step(3)

    @pl.loop(1, NJ)
    def _(d):
        from_owner(d).wait_recv()

    half = ROWS // 2
    up = device(z, lax.rem(y + 1, NY) * NH + h, x)
    down = device(z, lax.rem(y + 3, NY) * NH + h, x)
    across = device(z, lax.rem(y + 2, NY) * NH + h, x)

    def act_copy(part, side):
        cut = pl.ds(part * half, half)
        n = 2 * part + side
        return remote(acts.at[0, cut, :], acts.at[1 + side, cut, :], act_s.at[n], act_r.at[n], (up, down)[side])

    def fwd_copy(part):
        cut = pl.ds(part * half, half)
        return remote(acts.at[1 + part, cut, :], acts.at[3, cut, :], fwd_s.at[part], fwd_r.at[part], (up, down)[part])

    def carried_step(t, waves):
        waves = tuple(pole * wave for pole, wave in zip(poles, waves))
        filt[row(t), :] = featq[row(t), :] * (filt[row(t), :] + tree_sum(list(waves)))
        return waves

    waves = tuple(res_rows[m * SUBS : (m + 1) * SUBS, :] * carry[m * SUBS : (m + 1) * SUBS, :] for m in range(MODES))
    for part in range(2):
        waves = steps(part * half, (part + 1) * half, carried_step, waves)
        for sub in range(SUBS):
            from_rows = pl.ds(part * half * SUBS + sub, half, stride=SUBS)
            acts[0, part * half : (part + 1) * half, sub * LANES : (sub + 1) * LANES] = filt[from_rows, :].astype(BF16)
        act_copy(part, part).start()
    act_copy(1, 0).start()
    act_copy(0, 1).start()

    ring_step(4)
    for part in range(2):
        act_copy(part, part).wait_recv()
        fwd_copy(part).start()
    for step in range(1, 4):
        sib_copy(step).wait_recv()

    right, left = device(z, j, lax.rem(x + 1, NX)), device(z, j, lax.rem(x + 3, NX))
    sides = (right, left)

    def band(block, dx):
        first = lax.rem(x + dx, NX) * 4 + NZ - z
        chunks = [pl.ds(pl.multiple_of(lax.rem(first + i, NZ) * 64, 64), 64) for i in range(4)]
        return [parts[block, chunk, :] for chunk in chunks]

    def far_copy(block, side):
        n = 2 * block + side
        return remote(far_out.at[n], far_in.at[n], far_s.at[n], far_r.at[n], sides[side])

    def near_copy(block, side):
        n = 2 * block + side
        return remote(near_out.at[n], near_in.at[n], near_s.at[n], near_r.at[n], sides[side])

    def direct_copy(dx):
        n = dx - 1
        to = device(z, j, lax.rem(x + dx, NX))
        return remote(direct_out.at[n], direct_in.at[n], direct_s.at[n], direct_r.at[n], to)

    def begin(block):
        parts[block] = lax.dot_general(
            weights[...], acts[block], (((1,), (1,)), ((), ())), preferred_element_type=F32
        )
        far = band(block, 2)
        if block == 3:
            for dx, chunks in ((2, far), (1, band(block, 1)), (3, band(block, 3))):
                for i in range(4):
                    direct_out[dx - 1, 64 * i : 64 * i + 64, :] = chunks[i].astype(BF16)
                direct_copy(dx).start()
            return
        for side in range(2):
            for i in range(2):
                far_out[2 * block + side, 64 * i : 64 * i + 64, :] = far[2 * side + i].astype(BF16)
            far_copy(block, side).start()

    def middle(block):
        for side in range(2):
            n = 2 * block + side
            part = band(block, (1, 3)[side])
            far_copy(block, side).wait_recv()
            for i in range(4):
                value = part[i]
                if i // 2 == side:
                    value = value + far_in[n, 64 * (i % 2) : 64 * (i % 2) + 64, :].astype(F32)
                near_out[n, 64 * i : 64 * i + 64, :] = value.astype(BF16)
            near_copy(block, side).start()

    def fin_copy(block):
        return remote(
            back_rows.at[block - 1], final_in.at[y], fin_s.at[block - 1], fin_r.at[block - 1], beside(block)
        )

    def stat_copy(block, dx):
        n = 4 * block + dx
        return remote(stat_out.at[block], stat_in.at[n], stat_s.at[n], stat_r.at[n], beside(block, dx))

    stat_pairs = [(block, dx) for block in range(4) for dx in range(4) if (block, dx) != (0, 0)]

    def finish(block):
        value = jnp.concatenate(band(block, 0), axis=0)
        if block == 3:
            for dx in range(1, NX):
                direct_copy(dx).wait_recv()
                value = value + direct_in[dx - 1].astype(F32)
        else:
            for side in range(2):
                near_copy(block, side).wait_recv()
                value = value + near_in[2 * block + side].astype(F32)
        if block == 0:
            value = value + res_out[y].astype(F32)
        else:
            res_copy(block).wait_recv()
            value = value + res_in[block - 1].astype(F32)
        squares = jnp.sum(value * value, axis=0, keepdims=True)
        stat_out[block] = jnp.broadcast_to(squares, (SUBS, LANES))
        if block == 0:
            final_in[y] = value.astype(BF16)
            stat_in[0] = stat_out[0]
        else:
            back_rows[block - 1] = value.astype(BF16)
            fin_copy(block).start()
        for dx in range(NX):
            if (block, dx) in stat_pairs:
                stat_copy(block, dx).start()

    begin(0)
    act_copy(1, 0).wait_recv()
    act_copy(0, 1).wait_recv()
    begin(1)
    middle(0)
    begin(2)
    middle(1)
    finish(0)
    for part in range(2):
        fwd_copy(part).wait_recv()
    begin(3)
    middle(2)
    finish(1)
    finish(2)
    finish(3)
    for block in range(1, 4):
        fin_copy(block).wait_recv()

    for tile in range(SUBS):
        cut = slice(tile * LANES, (tile + 1) * LANES)
        from_rows = slice((tile // 2) * 64, (tile // 2) * 64 + 64)
        mixed = [final_in[2 * (tile % 2) + odd, from_rows, :].astype(F32) for odd in range(2)]
        value = jnp.concatenate(mixed, axis=0).T
        summed[:, cut] = value
        hidden_ref[:, cut] = value.astype(BF16)
    for block, dx in stat_pairs:
        stat_copy(block, dx).wait_recv()
    total = tree_sum([stat_in[n] for n in range(16)])
    scale = lax.rsqrt(total * (1.0 / (NX * CHANS)) + 1e-05)
    scale = jnp.broadcast_to(scale[0:1, :], (ROWS, LANES)).T
    for tile in range(SUBS):
        cut = slice(tile * LANES, (tile + 1) * LANES)
        normed_ref[:, cut] = (summed[:, cut] * scale * gain_ref[tile : tile + 1, :]).astype(BF16)

    pl.when(has_next)(halo_copy.wait_send)

    @pl.loop(1, NJ)
    def _(d):
        to_owner(d).wait_send()
        from_owner(d).wait_send()

    @pl.loop(1, NZ - z)
    def _(d):
        along_line(d).wait_send()

    for step in range(4):
        sib_copy(step).wait_send()
    for far in range(3, 8):
        ring_copy(far).wait_send()
    ring_copy(7, other=True).wait_send()

    @pl.when(upward)
    def _():
        ring_copy(8).wait_send()
        ring_copy(8, other=True).wait_send()

    for part in range(2):
        ring_copy(1, part).wait_send()
        ring_copy(2, part).wait_send()
        for side in range(2):
            act_copy(part, side).wait_send()
        fwd_copy(part).wait_send()
    for block in range(3):
        for side in range(2):
            far_copy(block, side).wait_send()
            near_copy(block, side).wait_send()
    for dx in range(1, NX):
        direct_copy(dx).wait_send()
    for block in range(1, 4):
        fin_copy(block).wait_send()
        res_copy(block).wait_send()
    for block, dx in stat_pairs:
        stat_copy(block, dx).wait_send()


def shard_rows(slot, h):
    return pl.ds(pl.multiple_of(slot * 64 + h * 32, 32), 32)


def tree_sum(terms):
    while len(terms) > 1:
        rest = [terms[-1]] if len(terms) % 2 else []
        terms = [a + b for a, b in zip(terms[0::2], terms[1::2])] + rest
    return terms[0]


def local(
    q_stream, k_stream, v_stream, short_filter, rates, residues, skip, prior_state, out_weight, residual, norm_gain
):
    vmem = pl.BlockSpec(memory_space=pltpu.VMEM)
    hbm = pl.BlockSpec(memory_space=pltpu.HBM)
    dma = pltpu.SemaphoreType.DMA
    wide = (ROWS * SUBS, LANES)
    params = (MODES * SUBS, LANES)
    pair = (2 * SUBS, LANES)
    rows = (ROWS, CHANS)
    scratch = [
        pltpu.VMEM(rows, BF16),
        pltpu.VMEM(rows, BF16),
        pltpu.VMEM(rows, BF16),
        pltpu.VMEM(short_filter.shape, F32),
        pltpu.VMEM((MODES, CHANS), F32),
        pltpu.VMEM((MODES, CHANS), F32),
        pltpu.VMEM((SUBS, LANES), F32),
        pltpu.VMEM((MODES, CHANS), F32),
        pltpu.VMEM(rows, BF16),
        pltpu.VMEM((SUBS, LANES), F32),
        pltpu.VMEM((3,) + wide, F32),
        pltpu.VMEM((3, 2 * SUBS, LANES), F32),
        pltpu.VMEM(wide, F32),
        pltpu.VMEM(wide, F32),
        pltpu.VMEM(wide, F32),
        pltpu.VMEM((9 * SUBS, LANES), F32),
        pltpu.VMEM(params, F32),
        pltpu.VMEM(params, F32),
        pltpu.VMEM(params, F32),
        pltpu.VMEM(params, F32),
        pltpu.VMEM(params, F32),
        pltpu.VMEM(params, F32),
        pltpu.VMEM(params, F32),
        pltpu.VMEM((NJ,) + pair, F32),
        pltpu.VMEM((NZ,) + pair, F32),
        pltpu.VMEM(pair, F32),
        pltpu.VMEM((NJ,) + pair, F32),
        pltpu.VMEM(params, F32),
        pltpu.VMEM((CHANS, CHANS), BF16),
        pltpu.VMEM((NY, ROWS, CHANS), BF16),
        pltpu.VMEM((6, ROWS, LANES), BF16),
        pltpu.VMEM((6, ROWS, LANES), BF16),
        pltpu.VMEM((6, BAND, ROWS), BF16),
        pltpu.VMEM((6, BAND, ROWS), BF16),
        pltpu.VMEM((NX - 1, BAND, ROWS), BF16),
        pltpu.VMEM((NX - 1, BAND, ROWS), BF16),
        pltpu.VMEM((NY, CHANS, ROWS), F32),
        pltpu.VMEM((NY - 1, BAND, ROWS), BF16),
        pltpu.VMEM((NY, BAND, ROWS), BF16),
        pltpu.VMEM((NY, BAND, ROWS), BF16),
        pltpu.VMEM((NY - 1, BAND, ROWS), BF16),
        pltpu.VMEM((ROWS, CHANS), F32),
        pltpu.VMEM((NY, SUBS, LANES), F32),
        pltpu.VMEM((16, SUBS, LANES), F32),
    ]
    sems = [dma((11,))]
    for count in (0, NJ, NZ, NJ, 18, 4, 4, 2, 6, 6, 3, 3, 3, 16):
        sems += [dma(()), dma(())] if count == 0 else [dma((count,)), dma((count,))]
    return pl.pallas_call(
        kernel,
        out_shape=(jax.ShapeDtypeStruct((ROWS, CHANS), BF16), jax.ShapeDtypeStruct((ROWS, CHANS), BF16)),
        in_specs=[hbm] * 11,
        out_specs=(vmem, vmem),
        scratch_shapes=scratch + sems,
        compiler_params=pltpu.CompilerParams(
            collective_id=0, has_side_effects=True, vmem_limit_bytes=63 * 1024 * 1024
        ),
        name="mixer",
    )(
        q_stream, k_stream, v_stream, short_filter, rates, residues, skip.reshape(SUBS, LANES), prior_state,
        out_weight.T, residual, norm_gain.reshape(SUBS, LANES),
    )


def solution(mesh):
    placed = (
        P("seq", "ch"),
        P("seq", "ch"),
        P("seq", "ch"),
        P(None, None, "ch"),
        P(None, "ch"),
        P(None, "ch"),
        P("ch"),
        P(None, "ch"),
        P("ch", "seq"),
        P("seq", "ch"),
        P("ch"),
    )
    return jax.shard_map(
        local,
        mesh=mesh,
        in_specs=placed,
        out_specs=(P("seq", "ch"), P("seq", "ch")),
        check_vma=False,
    )
```

```python
import functools

import jax
import jax.numpy as jnp
from jax import lax
from jax.experimental import pallas as pl
from jax.experimental.pallas import tpu as pltpu
from jax.sharding import PartitionSpec as P

MESH = pl.DeviceIdType.MESH
F32 = jnp.float32
BF16 = jnp.bfloat16
NX, NY, NZ, NH = 4, 4, 16, 2
NJ = NY * NH
ROWS = 128
CHANS = 1024
LANES = 128
SUBS = 8
MODES = 16
BAND = CHANS // NX


def one_minus_exp(x):
    series = jnp.full_like(x, 1.0 / 8.0)
    for n in (7.0, 6.0, 5.0, 4.0, 3.0, 2.0):
        series = (1.0 - x * series) * (1.0 / n)
    return jnp.where(x < 0.25, x * (1.0 - x * series), 1.0 - jnp.exp(-x))


def kernel(
    q_hbm, k_hbm, v_hbm, taps_hbm, rates_hbm, residues_hbm, skip_hbm, prior_hbm, weight_hbm, residual_hbm, gain_hbm,
    hidden_ref, normed_ref,
    q_ref, k_ref, v_ref, taps_ref, rates_ref, residues_ref, skip_ref, prior_ref, residual_ref, gain_ref,
    streams, halo, gated, featq, filt, tap_rows, rate_rows, res_rows, prior_rows, pole_rows, inres_rows, inflow_rows,
    ends, plane_in, line_in, line_out, back_out, carry,
    weights, acts, far_out, far_in, near_out, near_in, direct_out, direct_in, parts, back_rows, final_in,
    res_out, res_in, summed, stat_out, stat_in,
    input_s, halo_s, halo_r, s1_s, s1_r, s2_s, s2_r, s3_s, s3_r, ring_s, ring_r, sib_s, sib_r,
    act_s, act_r, fwd_s, fwd_r, far_s, far_r, near_s, near_r, direct_s, direct_r,
    fin_s, fin_r, res_s, res_r, stat_s, stat_r,
):
    seq, x = lax.axis_index("seq"), lax.axis_index("ch")
    z, j = lax.div(seq, NJ), lax.rem(seq, NJ)
    y, h = lax.div(j, NH), lax.rem(j, NH)

    def device(z_, j_, x_):
        return (z_ * NJ + j_, x_)

    def remote(src, dst, send, recv, target):
        return pltpu.make_async_remote_copy(
            src_ref=src, dst_ref=dst, send_sem=send, recv_sem=recv, device_id=target, device_id_type=MESH
        )

    def row(t):
        return pl.ds(pl.multiple_of(t * SUBS, SUBS), SUBS)

    own_weights = weights.at[shard_rows(0, h), :]
    inputs = [
        pltpu.make_async_copy(src, dst, input_s.at[n])
        for n, (src, dst) in enumerate((
            (k_hbm, k_ref), (v_hbm, v_ref), (q_hbm, q_ref), (weight_hbm, own_weights), (rates_hbm, rates_ref),
            (taps_hbm, taps_ref), (residues_hbm, residues_ref), (prior_hbm, prior_ref), (skip_hbm, skip_ref),
            (residual_hbm, residual_ref), (gain_hbm, gain_ref),
        ))
    ]
    for copy in inputs:
        copy.start()

    barrier = pltpu.get_barrier_semaphore()

    def greet(target):
        pl.semaphore_signal(barrier, inc=1, device_id=target, device_id_type=MESH)

    @pl.loop(1, NJ)
    def _(d):
        greet(device(z, lax.rem(j + d, NJ), x))

    @pl.loop(1, NZ)
    def _(d):
        greet(device(lax.rem(z + d, NZ), j, x))

    @pl.loop(1, NX)
    def _(d):
        greet(device(z, j, lax.rem(x + d, NX)))

    has_next, has_prev = seq < NZ * NJ - 1, seq > 0
    first_j, last_j = j == 0, j == NJ - 1

    @pl.when(last_j)
    def _():
        greet(device(lax.rem(z + 1, NZ), 0, x))

    @pl.when(first_j)
    def _():
        greet(device(lax.rem(z + NZ - 1, NZ), NJ - 1, x))

    @pl.loop(1, 3)
    def _(d):
        greet(device(lax.rem(z + d, NZ), y * NH + 1 - h, x))
        greet(device(lax.rem(z + NZ - d, NZ), y * NH + 1 - h, x))

    @pl.loop(1, NX)
    def _(d):
        @pl.loop(1, NY)
        def _(e):
            greet(device(z, lax.rem(y + e, NY) * NH + h, lax.rem(x + d, NX)))

    peers = NJ + NZ + NX - 3 + 4 + (NX - 1) * (NY - 1)
    edge = jnp.logical_or(first_j, last_j)

    @pl.when(edge)
    def _():
        pl.semaphore_wait(barrier, peers + 1)

    @pl.when(jnp.logical_not(edge))
    def _():
        pl.semaphore_wait(barrier, peers)

    direction = 1 - 2 * h
    sibling = device(z, y * NH + 1 - h, x)
    ring_to = [None] + [device(lax.rem(z + direction * d + NZ, NZ), j, x) for d in (1, 2)]
    other_to = [None] + [device(lax.rem(z + direction * d + NZ, NZ), y * NH + 1 - h, x) for d in (1, 2)]

    def slot(far):
        return far if far == 0 else (1 - h) * (NZ - far) + h * far

    def ring_copy(far, part=None, other=False):
        hops = 2 - far % 2
        if far > 2:
            rows = [pl.ds(pl.multiple_of(slot(f) * 64, 64), 64) for f in (far - hops, far)]
            src, n = weights.at[rows[0], :], 2 * far
        else:
            shard = part + h - 2 * part * h
            rows = [shard_rows(slot(f), shard) for f in (0, far)]
            src, n = (weight_hbm if part == 0 else weights.at[rows[0], :]), 2 * far + part
        if other:
            return remote(src, weights.at[rows[1], :], ring_s.at[n + 1], ring_r.at[n + 1], other_to[hops])
        return remote(src, weights.at[rows[1], :], ring_s.at[n], ring_r.at[n], ring_to[hops])

    def sib_copy(step):
        if step == 0:
            return remote(weight_hbm, own_weights, sib_s.at[0], sib_r.at[0], sibling)
        first = (1 - h) * (NZ - 2 * step) + h * (2 * step - 1)
        both = weights.at[pl.ds(pl.multiple_of(first * 64, 64), 128), :]
        return remote(both, both, sib_s.at[step], sib_r.at[step], sibling)

    upward = h == 0

    def arrived(far):
        if far > 2:
            ring_copy(far).wait_recv()
        else:
            ring_copy(far, 0).wait_recv()
            ring_copy(far, 1).wait_recv()

    def ring_step(step):
        far = 2 * step
        if step < 4:
            arrived(far)
            if step < 3:
                ring_copy(far + 2).start()
                ring_copy(far + 1).start()
            else:

                @pl.when(upward)
                def _():
                    ring_copy(8).start()
                    ring_copy(8, other=True).start()

                ring_copy(7).start()
                ring_copy(7, other=True).start()
            arrived(far - 1)
            sib_copy(step).start()
        else:
            arrived(7)
            ring_copy(7, other=True).wait_recv()

            @pl.when(upward)
            def _():
                arrived(8)

            @pl.when(jnp.logical_not(upward))
            def _():
                ring_copy(8, other=True).wait_recv()

    ring_copy(2, 0).start()
    sib_copy(0).start()
    ring_copy(1, 0).start()

    def convert(stream, ref, begin, end):
        for part in range(SUBS):
            to = pl.ds(begin * SUBS + part, end - begin, stride=SUBS)
            streams[stream, to, :] = ref[begin:end, part * LANES : (part + 1) * LANES].astype(F32)

    for n in range(3):
        inputs[n].wait()
    for stream, ref in enumerate((q_ref, k_ref, v_ref)):
        convert(stream, ref, ROWS - 16, ROWS)
    last = (ROWS - 2) * SUBS
    halo_copy = remote(
        streams.at[:, pl.ds(last, 2 * SUBS), :], halo, halo_s, halo_r, (lax.rem(seq + 1, NZ * NJ), x)
    )
    pl.when(has_next)(halo_copy.start)
    convert(1, k_ref, 0, ROWS - 16)
    sib_copy(0).wait_recv()
    ring_copy(2, 1).start()
    ring_copy(1, 1).start()
    convert(2, v_ref, 0, ROWS - 16)
    for n in range(3, len(inputs)):
        inputs[n].wait()

    for part in range(SUBS):
        cut = slice(part * LANES, (part + 1) * LANES)
        to = pl.ds(part, MODES, stride=SUBS)
        rate_rows[to, :] = rates_ref[:, cut]
        res_rows[to, :] = residues_ref[:, cut]
        prior_rows[to, :] = prior_ref[:, cut]
        for stream in range(3):
            for tap in range(3):
                n = (3 * stream + tap) * SUBS + part
                tap_rows[n : n + 1, :] = taps_ref[stream, tap : tap + 1, cut]
    rates = rate_rows[...]
    inflow = jnp.sqrt(one_minus_exp(2.0 * rates))
    pole_rows[...] = jnp.exp(-rates)
    inflow_rows[...] = inflow
    inres_rows[...] = res_rows[...] * inflow

    def modes_of(ref):
        return [ref[m * SUBS : (m + 1) * SUBS, :] for m in range(MODES)]

    taps = [tap_rows[n * SUBS : (n + 1) * SUBS, :] for n in range(9)]
    poles = modes_of(pole_rows)
    skip = skip_ref[...]

    def feature(stream, now, back1, back2):
        return taps[3 * stream] * now + taps[3 * stream + 1] * back1 + taps[3 * stream + 2] * back2

    def gate(t, history):
        later, feats = [], []
        for stream, (back1, back2) in zip((1, 2), history):
            now = streams[stream, row(t), :]
            feats.append(feature(stream, now, back1, back2))
            later.append((now, back1))
        value = feats[0] * feats[1]
        gated[row(t), :] = value
        return value, tuple(later)

    def steps(begin, end, step, carried):
        def eight(block, carried):
            for t in range(8):
                carried = step(block * 8 + t, carried)
            return carried

        return lax.fori_loop(begin // 8, end // 8, eight, carried)

    def advance(states, value):
        return tuple(pole * state + value for pole, state in zip(poles, states))

    history = tuple((streams[s, SUBS : 2 * SUBS, :], streams[s, 0:SUBS, :]) for s in (1, 2))
    states = tuple(jnp.zeros((SUBS, LANES), F32) for _ in range(MODES))

    def scan_step(t, carried):
        states, history = carried
        value, history = gate(t, history)
        return advance(states, value), history

    scan = (states, history)
    for t in range(2, 8):
        scan = scan_step(t, scan)
    states, history = steps(8, ROWS, scan_step, scan)

    @pl.when(has_prev)
    def _():
        halo_copy.wait_recv()

    @pl.when(jnp.logical_not(has_prev))
    def _():
        halo[...] = jnp.zeros_like(halo)

    def halo_rows(s):
        return halo[s, SUBS : 2 * SUBS, :], halo[s, 0:SUBS, :]

    first, history = gate(0, (halo_rows(1), halo_rows(2)))
    second, history = gate(1, history)
    for m in range(MODES):
        at = slice(m * SUBS, (m + 1) * SUBS)
        late = jnp.exp(-(ROWS - 2.0) * rate_rows[at, :])
        ends[at, :] = inflow_rows[at, :] * (states[m] + late * (poles[m] * first + second))

    pair = 2 * SUBS

    def pair_rows(n):
        return pl.ds(pl.multiple_of(n * pair, pair), pair)

    def to_owner(d):
        to = lax.rem(j + d, NJ)
        return remote(ends.at[pair_rows(to), :], plane_in.at[j], s1_s.at[d], s1_r.at[d], device(z, to, x))

    def along_line(d):
        return remote(line_out, line_in.at[z], s2_s.at[d], s2_r.at[d], device(lax.rem(z + d, NZ), j, x))

    def from_owner(d):
        to = lax.rem(j + d, NJ)
        return remote(back_out.at[to], carry.at[pair_rows(j), :], s3_s.at[d], s3_r.at[d], device(z, to, x))

    @pl.loop(1, NJ)
    def _(d):
        to_owner(d).start()

    plane_in[j] = ends[pair_rows(j), :]
    ring_step(1)

    inres = modes_of(inres_rows)

    def output_step(t, carried):
        states, (back1, back2) = carried
        now = streams[0, row(t), :]
        featq[row(t), :] = feature(0, now, back1, back2)
        value = gated[row(t), :]
        states = advance(states, value)
        terms = [r * s for r, s in zip(inres, states)] + [skip * value]
        filt[row(t), :] = tree_sum(terms)
        return states, (now, back1)

    for tile in range(SUBS):
        turned = residual_ref[:, tile * LANES : (tile + 1) * LANES].astype(F32).T.astype(BF16)
        to_rows = slice((tile // 2) * 64, (tile // 2) * 64 + 64)
        for odd in range(2):
            res_out[2 * (tile % 2) + odd, to_rows, :] = turned[64 * odd : 64 * odd + 64, :]

    def beside(block, dx=0):
        return device(z, lax.rem(y + (0, 3, 1, 2)[block], NY) * NH + h, x if dx == 0 else lax.rem(x + dx, NX))

    def res_copy(block):
        ahead = (0, 1, 3, 2)[block]
        to = lax.rem(y + ahead, NY)
        n = block - 1
        return remote(res_out.at[to], res_in.at[n], res_s.at[n], res_r.at[n], device(z, to * NH + h, x))

    for block in range(1, 4):
        res_copy(block).start()

    convert(0, q_ref, 0, ROWS - 16)
    states = tuple(jnp.zeros((SUBS, LANES), F32) for _ in range(MODES))
    outputs = steps(0, 64, output_step, (states, halo_rows(0)))

    @pl.loop(1, NJ)
    def _(d):
        to_owner(d).wait_recv()

    my_rates = rate_rows[pair_rows(j), :]
    block_decay = jnp.exp(-float(ROWS) * my_rates)
    plane_decay = jnp.exp(-float(ROWS * NJ) * my_rates)
    total = plane_in[0]
    for i in range(1, NJ):
        total = block_decay * total + plane_in[i]
    line_out[...] = total

    @pl.loop(1, NZ - z)
    def _(d):
        along_line(d).start()

    ring_step(2)
    steps(64, ROWS, output_step, outputs)
    ring_step(3)

    @pl.loop(1, z + 1)
    def _(d):
        along_line(d).wait_recv()

    incoming = lax.fori_loop(0, z, lambda i, s: plane_decay * s + line_in[i], prior_rows[pair_rows(j), :])
    for i in range(NJ):
        back_out[i] = incoming
        incoming = block_decay * incoming + plane_in[i]

    @pl.loop(1, NJ)
    def _(d):
        from_owner(d).start()

    carry[pair_rows(j), :] = back_out[j]

    @pl.loop(1, NJ)
    def _(d):
        from_owner(d).wait_recv()

    half = ROWS // 2
    up = device(z, lax.rem(y + 1, NY) * NH + h, x)
    down = device(z, lax.rem(y + 3, NY) * NH + h, x)
    across = device(z, lax.rem(y + 2, NY) * NH + h, x)

    def act_copy(part, side):
        cut = pl.ds(part * half, half)
        n = 2 * part + side
        return remote(acts.at[0, cut, :], acts.at[1 + side, cut, :], act_s.at[n], act_r.at[n], (up, down)[side])

    def fwd_copy(part):
        cut = pl.ds(part * half, half)
        return remote(acts.at[1 + part, cut, :], acts.at[3, cut, :], fwd_s.at[part], fwd_r.at[part], (up, down)[part])

    def carried_step(t, waves):
        waves = tuple(pole * wave for pole, wave in zip(poles, waves))
        filt[row(t), :] = featq[row(t), :] * (filt[row(t), :] + tree_sum(list(waves)))
        return waves

    waves = tuple(res_rows[m * SUBS : (m + 1) * SUBS, :] * carry[m * SUBS : (m + 1) * SUBS, :] for m in range(MODES))
    for part in range(2):
        waves = steps(part * half, (part + 1) * half, carried_step, waves)
        for sub in range(SUBS):
            from_rows = pl.ds(part * half * SUBS + sub, half, stride=SUBS)
            acts[0, part * half : (part + 1) * half, sub * LANES : (sub + 1) * LANES] = filt[from_rows, :].astype(BF16)
        act_copy(part, part).start()
    act_copy(1, 0).start()
    act_copy(0, 1).start()

    ring_step(4)
    for part in range(2):
        act_copy(part, part).wait_recv()
        fwd_copy(part).start()
    for step in range(1, 4):
        sib_copy(step).wait_recv()

    right, left = device(z, j, lax.rem(x + 1, NX)), device(z, j, lax.rem(x + 3, NX))
    sides = (right, left)

    def band(block, dx):
        first = lax.rem(x + dx, NX) * 4 + NZ - z
        chunks = [pl.ds(pl.multiple_of(lax.rem(first + i, NZ) * 64, 64), 64) for i in range(4)]
        return [parts[block, chunk, :] for chunk in chunks]

    def far_copy(block, side):
        n = 2 * block + side
        return remote(far_out.at[n], far_in.at[n], far_s.at[n], far_r.at[n], sides[side])

    def near_copy(block, side):
        n = 2 * block + side
        return remote(near_out.at[n], near_in.at[n], near_s.at[n], near_r.at[n], sides[side])

    def direct_copy(dx):
        n = dx - 1
        to = device(z, j, lax.rem(x + dx, NX))
        return remote(direct_out.at[n], direct_in.at[n], direct_s.at[n], direct_r.at[n], to)

    def begin(block):
        parts[block] = lax.dot_general(
            weights[...], acts[block], (((1,), (1,)), ((), ())), preferred_element_type=F32
        )
        far = band(block, 2)
        if block == 3:
            for dx, chunks in ((2, far), (1, band(block, 1)), (3, band(block, 3))):
                for i in range(4):
                    direct_out[dx - 1, 64 * i : 64 * i + 64, :] = chunks[i].astype(BF16)
                direct_copy(dx).start()
            return
        for side in range(2):
            for i in range(2):
                far_out[2 * block + side, 64 * i : 64 * i + 64, :] = far[2 * side + i].astype(BF16)
            far_copy(block, side).start()

    def middle(block):
        for side in range(2):
            n = 2 * block + side
            part = band(block, (1, 3)[side])
            far_copy(block, side).wait_recv()
            for i in range(4):
                value = part[i]
                if i // 2 == side:
                    value = value + far_in[n, 64 * (i % 2) : 64 * (i % 2) + 64, :].astype(F32)
                near_out[n, 64 * i : 64 * i + 64, :] = value.astype(BF16)
            near_copy(block, side).start()

    def fin_copy(block):
        return remote(
            back_rows.at[block - 1], final_in.at[y], fin_s.at[block - 1], fin_r.at[block - 1], beside(block)
        )

    def stat_copy(block, dx):
        n = 4 * block + dx
        return remote(stat_out.at[block], stat_in.at[n], stat_s.at[n], stat_r.at[n], beside(block, dx))

    stat_pairs = [(block, dx) for block in range(4) for dx in range(4) if (block, dx) != (0, 0)]

    def finish(block):
        value = jnp.concatenate(band(block, 0), axis=0)
        if block == 3:
            for dx in range(1, NX):
                direct_copy(dx).wait_recv()
                value = value + direct_in[dx - 1].astype(F32)
        else:
            for side in range(2):
                near_copy(block, side).wait_recv()
                value = value + near_in[2 * block + side].astype(F32)
        if block == 0:
            value = value + res_out[y].astype(F32)
        else:
            res_copy(block).wait_recv()
            value = value + res_in[block - 1].astype(F32)
        squares = jnp.sum(value * value, axis=0, keepdims=True)
        stat_out[block] = jnp.broadcast_to(squares, (SUBS, LANES))
        if block == 0:
            final_in[y] = value.astype(BF16)
            stat_in[0] = stat_out[0]
        else:
            back_rows[block - 1] = value.astype(BF16)
            fin_copy(block).start()
        for dx in range(NX):
            if (block, dx) in stat_pairs:
                stat_copy(block, dx).start()

    begin(0)
    act_copy(1, 0).wait_recv()
    act_copy(0, 1).wait_recv()
    begin(1)
    middle(0)
    begin(2)
    middle(1)
    finish(0)
    for part in range(2):
        fwd_copy(part).wait_recv()
    begin(3)
    middle(2)
    finish(1)
    finish(2)
    finish(3)
    for block in range(1, 4):
        fin_copy(block).wait_recv()

    for tile in range(SUBS):
        cut = slice(tile * LANES, (tile + 1) * LANES)
        from_rows = slice((tile // 2) * 64, (tile // 2) * 64 + 64)
        mixed = [final_in[2 * (tile % 2) + odd, from_rows, :].astype(F32) for odd in range(2)]
        value = jnp.concatenate(mixed, axis=0).T
        summed[:, cut] = value
        hidden_ref[:, cut] = value.astype(BF16)
    for block, dx in stat_pairs:
        stat_copy(block, dx).wait_recv()
    total = tree_sum([stat_in[n] for n in range(16)])
    scale = lax.rsqrt(total * (1.0 / (NX * CHANS)) + 1e-05)
    scale = jnp.broadcast_to(scale[0:1, :], (ROWS, LANES)).T
    for tile in range(SUBS):
        cut = slice(tile * LANES, (tile + 1) * LANES)
        normed_ref[:, cut] = (summed[:, cut] * scale * gain_ref[tile : tile + 1, :]).astype(BF16)

    pl.when(has_next)(halo_copy.wait_send)

    @pl.loop(1, NJ)
    def _(d):
        to_owner(d).wait_send()
        from_owner(d).wait_send()

    @pl.loop(1, NZ - z)
    def _(d):
        along_line(d).wait_send()

    for step in range(4):
        sib_copy(step).wait_send()
    for far in range(3, 8):
        ring_copy(far).wait_send()
    ring_copy(7, other=True).wait_send()

    @pl.when(upward)
    def _():
        ring_copy(8).wait_send()
        ring_copy(8, other=True).wait_send()

    for part in range(2):
        ring_copy(1, part).wait_send()
        ring_copy(2, part).wait_send()
        for side in range(2):
            act_copy(part, side).wait_send()
        fwd_copy(part).wait_send()
    for block in range(3):
        for side in range(2):
            far_copy(block, side).wait_send()
            near_copy(block, side).wait_send()
    for dx in range(1, NX):
        direct_copy(dx).wait_send()
    for block in range(1, 4):
        fin_copy(block).wait_send()
        res_copy(block).wait_send()
    for block, dx in stat_pairs:
        stat_copy(block, dx).wait_send()


def shard_rows(slot, h):
    return pl.ds(pl.multiple_of(slot * 64 + h * 32, 32), 32)


def tree_sum(terms):
    while len(terms) > 1:
        rest = [terms[-1]] if len(terms) % 2 else []
        terms = [a + b for a, b in zip(terms[0::2], terms[1::2])] + rest
    return terms[0]


def local(
    q_stream, k_stream, v_stream, short_filter, rates, residues, skip, prior_state, out_weight, residual, norm_gain
):
    vmem = pl.BlockSpec(memory_space=pltpu.VMEM)
    hbm = pl.BlockSpec(memory_space=pltpu.HBM)
    dma = pltpu.SemaphoreType.DMA
    wide = (ROWS * SUBS, LANES)
    params = (MODES * SUBS, LANES)
    pair = (2 * SUBS, LANES)
    rows = (ROWS, CHANS)
    scratch = [
        pltpu.VMEM(rows, BF16),
        pltpu.VMEM(rows, BF16),
        pltpu.VMEM(rows, BF16),
        pltpu.VMEM(short_filter.shape, F32),
        pltpu.VMEM((MODES, CHANS), F32),
        pltpu.VMEM((MODES, CHANS), F32),
        pltpu.VMEM((SUBS, LANES), F32),
        pltpu.VMEM((MODES, CHANS), F32),
        pltpu.VMEM(rows, BF16),
        pltpu.VMEM((SUBS, LANES), F32),
        pltpu.VMEM((3,) + wide, F32),
        pltpu.VMEM((3, 2 * SUBS, LANES), F32),
        pltpu.VMEM(wide, F32),
        pltpu.VMEM(wide, F32),
        pltpu.VMEM(wide, F32),
        pltpu.VMEM((9 * SUBS, LANES), F32),
        pltpu.VMEM(params, F32),
        pltpu.VMEM(params, F32),
        pltpu.VMEM(params, F32),
        pltpu.VMEM(params, F32),
        pltpu.VMEM(params, F32),
        pltpu.VMEM(params, F32),
        pltpu.VMEM(params, F32),
        pltpu.VMEM((NJ,) + pair, F32),
        pltpu.VMEM((NZ,) + pair, F32),
        pltpu.VMEM(pair, F32),
        pltpu.VMEM((NJ,) + pair, F32),
        pltpu.VMEM(params, F32),
        pltpu.VMEM((CHANS, CHANS), BF16),
        pltpu.VMEM((NY, ROWS, CHANS), BF16),
        pltpu.VMEM((6, ROWS, LANES), BF16),
        pltpu.VMEM((6, ROWS, LANES), BF16),
        pltpu.VMEM((6, BAND, ROWS), BF16),
        pltpu.VMEM((6, BAND, ROWS), BF16),
        pltpu.VMEM((NX - 1, BAND, ROWS), BF16),
        pltpu.VMEM((NX - 1, BAND, ROWS), BF16),
        pltpu.VMEM((NY, CHANS, ROWS), F32),
        pltpu.VMEM((NY - 1, BAND, ROWS), BF16),
        pltpu.VMEM((NY, BAND, ROWS), BF16),
        pltpu.VMEM((NY, BAND, ROWS), BF16),
        pltpu.VMEM((NY - 1, BAND, ROWS), BF16),
        pltpu.VMEM((ROWS, CHANS), F32),
        pltpu.VMEM((NY, SUBS, LANES), F32),
        pltpu.VMEM((16, SUBS, LANES), F32),
    ]
    sems = [dma((11,))]
    for count in (0, NJ, NZ, NJ, 18, 4, 4, 2, 6, 6, 3, 3, 3, 16):
        sems += [dma(()), dma(())] if count == 0 else [dma((count,)), dma((count,))]
    return pl.pallas_call(
        kernel,
        out_shape=(jax.ShapeDtypeStruct((ROWS, CHANS), BF16), jax.ShapeDtypeStruct((ROWS, CHANS), BF16)),
        in_specs=[hbm] * 11,
        out_specs=(vmem, vmem),
        scratch_shapes=scratch + sems,
        compiler_params=pltpu.CompilerParams(
            collective_id=0, has_side_effects=True, vmem_limit_bytes=63 * 1024 * 1024
        ),
        name="mixer",
    )(
        q_stream, k_stream, v_stream, short_filter, rates, residues, skip.reshape(SUBS, LANES), prior_state,
        out_weight.T, residual, norm_gain.reshape(SUBS, LANES),
    )


def solution(mesh):
    placed = (
        P("seq", "ch"),
        P("seq", "ch"),
        P("seq", "ch"),
        P(None, None, "ch"),
        P(None, "ch"),
        P(None, "ch"),
        P("ch"),
        P(None, "ch"),
        P("ch", "seq"),
        P("seq", "ch"),
        P("ch"),
    )
    return jax.shard_map(
        local,
        mesh=mesh,
        in_specs=placed,
        out_specs=(P("seq", "ch"), P("seq", "ch")),
        check_vma=False,
    )
```

```python
import functools

import jax
import jax.numpy as jnp
from jax import lax
from jax.experimental import pallas as pl
from jax.experimental.pallas import tpu as pltpu
from jax.sharding import PartitionSpec as P

MESH = pl.DeviceIdType.MESH
F32 = jnp.float32
BF16 = jnp.bfloat16
NX, NY, NZ, NH = 4, 4, 16, 2
NJ = NY * NH
ROWS = 128
CHANS = 1024
LANES = 128
SUBS = 8
MODES = 16
BAND = CHANS // NX


def one_minus_exp(x):
    series = jnp.full_like(x, 1.0 / 8.0)
    for n in (7.0, 6.0, 5.0, 4.0, 3.0, 2.0):
        series = (1.0 - x * series) * (1.0 / n)
    return jnp.where(x < 0.25, x * (1.0 - x * series), 1.0 - jnp.exp(-x))


def kernel(
    q_hbm, k_hbm, v_hbm, taps_hbm, rates_hbm, residues_hbm, skip_hbm, prior_hbm, weight_hbm, residual_hbm, gain_hbm,
    hidden_ref, normed_ref,
    q_ref, k_ref, v_ref, taps_ref, rates_ref, residues_ref, skip_ref, prior_ref, residual_ref, gain_ref,
    streams, halo, gated, featq, filt, tap_rows, rate_rows, res_rows, prior_rows, pole_rows, inres_rows, inflow_rows,
    ends, plane_in, line_in, line_out, back_out, carry,
    weights, acts, far_out, far_in, near_out, near_in, direct_out, direct_in, parts, back_rows, final_in,
    res_out, res_in, summed, stat_out, stat_in,
    input_s, halo_s, halo_r, s1_s, s1_r, s2_s, s2_r, s3_s, s3_r, ring_s, ring_r, sib_s, sib_r,
    act_s, act_r, fwd_s, fwd_r, far_s, far_r, near_s, near_r, direct_s, direct_r,
    fin_s, fin_r, res_s, res_r, stat_s, stat_r,
):
    seq, x = lax.axis_index("seq"), lax.axis_index("ch")
    z, j = lax.div(seq, NJ), lax.rem(seq, NJ)
    y, h = lax.div(j, NH), lax.rem(j, NH)

    def device(z_, j_, x_):
        return (z_ * NJ + j_, x_)

    def remote(src, dst, send, recv, target):
        return pltpu.make_async_remote_copy(
            src_ref=src, dst_ref=dst, send_sem=send, recv_sem=recv, device_id=target, device_id_type=MESH
        )

    def row(t):
        return pl.ds(pl.multiple_of(t * SUBS, SUBS), SUBS)

    own_weights = weights.at[shard_rows(0, h), :]
    inputs = [
        pltpu.make_async_copy(src, dst, input_s.at[n])
        for n, (src, dst) in enumerate((
            (k_hbm, k_ref), (v_hbm, v_ref), (q_hbm, q_ref), (weight_hbm, own_weights), (rates_hbm, rates_ref),
            (taps_hbm, taps_ref), (residues_hbm, residues_ref), (prior_hbm, prior_ref), (skip_hbm, skip_ref),
            (residual_hbm, residual_ref), (gain_hbm, gain_ref),
        ))
    ]
    for copy in inputs:
        copy.start()

    barrier = pltpu.get_barrier_semaphore()

    def greet(target):
        pl.semaphore_signal(barrier, inc=1, device_id=target, device_id_type=MESH)

    @pl.loop(1, NJ)
    def _(d):
        greet(device(z, lax.rem(j + d, NJ), x))

    @pl.loop(1, NZ)
    def _(d):
        greet(device(lax.rem(z + d, NZ), j, x))

    @pl.loop(1, NX)
    def _(d):
        greet(device(z, j, lax.rem(x + d, NX)))

    has_next, has_prev = seq < NZ * NJ - 1, seq > 0
    first_j, last_j = j == 0, j == NJ - 1

    @pl.when(last_j)
    def _():
        greet(device(lax.rem(z + 1, NZ), 0, x))

    @pl.when(first_j)
    def _():
        greet(device(lax.rem(z + NZ - 1, NZ), NJ - 1, x))

    @pl.loop(1, 3)
    def _(d):
        greet(device(lax.rem(z + d, NZ), y * NH + 1 - h, x))
        greet(device(lax.rem(z + NZ - d, NZ), y * NH + 1 - h, x))

    @pl.loop(1, NX)
    def _(d):
        @pl.loop(1, NY)
        def _(e):
            greet(device(z, lax.rem(y + e, NY) * NH + h, lax.rem(x + d, NX)))

    peers = NJ + NZ + NX - 3 + 4 + (NX - 1) * (NY - 1)
    edge = jnp.logical_or(first_j, last_j)

    @pl.when(edge)
    def _():
        pl.semaphore_wait(barrier, peers + 1)

    @pl.when(jnp.logical_not(edge))
    def _():
        pl.semaphore_wait(barrier, peers)

    direction = 1 - 2 * h
    sibling = device(z, y * NH + 1 - h, x)
    ring_to = [None] + [device(lax.rem(z + direction * d + NZ, NZ), j, x) for d in (1, 2)]
    other_to = [None] + [device(lax.rem(z + direction * d + NZ, NZ), y * NH + 1 - h, x) for d in (1, 2)]

    def slot(far):
        return far if far == 0 else (1 - h) * (NZ - far) + h * far

    def ring_copy(far, part=None, other=False):
        hops = 2 - far % 2
        if far > 2:
            rows = [pl.ds(pl.multiple_of(slot(f) * 64, 64), 64) for f in (far - hops, far)]
            src, n = weights.at[rows[0], :], 2 * far
        else:
            shard = part + h - 2 * part * h
            rows = [shard_rows(slot(f), shard) for f in (0, far)]
            src, n = (weight_hbm if part == 0 else weights.at[rows[0], :]), 2 * far + part
        if other:
            return remote(src, weights.at[rows[1], :], ring_s.at[n + 1], ring_r.at[n + 1], other_to[hops])
        return remote(src, weights.at[rows[1], :], ring_s.at[n], ring_r.at[n], ring_to[hops])

    def sib_copy(step):
        if step == 0:
            return remote(weight_hbm, own_weights, sib_s.at[0], sib_r.at[0], sibling)
        first = (1 - h) * (NZ - 2 * step) + h * (2 * step - 1)
        both = weights.at[pl.ds(pl.multiple_of(first * 64, 64), 128), :]
        return remote(both, both, sib_s.at[1], sib_r.at[1], sibling)

    upward = h == 0

    def arrived(far):
        if far > 2:
            ring_copy(far).wait_recv()
        else:
            ring_copy(far, 0).wait_recv()
            ring_copy(far, 1).wait_recv()

    def ring_step(step):
        far = 2 * step
        if step < 4:
            arrived(far)
            if step < 3:
                ring_copy(far + 2).start()
                ring_copy(far + 1).start()
            else:

                @pl.when(upward)
                def _():
                    ring_copy(8).start()
                    ring_copy(8, other=True).start()

                ring_copy(7).start()
                ring_copy(7, other=True).start()
            arrived(far - 1)
            sib_copy(step).start()
        else:
            arrived(7)
            ring_copy(7, other=True).wait_recv()

            @pl.when(upward)
            def _():
                arrived(8)

            @pl.when(jnp.logical_not(upward))
            def _():
                ring_copy(8, other=True).wait_recv()

    ring_copy(2, 0).start()
    sib_copy(0).start()
    ring_copy(1, 0).start()

    def convert(stream, ref, begin, end):
        for part in range(SUBS):
            to = pl.ds(begin * SUBS + part, end - begin, stride=SUBS)
            streams[stream, to, :] = ref[begin:end, part * LANES : (part + 1) * LANES].astype(F32)

    for n in range(3):
        inputs[n].wait()
    for stream, ref in enumerate((q_ref, k_ref, v_ref)):
        convert(stream, ref, ROWS - 16, ROWS)
    last = (ROWS - 2) * SUBS
    halo_copy = remote(
        streams.at[:, pl.ds(last, 2 * SUBS), :], halo, halo_s, halo_r, (lax.rem(seq + 1, NZ * NJ), x)
    )
    pl.when(has_next)(halo_copy.start)
    convert(1, k_ref, 0, ROWS - 16)
    sib_copy(0).wait_recv()
    ring_copy(2, 1).start()
    ring_copy(1, 1).start()
    convert(2, v_ref, 0, ROWS - 16)
    for n in range(3, len(inputs)):
        inputs[n].wait()

    for part in range(SUBS):
        cut = slice(part * LANES, (part + 1) * LANES)
        to = pl.ds(part, MODES, stride=SUBS)
        rate_rows[to, :] = rates_ref[:, cut]
        res_rows[to, :] = residues_ref[:, cut]
        prior_rows[to, :] = prior_ref[:, cut]
        for stream in range(3):
            for tap in range(3):
                n = (3 * stream + tap) * SUBS + part
                tap_rows[n : n + 1, :] = taps_ref[stream, tap : tap + 1, cut]
    rates = rate_rows[...]
    inflow = jnp.sqrt(one_minus_exp(2.0 * rates))
    pole_rows[...] = jnp.exp(-rates)
    inflow_rows[...] = inflow
    inres_rows[...] = res_rows[...] * inflow

    def modes_of(ref):
        return [ref[m * SUBS : (m + 1) * SUBS, :] for m in range(MODES)]

    taps = [tap_rows[n * SUBS : (n + 1) * SUBS, :] for n in range(9)]
    poles = modes_of(pole_rows)
    skip = skip_ref[...]

    def feature(stream, now, back1, back2):
        return taps[3 * stream] * now + taps[3 * stream + 1] * back1 + taps[3 * stream + 2] * back2

    def gate(t, history):
        later, feats = [], []
        for stream, (back1, back2) in zip((1, 2), history):
            now = streams[stream, row(t), :]
            feats.append(feature(stream, now, back1, back2))
            later.append((now, back1))
        value = feats[0] * feats[1]
        gated[row(t), :] = value
        return value, tuple(later)

    def steps(begin, end, step, carried):
        def eight(block, carried):
            for t in range(8):
                carried = step(block * 8 + t, carried)
            return carried

        return lax.fori_loop(begin // 8, end // 8, eight, carried)

    def advance(states, value):
        return tuple(pole * state + value for pole, state in zip(poles, states))

    history = tuple((streams[s, SUBS : 2 * SUBS, :], streams[s, 0:SUBS, :]) for s in (1, 2))
    states = tuple(jnp.zeros((SUBS, LANES), F32) for _ in range(MODES))

    def scan_step(t, carried):
        states, history = carried
        value, history = gate(t, history)
        return advance(states, value), history

    scan = (states, history)
    for t in range(2, 8):
        scan = scan_step(t, scan)
    states, history = steps(8, ROWS, scan_step, scan)

    @pl.when(has_prev)
    def _():
        halo_copy.wait_recv()

    @pl.when(jnp.logical_not(has_prev))
    def _():
        halo[...] = jnp.zeros_like(halo)

    def halo_rows(s):
        return halo[s, SUBS : 2 * SUBS, :], halo[s, 0:SUBS, :]

    first, history = gate(0, (halo_rows(1), halo_rows(2)))
    second, history = gate(1, history)
    for m in range(MODES):
        at = slice(m * SUBS, (m + 1) * SUBS)
        late = jnp.exp(-(ROWS - 2.0) * rate_rows[at, :])
        ends[at, :] = inflow_rows[at, :] * (states[m] + late * (poles[m] * first + second))

    pair = 2 * SUBS

    def pair_rows(n):
        return pl.ds(pl.multiple_of(n * pair, pair), pair)

    def to_owner(d):
        to = lax.rem(j + d, NJ)
        return remote(ends.at[pair_rows(to), :], plane_in.at[j], s1_s, s1_r, device(z, to, x))

    def along_line(d):
        return remote(line_out, line_in.at[z], s2_s.at[d], s2_r.at[d], device(lax.rem(z + d, NZ), j, x))

    def from_owner(d):
        to = lax.rem(j + d, NJ)
        return remote(back_out.at[to], carry.at[pair_rows(j), :], s3_s, s3_r, device(z, to, x))

    @pl.loop(1, NJ)
    def _(d):
        to_owner(d).start()

    plane_in[j] = ends[pair_rows(j), :]
    ring_step(1)

    inres = modes_of(inres_rows)

    def output_step(t, carried):
        states, (back1, back2) = carried
        now = streams[0, row(t), :]
        featq[row(t), :] = feature(0, now, back1, back2)
        value = gated[row(t), :]
        states = advance(states, value)
        terms = [r * s for r, s in zip(inres, states)] + [skip * value]
        filt[row(t), :] = tree_sum(terms)
        return states, (now, back1)

    for tile in range(SUBS):
        turned = residual_ref[:, tile * LANES : (tile + 1) * LANES].astype(F32).T.astype(BF16)
        to_rows = slice((tile // 2) * 64, (tile // 2) * 64 + 64)
        for odd in range(2):
            res_out[2 * (tile % 2) + odd, to_rows, :] = turned[64 * odd : 64 * odd + 64, :]

    def beside(block, dx=0):
        return device(z, lax.rem(y + (0, 3, 1, 2)[block], NY) * NH + h, x if dx == 0 else lax.rem(x + dx, NX))

    def res_copy(block):
        ahead = (0, 1, 3, 2)[block]
        to = lax.rem(y + ahead, NY)
        n = block - 1
        return remote(res_out.at[to], res_in.at[n], res_s, res_r, device(z, to * NH + h, x))

    for block in range(1, 4):
        res_copy(block).start()

    convert(0, q_ref, 0, ROWS - 16)
    states = tuple(jnp.zeros((SUBS, LANES), F32) for _ in range(MODES))
    outputs = steps(0, 64, output_step, (states, halo_rows(0)))

    others = plane_in.at[pl.ds(0, NJ - 1)]
    to_owner_all = remote(others, others, s1_s, s1_r, sibling)
    to_owner_all.wait_recv()

    my_rates = rate_rows[pair_rows(j), :]
    block_decay = jnp.exp(-float(ROWS) * my_rates)
    plane_decay = jnp.exp(-float(ROWS * NJ) * my_rates)
    total = plane_in[0]
    for i in range(1, NJ):
        total = block_decay * total + plane_in[i]
    line_out[...] = total

    @pl.loop(1, NZ - z)
    def _(d):
        along_line(d).start()

    ring_step(2)
    steps(64, ROWS, output_step, outputs)
    ring_step(3)

    @pl.loop(1, z + 1)
    def _(d):
        along_line(d).wait_recv()

    incoming = lax.fori_loop(0, z, lambda i, s: plane_decay * s + line_in[i], prior_rows[pair_rows(j), :])
    for i in range(NJ):
        back_out[i] = incoming
        incoming = block_decay * incoming + plane_in[i]

    @pl.loop(1, NJ)
    def _(d):
        from_owner(d).start()

    carry[pair_rows(j), :] = back_out[j]

    others = back_out.at[pl.ds(0, NJ - 1)]
    from_owner_all = remote(others, others, s3_s, s3_r, sibling)
    from_owner_all.wait_recv()

    half = ROWS // 2
    up = device(z, lax.rem(y + 1, NY) * NH + h, x)
    down = device(z, lax.rem(y + 3, NY) * NH + h, x)
    across = device(z, lax.rem(y + 2, NY) * NH + h, x)

    act_wait = (0, 2, 2, 1)

    def act_copy(part, side):
        cut = pl.ds(part * half, half)
        n = 2 * part + side
        return remote(acts.at[0, cut, :], acts.at[1 + side, cut, :], act_s, act_r.at[act_wait[n]], (up, down)[side])

    def fwd_copy(part):
        cut = pl.ds(part * half, half)
        return remote(acts.at[1 + part, cut, :], acts.at[3, cut, :], fwd_s, fwd_r, (up, down)[part])

    def carried_step(t, waves):
        waves = tuple(pole * wave for pole, wave in zip(poles, waves))
        filt[row(t), :] = featq[row(t), :] * (filt[row(t), :] + tree_sum(list(waves)))
        return waves

    waves = tuple(res_rows[m * SUBS : (m + 1) * SUBS, :] * carry[m * SUBS : (m + 1) * SUBS, :] for m in range(MODES))
    for part in range(2):
        waves = steps(part * half, (part + 1) * half, carried_step, waves)
        for sub in range(SUBS):
            from_rows = pl.ds(part * half * SUBS + sub, half, stride=SUBS)
            acts[0, part * half : (part + 1) * half, sub * LANES : (sub + 1) * LANES] = filt[from_rows, :].astype(BF16)
        act_copy(part, part).start()
    act_copy(1, 0).start()
    act_copy(0, 1).start()

    pl.when(has_next)(halo_copy.wait_send)
    to_owner_all.wait_send()
    from_owner_all.wait_send()

    @pl.loop(1, NZ - z)
    def _(d):
        along_line(d).wait_send()

    res_all = remote(res_in, res_in, res_s, res_r, sibling)
    res_all.wait_send()
    sib_copy(0).wait_send()
    for part in range(2):
        ring_copy(1, part).wait_send()
        ring_copy(2, part).wait_send()
    for far in range(3, 7):
        ring_copy(far).wait_send()

    ring_step(4)
    for part in range(2):
        act_copy(part, part).wait_recv()
        fwd_copy(part).start()
    three = weights.at[pl.ds(0, 3 * 128), :]
    sib_all = remote(three, three, sib_s.at[1], sib_r.at[1], sibling)
    sib_all.wait_recv()
    res_all.wait_recv()

    right, left = device(z, j, lax.rem(x + 1, NX)), device(z, j, lax.rem(x + 3, NX))
    sides = (right, left)

    def band(block, dx):
        first = lax.rem(x + dx, NX) * 4 + NZ - z
        chunks = [pl.ds(pl.multiple_of(lax.rem(first + i, NZ) * 64, 64), 64) for i in range(4)]
        lanes = slice(block % 2 * ROWS, (block % 2 + 1) * ROWS)
        return [parts[block // 2, chunk, lanes] for chunk in chunks]

    def far_copy(block, side):
        n = 2 * block + side
        return remote(far_out.at[n], far_in.at[n], far_s.at[block], far_r.at[block], sides[side])

    def far_all(block):
        both = far_in.at[pl.ds(2 * block, 2)]
        return remote(both, both, far_s.at[block], far_r.at[block], right)

    def near_copy(block, side):
        n = 2 * block + side
        return remote(near_out.at[n], near_in.at[n], near_s.at[block], near_r.at[block], sides[side])

    def near_all(block):
        both = near_in.at[pl.ds(2 * block, 2)]
        return remote(both, both, near_s.at[block], near_r.at[block], right)

    def direct_copy(dx):
        n = dx - 1
        to = device(z, j, lax.rem(x + dx, NX))
        return remote(direct_out.at[n], direct_in.at[n], direct_s, direct_r, to)

    direct_all = remote(direct_in, direct_in, direct_s, direct_r, right)

    def project(pair):
        rows = acts[2 * pair : 2 * pair + 2].reshape(2 * ROWS, CHANS)
        parts[pair] = lax.dot_general(weights[...], rows, (((1,), (1,)), ((), ())), preferred_element_type=F32)

    def begin(block):
        far = band(block, 2)
        if block == 3:
            for dx, chunks in ((2, far), (1, band(block, 1)), (3, band(block, 3))):
                for i in range(4):
                    direct_out[dx - 1, 64 * i : 64 * i + 64, :] = chunks[i].astype(BF16)
                direct_copy(dx).start()
            return
        for side in range(2):
            for i in range(2):
                far_out[2 * block + side, 64 * i : 64 * i + 64, :] = far[2 * side + i].astype(BF16)
            far_copy(block, side).start()

    def middle(block):
        far_all(block).wait_recv()
        for side in range(2):
            n = 2 * block + side
            part = band(block, (1, 3)[side])
            for i in range(4):
                value = part[i]
                if i // 2 == side:
                    value = value + far_in[n, 64 * (i % 2) : 64 * (i % 2) + 64, :].astype(F32)
                near_out[n, 64 * i : 64 * i + 64, :] = value.astype(BF16)
            near_copy(block, side).start()

    def fin_copy(block):
        return remote(
            back_rows.at[block - 1], final_in.at[y], fin_s, fin_r, beside(block)
        )

    def stat_copy(block, dx):
        n = 4 * block + dx
        return remote(stat_out.at[block], stat_in.at[n], stat_s, stat_r, beside(block, dx))

    stat_pairs = [(block, dx) for block in range(4) for dx in range(4) if (block, dx) != (0, 0)]

    def finish(block):
        value = jnp.concatenate(band(block, 0), axis=0)
        if block == 3:
            direct_all.wait_recv()
            for dx in range(1, NX):
                value = value + direct_in[dx - 1].astype(F32)
        else:
            near_all(block).wait_recv()
            for side in range(2):
                value = value + near_in[2 * block + side].astype(F32)
        if block == 0:
            value = value + res_out[y].astype(F32)
        else:
            value = value + res_in[block - 1].astype(F32)
        squares = jnp.sum(value * value, axis=0, keepdims=True)
        stat_out[block] = jnp.broadcast_to(squares, (SUBS, LANES))
        if block == 0:
            final_in[y] = value.astype(BF16)
            stat_in[0] = stat_out[0]
        else:
            back_rows[block - 1] = value.astype(BF16)
            fin_copy(block).start()
        for dx in range(NX):
            if (block, dx) in stat_pairs:
                stat_copy(block, dx).start()

    late_halves = remote(acts.at[1], acts.at[1], act_s, act_r.at[2], up)
    late_halves.wait_recv()
    project(0)
    begin(0)
    begin(1)
    fwd_all = remote(acts.at[3], acts.at[3], fwd_s, fwd_r, up)
    fwd_all.wait_recv()
    project(1)
    begin(2)
    begin(3)
    middle(0)
    middle(1)
    middle(2)
    finish(0)
    finish(1)
    finish(2)
    finish(3)
    fin_all = remote(back_rows, final_in.at[pl.ds(0, NY - 1)], fin_s, fin_r, up)
    fin_all.wait_recv()

    for tile in range(SUBS):
        cut = slice(tile * LANES, (tile + 1) * LANES)
        from_rows = slice((tile // 2) * 64, (tile // 2) * 64 + 64)
        mixed = [final_in[2 * (tile % 2) + odd, from_rows, :].astype(F32) for odd in range(2)]
        value = jnp.concatenate(mixed, axis=0).T
        summed[:, cut] = value
        hidden_ref[:, cut] = value.astype(BF16)
    fifteen = stat_in.at[pl.ds(1, 15)]
    stat_all = remote(fifteen, fifteen, stat_s, stat_r, up)
    stat_all.wait_recv()
    total = tree_sum([stat_in[n] for n in range(16)])
    scale = lax.rsqrt(total * (1.0 / (NX * CHANS)) + 1e-05)
    scale = jnp.broadcast_to(scale[0:1, :], (ROWS, LANES)).T
    for tile in range(SUBS):
        cut = slice(tile * LANES, (tile + 1) * LANES)
        normed_ref[:, cut] = (summed[:, cut] * scale * gain_ref[tile : tile + 1, :]).astype(BF16)

    sib_all.wait_send()
    ring_copy(7).wait_send()
    ring_copy(7, other=True).wait_send()

    @pl.when(upward)
    def _():
        ring_copy(8).wait_send()
        ring_copy(8, other=True).wait_send()

    remote(acts.at[pl.ds(0, 2)], acts.at[pl.ds(0, 2)], act_s, act_r.at[2], up).wait_send()
    fwd_all.wait_send()
    for block in range(3):
        far_all(block).wait_send()
        near_all(block).wait_send()
    direct_all.wait_send()
    fin_all.wait_send()
    stat_all.wait_send()


def shard_rows(slot, h):
    return pl.ds(pl.multiple_of(slot * 64 + h * 32, 32), 32)


def tree_sum(terms):
    while len(terms) > 1:
        rest = [terms[-1]] if len(terms) % 2 else []
        terms = [a + b for a, b in zip(terms[0::2], terms[1::2])] + rest
    return terms[0]


def local(
    q_stream, k_stream, v_stream, short_filter, rates, residues, skip, prior_state, out_weight, residual, norm_gain
):
    vmem = pl.BlockSpec(memory_space=pltpu.VMEM)
    hbm = pl.BlockSpec(memory_space=pltpu.HBM)
    dma = pltpu.SemaphoreType.DMA
    wide = (ROWS * SUBS, LANES)
    params = (MODES * SUBS, LANES)
    pair = (2 * SUBS, LANES)
    rows = (ROWS, CHANS)
    scratch = [
        pltpu.VMEM(rows, BF16),
        pltpu.VMEM(rows, BF16),
        pltpu.VMEM(rows, BF16),
        pltpu.VMEM(short_filter.shape, F32),
        pltpu.VMEM((MODES, CHANS), F32),
        pltpu.VMEM((MODES, CHANS), F32),
        pltpu.VMEM((SUBS, LANES), F32),
        pltpu.VMEM((MODES, CHANS), F32),
        pltpu.VMEM(rows, BF16),
        pltpu.VMEM((SUBS, LANES), F32),
        pltpu.VMEM((3,) + wide, F32),
        pltpu.VMEM((3, 2 * SUBS, LANES), F32),
        pltpu.VMEM(wide, F32),
        pltpu.VMEM(wide, F32),
        pltpu.VMEM(wide, F32),
        pltpu.VMEM((9 * SUBS, LANES), F32),
        pltpu.VMEM(params, F32),
        pltpu.VMEM(params, F32),
        pltpu.VMEM(params, F32),
        pltpu.VMEM(params, F32),
        pltpu.VMEM(params, F32),
        pltpu.VMEM(params, F32),
        pltpu.VMEM(params, F32),
        pltpu.VMEM((NJ,) + pair, F32),
        pltpu.VMEM((NZ,) + pair, F32),
        pltpu.VMEM(pair, F32),
        pltpu.VMEM((NJ,) + pair, F32),
        pltpu.VMEM(params, F32),
        pltpu.VMEM((CHANS, CHANS), BF16),
        pltpu.VMEM((NY, ROWS, CHANS), BF16),
        pltpu.VMEM((6, ROWS, LANES), BF16),
        pltpu.VMEM((6, ROWS, LANES), BF16),
        pltpu.VMEM((6, BAND, ROWS), BF16),
        pltpu.VMEM((6, BAND, ROWS), BF16),
        pltpu.VMEM((NX - 1, BAND, ROWS), BF16),
        pltpu.VMEM((NX - 1, BAND, ROWS), BF16),
        pltpu.VMEM((2, CHANS, 2 * ROWS), F32),
        pltpu.VMEM((NY - 1, BAND, ROWS), BF16),
        pltpu.VMEM((NY, BAND, ROWS), BF16),
        pltpu.VMEM((NY, BAND, ROWS), BF16),
        pltpu.VMEM((NY - 1, BAND, ROWS), BF16),
        pltpu.VMEM((ROWS, CHANS), F32),
        pltpu.VMEM((NY, SUBS, LANES), F32),
        pltpu.VMEM((16, SUBS, LANES), F32),
    ]
    sems = [dma((11,))]
    for sent, got in (
        (0, 0), (0, 0), (NZ, NZ), (0, 0), (18, 18), (2, 2), (0, 3), (0, 0), (3, 3), (3, 3), (0, 0), (0, 0), (0, 0), (0, 0)
    ):
        sems += [dma((n,)) if n else dma(()) for n in (sent, got)]
    return pl.pallas_call(
        kernel,
        out_shape=(jax.ShapeDtypeStruct((ROWS, CHANS), BF16), jax.ShapeDtypeStruct((ROWS, CHANS), BF16)),
        in_specs=[hbm] * 11,
        out_specs=(vmem, vmem),
        scratch_shapes=scratch + sems,
        compiler_params=pltpu.CompilerParams(
            collective_id=0, has_side_effects=True, vmem_limit_bytes=63 * 1024 * 1024
        ),
        name="mixer",
    )(
        q_stream, k_stream, v_stream, short_filter, rates, residues, skip.reshape(SUBS, LANES), prior_state,
        out_weight.T, residual, norm_gain.reshape(SUBS, LANES),
    )


def solution(mesh):
    placed = (
        P("seq", "ch"),
        P("seq", "ch"),
        P("seq", "ch"),
        P(None, None, "ch"),
        P(None, "ch"),
        P(None, "ch"),
        P("ch"),
        P(None, "ch"),
        P("ch", "seq"),
        P("seq", "ch"),
        P("ch"),
    )
    return jax.shard_map(
        local,
        mesh=mesh,
        in_specs=placed,
        out_specs=(P("seq", "ch"), P("seq", "ch")),
        check_vma=False,
    )
```

```python
import functools

import jax
import jax.numpy as jnp
from jax import lax
from jax.experimental import pallas as pl
from jax.experimental.pallas import tpu as pltpu
from jax.sharding import PartitionSpec as P

MESH = pl.DeviceIdType.MESH
F32 = jnp.float32
BF16 = jnp.bfloat16
NX, NY, NZ, NH = 4, 4, 16, 2
NJ = NY * NH
ROWS = 128
CHANS = 1024
LANES = 128
SUBS = 8
MODES = 16
BAND = CHANS // NX


def one_minus_exp(x):
    series = jnp.full_like(x, 1.0 / 8.0)
    for n in (7.0, 6.0, 5.0, 4.0, 3.0, 2.0):
        series = (1.0 - x * series) * (1.0 / n)
    return jnp.where(x < 0.25, x * (1.0 - x * series), 1.0 - jnp.exp(-x))


def kernel(
    q_hbm, k_hbm, v_hbm, taps_hbm, rates_hbm, residues_hbm, skip_hbm, prior_hbm, weight_hbm, residual_hbm, gain_hbm,
    hidden_ref, normed_ref,
    q_ref, k_ref, v_ref, taps_ref, rates_ref, residues_ref, skip_ref, prior_ref, residual_ref, gain_ref,
    streams, halo, gated, featq, filt, tap_rows, rate_rows, res_rows, prior_rows, pole_rows, inres_rows, inflow_rows,
    ends, plane_in, line_in, line_out, back_out, carry,
    weights, acts, far_out, far_in, near_out, near_in, direct_out, direct_in, parts, back_rows, final_in,
    res_out, res_in, summed, stat_out, stat_in,
    input_s, halo_s, halo_r, s1_s, s1_r, s2_s, s2_r, s3_s, s3_r, ring_s, ring_r, sib_s, sib_r,
    act_s, act_r, fwd_s, fwd_r, far_s, far_r, near_s, near_r, direct_s, direct_r,
    fin_s, fin_r, res_s, res_r, stat_s, stat_r,
):
    seq, x = lax.axis_index("seq"), lax.axis_index("ch")
    z, j = lax.div(seq, NJ), lax.rem(seq, NJ)
    y, h = lax.div(j, NH), lax.rem(j, NH)

    def device(z_, j_, x_):
        return (z_ * NJ + j_, x_)

    def remote(src, dst, send, recv, target):
        return pltpu.make_async_remote_copy(
            src_ref=src, dst_ref=dst, send_sem=send, recv_sem=recv, device_id=target, device_id_type=MESH
        )

    def row(t):
        return pl.ds(pl.multiple_of(t * SUBS, SUBS), SUBS)

    own_weights = weights.at[shard_rows(0, h), :]
    inputs = [
        pltpu.make_async_copy(src, dst, input_s.at[n])
        for n, (src, dst) in enumerate((
            (k_hbm, k_ref), (v_hbm, v_ref), (q_hbm, q_ref), (weight_hbm, own_weights), (rates_hbm, rates_ref),
            (taps_hbm, taps_ref), (residues_hbm, residues_ref), (prior_hbm, prior_ref), (skip_hbm, skip_ref),
            (residual_hbm, residual_ref), (gain_hbm, gain_ref),
        ))
    ]
    for copy in inputs:
        copy.start()

    barrier = pltpu.get_barrier_semaphore()

    def greet(target):
        pl.semaphore_signal(barrier, inc=1, device_id=target, device_id_type=MESH)

    @pl.loop(1, NJ)
    def _(d):
        greet(device(z, lax.rem(j + d, NJ), x))

    @pl.loop(1, NZ)
    def _(d):
        greet(device(lax.rem(z + d, NZ), j, x))

    @pl.loop(1, NX)
    def _(d):
        greet(device(z, j, lax.rem(x + d, NX)))

    has_next, has_prev = seq < NZ * NJ - 1, seq > 0
    first_j, last_j = j == 0, j == NJ - 1

    @pl.when(last_j)
    def _():
        greet(device(lax.rem(z + 1, NZ), 0, x))

    @pl.when(first_j)
    def _():
        greet(device(lax.rem(z + NZ - 1, NZ), NJ - 1, x))

    @pl.loop(1, 3)
    def _(d):
        greet(device(lax.rem(z + d, NZ), y * NH + 1 - h, x))
        greet(device(lax.rem(z + NZ - d, NZ), y * NH + 1 - h, x))

    @pl.loop(1, NX)
    def _(d):
        @pl.loop(1, NY)
        def _(e):
            greet(device(z, lax.rem(y + e, NY) * NH + h, lax.rem(x + d, NX)))

    peers = NJ + NZ + NX - 3 + 4 + (NX - 1) * (NY - 1)
    edge = jnp.logical_or(first_j, last_j)

    @pl.when(edge)
    def _():
        pl.semaphore_wait(barrier, peers + 1)

    @pl.when(jnp.logical_not(edge))
    def _():
        pl.semaphore_wait(barrier, peers)

    sibling = device(z, y * NH + 1 - h, x)

    def along(hops, core):
        return device(lax.rem(z + hops + NZ, NZ), y * NH + core, x)

    def shard(slot):
        return weights.at[shard_rows(slot, h), :]

    def ring_copy(src, hops, slot, sent, got, core=None):
        to = along(hops, h if core is None else core)
        return remote(src, shard(slot), ring_s.at[sent], ring_r.at[got], to)

    def ring_first():
        for d in (3, 2, 1):
            ring_copy(weight_hbm, d, NZ - d, 0, 0 if d == 3 else 2).start()
            ring_copy(weight_hbm, -d, d, 0, 1 if d == 3 else 2).start()

    def ring_second():
        shards_wait(1, 0)
        for d in (3, 2, 1):
            ring_copy(shard(NZ - 3), d, NZ - 3 - d, 1, 3 if d == 3 else 5).start()
        shards_wait(1, 1)
        for d in (3, 2, 1):
            ring_copy(shard(3), -d, 3 + d, 1, 4 if d == 3 else 5).start()

    def ring_third():
        shards_wait(1, 3)
        shards_wait(1, 4)
        for core in (h, 1 - h):
            ring_copy(shard(NZ - 6 - 4 * h), 2 - 4 * h, 8, 2, 6, core).start()
        for core in (h, 1 - h):
            ring_copy(shard(NZ - 6), 1, NZ - 7, 2, 6, core).start()
            ring_copy(shard(6), -1, 7, 2, 6, core).start()

    def shards_all(count, sent, got):
        some = weights.at[pl.ds(0, count * 32), :]
        return remote(some, some, ring_s.at[sent], ring_r.at[got], sibling)

    def shards_wait(count, got):
        shards_all(count, 0, got).wait_recv()

    def sib_first():
        remote(weight_hbm, own_weights, sib_s.at[0], sib_r.at[0], sibling).start()

    def sib_copy(slot):
        three = weights.at[pl.ds(pl.multiple_of(h * (NZ * 32) + slot * 32, 32), 3 * 32), :]
        return remote(three, three, sib_s.at[1], sib_r.at[1], sibling)

    ring_first()
    sib_first()

    def convert(stream, ref, begin, end):
        for part in range(SUBS):
            to = pl.ds(begin * SUBS + part, end - begin, stride=SUBS)
            streams[stream, to, :] = ref[begin:end, part * LANES : (part + 1) * LANES].astype(F32)

    for n in range(3):
        inputs[n].wait()
    for stream, ref in enumerate((q_ref, k_ref, v_ref)):
        convert(stream, ref, ROWS - 16, ROWS)
    last = (ROWS - 2) * SUBS
    halo_copy = remote(
        streams.at[:, pl.ds(last, 2 * SUBS), :], halo, halo_s, halo_r, (lax.rem(seq + 1, NZ * NJ), x)
    )
    pl.when(has_next)(halo_copy.start)
    convert(1, k_ref, 0, ROWS - 16)
    convert(2, v_ref, 0, ROWS - 16)
    for n in range(3, len(inputs)):
        inputs[n].wait()

    for part in range(SUBS):
        cut = slice(part * LANES, (part + 1) * LANES)
        to = pl.ds(part, MODES, stride=SUBS)
        rate_rows[to, :] = rates_ref[:, cut]
        res_rows[to, :] = residues_ref[:, cut]
        prior_rows[to, :] = prior_ref[:, cut]
        for stream in range(3):
            for tap in range(3):
                n = (3 * stream + tap) * SUBS + part
                tap_rows[n : n + 1, :] = taps_ref[stream, tap : tap + 1, cut]
    rates = rate_rows[...]
    inflow = jnp.sqrt(one_minus_exp(2.0 * rates))
    pole_rows[...] = jnp.exp(-rates)
    inflow_rows[...] = inflow
    inres_rows[...] = res_rows[...] * inflow

    def modes_of(ref):
        return [ref[m * SUBS : (m + 1) * SUBS, :] for m in range(MODES)]

    taps = [tap_rows[n * SUBS : (n + 1) * SUBS, :] for n in range(9)]
    poles = modes_of(pole_rows)
    skip = skip_ref[...]

    def feature(stream, now, back1, back2):
        return taps[3 * stream] * now + taps[3 * stream + 1] * back1 + taps[3 * stream + 2] * back2

    def gate(t, history):
        later, feats = [], []
        for stream, (back1, back2) in zip((1, 2), history):
            now = streams[stream, row(t), :]
            feats.append(feature(stream, now, back1, back2))
            later.append((now, back1))
        value = feats[0] * feats[1]
        gated[row(t), :] = value
        return value, tuple(later)

    def steps(begin, end, step, carried):
        def eight(block, carried):
            for t in range(8):
                carried = step(block * 8 + t, carried)
            return carried

        return lax.fori_loop(begin // 8, end // 8, eight, carried)

    def advance(states, value):
        return tuple(pole * state + value for pole, state in zip(poles, states))

    history = tuple((streams[s, SUBS : 2 * SUBS, :], streams[s, 0:SUBS, :]) for s in (1, 2))
    states = tuple(jnp.zeros((SUBS, LANES), F32) for _ in range(MODES))

    def scan_step(t, carried):
        states, history = carried
        value, history = gate(t, history)
        return advance(states, value), history

    scan = (states, history)
    for t in range(2, 8):
        scan = scan_step(t, scan)
    states, history = steps(8, ROWS, scan_step, scan)

    @pl.when(has_prev)
    def _():
        halo_copy.wait_recv()

    @pl.when(jnp.logical_not(has_prev))
    def _():
        halo[...] = jnp.zeros_like(halo)

    def halo_rows(s):
        return halo[s, SUBS : 2 * SUBS, :], halo[s, 0:SUBS, :]

    first, history = gate(0, (halo_rows(1), halo_rows(2)))
    second, history = gate(1, history)
    for m in range(MODES):
        at = slice(m * SUBS, (m + 1) * SUBS)
        late = jnp.exp(-(ROWS - 2.0) * rate_rows[at, :])
        ends[at, :] = inflow_rows[at, :] * (states[m] + late * (poles[m] * first + second))

    pair = 2 * SUBS

    def pair_rows(n):
        return pl.ds(pl.multiple_of(n * pair, pair), pair)

    def to_owner(d):
        to = lax.rem(j + d, NJ)
        return remote(ends.at[pair_rows(to), :], plane_in.at[j], s1_s, s1_r, device(z, to, x))

    def along_line(d):
        return remote(line_out, line_in.at[z], s2_s.at[d], s2_r.at[d], device(lax.rem(z + d, NZ), j, x))

    def from_owner(d):
        to = lax.rem(j + d, NJ)
        return remote(back_out.at[to], carry.at[pair_rows(j), :], s3_s, s3_r, device(z, to, x))

    @pl.loop(1, NJ)
    def _(d):
        to_owner(d).start()

    plane_in[j] = ends[pair_rows(j), :]

    inres = modes_of(inres_rows)

    def output_step(t, carried):
        states, (back1, back2) = carried
        now = streams[0, row(t), :]
        featq[row(t), :] = feature(0, now, back1, back2)
        value = gated[row(t), :]
        states = advance(states, value)
        terms = [r * s for r, s in zip(inres, states)] + [skip * value]
        filt[row(t), :] = tree_sum(terms)
        return states, (now, back1)

    for tile in range(SUBS):
        turned = residual_ref[:, tile * LANES : (tile + 1) * LANES].astype(F32).T.astype(BF16)
        to_rows = slice((tile // 2) * 64, (tile // 2) * 64 + 64)
        for odd in range(2):
            res_out[2 * (tile % 2) + odd, to_rows, :] = turned[64 * odd : 64 * odd + 64, :]

    def beside(block, dx=0):
        return device(z, lax.rem(y + (0, 3, 1, 2)[block], NY) * NH + h, x if dx == 0 else lax.rem(x + dx, NX))

    def res_copy(block):
        ahead = (0, 1, 3, 2)[block]
        to = lax.rem(y + ahead, NY)
        n = block - 1
        return remote(res_out.at[to], res_in.at[n], res_s, res_r, device(z, to * NH + h, x))

    for block in range(1, 4):
        res_copy(block).start()

    convert(0, q_ref, 0, ROWS - 16)
    states = tuple(jnp.zeros((SUBS, LANES), F32) for _ in range(MODES))
    outputs = steps(0, 64, output_step, (states, halo_rows(0)))

    others = plane_in.at[pl.ds(0, NJ - 1)]
    to_owner_all = remote(others, others, s1_s, s1_r, sibling)
    to_owner_all.wait_recv()

    my_rates = rate_rows[pair_rows(j), :]
    block_decay = jnp.exp(-float(ROWS) * my_rates)
    plane_decay = jnp.exp(-float(ROWS * NJ) * my_rates)
    total = plane_in[0]
    for i in range(1, NJ):
        total = block_decay * total + plane_in[i]
    line_out[...] = total

    @pl.loop(1, NZ - z)
    def _(d):
        along_line(d).start()

    ring_second()
    steps(64, ROWS, output_step, outputs)

    @pl.loop(1, z + 1)
    def _(d):
        along_line(d).wait_recv()

    incoming = lax.fori_loop(0, z, lambda i, s: plane_decay * s + line_in[i], prior_rows[pair_rows(j), :])
    for i in range(NJ):
        back_out[i] = incoming
        incoming = block_decay * incoming + plane_in[i]

    @pl.loop(1, NJ)
    def _(d):
        from_owner(d).start()

    carry[pair_rows(j), :] = back_out[j]
    ring_third()
    shards_wait(4, 2)
    sib_copy(NZ - 3).start()
    sib_copy(1).start()

    others = back_out.at[pl.ds(0, NJ - 1)]
    from_owner_all = remote(others, others, s3_s, s3_r, sibling)
    from_owner_all.wait_recv()

    half = ROWS // 2
    up = device(z, lax.rem(y + 1, NY) * NH + h, x)
    down = device(z, lax.rem(y + 3, NY) * NH + h, x)
    across = device(z, lax.rem(y + 2, NY) * NH + h, x)

    act_wait = (0, 2, 2, 1)

    def act_copy(part, side):
        cut = pl.ds(part * half, half)
        n = 2 * part + side
        return remote(acts.at[0, cut, :], acts.at[1 + side, cut, :], act_s, act_r.at[act_wait[n]], (up, down)[side])

    def fwd_copy(part):
        cut = pl.ds(part * half, half)
        return remote(acts.at[1 + part, cut, :], acts.at[3, cut, :], fwd_s, fwd_r, (up, down)[part])

    def carried_step(t, waves):
        waves = tuple(pole * wave for pole, wave in zip(poles, waves))
        filt[row(t), :] = featq[row(t), :] * (filt[row(t), :] + tree_sum(list(waves)))
        return waves

    waves = tuple(res_rows[m * SUBS : (m + 1) * SUBS, :] * carry[m * SUBS : (m + 1) * SUBS, :] for m in range(MODES))
    for part in range(2):
        waves = steps(part * half, (part + 1) * half, carried_step, waves)
        for sub in range(SUBS):
            from_rows = pl.ds(part * half * SUBS + sub, half, stride=SUBS)
            acts[0, part * half : (part + 1) * half, sub * LANES : (sub + 1) * LANES] = filt[from_rows, :].astype(BF16)
        act_copy(part, part).start()
    act_copy(1, 0).start()
    act_copy(0, 1).start()

    pl.when(has_next)(halo_copy.wait_send)
    to_owner_all.wait_send()
    from_owner_all.wait_send()

    @pl.loop(1, NZ - z)
    def _(d):
        along_line(d).wait_send()

    res_all = remote(res_in, res_in, res_s, res_r, sibling)
    res_all.wait_send()
    shards_wait(4, 5)
    sib_copy(NZ - 6).start()
    sib_copy(4).start()
    own_all = remote(weight_hbm, own_weights, sib_s.at[0], sib_r.at[0], sibling)
    own_all.wait_send()
    own_all.wait_recv()
    shards_all(6, 0, 2).wait_send()
    shards_all(6, 1, 2).wait_send()
    for part in range(2):
        act_copy(part, part).wait_recv()
        fwd_copy(part).start()
    res_all.wait_recv()
    shards_wait(6, 6)
    twelve = weights.at[pl.ds(0, 12 * 32), :]
    sib_all = remote(twelve, twelve, sib_s.at[1], sib_r.at[1], sibling)
    sib_all.wait_recv()

    right, left = device(z, j, lax.rem(x + 1, NX)), device(z, j, lax.rem(x + 3, NX))
    sides = (right, left)

    def band(block, dx):
        first = lax.rem(x + dx, NX) * 4 + NZ - z
        slots = [lax.rem(first + i, NZ) for i in range(4)]
        lanes = slice(block % 2 * ROWS, (block % 2 + 1) * ROWS)
        return [parts[block // 2, shard_rows(slot, core), lanes] for slot in slots for core in range(2)]

    def far_copy(block, side):
        n = 2 * block + side
        return remote(far_out.at[n], far_in.at[n], far_s.at[block], far_r.at[block], sides[side])

    def far_all(block):
        both = far_in.at[pl.ds(2 * block, 2)]
        return remote(both, both, far_s.at[block], far_r.at[block], right)

    def near_copy(block, side):
        n = 2 * block + side
        return remote(near_out.at[n], near_in.at[n], near_s.at[block], near_r.at[block], sides[side])

    def near_all(block):
        both = near_in.at[pl.ds(2 * block, 2)]
        return remote(both, both, near_s.at[block], near_r.at[block], right)

    def direct_copy(dx):
        n = dx - 1
        to = device(z, j, lax.rem(x + dx, NX))
        return remote(direct_out.at[n], direct_in.at[n], direct_s, direct_r, to)

    direct_all = remote(direct_in, direct_in, direct_s, direct_r, right)

    def project(pair):
        rows = acts[2 * pair : 2 * pair + 2].reshape(2 * ROWS, CHANS)
        parts[pair] = lax.dot_general(weights[...], rows, (((1,), (1,)), ((), ())), preferred_element_type=F32)

    def begin(block):
        far = band(block, 2)
        if block == 3:
            for dx, chunks in ((2, far), (1, band(block, 1)), (3, band(block, 3))):
                for i in range(8):
                    direct_out[dx - 1, 32 * i : 32 * i + 32, :] = chunks[i].astype(BF16)
                direct_copy(dx).start()
            return
        for side in range(2):
            for i in range(4):
                far_out[2 * block + side, 32 * i : 32 * i + 32, :] = far[4 * side + i].astype(BF16)
            far_copy(block, side).start()

    def middle(block):
        far_all(block).wait_recv()
        for side in range(2):
            n = 2 * block + side
            part = band(block, (1, 3)[side])
            for i in range(8):
                value = part[i]
                if i // 4 == side:
                    value = value + far_in[n, 32 * (i % 4) : 32 * (i % 4) + 32, :].astype(F32)
                near_out[n, 32 * i : 32 * i + 32, :] = value.astype(BF16)
            near_copy(block, side).start()

    def fin_copy(block):
        return remote(
            back_rows.at[block - 1], final_in.at[y], fin_s, fin_r, beside(block)
        )

    def stat_copy(block, dx):
        n = 4 * block + dx
        return remote(stat_out.at[block], stat_in.at[n], stat_s, stat_r, beside(block, dx))

    stat_pairs = [(block, dx) for block in range(4) for dx in range(4) if (block, dx) != (0, 0)]

    def finish(block):
        value = jnp.concatenate(band(block, 0), axis=0)
        if block == 3:
            direct_all.wait_recv()
            for dx in range(1, NX):
                value = value + direct_in[dx - 1].astype(F32)
        else:
            near_all(block).wait_recv()
            for side in range(2):
                value = value + near_in[2 * block + side].astype(F32)
        if block == 0:
            value = value + res_out[y].astype(F32)
        else:
            value = value + res_in[block - 1].astype(F32)
        squares = jnp.sum(value * value, axis=0, keepdims=True)
        stat_out[block] = jnp.broadcast_to(squares, (SUBS, LANES))
        if block == 0:
            final_in[y] = value.astype(BF16)
            stat_in[0] = stat_out[0]
        else:
            back_rows[block - 1] = value.astype(BF16)
            fin_copy(block).start()
        for dx in range(NX):
            if (block, dx) in stat_pairs:
                stat_copy(block, dx).start()

    late_halves = remote(acts.at[1], acts.at[1], act_s, act_r.at[2], up)
    late_halves.wait_recv()
    project(0)
    begin(0)
    begin(1)
    fwd_all = remote(acts.at[3], acts.at[3], fwd_s, fwd_r, up)
    fwd_all.wait_recv()
    project(1)
    begin(2)
    begin(3)
    middle(0)
    middle(1)
    middle(2)
    finish(0)
    finish(1)
    finish(2)
    finish(3)
    fin_all = remote(back_rows, final_in.at[pl.ds(0, NY - 1)], fin_s, fin_r, up)
    fin_all.wait_recv()

    for tile in range(SUBS):
        cut = slice(tile * LANES, (tile + 1) * LANES)
        from_rows = slice((tile // 2) * 64, (tile // 2) * 64 + 64)
        mixed = [final_in[2 * (tile % 2) + odd, from_rows, :].astype(F32) for odd in range(2)]
        value = jnp.concatenate(mixed, axis=0).T
        summed[:, cut] = value
        hidden_ref[:, cut] = value.astype(BF16)
    fifteen = stat_in.at[pl.ds(1, 15)]
    stat_all = remote(fifteen, fifteen, stat_s, stat_r, up)
    stat_all.wait_recv()
    total = tree_sum([stat_in[n] for n in range(16)])
    scale = lax.rsqrt(total * (1.0 / (NX * CHANS)) + 1e-05)
    scale = jnp.broadcast_to(scale[0:1, :], (ROWS, LANES)).T
    for tile in range(SUBS):
        cut = slice(tile * LANES, (tile + 1) * LANES)
        normed_ref[:, cut] = (summed[:, cut] * scale * gain_ref[tile : tile + 1, :]).astype(BF16)

    sib_all.wait_send()
    shards_all(6, 2, 2).wait_send()
    remote(acts.at[pl.ds(0, 2)], acts.at[pl.ds(0, 2)], act_s, act_r.at[2], up).wait_send()
    fwd_all.wait_send()
    for block in range(3):
        far_all(block).wait_send()
        near_all(block).wait_send()
    direct_all.wait_send()
    fin_all.wait_send()
    stat_all.wait_send()


def shard_rows(slot, h):
    return pl.ds(pl.multiple_of(h * (NZ * 32) + slot * 32, 32), 32)


def tree_sum(terms):
    while len(terms) > 1:
        rest = [terms[-1]] if len(terms) % 2 else []
        terms = [a + b for a, b in zip(terms[0::2], terms[1::2])] + rest
    return terms[0]


def local(
    q_stream, k_stream, v_stream, short_filter, rates, residues, skip, prior_state, out_weight, residual, norm_gain
):
    vmem = pl.BlockSpec(memory_space=pltpu.VMEM)
    hbm = pl.BlockSpec(memory_space=pltpu.HBM)
    dma = pltpu.SemaphoreType.DMA
    wide = (ROWS * SUBS, LANES)
    params = (MODES * SUBS, LANES)
    pair = (2 * SUBS, LANES)
    rows = (ROWS, CHANS)
    scratch = [
        pltpu.VMEM(rows, BF16),
        pltpu.VMEM(rows, BF16),
        pltpu.VMEM(rows, BF16),
        pltpu.VMEM(short_filter.shape, F32),
        pltpu.VMEM((MODES, CHANS), F32),
        pltpu.VMEM((MODES, CHANS), F32),
        pltpu.VMEM((SUBS, LANES), F32),
        pltpu.VMEM((MODES, CHANS), F32),
        pltpu.VMEM(rows, BF16),
        pltpu.VMEM((SUBS, LANES), F32),
        pltpu.VMEM((3,) + wide, F32),
        pltpu.VMEM((3, 2 * SUBS, LANES), F32),
        pltpu.VMEM(wide, F32),
        pltpu.VMEM(wide, F32),
        pltpu.VMEM(wide, F32),
        pltpu.VMEM((9 * SUBS, LANES), F32),
        pltpu.VMEM(params, F32),
        pltpu.VMEM(params, F32),
        pltpu.VMEM(params, F32),
        pltpu.VMEM(params, F32),
        pltpu.VMEM(params, F32),
        pltpu.VMEM(params, F32),
        pltpu.VMEM(params, F32),
        pltpu.VMEM((NJ,) + pair, F32),
        pltpu.VMEM((NZ,) + pair, F32),
        pltpu.VMEM(pair, F32),
        pltpu.VMEM((NJ,) + pair, F32),
        pltpu.VMEM(params, F32),
        pltpu.VMEM((CHANS, CHANS), BF16),
        pltpu.VMEM((NY, ROWS, CHANS), BF16),
        pltpu.VMEM((6, ROWS, LANES), BF16),
        pltpu.VMEM((6, ROWS, LANES), BF16),
        pltpu.VMEM((6, BAND, ROWS), BF16),
        pltpu.VMEM((6, BAND, ROWS), BF16),
        pltpu.VMEM((NX - 1, BAND, ROWS), BF16),
        pltpu.VMEM((NX - 1, BAND, ROWS), BF16),
        pltpu.VMEM((2, CHANS, 2 * ROWS), F32),
        pltpu.VMEM((NY - 1, BAND, ROWS), BF16),
        pltpu.VMEM((NY, BAND, ROWS), BF16),
        pltpu.VMEM((NY, BAND, ROWS), BF16),
        pltpu.VMEM((NY - 1, BAND, ROWS), BF16),
        pltpu.VMEM((ROWS, CHANS), F32),
        pltpu.VMEM((NY, SUBS, LANES), F32),
        pltpu.VMEM((16, SUBS, LANES), F32),
    ]
    sems = [dma((11,))]
    for sent, got in (
        (0, 0), (0, 0), (NZ, NZ), (0, 0), (3, 7), (2, 2), (0, 3), (0, 0), (3, 3), (3, 3), (0, 0), (0, 0), (0, 0), (0, 0)
    ):
        sems += [dma((n,)) if n else dma(()) for n in (sent, got)]
    return pl.pallas_call(
        kernel,
        out_shape=(jax.ShapeDtypeStruct((ROWS, CHANS), BF16), jax.ShapeDtypeStruct((ROWS, CHANS), BF16)),
        in_specs=[hbm] * 11,
        out_specs=(vmem, vmem),
        scratch_shapes=scratch + sems,
        compiler_params=pltpu.CompilerParams(
            collective_id=0, has_side_effects=True, vmem_limit_bytes=63 * 1024 * 1024
        ),
        name="mixer",
    )(
        q_stream, k_stream, v_stream, short_filter, rates, residues, skip.reshape(SUBS, LANES), prior_state,
        out_weight.T, residual, norm_gain.reshape(SUBS, LANES),
    )


def solution(mesh):
    placed = (
        P("seq", "ch"),
        P("seq", "ch"),
        P("seq", "ch"),
        P(None, None, "ch"),
        P(None, "ch"),
        P(None, "ch"),
        P("ch"),
        P(None, "ch"),
        P("ch", "seq"),
        P("seq", "ch"),
        P("ch"),
    )
    return jax.shard_map(
        local,
        mesh=mesh,
        in_specs=placed,
        out_specs=(P("seq", "ch"), P("seq", "ch")),
        check_vma=False,
    )
```

```python
import functools

import jax
import jax.numpy as jnp
from jax import lax
from jax.experimental import pallas as pl
from jax.experimental.pallas import tpu as pltpu
from jax.sharding import PartitionSpec as P

MESH = pl.DeviceIdType.MESH
F32 = jnp.float32
BF16 = jnp.bfloat16
NX, NY, NZ, NH = 4, 4, 16, 2
NJ = NY * NH
ROWS = 128
CHANS = 1024
LANES = 128
SUBS = 8
MODES = 16
BAND = CHANS // NX


def one_minus_exp(x):
    series = jnp.full_like(x, 1.0 / 8.0)
    for n in (7.0, 6.0, 5.0, 4.0, 3.0, 2.0):
        series = (1.0 - x * series) * (1.0 / n)
    return jnp.where(x < 0.25, x * (1.0 - x * series), 1.0 - jnp.exp(-x))


def kernel(
    q_hbm, k_hbm, v_hbm, taps_hbm, rates_hbm, residues_hbm, skip_hbm, prior_hbm, weight_hbm, residual_hbm, gain_hbm,
    hidden_ref, normed_ref,
    q_ref, k_ref, v_ref, taps_ref, rates_ref, residues_ref, skip_ref, prior_ref, residual_ref, gain_ref,
    streams, halo, gated, featq, filt, tap_rows, rate_rows, res_rows, prior_rows, pole_rows, inres_rows, inflow_rows,
    ends, plane_in, line_in, line_out, line_sums, back_out, carry,
    weights, acts, far_out, far_in, near_out, near_in, direct_out, direct_in, parts, back_rows, final_in,
    summed, stat_out, stat_in,
    input_s, halo_s, halo_r, s1_s, s1_r, s2_s, s2_r, s3_s, s3_r, ring_s, ring_r, sib_s, sib_r,
    act_s, act_r, fwd_s, fwd_r, far_s, far_r, near_s, near_r, direct_s, direct_r,
    fin_s, fin_r, stat_s, stat_r,
):
    seq, x = lax.axis_index("seq"), lax.axis_index("ch")
    z, j = lax.div(seq, NJ), lax.rem(seq, NJ)
    y, h = lax.div(j, NH), lax.rem(j, NH)

    def device(z_, j_, x_):
        return (z_ * NJ + j_, x_)

    def remote(src, dst, send, recv, target):
        return pltpu.make_async_remote_copy(
            src_ref=src, dst_ref=dst, send_sem=send, recv_sem=recv, device_id=target, device_id_type=MESH
        )

    def row(t):
        return pl.ds(pl.multiple_of(t * SUBS, SUBS), SUBS)

    own_weights = weights.at[shard_rows(0, h), :]
    inputs = [
        pltpu.make_async_copy(src, dst, input_s.at[n])
        for n, (src, dst) in enumerate((
            (k_hbm, k_ref), (v_hbm, v_ref), (q_hbm, q_ref), (weight_hbm, own_weights), (rates_hbm, rates_ref),
            (taps_hbm, taps_ref), (residues_hbm, residues_ref), (prior_hbm, prior_ref), (skip_hbm, skip_ref),
            (residual_hbm, residual_ref), (gain_hbm, gain_ref),
        ))
    ]
    for copy in inputs[:4]:
        copy.start()

    barrier = pltpu.get_barrier_semaphore()

    def greet(target):
        pl.semaphore_signal(barrier, inc=1, device_id=target, device_id_type=MESH)

    direction = 1 - 2 * h
    sibling = device(z, y * NH + 1 - h, x)
    ring_to, other_to = [
        [None] + [device(lax.rem(z + direction * d + NZ, NZ), y * NH + core, x) for d in (1, 2)] for core in (h, 1 - h)
    ]
    line = (1, 2, 3, 4, 8, 12, 13, 14, 15)
    for d in line:
        greet(device(lax.rem(z + d, NZ), j, x))
    for d in (1, 2):
        greet(other_to[d])
    for d in range(1, NJ):
        greet(device(z, lax.rem(j + d, NJ), x))
    for d in range(1, NX):
        greet(device(z, j, lax.rem(x + d, NX)))

    has_next, has_prev = seq < NZ * NJ - 1, seq > 0
    first_j, last_j = j == 0, j == NJ - 1

    @pl.when(last_j)
    def _():
        greet(device(lax.rem(z + 1, NZ), 0, x))

    @pl.when(first_j)
    def _():
        greet(device(lax.rem(z + NZ - 1, NZ), NJ - 1, x))

    for copy in inputs[4:]:
        copy.start()

    peers = NJ - 1 + NX - 1 + len(line) + 2
    edge = jnp.logical_or(first_j, last_j)

    @pl.when(edge)
    def _():
        pl.semaphore_wait(barrier, peers + 1)

    @pl.when(jnp.logical_not(edge))
    def _():
        pl.semaphore_wait(barrier, peers)

    def slot(far):
        return far if far == 0 else (1 - h) * (NZ - far) + h * far

    def ring_copy(far, part=None, other=False):
        hops = 2 - far % 2
        if far > 2:
            rows = [pl.ds(pl.multiple_of(slot(f) * 64, 64), 64) for f in (far - hops, far)]
            src, n = weights.at[rows[0], :], 2 * far
        else:
            shard = part + h - 2 * part * h
            rows = [shard_rows(slot(f), shard) for f in (0, far)]
            src, n = (weight_hbm if part == 0 else weights.at[rows[0], :]), 2 * far + part
        if other:
            return remote(src, weights.at[rows[1], :], ring_s.at[n + 1], ring_r.at[n + 1], other_to[hops])
        return remote(src, weights.at[rows[1], :], ring_s.at[n], ring_r.at[n], ring_to[hops])

    def sib_copy(step):
        if step == 0:
            return remote(weight_hbm, own_weights, sib_s.at[0], sib_r.at[0], sibling)
        first = (1 - h) * (NZ - 2 * step) + h * (2 * step - 1)
        both = weights.at[pl.ds(pl.multiple_of(first * 64, 64), 128), :]
        return remote(both, both, sib_s.at[1], sib_r.at[1], sibling)

    upward = h == 0

    def arrived(far):
        if far > 2:
            ring_copy(far).wait_recv()
        else:
            ring_copy(far, 0).wait_recv()
            ring_copy(far, 1).wait_recv()

    def ring_step(step):
        far = 2 * step
        if step < 4:
            arrived(far)
            if step < 3:
                ring_copy(far + 2).start()
                ring_copy(far + 1).start()
            else:

                @pl.when(upward)
                def _():
                    ring_copy(8).start()
                    ring_copy(8, other=True).start()

                ring_copy(7).start()
                ring_copy(7, other=True).start()
            arrived(far - 1)
            sib_copy(step).start()
        else:
            arrived(7)
            ring_copy(7, other=True).wait_recv()

            @pl.when(upward)
            def _():
                arrived(8)

            @pl.when(jnp.logical_not(upward))
            def _():
                ring_copy(8, other=True).wait_recv()

    ring_copy(2, 0).start()
    sib_copy(0).start()
    ring_copy(1, 0).start()

    def convert(stream, ref, begin, end):
        for part in range(SUBS):
            to = pl.ds(begin * SUBS + part, end - begin, stride=SUBS)
            streams[stream, to, :] = ref[begin:end, part * LANES : (part + 1) * LANES].astype(F32)

    for n in range(3):
        inputs[n].wait()
    for stream, ref in enumerate((q_ref, k_ref, v_ref)):
        convert(stream, ref, ROWS - 16, ROWS)
    last = (ROWS - 2) * SUBS
    halo_copy = remote(
        streams.at[:, pl.ds(last, 2 * SUBS), :], halo, halo_s, halo_r, (lax.rem(seq + 1, NZ * NJ), x)
    )
    pl.when(has_next)(halo_copy.start)
    convert(1, k_ref, 0, ROWS - 16)
    sib_copy(0).wait_recv()
    ring_copy(2, 1).start()
    ring_copy(1, 1).start()
    convert(2, v_ref, 0, ROWS - 16)
    for n in range(3, len(inputs)):
        inputs[n].wait()

    for part in range(SUBS):
        cut = slice(part * LANES, (part + 1) * LANES)
        to = pl.ds(part, MODES, stride=SUBS)
        rate_rows[to, :] = rates_ref[:, cut]
        res_rows[to, :] = residues_ref[:, cut]
        prior_rows[to, :] = prior_ref[:, cut]
        for stream in range(3):
            for tap in range(3):
                n = (3 * stream + tap) * SUBS + part
                tap_rows[n : n + 1, :] = taps_ref[stream, tap : tap + 1, cut]
    rates = rate_rows[...]
    inflow = jnp.sqrt(one_minus_exp(2.0 * rates))
    pole_rows[...] = jnp.exp(-rates)
    inflow_rows[...] = inflow
    inres_rows[...] = res_rows[...] * inflow

    def modes_of(ref):
        return [ref[m * SUBS : (m + 1) * SUBS, :] for m in range(MODES)]

    taps = [tap_rows[n * SUBS : (n + 1) * SUBS, :] for n in range(9)]
    poles = modes_of(pole_rows)
    skip = skip_ref[...]

    def feature(stream, now, back1, back2):
        return taps[3 * stream] * now + taps[3 * stream + 1] * back1 + taps[3 * stream + 2] * back2

    def gate(t, history):
        later, feats = [], []
        for stream, (back1, back2) in zip((1, 2), history):
            now = streams[stream, row(t), :]
            feats.append(feature(stream, now, back1, back2))
            later.append((now, back1))
        value = feats[0] * feats[1]
        gated[row(t), :] = value
        return value, tuple(later)

    def steps(begin, end, step, carried):
        def eight(block, carried):
            for t in range(8):
                carried = step(block * 8 + t, carried)
            return carried

        return lax.fori_loop(begin // 8, end // 8, eight, carried)

    def advance(states, value):
        return tuple(pole * state + value for pole, state in zip(poles, states))

    history = tuple((streams[s, SUBS : 2 * SUBS, :], streams[s, 0:SUBS, :]) for s in (1, 2))
    states = tuple(jnp.zeros((SUBS, LANES), F32) for _ in range(MODES))

    def scan_step(t, carried):
        states, history = carried
        value, history = gate(t, history)
        return advance(states, value), history

    scan = (states, history)
    for t in range(2, 8):
        scan = scan_step(t, scan)
    states, history = steps(8, ROWS, scan_step, scan)

    @pl.when(has_prev)
    def _():
        halo_copy.wait_recv()

    @pl.when(jnp.logical_not(has_prev))
    def _():
        halo[...] = jnp.zeros_like(halo)

    def halo_rows(s):
        return halo[s, SUBS : 2 * SUBS, :], halo[s, 0:SUBS, :]

    first, history = gate(0, (halo_rows(1), halo_rows(2)))
    second, history = gate(1, history)
    for m in range(MODES):
        at = slice(m * SUBS, (m + 1) * SUBS)
        late = jnp.exp(-(ROWS - 2.0) * rate_rows[at, :])
        ends[at, :] = inflow_rows[at, :] * (states[m] + late * (poles[m] * first + second))

    pair = 2 * SUBS

    def pair_rows(n):
        return pl.ds(pl.multiple_of(n * pair, pair), pair)

    def to_owner(d):
        to = lax.rem(j + d, NJ)
        return remote(ends.at[pair_rows(to), :], plane_in.at[j], s1_s, s1_r, device(z, to, x))

    near_line, far_line = (1, 2, 3, 4), (4, 8, 12)

    def along_line(step, n):
        d = (near_line, far_line)[step][n]
        at = 4 * step + n
        to = device(lax.rem(z + d, NZ), j, x)
        return remote(line_out.at[step], line_in.at[at], s2_s.at[at], s2_r.at[at], to)

    def from_owner(d):
        to = lax.rem(j + d, NJ)
        return remote(back_out.at[to], carry.at[pair_rows(j), :], s3_s, s3_r, device(z, to, x))

    for d in range(1, NJ):
        to_owner(d).start()

    plane_in[j] = ends[pair_rows(j), :]
    ring_step(1)

    inres = modes_of(inres_rows)

    def output_step(t, carried):
        states, (back1, back2) = carried
        now = streams[0, row(t), :]
        featq[row(t), :] = feature(0, now, back1, back2)
        value = gated[row(t), :]
        states = advance(states, value)
        terms = [r * s for r, s in zip(inres, states)] + [skip * value]
        filt[row(t), :] = tree_sum(terms)
        return states, (now, back1)

    convert(0, q_ref, 0, ROWS - 16)
    states = tuple(jnp.zeros((SUBS, LANES), F32) for _ in range(MODES))
    outputs = steps(0, 64, output_step, (states, halo_rows(0)))

    others = plane_in.at[pl.ds(0, NJ - 1)]
    to_owner_all = remote(others, others, s1_s, s1_r, sibling)
    to_owner_all.wait_recv()

    my_rates = rate_rows[pair_rows(j), :]
    block_decay = jnp.exp(-float(ROWS) * my_rates)
    plane_decay = jnp.exp(-float(ROWS * NJ) * my_rates)
    total = plane_in[0]
    for i in range(1, NJ):
        total = block_decay * total + plane_in[i]
    def line_sum(step, decay):
        line_sums[...] = jnp.zeros_like(line_sums)
        for n in reversed(range((4, 3)[step])):

            @pl.when(z >= (near_line, far_line)[step][n])
            def _():
                copy = along_line(step, n)
                copy.wait_recv()
                line_sums[...] = decay * line_sums[...] + line_in[4 * step + n]

        return line_sums[...]

    def line_start(step):
        for n in range((4, 3)[step]):
            pl.when(z + (near_line, far_line)[step][n] < NZ)(along_line(step, n).start)

    line_out[0] = total
    line_start(0)
    ring_step(2)
    steps(64, ROWS, output_step, outputs)
    four = line_sum(0, plane_decay)
    line_out[1] = four
    line_start(1)
    ring_step(3)
    before = jnp.exp(-(z * (ROWS * NJ)).astype(F32) * my_rates) * prior_rows[pair_rows(j), :]
    incoming = before + four + jnp.exp(-float(ROWS * NJ * 4) * my_rates) * line_sum(
        1, jnp.exp(-float(ROWS * NJ * 4) * my_rates)
    )
    for i in range(NJ):
        back_out[i] = incoming
        incoming = block_decay * incoming + plane_in[i]

    for d in range(1, NJ):
        from_owner(d).start()

    carry[pair_rows(j), :] = back_out[j]

    others = back_out.at[pl.ds(0, NJ - 1)]
    from_owner_all = remote(others, others, s3_s, s3_r, sibling)
    from_owner_all.wait_recv()

    half = ROWS // 2
    up = device(z, lax.rem(y + 1, NY) * NH + h, x)
    down = device(z, lax.rem(y + 3, NY) * NH + h, x)
    across = device(z, lax.rem(y + 2, NY) * NH + h, x)

    act_wait = (0, 2, 2, 1)

    def act_copy(part, side):
        cut = pl.ds(part * half, half)
        n = 2 * part + side
        return remote(acts.at[0, cut, :], acts.at[1 + side, cut, :], act_s, act_r.at[act_wait[n]], (up, down)[side])

    def fwd_copy(part):
        cut = pl.ds(part * half, half)
        return remote(acts.at[1 + part, cut, :], acts.at[3, cut, :], fwd_s, fwd_r, (up, down)[part])

    def carried_step(t, waves):
        waves = tuple(pole * wave for pole, wave in zip(poles, waves))
        filt[row(t), :] = featq[row(t), :] * (filt[row(t), :] + tree_sum(list(waves)))
        return waves

    waves = tuple(res_rows[m * SUBS : (m + 1) * SUBS, :] * carry[m * SUBS : (m + 1) * SUBS, :] for m in range(MODES))
    for part in range(2):
        waves = steps(part * half, (part + 1) * half, carried_step, waves)
        for sub in range(SUBS):
            from_rows = pl.ds(part * half * SUBS + sub, half, stride=SUBS)
            acts[0, part * half : (part + 1) * half, sub * LANES : (sub + 1) * LANES] = filt[from_rows, :].astype(BF16)
        act_copy(part, part).start()
    act_copy(1, 0).start()
    act_copy(0, 1).start()

    pl.when(has_next)(halo_copy.wait_send)
    to_owner_all.wait_send()
    from_owner_all.wait_send()

    for step in range(2):
        for n in range((4, 3)[step]):
            pl.when(z + (near_line, far_line)[step][n] < NZ)(along_line(step, n).wait_send)
    sib_copy(0).wait_send()
    for part in range(2):
        ring_copy(1, part).wait_send()
        ring_copy(2, part).wait_send()
    for far in range(3, 7):
        ring_copy(far).wait_send()

    ring_step(4)
    for part in range(2):
        act_copy(part, part).wait_recv()
        fwd_copy(part).start()
    three = weights.at[pl.ds(0, 3 * 128), :]
    sib_all = remote(three, three, sib_s.at[1], sib_r.at[1], sibling)
    sib_all.wait_recv()

    right, left = device(z, j, lax.rem(x + 1, NX)), device(z, j, lax.rem(x + 3, NX))
    sides = (right, left)

    def project(pair):
        rows = acts[2 * pair : 2 * pair + 2].reshape(2 * ROWS, CHANS)
        parts[pair] = lax.dot_general(weights[...], rows, (((1,), (1,)), ((), ())), preferred_element_type=F32)

    def band(pair, dx):
        first = lax.rem(x + dx, NX) * 4 + NZ - z
        chunks = [pl.ds(pl.multiple_of(lax.rem(first + i, NZ) * 64, 64), 64) for i in range(4)]
        return [parts[pair, chunk, :] for chunk in chunks]

    def far_copy(side):
        return remote(far_out.at[side], far_in.at[side], far_s, far_r, sides[side])

    def near_copy(side):
        return remote(near_out.at[side], near_in.at[side], near_s, near_r, sides[side])

    def direct_copy(dx):
        n = dx - 1
        to = device(z, j, lax.rem(x + dx, NX))
        return remote(direct_out.at[n], direct_in.at[n], direct_s, direct_r, to)

    far_all = remote(far_in, far_in, far_s, far_r, right)
    near_all = remote(near_in, near_in, near_s, near_r, right)
    direct_all = remote(direct_in, direct_in, direct_s, direct_r, right)

    def fin_copy(block):
        to = (None, down, up, across)[block]
        return remote(back_rows.at[block - 1], final_in.at[y], fin_s, fin_r, to)

    def finish(pair, arrived):
        value = jnp.concatenate(band(pair, 0), axis=0)
        for got in arrived:
            value = value + got.astype(F32)
        for block in (2 * pair, 2 * pair + 1):
            lanes = slice(block % 2 * ROWS, (block % 2 + 1) * ROWS)
            if block == 0:
                final_in[y] = value[:, lanes].astype(BF16)
            else:
                back_rows[block - 1] = value[:, lanes].astype(BF16)
                fin_copy(block).start()

    late_halves = remote(acts.at[1], acts.at[1], act_s, act_r.at[2], up)
    late_halves.wait_recv()
    project(0)
    chunks = band(0, 2)
    for side in range(2):
        for i in range(2):
            far_out[side, 64 * i : 64 * i + 64, :] = chunks[2 * side + i].astype(BF16)
        far_copy(side).start()

    fwd_all = remote(acts.at[3], acts.at[3], fwd_s, fwd_r, up)
    fwd_all.wait_recv()
    project(1)
    for dx in (2, 1, 3):
        for i, chunk in enumerate(band(1, dx)):
            direct_out[dx - 1, 64 * i : 64 * i + 64, :] = chunk.astype(BF16)
        direct_copy(dx).start()

    far_all.wait_recv()
    for side in range(2):
        for i, chunk in enumerate(band(0, (1, 3)[side])):
            if i // 2 == side:
                chunk = chunk + far_in[side, 64 * (i % 2) : 64 * (i % 2) + 64, :].astype(F32)
            near_out[side, 64 * i : 64 * i + 64, :] = chunk.astype(BF16)
        near_copy(side).start()
    near_all.wait_recv()
    finish(0, [near_in[side] for side in range(2)])
    direct_all.wait_recv()
    finish(1, [direct_in[n] for n in range(NX - 1)])
    fin_all = remote(back_rows, final_in.at[pl.ds(0, NY - 1)], fin_s, fin_r, up)
    fin_all.wait_recv()

    squares = jnp.zeros((ROWS, LANES), F32)
    for tile in range(SUBS):
        cut = slice(tile * LANES, (tile + 1) * LANES)
        from_rows = slice((tile // 2) * 64, (tile // 2) * 64 + 64)
        mixed = [final_in[2 * (tile % 2) + odd, from_rows, :].astype(F32) for odd in range(2)]
        value = residual_ref[:, cut].astype(F32) + jnp.concatenate(mixed, axis=0).T
        summed[:, cut] = value
        hidden_ref[:, cut] = value.astype(BF16)
        squares = squares + value * value
    stat_out[...] = jnp.broadcast_to(jnp.sum(squares.T, axis=0, keepdims=True), (SUBS, LANES))

    def stat_copy(d):
        to = device(z, j, lax.rem(x + d, NX))
        return remote(stat_out, stat_in.at[d - 1], stat_s, stat_r, to)

    for d in range(1, NX):
        stat_copy(d).start()
    stat_all = remote(stat_in, stat_in, stat_s, stat_r, right)
    stat_all.wait_recv()
    total = stat_out[...] + stat_in[0] + stat_in[1] + stat_in[2]
    scale = lax.rsqrt(total * (1.0 / (NX * CHANS)) + 1e-05)
    scale = jnp.broadcast_to(scale[0:1, :], (ROWS, LANES)).T
    for tile in range(SUBS):
        cut = slice(tile * LANES, (tile + 1) * LANES)
        normed_ref[:, cut] = (summed[:, cut] * scale * gain_ref[tile : tile + 1, :]).astype(BF16)

    sib_all.wait_send()
    ring_copy(7).wait_send()
    ring_copy(7, other=True).wait_send()

    @pl.when(upward)
    def _():
        ring_copy(8).wait_send()
        ring_copy(8, other=True).wait_send()

    remote(acts.at[pl.ds(0, 2)], acts.at[pl.ds(0, 2)], act_s, act_r.at[2], up).wait_send()
    fwd_all.wait_send()
    for copies in (far_all, near_all, direct_all, fin_all, stat_all):
        copies.wait_send()


def shard_rows(slot, h):
    return pl.ds(pl.multiple_of(slot * 64 + h * 32, 32), 32)


def tree_sum(terms):
    while len(terms) > 1:
        rest = [terms[-1]] if len(terms) % 2 else []
        terms = [a + b for a, b in zip(terms[0::2], terms[1::2])] + rest
    return terms[0]


def local(
    q_stream, k_stream, v_stream, short_filter, rates, residues, skip, prior_state, out_weight, residual, norm_gain
):
    vmem = pl.BlockSpec(memory_space=pltpu.VMEM)
    hbm = pl.BlockSpec(memory_space=pltpu.HBM)
    dma = pltpu.SemaphoreType.DMA
    wide = (ROWS * SUBS, LANES)
    params = (MODES * SUBS, LANES)
    pair = (2 * SUBS, LANES)
    rows = (ROWS, CHANS)
    scratch = [
        pltpu.VMEM(rows, BF16),
        pltpu.VMEM(rows, BF16),
        pltpu.VMEM(rows, BF16),
        pltpu.VMEM(short_filter.shape, F32),
        pltpu.VMEM((MODES, CHANS), F32),
        pltpu.VMEM((MODES, CHANS), F32),
        pltpu.VMEM((SUBS, LANES), F32),
        pltpu.VMEM((MODES, CHANS), F32),
        pltpu.VMEM(rows, BF16),
        pltpu.VMEM((SUBS, LANES), F32),
        pltpu.VMEM((3,) + wide, F32),
        pltpu.VMEM((3, 2 * SUBS, LANES), F32),
        pltpu.VMEM(wide, F32),
        pltpu.VMEM(wide, F32),
        pltpu.VMEM(wide, F32),
        pltpu.VMEM((9 * SUBS, LANES), F32),
        pltpu.VMEM(params, F32),
        pltpu.VMEM(params, F32),
        pltpu.VMEM(params, F32),
        pltpu.VMEM(params, F32),
        pltpu.VMEM(params, F32),
        pltpu.VMEM(params, F32),
        pltpu.VMEM(params, F32),
        pltpu.VMEM((NJ,) + pair, F32),
        pltpu.VMEM((7,) + pair, F32),
        pltpu.VMEM((2,) + pair, F32),
        pltpu.VMEM(pair, F32),
        pltpu.VMEM((NJ,) + pair, F32),
        pltpu.VMEM(params, F32),
        pltpu.VMEM((CHANS, CHANS), BF16),
        pltpu.VMEM((NY, ROWS, CHANS), BF16),
        pltpu.VMEM((2, LANES, 2 * ROWS), BF16),
        pltpu.VMEM((2, LANES, 2 * ROWS), BF16),
        pltpu.VMEM((2, BAND, 2 * ROWS), BF16),
        pltpu.VMEM((2, BAND, 2 * ROWS), BF16),
        pltpu.VMEM((NX - 1, BAND, 2 * ROWS), BF16),
        pltpu.VMEM((NX - 1, BAND, 2 * ROWS), BF16),
        pltpu.VMEM((2, CHANS, 2 * ROWS), F32),
        pltpu.VMEM((NY - 1, BAND, ROWS), BF16),
        pltpu.VMEM((NY, BAND, ROWS), BF16),
        pltpu.VMEM((ROWS, CHANS), F32),
        pltpu.VMEM((SUBS, LANES), F32),
        pltpu.VMEM((NX - 1, SUBS, LANES), F32),
    ]
    sems = [dma((11,))]
    for sent, got in ((0, 0), (0, 0), (7, 7), (0, 0), (18, 18), (2, 2), (0, 3)) + ((0, 0),) * 6:
        sems += [dma((n,)) if n else dma(()) for n in (sent, got)]
    return pl.pallas_call(
        kernel,
        out_shape=(jax.ShapeDtypeStruct((ROWS, CHANS), BF16), jax.ShapeDtypeStruct((ROWS, CHANS), BF16)),
        in_specs=[hbm] * 11,
        out_specs=(vmem, vmem),
        scratch_shapes=scratch + sems,
        compiler_params=pltpu.CompilerParams(
            collective_id=0, has_side_effects=True, vmem_limit_bytes=63 * 1024 * 1024
        ),
        name="mixer",
    )(
        q_stream, k_stream, v_stream, short_filter, rates, residues, skip.reshape(SUBS, LANES), prior_state,
        out_weight.T, residual, norm_gain.reshape(SUBS, LANES),
    )


def solution(mesh):
    placed = (
        P("seq", "ch"),
        P("seq", "ch"),
        P("seq", "ch"),
        P(None, None, "ch"),
        P(None, "ch"),
        P(None, "ch"),
        P("ch"),
        P(None, "ch"),
        P("ch", "seq"),
        P("seq", "ch"),
        P("ch"),
    )
    return jax.shard_map(
        local,
        mesh=mesh,
        in_specs=placed,
        out_specs=(P("seq", "ch"), P("seq", "ch")),
        check_vma=False,
    )
```

```python
import functools

import jax
import jax.numpy as jnp
from jax import lax
from jax.experimental import pallas as pl
from jax.experimental.pallas import tpu as pltpu
from jax.sharding import PartitionSpec as P

MESH = pl.DeviceIdType.MESH
F32 = jnp.float32
BF16 = jnp.bfloat16
NX, NY, NZ, NH = 4, 4, 16, 2
NJ = NY * NH
ROWS = 128
CHANS = 1024
LANES = 128
SUBS = 8
MODES = 16
BAND = CHANS // NX


def one_minus_exp(x):
    series = jnp.full_like(x, 1.0 / 8.0)
    for n in (7.0, 6.0, 5.0, 4.0, 3.0, 2.0):
        series = (1.0 - x * series) * (1.0 / n)
    return jnp.where(x < 0.25, x * (1.0 - x * series), 1.0 - jnp.exp(-x))


def kernel(
    q_hbm, k_hbm, v_hbm, taps_hbm, rates_hbm, residues_hbm, skip_hbm, prior_hbm, weight_hbm, residual_hbm, gain_hbm,
    hidden_ref, normed_ref,
    q_ref, k_ref, v_ref, taps_ref, rates_ref, residues_ref, skip_ref, prior_ref, residual_ref, gain_ref,
    streams, halo, gated, featq, filt, tap_rows, rate_rows, res_rows, prior_rows, pole_rows, inres_rows, inflow_rows,
    ends, plane_in, line_in, line_out, back_out, carry,
    weights, acts, far_out, far_in, near_out, near_in, parts, back_rows, final_in,
    summed, stat_out, stat_in,
    input_s, halo_s, halo_r, s1_s, s1_r, s2_s, s2_r, s3_s, s3_r, ring_s, ring_r, sib_s, sib_r,
    act_s, act_r, fwd_s, fwd_r, far_s, far_r, near_s, near_r,
    fin_s, fin_r, stat_s, stat_r,
):
    seq, x = lax.axis_index("seq"), lax.axis_index("ch")
    z, j = lax.div(seq, NJ), lax.rem(seq, NJ)
    y, h = lax.div(j, NH), lax.rem(j, NH)

    def device(z_, j_, x_):
        return (z_ * NJ + j_, x_)

    def remote(src, dst, send, recv, target):
        return pltpu.make_async_remote_copy(
            src_ref=src, dst_ref=dst, send_sem=send, recv_sem=recv, device_id=target, device_id_type=MESH
        )

    def row(t):
        return pl.ds(pl.multiple_of(t * SUBS, SUBS), SUBS)

    own_weights = weights.at[shard_rows(0, h), :]
    inputs = [
        pltpu.make_async_copy(src, dst, input_s.at[n])
        for n, (src, dst) in enumerate((
            (k_hbm, k_ref), (v_hbm, v_ref), (q_hbm, q_ref), (weight_hbm, own_weights), (rates_hbm, rates_ref),
            (taps_hbm, taps_ref), (residues_hbm, residues_ref), (prior_hbm, prior_ref), (skip_hbm, skip_ref),
            (residual_hbm, residual_ref), (gain_hbm, gain_ref),
        ))
    ]
    for copy in inputs[:4]:
        copy.start()

    barrier = pltpu.get_barrier_semaphore()

    def greet(target):
        pl.semaphore_signal(barrier, inc=1, device_id=target, device_id_type=MESH)

    sibling = device(z, y * NH + 1 - h, x)

    def along(hops, core):
        return device(lax.rem(z + hops + NZ, NZ), y * NH + core, x)

    for d in range(1, NZ):
        greet(along(d, h))
    for d in (1, -1, 2 - 4 * h):
        greet(along(d, 1 - h))
    for d in range(1, NJ):
        greet(device(z, lax.rem(j + d, NJ), x))
    for d in range(1, NX):
        greet(device(z, j, lax.rem(x + d, NX)))

    has_next, has_prev = seq < NZ * NJ - 1, seq > 0
    first_j, last_j = j == 0, j == NJ - 1

    @pl.when(last_j)
    def _():
        greet(device(lax.rem(z + 1, NZ), 0, x))

    @pl.when(first_j)
    def _():
        greet(device(lax.rem(z + NZ - 1, NZ), NJ - 1, x))

    for copy in inputs[4:]:
        copy.start()

    def shard(slot):
        return weights.at[shard_rows(slot, h), :]

    def ring_copy(src, hops, slot, sent, got, core=None):
        to = along(hops, h if core is None else core)
        return remote(src, shard(slot), ring_s.at[sent], ring_r.at[got], to)

    def ring_first():
        for d in (2, 1):
            ring_copy(weight_hbm, d, NZ - d, 0, 0 if d == 2 else 2).start()
            ring_copy(weight_hbm, -d, d, 0, 1 if d == 2 else 2).start()
        remote(weight_hbm, own_weights, sib_s.at[0], sib_r.at[0], sibling).start()

    def shards_all(count, sent, got):
        some = weights.at[pl.ds(0, count * 32), :]
        return remote(some, some, ring_s.at[sent], ring_r.at[got], sibling)

    def shards_wait(count, got):
        shards_all(count, 0, got).wait_recv()

    def ring_next(step):
        far, got = 2 * step, 3 * step
        shards_wait(1, got - 3)
        for d in (2, 1):
            ring_copy(shard(NZ - far), d, NZ - far - d, step, got if d == 2 else got + 2).start()
        shards_wait(1, got - 2)
        for d in (2, 1):
            ring_copy(shard(far), -d, far + d, step, got + 1 if d == 2 else got + 2).start()

    def ring_last():
        shards_wait(1, 6)
        shards_wait(1, 7)
        for core in (h, 1 - h):
            ring_copy(shard(NZ - 6 - 4 * h), 2 - 4 * h, 8, 3, 9, core).start()
        for core in (h, 1 - h):
            ring_copy(shard(NZ - 6), 1, NZ - 7, 3, 9, core).start()
            ring_copy(shard(6), -1, 7, 3, 9, core).start()

    def sib_copy(slot):
        two = weights.at[pl.ds(pl.multiple_of(h * (NZ * 32) + slot * 32, 32), 2 * 32), :]
        return remote(two, two, sib_s.at[1], sib_r.at[1], sibling)

    def sib_give(step):
        shards_wait(2, 3 * step - 1)
        sib_copy(NZ - 2 * step).start()
        sib_copy(2 * step - 1).start()

    peers = NJ - 1 + NX - 1 + NZ - 1 + 3
    edge = jnp.logical_or(first_j, last_j)
    early = z < 7

    def enter(when):
        @pl.when(jnp.logical_and(when, edge))
        def _():
            pl.semaphore_wait(barrier, peers + 1)

        @pl.when(jnp.logical_and(when, jnp.logical_not(edge)))
        def _():
            pl.semaphore_wait(barrier, peers)

        pl.when(when)(ring_first)

    enter(jnp.logical_not(early))

    def convert(stream, ref, begin, end):
        for part in range(SUBS):
            to = pl.ds(begin * SUBS + part, end - begin, stride=SUBS)
            streams[stream, to, :] = ref[begin:end, part * LANES : (part + 1) * LANES].astype(F32)

    for n in range(3):
        inputs[n].wait()
    for stream, ref in enumerate((q_ref, k_ref, v_ref)):
        convert(stream, ref, ROWS - 16, ROWS)
    last = (ROWS - 2) * SUBS
    halo_copy = remote(
        streams.at[:, pl.ds(last, 2 * SUBS), :], halo, halo_s, halo_r, (lax.rem(seq + 1, NZ * NJ), x)
    )
    pl.when(jnp.logical_and(has_next, jnp.logical_not(early)))(halo_copy.start)
    convert(1, k_ref, 0, ROWS - 16)
    convert(2, v_ref, 0, ROWS - 16)
    for n in range(3, len(inputs)):
        inputs[n].wait()

    for part in range(SUBS):
        cut = slice(part * LANES, (part + 1) * LANES)
        to = pl.ds(part, MODES, stride=SUBS)
        rate_rows[to, :] = rates_ref[:, cut]
        res_rows[to, :] = residues_ref[:, cut]
        prior_rows[to, :] = prior_ref[:, cut]
        for stream in range(3):
            for tap in range(3):
                n = (3 * stream + tap) * SUBS + part
                tap_rows[n : n + 1, :] = taps_ref[stream, tap : tap + 1, cut]
    rates = rate_rows[...]
    inflow = jnp.sqrt(one_minus_exp(2.0 * rates))
    pole_rows[...] = jnp.exp(-rates)
    inflow_rows[...] = inflow
    inres_rows[...] = res_rows[...] * inflow

    def modes_of(ref):
        return [ref[m * SUBS : (m + 1) * SUBS, :] for m in range(MODES)]

    taps = [tap_rows[n * SUBS : (n + 1) * SUBS, :] for n in range(9)]
    poles = modes_of(pole_rows)
    skip = skip_ref[...]

    def feature(stream, now, back1, back2):
        return taps[3 * stream] * now + taps[3 * stream + 1] * back1 + taps[3 * stream + 2] * back2

    def gate(t, history):
        later, feats = [], []
        for stream, (back1, back2) in zip((1, 2), history):
            now = streams[stream, row(t), :]
            feats.append(feature(stream, now, back1, back2))
            later.append((now, back1))
        value = feats[0] * feats[1]
        gated[row(t), :] = value
        return value, tuple(later)

    def steps(begin, end, step, carried):
        def eight(block, carried):
            for t in range(8):
                carried = step(block * 8 + t, carried)
            return carried

        return lax.fori_loop(begin // 8, end // 8, eight, carried)

    def advance(states, value):
        return tuple(pole * state + value for pole, state in zip(poles, states))

    history = tuple((streams[s, SUBS : 2 * SUBS, :], streams[s, 0:SUBS, :]) for s in (1, 2))
    states = tuple(jnp.zeros((SUBS, LANES), F32) for _ in range(MODES))

    def scan_step(t, carried):
        states, history = carried
        value, history = gate(t, history)
        return advance(states, value), history

    scan = (states, history)
    for t in range(2, 8):
        scan = scan_step(t, scan)
    states, history = steps(8, ROWS, scan_step, scan)

    enter(early)
    pl.when(jnp.logical_and(has_next, early))(halo_copy.start)

    @pl.when(has_prev)
    def _():
        halo_copy.wait_recv()

    @pl.when(jnp.logical_not(has_prev))
    def _():
        halo[...] = jnp.zeros_like(halo)

    def halo_rows(s):
        return halo[s, SUBS : 2 * SUBS, :], halo[s, 0:SUBS, :]

    first, history = gate(0, (halo_rows(1), halo_rows(2)))
    second, history = gate(1, history)
    for m in range(MODES):
        at = slice(m * SUBS, (m + 1) * SUBS)
        late = jnp.exp(-(ROWS - 2.0) * rate_rows[at, :])
        ends[at, :] = inflow_rows[at, :] * (states[m] + late * (poles[m] * first + second))

    pair = 2 * SUBS

    def pair_rows(n):
        return pl.ds(pl.multiple_of(n * pair, pair), pair)

    def to_owner(d):
        to = lax.rem(j + d, NJ)
        return remote(ends.at[pair_rows(to), :], plane_in.at[j], s1_s, s1_r, device(z, to, x))

    def along_line(d):
        return remote(line_out, line_in.at[z], s2_s.at[d], s2_r.at[d], along(d, h))

    def from_owner(d):
        to = lax.rem(j + d, NJ)
        return remote(back_out.at[to], carry.at[pair_rows(j), :], s3_s, s3_r, device(z, to, x))

    for d in range(1, NJ):
        to_owner(d).start()

    plane_in[j] = ends[pair_rows(j), :]
    ring_next(1)

    inres = modes_of(inres_rows)

    def output_step(t, carried):
        states, (back1, back2) = carried
        now = streams[0, row(t), :]
        featq[row(t), :] = feature(0, now, back1, back2)
        value = gated[row(t), :]
        states = advance(states, value)
        terms = [r * s for r, s in zip(inres, states)] + [skip * value]
        filt[row(t), :] = tree_sum(terms)
        return states, (now, back1)

    convert(0, q_ref, 0, ROWS - 16)
    states = tuple(jnp.zeros((SUBS, LANES), F32) for _ in range(MODES))
    outputs = steps(0, 64, output_step, (states, halo_rows(0)))

    others = plane_in.at[pl.ds(0, NJ - 1)]
    to_owner_all = remote(others, others, s1_s, s1_r, sibling)
    to_owner_all.wait_recv()

    my_rates = rate_rows[pair_rows(j), :]
    block_decay = jnp.exp(-float(ROWS) * my_rates)
    plane_decay = jnp.exp(-float(ROWS * NJ) * my_rates)
    total = plane_in[0]
    for i in range(1, NJ):
        total = block_decay * total + plane_in[i]
    line_out[...] = total

    @pl.loop(1, NZ - z)
    def _(d):
        along_line(d).start()

    ring_next(2)
    sib_give(1)
    steps(64, ROWS, output_step, outputs)
    ring_last()

    @pl.loop(1, z + 1)
    def _(d):
        along_line(d).wait_recv()

    incoming = lax.fori_loop(0, z, lambda i, s: plane_decay * s + line_in[i], prior_rows[pair_rows(j), :])
    for i in range(NJ):
        back_out[i] = incoming
        incoming = block_decay * incoming + plane_in[i]

    for d in range(1, NJ):
        from_owner(d).start()

    carry[pair_rows(j), :] = back_out[j]

    others = back_out.at[pl.ds(0, NJ - 1)]
    from_owner_all = remote(others, others, s3_s, s3_r, sibling)
    from_owner_all.wait_recv()

    half = ROWS // 2
    up = device(z, lax.rem(y + 1, NY) * NH + h, x)
    down = device(z, lax.rem(y + 3, NY) * NH + h, x)
    across = device(z, lax.rem(y + 2, NY) * NH + h, x)

    act_wait = (0, 2, 2, 1)

    def act_copy(part, side):
        cut = pl.ds(part * half, half)
        n = 2 * part + side
        return remote(acts.at[0, cut, :], acts.at[1 + side, cut, :], act_s, act_r.at[act_wait[n]], (up, down)[side])

    def fwd_copy(part):
        cut = pl.ds(part * half, half)
        return remote(acts.at[1 + part, cut, :], acts.at[3, cut, :], fwd_s, fwd_r, (up, down)[part])

    def carried_step(t, waves):
        waves = tuple(pole * wave for pole, wave in zip(poles, waves))
        filt[row(t), :] = featq[row(t), :] * (filt[row(t), :] + tree_sum(list(waves)))
        return waves

    waves = tuple(res_rows[m * SUBS : (m + 1) * SUBS, :] * carry[m * SUBS : (m + 1) * SUBS, :] for m in range(MODES))
    for part in range(2):
        waves = steps(part * half, (part + 1) * half, carried_step, waves)
        for sub in range(SUBS):
            from_rows = pl.ds(part * half * SUBS + sub, half, stride=SUBS)
            acts[0, part * half : (part + 1) * half, sub * LANES : (sub + 1) * LANES] = filt[from_rows, :].astype(BF16)
        act_copy(part, part).start()
    act_copy(1, 0).start()
    act_copy(0, 1).start()

    pl.when(has_next)(halo_copy.wait_send)
    to_owner_all.wait_send()
    from_owner_all.wait_send()

    @pl.loop(1, NZ - z)
    def _(d):
        along_line(d).wait_send()

    sib_give(2)
    sib_give(3)
    own_all = remote(weight_hbm, own_weights, sib_s.at[0], sib_r.at[0], sibling)
    own_all.wait_send()
    own_all.wait_recv()
    for sent in range(3):
        shards_all(4, sent, 0).wait_send()
    for part in range(2):
        act_copy(part, part).wait_recv()
        fwd_copy(part).start()
    shards_wait(6, 9)
    twelve = weights.at[pl.ds(0, 12 * 32), :]
    sib_all = remote(twelve, twelve, sib_s.at[1], sib_r.at[1], sibling)
    sib_all.wait_recv()

    right, left = device(z, j, lax.rem(x + 1, NX)), device(z, j, lax.rem(x + 3, NX))
    sides = (right, left)

    def project(pair):
        rows = acts[2 * pair : 2 * pair + 2].reshape(2 * ROWS, CHANS)
        parts[pair] = lax.dot_general(weights[...], rows, (((1,), (1,)), ((), ())), preferred_element_type=F32)

    def band(pair, dx):
        first = lax.rem(x + dx, NX) * 4 + NZ - z
        slots = [lax.rem(first + i, NZ) for i in range(4)]
        return [parts[pair, shard_rows(slot, core), :] for slot in slots for core in range(2)]

    def far_copy(pair, side):
        n = 2 * pair + side
        return remote(far_out.at[n], far_in.at[n], far_s.at[pair], far_r.at[pair], sides[side])

    def near_copy(pair, side):
        n = 2 * pair + side
        return remote(near_out.at[n], near_in.at[n], near_s.at[pair], near_r.at[pair], sides[side])

    def far_all(pair):
        both = far_in.at[pl.ds(2 * pair, 2)]
        return remote(both, both, far_s.at[pair], far_r.at[pair], right)

    def near_all(pair):
        both = near_in.at[pl.ds(2 * pair, 2)]
        return remote(both, both, near_s.at[pair], near_r.at[pair], right)

    def begin(pair):
        project(pair)
        chunks = band(pair, 2)
        for side in range(2):
            for i in range(4):
                far_out[2 * pair + side, 32 * i : 32 * i + 32, :] = chunks[4 * side + i].astype(BF16)
            far_copy(pair, side).start()

    def middle(pair):
        far_all(pair).wait_recv()
        for side in range(2):
            n = 2 * pair + side
            for i, chunk in enumerate(band(pair, (1, 3)[side])):
                if i // 4 == side:
                    chunk = chunk + far_in[n, 32 * (i % 4) : 32 * (i % 4) + 32, :].astype(F32)
                near_out[n, 32 * i : 32 * i + 32, :] = chunk.astype(BF16)
            near_copy(pair, side).start()

    def fin_copy(block):
        to = (None, down, up, across)[block]
        return remote(back_rows.at[block - 1], final_in.at[y], fin_s, fin_r, to)

    def finish(pair):
        near_all(pair).wait_recv()
        value = jnp.concatenate(band(pair, 0), axis=0)
        for side in range(2):
            value = value + near_in[2 * pair + side].astype(F32)
        for block in (2 * pair + 1, 2 * pair):
            lanes = slice(block % 2 * ROWS, (block % 2 + 1) * ROWS)
            if block == 0:
                final_in[y] = value[:, lanes].astype(BF16)
            else:
                back_rows[block - 1] = value[:, lanes].astype(BF16)
                fin_copy(block).start()

    late_halves = remote(acts.at[1], acts.at[1], act_s, act_r.at[2], up)
    late_halves.wait_recv()
    fwd_all = remote(acts.at[3], acts.at[3], fwd_s, fwd_r, up)
    fwd_all.wait_recv()
    begin(1)
    begin(0)
    middle(1)
    middle(0)
    finish(1)
    finish(0)
    fin_all = remote(back_rows, final_in.at[pl.ds(0, NY - 1)], fin_s, fin_r, up)
    fin_all.wait_recv()

    squares = jnp.zeros((ROWS, LANES), F32)
    for tile in range(SUBS):
        cut = slice(tile * LANES, (tile + 1) * LANES)
        from_rows = slice((tile // 2) * 64, (tile // 2) * 64 + 64)
        mixed = [final_in[2 * (tile % 2) + odd, from_rows, :].astype(F32) for odd in range(2)]
        value = residual_ref[:, cut].astype(F32) + jnp.concatenate(mixed, axis=0).T
        summed[:, cut] = value
        hidden_ref[:, cut] = value.astype(BF16)
        squares = squares + value * value
    stat_out[...] = jnp.broadcast_to(jnp.sum(squares.T, axis=0, keepdims=True), (SUBS, LANES))

    def stat_copy(d):
        to = device(z, j, lax.rem(x + d, NX))
        return remote(stat_out, stat_in.at[d - 1], stat_s, stat_r, to)

    for d in range(1, NX):
        stat_copy(d).start()
    stat_all = remote(stat_in, stat_in, stat_s, stat_r, right)
    stat_all.wait_recv()
    total = stat_out[...] + stat_in[0] + stat_in[1] + stat_in[2]
    scale = lax.rsqrt(total * (1.0 / (NX * CHANS)) + 1e-05)
    scale = jnp.broadcast_to(scale[0:1, :], (ROWS, LANES)).T
    for tile in range(SUBS):
        cut = slice(tile * LANES, (tile + 1) * LANES)
        normed_ref[:, cut] = (summed[:, cut] * scale * gain_ref[tile : tile + 1, :]).astype(BF16)

    sib_all.wait_send()
    shards_all(6, 3, 0).wait_send()
    remote(acts.at[pl.ds(0, 2)], acts.at[pl.ds(0, 2)], act_s, act_r.at[2], up).wait_send()
    fwd_all.wait_send()
    for pair in range(2):
        far_all(pair).wait_send()
        near_all(pair).wait_send()
    fin_all.wait_send()
    stat_all.wait_send()


def shard_rows(slot, h):
    return pl.ds(pl.multiple_of(h * (NZ * 32) + slot * 32, 32), 32)


def tree_sum(terms):
    while len(terms) > 1:
        rest = [terms[-1]] if len(terms) % 2 else []
        terms = [a + b for a, b in zip(terms[0::2], terms[1::2])] + rest
    return terms[0]


def local(
    q_stream, k_stream, v_stream, short_filter, rates, residues, skip, prior_state, out_weight, residual, norm_gain
):
    vmem = pl.BlockSpec(memory_space=pltpu.VMEM)
    hbm = pl.BlockSpec(memory_space=pltpu.HBM)
    dma = pltpu.SemaphoreType.DMA
    wide = (ROWS * SUBS, LANES)
    params = (MODES * SUBS, LANES)
    pair = (2 * SUBS, LANES)
    rows = (ROWS, CHANS)
    scratch = [
        pltpu.VMEM(rows, BF16),
        pltpu.VMEM(rows, BF16),
        pltpu.VMEM(rows, BF16),
        pltpu.VMEM(short_filter.shape, F32),
        pltpu.VMEM((MODES, CHANS), F32),
        pltpu.VMEM((MODES, CHANS), F32),
        pltpu.VMEM((SUBS, LANES), F32),
        pltpu.VMEM((MODES, CHANS), F32),
        pltpu.VMEM(rows, BF16),
        pltpu.VMEM((SUBS, LANES), F32),
        pltpu.VMEM((3,) + wide, F32),
        pltpu.VMEM((3, 2 * SUBS, LANES), F32),
        pltpu.VMEM(wide, F32),
        pltpu.VMEM(wide, F32),
        pltpu.VMEM(wide, F32),
        pltpu.VMEM((9 * SUBS, LANES), F32),
        pltpu.VMEM(params, F32),
        pltpu.VMEM(params, F32),
        pltpu.VMEM(params, F32),
        pltpu.VMEM(params, F32),
        pltpu.VMEM(params, F32),
        pltpu.VMEM(params, F32),
        pltpu.VMEM(params, F32),
        pltpu.VMEM((NJ,) + pair, F32),
        pltpu.VMEM((NZ,) + pair, F32),
        pltpu.VMEM(pair, F32),
        pltpu.VMEM((NJ,) + pair, F32),
        pltpu.VMEM(params, F32),
        pltpu.VMEM((CHANS, CHANS), BF16),
        pltpu.VMEM((NY, ROWS, CHANS), BF16),
        pltpu.VMEM((4, LANES, 2 * ROWS), BF16),
        pltpu.VMEM((4, LANES, 2 * ROWS), BF16),
        pltpu.VMEM((4, BAND, 2 * ROWS), BF16),
        pltpu.VMEM((4, BAND, 2 * ROWS), BF16),
        pltpu.VMEM((2, CHANS, 2 * ROWS), F32),
        pltpu.VMEM((NY - 1, BAND, ROWS), BF16),
        pltpu.VMEM((NY, BAND, ROWS), BF16),
        pltpu.VMEM((ROWS, CHANS), F32),
        pltpu.VMEM((SUBS, LANES), F32),
        pltpu.VMEM((NX - 1, SUBS, LANES), F32),
    ]
    sems = [dma((11,))]
    for sent, got in (
        (0, 0), (0, 0), (NZ, NZ), (0, 0), (4, 10), (2, 2), (0, 3), (0, 0), (2, 2), (2, 2), (0, 0), (0, 0)
    ):
        sems += [dma((n,)) if n else dma(()) for n in (sent, got)]
    return pl.pallas_call(
        kernel,
        out_shape=(jax.ShapeDtypeStruct((ROWS, CHANS), BF16), jax.ShapeDtypeStruct((ROWS, CHANS), BF16)),
        in_specs=[hbm] * 11,
        out_specs=(vmem, vmem),
        scratch_shapes=scratch + sems,
        compiler_params=pltpu.CompilerParams(
            collective_id=0, has_side_effects=True, vmem_limit_bytes=63 * 1024 * 1024
        ),
        name="mixer",
    )(
        q_stream, k_stream, v_stream, short_filter, rates, residues, skip.reshape(SUBS, LANES), prior_state,
        out_weight.T, residual, norm_gain.reshape(SUBS, LANES),
    )


def solution(mesh):
    placed = (
        P("seq", "ch"),
        P("seq", "ch"),
        P("seq", "ch"),
        P(None, None, "ch"),
        P(None, "ch"),
        P(None, "ch"),
        P("ch"),
        P(None, "ch"),
        P("ch", "seq"),
        P("seq", "ch"),
        P("ch"),
    )
    return jax.shard_map(
        local,
        mesh=mesh,
        in_specs=placed,
        out_specs=(P("seq", "ch"), P("seq", "ch")),
        check_vma=False,
    )
```

```python
import functools

import jax
import jax.numpy as jnp
from jax import lax
from jax.experimental import pallas as pl
from jax.experimental.pallas import tpu as pltpu
from jax.sharding import PartitionSpec as P

MESH = pl.DeviceIdType.MESH
F32 = jnp.float32
BF16 = jnp.bfloat16
NX, NY, NZ, NH = 4, 4, 16, 2
NJ = NY * NH
ROWS = 128
CHANS = 1024
LANES = 128
SUBS = 8
MODES = 16
BAND = CHANS // NX


def one_minus_exp(x):
    series = jnp.full_like(x, 1.0 / 8.0)
    for n in (7.0, 6.0, 5.0, 4.0, 3.0, 2.0):
        series = (1.0 - x * series) * (1.0 / n)
    return jnp.where(x < 0.25, x * (1.0 - x * series), 1.0 - jnp.exp(-x))


def kernel(
    q_hbm, k_hbm, v_hbm, taps_hbm, rates_hbm, residues_hbm, skip_hbm, prior_hbm, weight_hbm, residual_hbm, gain_hbm,
    hidden_ref, normed_ref,
    q_ref, k_ref, v_ref, taps_ref, rates_ref, residues_ref, skip_ref, prior_ref, residual_ref, gain_ref,
    streams, halo, gated, featq, filt, tap_rows, rate_rows, res_rows, prior_rows, pole_rows, inres_rows, inflow_rows,
    ends, plane_in, line_in, line_out, back_out, carry,
    weights, acts, far_out, far_in, near_out, near_in, parts, back_rows, final_in,
    summed, stat_out, stat_in,
    input_s, halo_s, halo_r, s1_s, s1_r, s2_s, s2_r, s3_s, s3_r, ring_s, ring_r, sib_s, sib_r,
    act_s, act_r, fwd_s, fwd_r, far_s, far_r, near_s, near_r,
    fin_s, fin_r, stat_s, stat_r,
):
    seq, x = lax.axis_index("seq"), lax.axis_index("ch")
    z, j = lax.div(seq, NJ), lax.rem(seq, NJ)
    y, h = lax.div(j, NH), lax.rem(j, NH)

    def device(z_, j_, x_):
        return (z_ * NJ + j_, x_)

    def remote(src, dst, send, recv, target):
        return pltpu.make_async_remote_copy(
            src_ref=src, dst_ref=dst, send_sem=send, recv_sem=recv, device_id=target, device_id_type=MESH
        )

    def row(t):
        return pl.ds(pl.multiple_of(t * SUBS, SUBS), SUBS)

    own_weights = weights.at[shard_rows(0, h), :]
    inputs = [
        pltpu.make_async_copy(src, dst, input_s.at[n])
        for n, (src, dst) in enumerate((
            (k_hbm, k_ref), (v_hbm, v_ref), (q_hbm, q_ref), (weight_hbm, own_weights), (rates_hbm, rates_ref),
            (taps_hbm, taps_ref), (residues_hbm, residues_ref), (prior_hbm, prior_ref), (skip_hbm, skip_ref),
            (residual_hbm, residual_ref), (gain_hbm, gain_ref),
        ))
    ]
    for copy in inputs[:4]:
        copy.start()

    barrier = pltpu.get_barrier_semaphore()

    def greet(target):
        pl.semaphore_signal(barrier, inc=1, device_id=target, device_id_type=MESH)

    sibling = device(z, y * NH + 1 - h, x)

    def along(hops, core):
        return device(lax.rem(z + hops + NZ, NZ), y * NH + core, x)

    for d in range(1, NZ):
        greet(along(d, h))
    for d in (1, -1, 2 - 4 * h):
        greet(along(d, 1 - h))
    for d in range(1, NJ):
        greet(device(z, lax.rem(j + d, NJ), x))
    for d in range(1, NX):
        greet(device(z, j, lax.rem(x + d, NX)))

    has_next, has_prev = seq < NZ * NJ - 1, seq > 0
    first_j, last_j = j == 0, j == NJ - 1

    @pl.when(last_j)
    def _():
        greet(device(lax.rem(z + 1, NZ), 0, x))

    @pl.when(first_j)
    def _():
        greet(device(lax.rem(z + NZ - 1, NZ), NJ - 1, x))

    for copy in inputs[4:]:
        copy.start()

    def shard(slot):
        return weights.at[shard_rows(slot, h), :]

    def ring_copy(src, hops, slot, sent, got, core=None):
        to = along(hops, h if core is None else core)
        return remote(src, shard(slot), ring_s.at[sent], ring_r.at[got], to)

    def ring_first():
        for d in (2, 1):
            ring_copy(weight_hbm, d, NZ - d, 0, 0 if d == 2 else 2).start()
            ring_copy(weight_hbm, -d, d, 0, 1 if d == 2 else 2).start()
        remote(weight_hbm, own_weights, sib_s.at[0], sib_r.at[0], sibling).start()

    def shards_all(count, sent, got):
        some = weights.at[pl.ds(0, count * 32), :]
        return remote(some, some, ring_s.at[sent], ring_r.at[got], sibling)

    def shards_wait(count, got):
        shards_all(count, 0, got).wait_recv()

    def ring_next(step):
        far, got = 2 * step, 3 * step
        shards_wait(1, got - 3)
        for d in (2, 1):
            ring_copy(shard(NZ - far), d, NZ - far - d, step, got if d == 2 else got + 2).start()
        shards_wait(1, got - 2)
        for d in (2, 1):
            ring_copy(shard(far), -d, far + d, step, got + 1 if d == 2 else got + 2).start()

    def ring_last():
        shards_wait(1, 6)
        shards_wait(1, 7)
        for core in (h, 1 - h):
            ring_copy(shard(NZ - 6 - 4 * h), 2 - 4 * h, 8, 3, 9, core).start()
        for core in (h, 1 - h):
            ring_copy(shard(NZ - 6), 1, NZ - 7, 3, 9, core).start()
            ring_copy(shard(6), -1, 7, 3, 9, core).start()

    def sib_copy(slot):
        two = weights.at[pl.ds(pl.multiple_of(h * (NZ * 32) + slot * 32, 32), 2 * 32), :]
        return remote(two, two, sib_s.at[1], sib_r.at[1], sibling)

    def sib_give(step):
        shards_wait(2, 3 * step - 1)
        sib_copy(NZ - 2 * step).start()
        sib_copy(2 * step - 1).start()

    peers = NJ - 1 + NX - 1 + NZ - 1 + 3
    edge = jnp.logical_or(first_j, last_j)
    early = z < 7

    def enter(when):
        @pl.when(jnp.logical_and(when, edge))
        def _():
            pl.semaphore_wait(barrier, peers + 1)

        @pl.when(jnp.logical_and(when, jnp.logical_not(edge)))
        def _():
            pl.semaphore_wait(barrier, peers)

        pl.when(when)(ring_first)

    enter(jnp.logical_not(early))

    def convert(stream, ref, begin, end):
        for part in range(SUBS):
            to = pl.ds(begin * SUBS + part, end - begin, stride=SUBS)
            streams[stream, to, :] = ref[begin:end, part * LANES : (part + 1) * LANES].astype(F32)

    for n in range(3):
        inputs[n].wait()
    for stream, ref in enumerate((q_ref, k_ref, v_ref)):
        convert(stream, ref, ROWS - 16, ROWS)
    last = (ROWS - 2) * SUBS
    halo_copy = remote(
        streams.at[:, pl.ds(last, 2 * SUBS), :], halo, halo_s, halo_r, (lax.rem(seq + 1, NZ * NJ), x)
    )
    pl.when(jnp.logical_and(has_next, jnp.logical_not(early)))(halo_copy.start)
    convert(1, k_ref, 0, ROWS - 16)
    convert(2, v_ref, 0, ROWS - 16)
    for n in range(3, len(inputs)):
        inputs[n].wait()

    for part in range(SUBS):
        cut = slice(part * LANES, (part + 1) * LANES)
        to = pl.ds(part, MODES, stride=SUBS)
        rate_rows[to, :] = rates_ref[:, cut]
        res_rows[to, :] = residues_ref[:, cut]
        prior_rows[to, :] = prior_ref[:, cut]
        for stream in range(3):
            for tap in range(3):
                n = (3 * stream + tap) * SUBS + part
                tap_rows[n : n + 1, :] = taps_ref[stream, tap : tap + 1, cut]
    rates = rate_rows[...]
    inflow = jnp.sqrt(one_minus_exp(2.0 * rates))
    pole_rows[...] = jnp.exp(-rates)
    inflow_rows[...] = inflow
    inres_rows[...] = res_rows[...] * inflow

    def modes_of(ref):
        return [ref[m * SUBS : (m + 1) * SUBS, :] for m in range(MODES)]

    taps = [tap_rows[n * SUBS : (n + 1) * SUBS, :] for n in range(9)]
    poles = modes_of(pole_rows)
    skip = skip_ref[...]

    def feature(stream, now, back1, back2):
        return taps[3 * stream] * now + taps[3 * stream + 1] * back1 + taps[3 * stream + 2] * back2

    def gate(t, history):
        later, feats = [], []
        for stream, (back1, back2) in zip((1, 2), history):
            now = streams[stream, row(t), :]
            feats.append(feature(stream, now, back1, back2))
            later.append((now, back1))
        value = feats[0] * feats[1]
        gated[row(t), :] = value
        return value, tuple(later)

    def steps(begin, end, step, carried):
        def eight(block, carried):
            for t in range(8):
                carried = step(block * 8 + t, carried)
            return carried

        return lax.fori_loop(begin // 8, end // 8, eight, carried)

    def advance(states, value):
        return tuple(pole * state + value for pole, state in zip(poles, states))

    history = tuple((streams[s, SUBS : 2 * SUBS, :], streams[s, 0:SUBS, :]) for s in (1, 2))
    states = tuple(jnp.zeros((SUBS, LANES), F32) for _ in range(MODES))

    def scan_step(t, carried):
        states, history = carried
        value, history = gate(t, history)
        return advance(states, value), history

    scan = (states, history)
    for t in range(2, 8):
        scan = scan_step(t, scan)
    states, history = steps(8, ROWS, scan_step, scan)

    enter(early)
    pl.when(jnp.logical_and(has_next, early))(halo_copy.start)

    @pl.when(has_prev)
    def _():
        halo_copy.wait_recv()

    @pl.when(jnp.logical_not(has_prev))
    def _():
        halo[...] = jnp.zeros_like(halo)

    def halo_rows(s):
        return halo[s, SUBS : 2 * SUBS, :], halo[s, 0:SUBS, :]

    first, history = gate(0, (halo_rows(1), halo_rows(2)))
    second, history = gate(1, history)
    for m in range(MODES):
        at = slice(m * SUBS, (m + 1) * SUBS)
        late = jnp.exp(-(ROWS - 2.0) * rate_rows[at, :])
        ends[at, :] = inflow_rows[at, :] * (states[m] + late * (poles[m] * first + second))

    pair = 2 * SUBS

    def pair_rows(n):
        return pl.ds(pl.multiple_of(n * pair, pair), pair)

    def to_owner(d):
        to = lax.rem(j + d, NJ)
        return remote(ends.at[pair_rows(to), :], plane_in.at[j], s1_s, s1_r, device(z, to, x))

    def along_line(d):
        return remote(line_out, line_in.at[z], s2_s.at[d], s2_r.at[d], along(d, h))

    def from_owner(d):
        to = lax.rem(j + d, NJ)
        return remote(back_out.at[to], carry.at[pair_rows(j), :], s3_s, s3_r, device(z, to, x))

    for d in range(1, NJ):
        to_owner(d).start()

    plane_in[j] = ends[pair_rows(j), :]
    ring_next(1)

    inres = modes_of(inres_rows)

    def output_step(t, carried):
        states, (back1, back2) = carried
        now = streams[0, row(t), :]
        featq[row(t), :] = feature(0, now, back1, back2)
        value = gated[row(t), :]
        states = advance(states, value)
        terms = [r * s for r, s in zip(inres, states)] + [skip * value]
        filt[row(t), :] = tree_sum(terms)
        return states, (now, back1)

    convert(0, q_ref, 0, ROWS - 16)
    states = tuple(jnp.zeros((SUBS, LANES), F32) for _ in range(MODES))
    outputs = steps(0, 64, output_step, (states, halo_rows(0)))

    others = plane_in.at[pl.ds(0, NJ - 1)]
    to_owner_all = remote(others, others, s1_s, s1_r, sibling)
    to_owner_all.wait_recv()

    my_rates = rate_rows[pair_rows(j), :]
    block_decay = jnp.exp(-float(ROWS) * my_rates)
    plane_decay = jnp.exp(-float(ROWS * NJ) * my_rates)
    total = plane_in[0]
    for i in range(1, NJ):
        total = block_decay * total + plane_in[i]
    line_out[...] = total

    @pl.loop(1, NZ - z)
    def _(d):
        along_line(d).start()

    late = jnp.logical_not(early)

    @pl.when(late)
    def _():
        ring_next(2)
        sib_give(1)

    steps(64, ROWS, output_step, outputs)
    pl.when(late)(ring_last)

    @pl.loop(1, z + 1)
    def _(d):
        along_line(d).wait_recv()

    incoming = lax.fori_loop(0, z, lambda i, s: plane_decay * s + line_in[i], prior_rows[pair_rows(j), :])
    for i in range(NJ):
        back_out[i] = incoming
        incoming = block_decay * incoming + plane_in[i]

    for d in range(1, NJ):
        from_owner(d).start()

    carry[pair_rows(j), :] = back_out[j]

    @pl.when(early)
    def _():
        ring_next(2)
        sib_give(1)

    others = back_out.at[pl.ds(0, NJ - 1)]
    from_owner_all = remote(others, others, s3_s, s3_r, sibling)
    from_owner_all.wait_recv()

    half = ROWS // 2
    up = device(z, lax.rem(y + 1, NY) * NH + h, x)
    down = device(z, lax.rem(y + 3, NY) * NH + h, x)
    across = device(z, lax.rem(y + 2, NY) * NH + h, x)

    act_wait = (0, 2, 2, 1)

    def act_copy(part, side):
        cut = pl.ds(part * half, half)
        n = 2 * part + side
        return remote(acts.at[0, cut, :], acts.at[1 + side, cut, :], act_s, act_r.at[act_wait[n]], (up, down)[side])

    def fwd_copy(part):
        cut = pl.ds(part * half, half)
        return remote(acts.at[1 + part, cut, :], acts.at[3, cut, :], fwd_s, fwd_r, (up, down)[part])

    def carried_step(t, waves):
        waves = tuple(pole * wave for pole, wave in zip(poles, waves))
        filt[row(t), :] = featq[row(t), :] * (filt[row(t), :] + tree_sum(list(waves)))
        return waves

    waves = tuple(res_rows[m * SUBS : (m + 1) * SUBS, :] * carry[m * SUBS : (m + 1) * SUBS, :] for m in range(MODES))
    for part in range(2):
        waves = steps(part * half, (part + 1) * half, carried_step, waves)
        for sub in range(SUBS):
            from_rows = pl.ds(part * half * SUBS + sub, half, stride=SUBS)
            acts[0, part * half : (part + 1) * half, sub * LANES : (sub + 1) * LANES] = filt[from_rows, :].astype(BF16)
        act_copy(part, part).start()
    act_copy(1, 0).start()
    act_copy(0, 1).start()

    pl.when(early)(ring_last)

    pl.when(has_next)(halo_copy.wait_send)
    to_owner_all.wait_send()
    from_owner_all.wait_send()

    @pl.loop(1, NZ - z)
    def _(d):
        along_line(d).wait_send()

    sib_give(2)
    sib_give(3)
    own_all = remote(weight_hbm, own_weights, sib_s.at[0], sib_r.at[0], sibling)
    own_all.wait_send()
    own_all.wait_recv()
    for sent in range(3):
        shards_all(4, sent, 0).wait_send()
    for part in range(2):
        act_copy(part, part).wait_recv()
        fwd_copy(part).start()
    shards_wait(6, 9)
    twelve = weights.at[pl.ds(0, 12 * 32), :]
    sib_all = remote(twelve, twelve, sib_s.at[1], sib_r.at[1], sibling)
    sib_all.wait_recv()

    right, left = device(z, j, lax.rem(x + 1, NX)), device(z, j, lax.rem(x + 3, NX))
    sides = (right, left)

    def project(pair):
        rows = acts[2 * pair : 2 * pair + 2].reshape(2 * ROWS, CHANS)
        parts[pair] = lax.dot_general(weights[...], rows, (((1,), (1,)), ((), ())), preferred_element_type=F32)

    def band(pair, dx):
        first = lax.rem(x + dx, NX) * 4 + NZ - z
        slots = [lax.rem(first + i, NZ) for i in range(4)]
        return [parts[pair, shard_rows(slot, core), :] for slot in slots for core in range(2)]

    def far_copy(pair, side):
        n = 2 * pair + side
        return remote(far_out.at[n], far_in.at[n], far_s.at[pair], far_r.at[pair], sides[side])

    def near_copy(pair, side):
        n = 2 * pair + side
        return remote(near_out.at[n], near_in.at[n], near_s.at[pair], near_r.at[pair], sides[side])

    def far_all(pair):
        both = far_in.at[pl.ds(2 * pair, 2)]
        return remote(both, both, far_s.at[pair], far_r.at[pair], right)

    def near_all(pair):
        both = near_in.at[pl.ds(2 * pair, 2)]
        return remote(both, both, near_s.at[pair], near_r.at[pair], right)

    def begin(pair):
        project(pair)
        chunks = band(pair, 2)
        for side in range(2):
            for i in range(4):
                far_out[2 * pair + side, 32 * i : 32 * i + 32, :] = chunks[4 * side + i].astype(BF16)
            far_copy(pair, side).start()

    def middle(pair):
        far_all(pair).wait_recv()
        for side in range(2):
            n = 2 * pair + side
            for i, chunk in enumerate(band(pair, (1, 3)[side])):
                if i // 4 == side:
                    chunk = chunk + far_in[n, 32 * (i % 4) : 32 * (i % 4) + 32, :].astype(F32)
                near_out[n, 32 * i : 32 * i + 32, :] = chunk.astype(BF16)
            near_copy(pair, side).start()

    def fin_copy(block):
        to = (None, down, up, across)[block]
        return remote(back_rows.at[block - 1], final_in.at[y], fin_s, fin_r, to)

    def finish(pair):
        near_all(pair).wait_recv()
        value = jnp.concatenate(band(pair, 0), axis=0)
        for side in range(2):
            value = value + near_in[2 * pair + side].astype(F32)
        for block in (2 * pair + 1, 2 * pair):
            lanes = slice(block % 2 * ROWS, (block % 2 + 1) * ROWS)
            if block == 0:
                final_in[y] = value[:, lanes].astype(BF16)
            else:
                back_rows[block - 1] = value[:, lanes].astype(BF16)
                fin_copy(block).start()

    late_halves = remote(acts.at[1], acts.at[1], act_s, act_r.at[2], up)
    late_halves.wait_recv()
    fwd_all = remote(acts.at[3], acts.at[3], fwd_s, fwd_r, up)
    fwd_all.wait_recv()
    begin(1)
    begin(0)
    middle(1)
    middle(0)
    finish(1)
    finish(0)
    fin_all = remote(back_rows, final_in.at[pl.ds(0, NY - 1)], fin_s, fin_r, up)
    fin_all.wait_recv()

    squares = jnp.zeros((ROWS, LANES), F32)
    for tile in range(SUBS):
        cut = slice(tile * LANES, (tile + 1) * LANES)
        from_rows = slice((tile // 2) * 64, (tile // 2) * 64 + 64)
        mixed = [final_in[2 * (tile % 2) + odd, from_rows, :].astype(F32) for odd in range(2)]
        value = residual_ref[:, cut].astype(F32) + jnp.concatenate(mixed, axis=0).T
        summed[:, cut] = value
        hidden_ref[:, cut] = value.astype(BF16)
        squares = squares + value * value
    stat_out[...] = jnp.broadcast_to(jnp.sum(squares.T, axis=0, keepdims=True), (SUBS, LANES))

    def stat_copy(d):
        to = device(z, j, lax.rem(x + d, NX))
        return remote(stat_out, stat_in.at[d - 1], stat_s, stat_r, to)

    for d in range(1, NX):
        stat_copy(d).start()
    stat_all = remote(stat_in, stat_in, stat_s, stat_r, right)
    stat_all.wait_recv()
    total = stat_out[...] + stat_in[0] + stat_in[1] + stat_in[2]
    scale = lax.rsqrt(total * (1.0 / (NX * CHANS)) + 1e-05)
    scale = jnp.broadcast_to(scale[0:1, :], (ROWS, LANES)).T
    for tile in range(SUBS):
        cut = slice(tile * LANES, (tile + 1) * LANES)
        normed_ref[:, cut] = (summed[:, cut] * scale * gain_ref[tile : tile + 1, :]).astype(BF16)

    sib_all.wait_send()
    shards_all(6, 3, 0).wait_send()
    remote(acts.at[pl.ds(0, 2)], acts.at[pl.ds(0, 2)], act_s, act_r.at[2], up).wait_send()
    fwd_all.wait_send()
    for pair in range(2):
        far_all(pair).wait_send()
        near_all(pair).wait_send()
    fin_all.wait_send()
    stat_all.wait_send()


def shard_rows(slot, h):
    return pl.ds(pl.multiple_of(h * (NZ * 32) + slot * 32, 32), 32)


def tree_sum(terms):
    while len(terms) > 1:
        rest = [terms[-1]] if len(terms) % 2 else []
        terms = [a + b for a, b in zip(terms[0::2], terms[1::2])] + rest
    return terms[0]


def local(
    q_stream, k_stream, v_stream, short_filter, rates, residues, skip, prior_state, out_weight, residual, norm_gain
):
    vmem = pl.BlockSpec(memory_space=pltpu.VMEM)
    hbm = pl.BlockSpec(memory_space=pltpu.HBM)
    dma = pltpu.SemaphoreType.DMA
    wide = (ROWS * SUBS, LANES)
    params = (MODES * SUBS, LANES)
    pair = (2 * SUBS, LANES)
    rows = (ROWS, CHANS)
    scratch = [
        pltpu.VMEM(rows, BF16),
        pltpu.VMEM(rows, BF16),
        pltpu.VMEM(rows, BF16),
        pltpu.VMEM(short_filter.shape, F32),
        pltpu.VMEM((MODES, CHANS), F32),
        pltpu.VMEM((MODES, CHANS), F32),
        pltpu.VMEM((SUBS, LANES), F32),
        pltpu.VMEM((MODES, CHANS), F32),
        pltpu.VMEM(rows, BF16),
        pltpu.VMEM((SUBS, LANES), F32),
        pltpu.VMEM((3,) + wide, F32),
        pltpu.VMEM((3, 2 * SUBS, LANES), F32),
        pltpu.VMEM(wide, F32),
        pltpu.VMEM(wide, F32),
        pltpu.VMEM(wide, F32),
        pltpu.VMEM((9 * SUBS, LANES), F32),
        pltpu.VMEM(params, F32),
        pltpu.VMEM(params, F32),
        pltpu.VMEM(params, F32),
        pltpu.VMEM(params, F32),
        pltpu.VMEM(params, F32),
        pltpu.VMEM(params, F32),
        pltpu.VMEM(params, F32),
        pltpu.VMEM((NJ,) + pair, F32),
        pltpu.VMEM((NZ,) + pair, F32),
        pltpu.VMEM(pair, F32),
        pltpu.VMEM((NJ,) + pair, F32),
        pltpu.VMEM(params, F32),
        pltpu.VMEM((CHANS, CHANS), BF16),
        pltpu.VMEM((NY, ROWS, CHANS), BF16),
        pltpu.VMEM((4, LANES, 2 * ROWS), BF16),
        pltpu.VMEM((4, LANES, 2 * ROWS), BF16),
        pltpu.VMEM((4, BAND, 2 * ROWS), BF16),
        pltpu.VMEM((4, BAND, 2 * ROWS), BF16),
        pltpu.VMEM((2, CHANS, 2 * ROWS), F32),
        pltpu.VMEM((NY - 1, BAND, ROWS), BF16),
        pltpu.VMEM((NY, BAND, ROWS), BF16),
        pltpu.VMEM((ROWS, CHANS), F32),
        pltpu.VMEM((SUBS, LANES), F32),
        pltpu.VMEM((NX - 1, SUBS, LANES), F32),
    ]
    sems = [dma((11,))]
    for sent, got in (
        (0, 0), (0, 0), (NZ, NZ), (0, 0), (4, 10), (2, 2), (0, 3), (0, 0), (2, 2), (2, 2), (0, 0), (0, 0)
    ):
        sems += [dma((n,)) if n else dma(()) for n in (sent, got)]
    return pl.pallas_call(
        kernel,
        out_shape=(jax.ShapeDtypeStruct((ROWS, CHANS), BF16), jax.ShapeDtypeStruct((ROWS, CHANS), BF16)),
        in_specs=[hbm] * 11,
        out_specs=(vmem, vmem),
        scratch_shapes=scratch + sems,
        compiler_params=pltpu.CompilerParams(
            collective_id=0, has_side_effects=True, vmem_limit_bytes=63 * 1024 * 1024
        ),
        name="mixer",
    )(
        q_stream, k_stream, v_stream, short_filter, rates, residues, skip.reshape(SUBS, LANES), prior_state,
        out_weight.T, residual, norm_gain.reshape(SUBS, LANES),
    )


def solution(mesh):
    placed = (
        P("seq", "ch"),
        P("seq", "ch"),
        P("seq", "ch"),
        P(None, None, "ch"),
        P(None, "ch"),
        P(None, "ch"),
        P("ch"),
        P(None, "ch"),
        P("ch", "seq"),
        P("seq", "ch"),
        P("ch"),
    )
    return jax.shard_map(
        local,
        mesh=mesh,
        in_specs=placed,
        out_specs=(P("seq", "ch"), P("seq", "ch")),
        check_vma=False,
    )
```

```python
import functools

import jax
import jax.numpy as jnp
from jax import lax
from jax.experimental import pallas as pl
from jax.experimental.pallas import tpu as pltpu
from jax.sharding import PartitionSpec as P

MESH = pl.DeviceIdType.MESH
F32 = jnp.float32
BF16 = jnp.bfloat16
NX, NY, NZ, NH = 4, 4, 16, 2
NJ = NY * NH
ROWS = 128
CHANS = 1024
LANES = 128
SUBS = 8
MODES = 16
BAND = CHANS // NX


def one_minus_exp(x):
    series = jnp.full_like(x, 1.0 / 8.0)
    for n in (7.0, 6.0, 5.0, 4.0, 3.0, 2.0):
        series = (1.0 - x * series) * (1.0 / n)
    return jnp.where(x < 0.25, x * (1.0 - x * series), 1.0 - jnp.exp(-x))


def kernel(
    q_hbm, k_hbm, v_hbm, taps_hbm, rates_hbm, residues_hbm, skip_hbm, prior_hbm, weight_hbm, residual_hbm, gain_hbm,
    hidden_ref, normed_ref,
    q_ref, k_ref, v_ref, taps_ref, rates_ref, residues_ref, skip_ref, prior_ref, residual_ref, gain_ref,
    streams, halo, gated, featq, filt, tap_rows, rate_rows, res_rows, prior_rows, pole_rows, inres_rows, inflow_rows,
    ends, plane_in, line_in, line_out, back_out, carry,
    weights, acts, far_out, far_in, near_out, near_in, parts, back_rows, final_in,
    summed, stat_out, stat_in,
    input_s, halo_s, halo_r, s1_s, s1_r, s2_s, s2_r, s3_s, s3_r, ring_s, ring_r, sib_s, sib_r,
    act_s, act_r, fwd_s, fwd_r, far_s, far_r, near_s, near_r,
    fin_s, fin_r, stat_s, stat_r,
):
    seq, x = lax.axis_index("seq"), lax.axis_index("ch")
    z, j = lax.div(seq, NJ), lax.rem(seq, NJ)
    y, h = lax.div(j, NH), lax.rem(j, NH)

    def device(z_, j_, x_):
        return (z_ * NJ + j_, x_)

    def remote(src, dst, send, recv, target):
        return pltpu.make_async_remote_copy(
            src_ref=src, dst_ref=dst, send_sem=send, recv_sem=recv, device_id=target, device_id_type=MESH
        )

    def row(t):
        return pl.ds(pl.multiple_of(t * SUBS, SUBS), SUBS)

    own_weights = weights.at[shard_rows(0, h), :]
    inputs = [
        pltpu.make_async_copy(src, dst, input_s.at[n])
        for n, (src, dst) in enumerate((
            (k_hbm, k_ref), (v_hbm, v_ref), (q_hbm, q_ref), (weight_hbm, own_weights), (rates_hbm, rates_ref),
            (taps_hbm, taps_ref), (residues_hbm, residues_ref), (prior_hbm, prior_ref), (skip_hbm, skip_ref),
            (residual_hbm, residual_ref), (gain_hbm, gain_ref),
        ))
    ]
    for copy in inputs[:4]:
        copy.start()

    barrier = pltpu.get_barrier_semaphore()

    def greet(target):
        pl.semaphore_signal(barrier, inc=1, device_id=target, device_id_type=MESH)

    sibling = device(z, y * NH + 1 - h, x)

    def along(hops, core):
        return device(lax.rem(z + hops + NZ, NZ), y * NH + core, x)

    for d in range(1, NZ):
        greet(along(d, h))
    for d in (1, -1, 2 - 4 * h):
        greet(along(d, 1 - h))
    for d in range(1, NJ):
        greet(device(z, lax.rem(j + d, NJ), x))
    for d in range(1, NX):
        greet(device(z, j, lax.rem(x + d, NX)))

    has_next, has_prev = seq < NZ * NJ - 1, seq > 0
    first_j, last_j = j == 0, j == NJ - 1

    @pl.when(last_j)
    def _():
        greet(device(lax.rem(z + 1, NZ), 0, x))

    @pl.when(first_j)
    def _():
        greet(device(lax.rem(z + NZ - 1, NZ), NJ - 1, x))

    for copy in inputs[4:]:
        copy.start()

    def shard(slot):
        return weights.at[shard_rows(slot, h), :]

    def ring_copy(src, hops, slot, sent, got, core=None):
        to = along(hops, h if core is None else core)
        return remote(src, shard(slot), ring_s.at[sent], ring_r.at[got], to)

    def ring_first():
        for d in (2, 1):
            ring_copy(weight_hbm, d, NZ - d, 0, 0 if d == 2 else 2).start()
            ring_copy(weight_hbm, -d, d, 0, 1 if d == 2 else 2).start()
        remote(weight_hbm, own_weights, sib_s.at[0], sib_r.at[0], sibling).start()

    def shards_all(count, sent, got):
        some = weights.at[pl.ds(0, count * 32), :]
        return remote(some, some, ring_s.at[sent], ring_r.at[got], sibling)

    def shards_wait(count, got):
        shards_all(count, 0, got).wait_recv()

    def ring_next(step):
        far, got = 2 * step, 3 * step
        shards_wait(1, got - 3)
        for d in (2, 1):
            ring_copy(shard(NZ - far), d, NZ - far - d, step, got if d == 2 else got + 2).start()
        shards_wait(1, got - 2)
        for d in (2, 1):
            ring_copy(shard(far), -d, far + d, step, got + 1 if d == 2 else got + 2).start()

    def ring_last():
        shards_wait(1, 6)
        shards_wait(1, 7)
        for core in (h, 1 - h):
            ring_copy(shard(NZ - 6 - 4 * h), 2 - 4 * h, 8, 3, 9, core).start()
        for core in (h, 1 - h):
            ring_copy(shard(NZ - 6), 1, NZ - 7, 3, 9, core).start()
            ring_copy(shard(6), -1, 7, 3, 9, core).start()

    def sib_copy(slot):
        two = weights.at[pl.ds(pl.multiple_of(h * (NZ * 32) + slot * 32, 32), 2 * 32), :]
        return remote(two, two, sib_s.at[1], sib_r.at[1], sibling)

    def sib_give(step):
        shards_wait(2, 3 * step - 1)
        sib_copy(NZ - 2 * step).start()
        sib_copy(2 * step - 1).start()

    peers = NJ - 1 + NX - 1 + NZ - 1 + 3
    edge = jnp.logical_or(first_j, last_j)
    early = z < 7

    def convert(stream, ref, begin, end):
        for part in range(SUBS):
            to = pl.ds(begin * SUBS + part, end - begin, stride=SUBS)
            streams[stream, to, :] = ref[begin:end, part * LANES : (part + 1) * LANES].astype(F32)

    for n in range(3):
        inputs[n].wait()
    for stream, ref in enumerate((q_ref, k_ref, v_ref)):
        convert(stream, ref, ROWS - 16, ROWS)
    last = (ROWS - 2) * SUBS
    halo_copy = remote(
        streams.at[:, pl.ds(last, 2 * SUBS), :], halo, halo_s, halo_r, (lax.rem(seq + 1, NZ * NJ), x)
    )
    convert(1, k_ref, 0, ROWS - 16)
    convert(2, v_ref, 0, ROWS - 16)
    for n in range(3, len(inputs)):
        inputs[n].wait()

    for part in range(SUBS):
        cut = slice(part * LANES, (part + 1) * LANES)
        to = pl.ds(part, MODES, stride=SUBS)
        rate_rows[to, :] = rates_ref[:, cut]
        res_rows[to, :] = residues_ref[:, cut]
        prior_rows[to, :] = prior_ref[:, cut]
        for stream in range(3):
            for tap in range(3):
                n = (3 * stream + tap) * SUBS + part
                tap_rows[n : n + 1, :] = taps_ref[stream, tap : tap + 1, cut]
    rates = rate_rows[...]
    inflow = jnp.sqrt(one_minus_exp(2.0 * rates))
    pole_rows[...] = jnp.exp(-rates)
    inflow_rows[...] = inflow
    inres_rows[...] = res_rows[...] * inflow

    def modes_of(ref):
        return [ref[m * SUBS : (m + 1) * SUBS, :] for m in range(MODES)]

    taps = [tap_rows[n * SUBS : (n + 1) * SUBS, :] for n in range(9)]
    poles = modes_of(pole_rows)
    skip = skip_ref[...]

    def feature(stream, now, back1, back2):
        return taps[3 * stream] * now + taps[3 * stream + 1] * back1 + taps[3 * stream + 2] * back2

    def gate(t, history):
        later, feats = [], []
        for stream, (back1, back2) in zip((1, 2), history):
            now = streams[stream, row(t), :]
            feats.append(feature(stream, now, back1, back2))
            later.append((now, back1))
        value = feats[0] * feats[1]
        gated[row(t), :] = value
        return value, tuple(later)

    def steps(begin, end, step, carried):
        def eight(block, carried):
            for t in range(8):
                carried = step(block * 8 + t, carried)
            return carried

        return lax.fori_loop(begin // 8, end // 8, eight, carried)

    def advance(states, value):
        return tuple(pole * state + value for pole, state in zip(poles, states))

    history = tuple((streams[s, SUBS : 2 * SUBS, :], streams[s, 0:SUBS, :]) for s in (1, 2))
    states = tuple(jnp.zeros((SUBS, LANES), F32) for _ in range(MODES))

    def scan_step(t, carried):
        states, history = carried
        value, history = gate(t, history)
        return advance(states, value), history

    scan = (states, history)
    for t in range(2, 8):
        scan = scan_step(t, scan)
    states, history = steps(8, ROWS, scan_step, scan)

    @pl.when(edge)
    def _():
        pl.semaphore_wait(barrier, peers + 1)

    @pl.when(jnp.logical_not(edge))
    def _():
        pl.semaphore_wait(barrier, peers)

    pl.when(has_next)(halo_copy.start)
    ring_first()

    @pl.when(has_prev)
    def _():
        halo_copy.wait_recv()

    @pl.when(jnp.logical_not(has_prev))
    def _():
        halo[...] = jnp.zeros_like(halo)

    def halo_rows(s):
        return halo[s, SUBS : 2 * SUBS, :], halo[s, 0:SUBS, :]

    first, history = gate(0, (halo_rows(1), halo_rows(2)))
    second, history = gate(1, history)
    for m in range(MODES):
        at = slice(m * SUBS, (m + 1) * SUBS)
        late = jnp.exp(-(ROWS - 2.0) * rate_rows[at, :])
        ends[at, :] = inflow_rows[at, :] * (states[m] + late * (poles[m] * first + second))

    pair = 2 * SUBS

    def pair_rows(n):
        return pl.ds(pl.multiple_of(n * pair, pair), pair)

    def to_owner(d):
        to = lax.rem(j + d, NJ)
        return remote(ends.at[pair_rows(to), :], plane_in.at[j], s1_s, s1_r, device(z, to, x))

    def along_line(d):
        return remote(line_out, line_in.at[z], s2_s.at[d], s2_r.at[d], along(d, h))

    def from_owner(d):
        to = lax.rem(j + d, NJ)
        return remote(back_out.at[to], carry.at[pair_rows(j), :], s3_s, s3_r, device(z, to, x))

    for d in range(1, NJ):
        to_owner(d).start()

    plane_in[j] = ends[pair_rows(j), :]
    ring_next(1)

    inres = modes_of(inres_rows)

    def output_step(t, carried):
        states, (back1, back2) = carried
        now = streams[0, row(t), :]
        featq[row(t), :] = feature(0, now, back1, back2)
        value = gated[row(t), :]
        states = advance(states, value)
        terms = [r * s for r, s in zip(inres, states)] + [skip * value]
        filt[row(t), :] = tree_sum(terms)
        return states, (now, back1)

    convert(0, q_ref, 0, ROWS - 16)
    states = tuple(jnp.zeros((SUBS, LANES), F32) for _ in range(MODES))
    outputs = steps(0, 64, output_step, (states, halo_rows(0)))

    others = plane_in.at[pl.ds(0, NJ - 1)]
    to_owner_all = remote(others, others, s1_s, s1_r, sibling)
    to_owner_all.wait_recv()

    my_rates = rate_rows[pair_rows(j), :]
    block_decay = jnp.exp(-float(ROWS) * my_rates)
    plane_decay = jnp.exp(-float(ROWS * NJ) * my_rates)
    total = plane_in[0]
    for i in range(1, NJ):
        total = block_decay * total + plane_in[i]
    line_out[...] = total

    @pl.loop(1, NZ - z)
    def _(d):
        along_line(d).start()

    late = jnp.logical_not(early)

    @pl.when(late)
    def _():
        ring_next(2)
        sib_give(1)

    steps(64, ROWS, output_step, outputs)
    pl.when(late)(ring_last)

    @pl.loop(1, z + 1)
    def _(d):
        along_line(d).wait_recv()

    incoming = lax.fori_loop(0, z, lambda i, s: plane_decay * s + line_in[i], prior_rows[pair_rows(j), :])
    for i in range(NJ):
        back_out[i] = incoming
        incoming = block_decay * incoming + plane_in[i]

    for d in range(1, NJ):
        from_owner(d).start()

    carry[pair_rows(j), :] = back_out[j]

    @pl.when(early)
    def _():
        ring_next(2)
        sib_give(1)

    others = back_out.at[pl.ds(0, NJ - 1)]
    from_owner_all = remote(others, others, s3_s, s3_r, sibling)
    from_owner_all.wait_recv()

    half = ROWS // 2
    up = device(z, lax.rem(y + 1, NY) * NH + h, x)
    down = device(z, lax.rem(y + 3, NY) * NH + h, x)
    across = device(z, lax.rem(y + 2, NY) * NH + h, x)

    act_wait = (0, 2, 2, 1)

    def act_copy(part, side):
        cut = pl.ds(part * half, half)
        n = 2 * part + side
        return remote(acts.at[0, cut, :], acts.at[1 + side, cut, :], act_s, act_r.at[act_wait[n]], (up, down)[side])

    def fwd_copy(part):
        cut = pl.ds(part * half, half)
        return remote(acts.at[1 + part, cut, :], acts.at[3, cut, :], fwd_s, fwd_r, (up, down)[part])

    def carried_step(t, waves):
        waves = tuple(pole * wave for pole, wave in zip(poles, waves))
        filt[row(t), :] = featq[row(t), :] * (filt[row(t), :] + tree_sum(list(waves)))
        return waves

    waves = tuple(res_rows[m * SUBS : (m + 1) * SUBS, :] * carry[m * SUBS : (m + 1) * SUBS, :] for m in range(MODES))
    for part in range(2):
        waves = steps(part * half, (part + 1) * half, carried_step, waves)
        for sub in range(SUBS):
            from_rows = pl.ds(part * half * SUBS + sub, half, stride=SUBS)
            acts[0, part * half : (part + 1) * half, sub * LANES : (sub + 1) * LANES] = filt[from_rows, :].astype(BF16)
        act_copy(part, part).start()
    act_copy(1, 0).start()
    act_copy(0, 1).start()

    pl.when(early)(ring_last)

    pl.when(has_next)(halo_copy.wait_send)
    to_owner_all.wait_send()
    from_owner_all.wait_send()

    @pl.loop(1, NZ - z)
    def _(d):
        along_line(d).wait_send()

    sib_give(2)
    sib_give(3)
    own_all = remote(weight_hbm, own_weights, sib_s.at[0], sib_r.at[0], sibling)
    own_all.wait_send()
    own_all.wait_recv()
    for sent in range(3):
        shards_all(4, sent, 0).wait_send()
    for part in range(2):
        act_copy(part, part).wait_recv()
        fwd_copy(part).start()
    shards_wait(6, 9)
    twelve = weights.at[pl.ds(0, 12 * 32), :]
    sib_all = remote(twelve, twelve, sib_s.at[1], sib_r.at[1], sibling)
    sib_all.wait_recv()

    right, left = device(z, j, lax.rem(x + 1, NX)), device(z, j, lax.rem(x + 3, NX))
    sides = (right, left)

    def project(pair):
        rows = acts[2 * pair : 2 * pair + 2].reshape(2 * ROWS, CHANS)
        parts[pair] = lax.dot_general(weights[...], rows, (((1,), (1,)), ((), ())), preferred_element_type=F32)

    def band(pair, dx):
        first = lax.rem(x + dx, NX) * 4 + NZ - z
        slots = [lax.rem(first + i, NZ) for i in range(4)]
        return [parts[pair, shard_rows(slot, core), :] for slot in slots for core in range(2)]

    def far_copy(pair, side):
        n = 2 * pair + side
        return remote(far_out.at[n], far_in.at[n], far_s.at[pair], far_r.at[pair], sides[side])

    def near_copy(pair, side):
        n = 2 * pair + side
        return remote(near_out.at[n], near_in.at[n], near_s.at[pair], near_r.at[pair], sides[side])

    def far_all(pair):
        both = far_in.at[pl.ds(2 * pair, 2)]
        return remote(both, both, far_s.at[pair], far_r.at[pair], right)

    def near_all(pair):
        both = near_in.at[pl.ds(2 * pair, 2)]
        return remote(both, both, near_s.at[pair], near_r.at[pair], right)

    def begin(pair):
        project(pair)
        chunks = band(pair, 2)
        for side in range(2):
            for i in range(4):
                far_out[2 * pair + side, 32 * i : 32 * i + 32, :] = chunks[4 * side + i].astype(BF16)
            far_copy(pair, side).start()

    def middle(pair):
        far_all(pair).wait_recv()
        for side in range(2):
            n = 2 * pair + side
            for i, chunk in enumerate(band(pair, (1, 3)[side])):
                if i // 4 == side:
                    chunk = chunk + far_in[n, 32 * (i % 4) : 32 * (i % 4) + 32, :].astype(F32)
                near_out[n, 32 * i : 32 * i + 32, :] = chunk.astype(BF16)
            near_copy(pair, side).start()

    def fin_copy(block):
        to = (None, down, up, across)[block]
        return remote(back_rows.at[block - 1], final_in.at[y], fin_s, fin_r, to)

    def finish(pair):
        near_all(pair).wait_recv()
        value = jnp.concatenate(band(pair, 0), axis=0)
        for side in range(2):
            value = value + near_in[2 * pair + side].astype(F32)
        for block in (2 * pair + 1, 2 * pair):
            lanes = slice(block % 2 * ROWS, (block % 2 + 1) * ROWS)
            if block == 0:
                final_in[y] = value[:, lanes].astype(BF16)
            else:
                back_rows[block - 1] = value[:, lanes].astype(BF16)
                fin_copy(block).start()

    late_halves = remote(acts.at[1], acts.at[1], act_s, act_r.at[2], up)
    late_halves.wait_recv()
    begin(0)
    fwd_all = remote(acts.at[3], acts.at[3], fwd_s, fwd_r, up)
    fwd_all.wait_recv()
    begin(1)
    middle(0)
    middle(1)
    finish(0)
    finish(1)
    fin_all = remote(back_rows, final_in.at[pl.ds(0, NY - 1)], fin_s, fin_r, up)
    fin_all.wait_recv()

    squares = jnp.zeros((ROWS, LANES), F32)
    for tile in range(SUBS):
        cut = slice(tile * LANES, (tile + 1) * LANES)
        from_rows = slice((tile // 2) * 64, (tile // 2) * 64 + 64)
        mixed = [final_in[2 * (tile % 2) + odd, from_rows, :].astype(F32) for odd in range(2)]
        value = residual_ref[:, cut].astype(F32) + jnp.concatenate(mixed, axis=0).T
        summed[:, cut] = value
        hidden_ref[:, cut] = value.astype(BF16)
        squares = squares + value * value
    stat_out[...] = jnp.broadcast_to(jnp.sum(squares.T, axis=0, keepdims=True), (SUBS, LANES))

    def stat_copy(d):
        to = device(z, j, lax.rem(x + d, NX))
        return remote(stat_out, stat_in.at[d - 1], stat_s, stat_r, to)

    for d in range(1, NX):
        stat_copy(d).start()
    stat_all = remote(stat_in, stat_in, stat_s, stat_r, right)
    stat_all.wait_recv()
    total = stat_out[...] + stat_in[0] + stat_in[1] + stat_in[2]
    scale = lax.rsqrt(total * (1.0 / (NX * CHANS)) + 1e-05)
    scale = jnp.broadcast_to(scale[0:1, :], (ROWS, LANES)).T
    for tile in range(SUBS):
        cut = slice(tile * LANES, (tile + 1) * LANES)
        normed_ref[:, cut] = (summed[:, cut] * scale * gain_ref[tile : tile + 1, :]).astype(BF16)

    sib_all.wait_send()
    shards_all(6, 3, 0).wait_send()
    remote(acts.at[pl.ds(0, 2)], acts.at[pl.ds(0, 2)], act_s, act_r.at[2], up).wait_send()
    fwd_all.wait_send()
    for pair in range(2):
        far_all(pair).wait_send()
        near_all(pair).wait_send()
    fin_all.wait_send()
    stat_all.wait_send()


def shard_rows(slot, h):
    return pl.ds(pl.multiple_of(h * (NZ * 32) + slot * 32, 32), 32)


def tree_sum(terms):
    while len(terms) > 1:
        rest = [terms[-1]] if len(terms) % 2 else []
        terms = [a + b for a, b in zip(terms[0::2], terms[1::2])] + rest
    return terms[0]


def local(
    q_stream, k_stream, v_stream, short_filter, rates, residues, skip, prior_state, out_weight, residual, norm_gain
):
    vmem = pl.BlockSpec(memory_space=pltpu.VMEM)
    hbm = pl.BlockSpec(memory_space=pltpu.HBM)
    dma = pltpu.SemaphoreType.DMA
    wide = (ROWS * SUBS, LANES)
    params = (MODES * SUBS, LANES)
    pair = (2 * SUBS, LANES)
    rows = (ROWS, CHANS)
    scratch = [
        pltpu.VMEM(rows, BF16),
        pltpu.VMEM(rows, BF16),
        pltpu.VMEM(rows, BF16),
        pltpu.VMEM(short_filter.shape, F32),
        pltpu.VMEM((MODES, CHANS), F32),
        pltpu.VMEM((MODES, CHANS), F32),
        pltpu.VMEM((SUBS, LANES), F32),
        pltpu.VMEM((MODES, CHANS), F32),
        pltpu.VMEM(rows, BF16),
        pltpu.VMEM((SUBS, LANES), F32),
        pltpu.VMEM((3,) + wide, F32),
        pltpu.VMEM((3, 2 * SUBS, LANES), F32),
        pltpu.VMEM(wide, F32),
        pltpu.VMEM(wide, F32),
        pltpu.VMEM(wide, F32),
        pltpu.VMEM((9 * SUBS, LANES), F32),
        pltpu.VMEM(params, F32),
        pltpu.VMEM(params, F32),
        pltpu.VMEM(params, F32),
        pltpu.VMEM(params, F32),
        pltpu.VMEM(params, F32),
        pltpu.VMEM(params, F32),
        pltpu.VMEM(params, F32),
        pltpu.VMEM((NJ,) + pair, F32),
        pltpu.VMEM((NZ,) + pair, F32),
        pltpu.VMEM(pair, F32),
        pltpu.VMEM((NJ,) + pair, F32),
        pltpu.VMEM(params, F32),
        pltpu.VMEM((CHANS, CHANS), BF16),
        pltpu.VMEM((NY, ROWS, CHANS), BF16),
        pltpu.VMEM((4, LANES, 2 * ROWS), BF16),
        pltpu.VMEM((4, LANES, 2 * ROWS), BF16),
        pltpu.VMEM((4, BAND, 2 * ROWS), BF16),
        pltpu.VMEM((4, BAND, 2 * ROWS), BF16),
        pltpu.VMEM((2, CHANS, 2 * ROWS), F32),
        pltpu.VMEM((NY - 1, BAND, ROWS), BF16),
        pltpu.VMEM((NY, BAND, ROWS), BF16),
        pltpu.VMEM((ROWS, CHANS), F32),
        pltpu.VMEM((SUBS, LANES), F32),
        pltpu.VMEM((NX - 1, SUBS, LANES), F32),
    ]
    sems = [dma((11,))]
    for sent, got in (
        (0, 0), (0, 0), (NZ, NZ), (0, 0), (4, 10), (2, 2), (0, 3), (0, 0), (2, 2), (2, 2), (0, 0), (0, 0)
    ):
        sems += [dma((n,)) if n else dma(()) for n in (sent, got)]
    return pl.pallas_call(
        kernel,
        out_shape=(jax.ShapeDtypeStruct((ROWS, CHANS), BF16), jax.ShapeDtypeStruct((ROWS, CHANS), BF16)),
        in_specs=[hbm] * 11,
        out_specs=(vmem, vmem),
        scratch_shapes=scratch + sems,
        compiler_params=pltpu.CompilerParams(
            collective_id=0, has_side_effects=True, vmem_limit_bytes=63 * 1024 * 1024
        ),
        name="mixer",
    )(
        q_stream, k_stream, v_stream, short_filter, rates, residues, skip.reshape(SUBS, LANES), prior_state,
        out_weight.T, residual, norm_gain.reshape(SUBS, LANES),
    )


def solution(mesh):
    placed = (
        P("seq", "ch"),
        P("seq", "ch"),
        P("seq", "ch"),
        P(None, None, "ch"),
        P(None, "ch"),
        P(None, "ch"),
        P("ch"),
        P(None, "ch"),
        P("ch", "seq"),
        P("seq", "ch"),
        P("ch"),
    )
    return jax.shard_map(
        local,
        mesh=mesh,
        in_specs=placed,
        out_specs=(P("seq", "ch"), P("seq", "ch")),
        check_vma=False,
    )
```

```python
import functools

import jax
import jax.numpy as jnp
from jax import lax
from jax.experimental import pallas as pl
from jax.experimental.pallas import tpu as pltpu
from jax.sharding import PartitionSpec as P

MESH = pl.DeviceIdType.MESH
F32 = jnp.float32
BF16 = jnp.bfloat16
NX, NY, NZ, NH = 4, 4, 16, 2
NJ = NY * NH
ROWS = 128
CHANS = 1024
LANES = 128
SUBS = 8
MODES = 16
BAND = CHANS // NX


def one_minus_exp(x):
    series = jnp.full_like(x, 1.0 / 8.0)
    for n in (7.0, 6.0, 5.0, 4.0, 3.0, 2.0):
        series = (1.0 - x * series) * (1.0 / n)
    return jnp.where(x < 0.25, x * (1.0 - x * series), 1.0 - jnp.exp(-x))


def kernel(
    q_hbm, k_hbm, v_hbm, taps_hbm, rates_hbm, residues_hbm, skip_hbm, prior_hbm, weight_hbm, residual_hbm, gain_hbm,
    hidden_ref, normed_ref,
    q_ref, k_ref, v_ref, taps_ref, rates_ref, residues_ref, skip_ref, prior_ref, residual_ref, gain_ref,
    streams, halo, gated, featq, filt, tap_rows, rate_rows, res_rows, prior_rows, pole_rows, inres_rows, inflow_rows,
    ends, plane_in, line_in, line_out, back_out, carry,
    weights, acts, far_out, far_in, near_out, near_in, parts, back_rows, final_in,
    res_out, res_in, summed, stat_out, stat_in,
    input_s, halo_s, halo_r, s1_s, s1_r, s2_s, s2_r, s3_s, s3_r, ring_s, ring_r, sib_s, sib_r,
    act_s, act_r, fwd_s, fwd_r, far_s, far_r, near_s, near_r,
    fin_s, fin_r, res_s, res_r, stat_s, stat_r,
):
    seq, x = lax.axis_index("seq"), lax.axis_index("ch")
    z, j = lax.div(seq, NJ), lax.rem(seq, NJ)
    y, h = lax.div(j, NH), lax.rem(j, NH)

    def device(z_, j_, x_):
        return (z_ * NJ + j_, x_)

    def remote(src, dst, send, recv, target):
        return pltpu.make_async_remote_copy(
            src_ref=src, dst_ref=dst, send_sem=send, recv_sem=recv, device_id=target, device_id_type=MESH
        )

    def row(t):
        return pl.ds(pl.multiple_of(t * SUBS, SUBS), SUBS)

    own_weights = weights.at[shard_rows(0, h), :]
    inputs = [
        pltpu.make_async_copy(src, dst, input_s.at[n])
        for n, (src, dst) in enumerate((
            (k_hbm, k_ref), (v_hbm, v_ref), (q_hbm, q_ref), (weight_hbm, own_weights), (rates_hbm, rates_ref),
            (taps_hbm, taps_ref), (residues_hbm, residues_ref), (prior_hbm, prior_ref), (skip_hbm, skip_ref),
            (residual_hbm, residual_ref), (gain_hbm, gain_ref),
        ))
    ]
    for copy in inputs[:4]:
        copy.start()

    barrier = pltpu.get_barrier_semaphore()

    def greet(target):
        pl.semaphore_signal(barrier, inc=1, device_id=target, device_id_type=MESH)

    sibling = device(z, y * NH + 1 - h, x)

    def along(hops, core):
        return device(lax.rem(z + hops + NZ, NZ), y * NH + core, x)

    for d in range(1, NZ):
        greet(along(d, h))
    for d in (1, -1, 2 - 4 * h):
        greet(along(d, 1 - h))
    for d in range(1, NJ):
        greet(device(z, lax.rem(j + d, NJ), x))
    for d in range(1, NX):
        for e in range(NY):
            greet(device(z, lax.rem(y + e, NY) * NH + h, lax.rem(x + d, NX)))

    has_next, has_prev = seq < NZ * NJ - 1, seq > 0
    first_j, last_j = j == 0, j == NJ - 1

    @pl.when(last_j)
    def _():
        greet(device(lax.rem(z + 1, NZ), 0, x))

    @pl.when(first_j)
    def _():
        greet(device(lax.rem(z + NZ - 1, NZ), NJ - 1, x))

    for copy in inputs[4:]:
        copy.start()

    def shard(slot):
        return weights.at[shard_rows(slot, h), :]

    def ring_copy(src, hops, slot, sent, got, core=None):
        to = along(hops, h if core is None else core)
        return remote(src, shard(slot), ring_s.at[sent], ring_r.at[got], to)

    def ring_first():
        for d in (2, 1):
            ring_copy(weight_hbm, d, NZ - d, 0, 0 if d == 2 else 2).start()
            ring_copy(weight_hbm, -d, d, 0, 1 if d == 2 else 2).start()
        remote(weight_hbm, own_weights, sib_s.at[0], sib_r.at[0], sibling).start()

    def shards_all(count, sent, got):
        some = weights.at[pl.ds(0, count * 32), :]
        return remote(some, some, ring_s.at[sent], ring_r.at[got], sibling)

    def shards_wait(count, got):
        shards_all(count, 0, got).wait_recv()

    def ring_next(step):
        far, got = 2 * step, 3 * step
        shards_wait(1, got - 3)
        for d in (2, 1):
            ring_copy(shard(NZ - far), d, NZ - far - d, step, got if d == 2 else got + 2).start()
        shards_wait(1, got - 2)
        for d in (2, 1):
            ring_copy(shard(far), -d, far + d, step, got + 1 if d == 2 else got + 2).start()

    def ring_last():
        shards_wait(1, 6)
        shards_wait(1, 7)
        for core in (h, 1 - h):
            ring_copy(shard(NZ - 6 - 4 * h), 2 - 4 * h, 8, 3, 9, core).start()
        for core in (h, 1 - h):
            ring_copy(shard(NZ - 6), 1, NZ - 7, 3, 9, core).start()
            ring_copy(shard(6), -1, 7, 3, 9, core).start()

    def sib_copy(slot):
        two = weights.at[pl.ds(pl.multiple_of(h * (NZ * 32) + slot * 32, 32), 2 * 32), :]
        return remote(two, two, sib_s.at[1], sib_r.at[1], sibling)

    def sib_give(step):
        shards_wait(2, 3 * step - 1)
        sib_copy(NZ - 2 * step).start()
        sib_copy(2 * step - 1).start()

    peers = NJ - 1 + (NX - 1) * NY + NZ - 1 + 3
    edge = jnp.logical_or(first_j, last_j)
    early = z < 7

    def convert(stream, ref, begin, end):
        for part in range(SUBS):
            to = pl.ds(begin * SUBS + part, end - begin, stride=SUBS)
            streams[stream, to, :] = ref[begin:end, part * LANES : (part + 1) * LANES].astype(F32)

    for n in range(3):
        inputs[n].wait()
    for stream, ref in enumerate((q_ref, k_ref, v_ref)):
        convert(stream, ref, ROWS - 16, ROWS)
    last = (ROWS - 2) * SUBS
    halo_copy = remote(
        streams.at[:, pl.ds(last, 2 * SUBS), :], halo, halo_s, halo_r, (lax.rem(seq + 1, NZ * NJ), x)
    )
    convert(1, k_ref, 0, ROWS - 16)
    convert(2, v_ref, 0, ROWS - 16)
    for n in range(3, len(inputs)):
        inputs[n].wait()

    for part in range(SUBS):
        cut = slice(part * LANES, (part + 1) * LANES)
        to = pl.ds(part, MODES, stride=SUBS)
        rate_rows[to, :] = rates_ref[:, cut]
        res_rows[to, :] = residues_ref[:, cut]
        prior_rows[to, :] = prior_ref[:, cut]
        for stream in range(3):
            for tap in range(3):
                n = (3 * stream + tap) * SUBS + part
                tap_rows[n : n + 1, :] = taps_ref[stream, tap : tap + 1, cut]
    rates = rate_rows[...]
    inflow = jnp.sqrt(one_minus_exp(2.0 * rates))
    pole_rows[...] = jnp.exp(-rates)
    inflow_rows[...] = inflow
    inres_rows[...] = res_rows[...] * inflow

    def modes_of(ref):
        return [ref[m * SUBS : (m + 1) * SUBS, :] for m in range(MODES)]

    taps = [tap_rows[n * SUBS : (n + 1) * SUBS, :] for n in range(9)]
    poles = modes_of(pole_rows)
    skip = skip_ref[...]

    def feature(stream, now, back1, back2):
        return taps[3 * stream] * now + taps[3 * stream + 1] * back1 + taps[3 * stream + 2] * back2

    def gate(t, history):
        later, feats = [], []
        for stream, (back1, back2) in zip((1, 2), history):
            now = streams[stream, row(t), :]
            feats.append(feature(stream, now, back1, back2))
            later.append((now, back1))
        value = feats[0] * feats[1]
        gated[row(t), :] = value
        return value, tuple(later)

    def steps(begin, end, step, carried):
        def eight(block, carried):
            for t in range(8):
                carried = step(block * 8 + t, carried)
            return carried

        return lax.fori_loop(begin // 8, end // 8, eight, carried)

    def advance(states, value):
        return tuple(pole * state + value for pole, state in zip(poles, states))

    history = tuple((streams[s, SUBS : 2 * SUBS, :], streams[s, 0:SUBS, :]) for s in (1, 2))
    states = tuple(jnp.zeros((SUBS, LANES), F32) for _ in range(MODES))

    def scan_step(t, carried):
        states, history = carried
        value, history = gate(t, history)
        return advance(states, value), history

    scan = (states, history)
    for t in range(2, 8):
        scan = scan_step(t, scan)
    states, history = steps(8, ROWS, scan_step, scan)

    @pl.when(edge)
    def _():
        pl.semaphore_wait(barrier, peers + 1)

    @pl.when(jnp.logical_not(edge))
    def _():
        pl.semaphore_wait(barrier, peers)

    pl.when(has_next)(halo_copy.start)
    ring_first()

    for tile in range(SUBS):
        turned = residual_ref[:, tile * LANES : (tile + 1) * LANES].astype(F32).T.astype(BF16)
        to_rows = slice((tile // 2) * 64, (tile // 2) * 64 + 64)
        for odd in range(2):
            res_out[2 * (tile % 2) + odd, to_rows, :] = turned[64 * odd : 64 * odd + 64, :]

    def beside(block, dx=0):
        return device(z, lax.rem(y + (0, 3, 1, 2)[block], NY) * NH + h, x if dx == 0 else lax.rem(x + dx, NX))

    def res_copy(block):
        to = lax.rem(y + (0, 1, 3, 2)[block], NY)
        return remote(res_out.at[to], res_in.at[block - 1], res_s, res_r, device(z, to * NH + h, x))

    for block in range(1, 4):
        res_copy(block).start()
    convert(0, q_ref, 0, ROWS - 16)

    @pl.when(has_prev)
    def _():
        halo_copy.wait_recv()

    @pl.when(jnp.logical_not(has_prev))
    def _():
        halo[...] = jnp.zeros_like(halo)

    def halo_rows(s):
        return halo[s, SUBS : 2 * SUBS, :], halo[s, 0:SUBS, :]

    first, history = gate(0, (halo_rows(1), halo_rows(2)))
    second, history = gate(1, history)
    for m in range(MODES):
        at = slice(m * SUBS, (m + 1) * SUBS)
        late = jnp.exp(-(ROWS - 2.0) * rate_rows[at, :])
        ends[at, :] = inflow_rows[at, :] * (states[m] + late * (poles[m] * first + second))

    pair = 2 * SUBS

    def pair_rows(n):
        return pl.ds(pl.multiple_of(n * pair, pair), pair)

    def to_owner(d):
        to = lax.rem(j + d, NJ)
        return remote(ends.at[pair_rows(to), :], plane_in.at[j], s1_s, s1_r, device(z, to, x))

    def along_line(d):
        return remote(line_out, line_in.at[z], s2_s.at[d], s2_r.at[d], along(d, h))

    def from_owner(d):
        to = lax.rem(j + d, NJ)
        return remote(back_out.at[to], carry.at[pair_rows(j), :], s3_s, s3_r, device(z, to, x))

    for d in range(1, NJ):
        to_owner(d).start()

    plane_in[j] = ends[pair_rows(j), :]

    inres = modes_of(inres_rows)

    def output_step(t, carried):
        states, (back1, back2) = carried
        now = streams[0, row(t), :]
        featq[row(t), :] = feature(0, now, back1, back2)
        value = gated[row(t), :]
        states = advance(states, value)
        terms = [r * s for r, s in zip(inres, states)] + [skip * value]
        filt[row(t), :] = tree_sum(terms)
        return states, (now, back1)

    states = tuple(jnp.zeros((SUBS, LANES), F32) for _ in range(MODES))
    outputs = steps(0, 64, output_step, (states, halo_rows(0)))
    ring_next(1)

    others = plane_in.at[pl.ds(0, NJ - 1)]
    to_owner_all = remote(others, others, s1_s, s1_r, sibling)
    to_owner_all.wait_recv()

    my_rates = rate_rows[pair_rows(j), :]
    block_decay = jnp.exp(-float(ROWS) * my_rates)
    plane_decay = jnp.exp(-float(ROWS * NJ) * my_rates)
    total = plane_in[0]
    for i in range(1, NJ):
        total = block_decay * total + plane_in[i]
    line_out[...] = total

    @pl.loop(1, NZ - z)
    def _(d):
        along_line(d).start()

    late = jnp.logical_not(early)

    @pl.when(late)
    def _():
        ring_next(2)
        sib_give(1)

    steps(64, ROWS, output_step, outputs)
    pl.when(late)(ring_last)

    @pl.loop(1, z + 1)
    def _(d):
        along_line(d).wait_recv()

    incoming = lax.fori_loop(0, z, lambda i, s: plane_decay * s + line_in[i], prior_rows[pair_rows(j), :])
    for i in range(NJ):
        back_out[i] = incoming
        incoming = block_decay * incoming + plane_in[i]

    for d in range(1, NJ):
        from_owner(d).start()

    carry[pair_rows(j), :] = back_out[j]


    others = back_out.at[pl.ds(0, NJ - 1)]
    from_owner_all = remote(others, others, s3_s, s3_r, sibling)
    from_owner_all.wait_recv()

    half = ROWS // 2
    up = device(z, lax.rem(y + 1, NY) * NH + h, x)
    down = device(z, lax.rem(y + 3, NY) * NH + h, x)
    across = device(z, lax.rem(y + 2, NY) * NH + h, x)

    act_wait = (0, 2, 2, 1)

    def act_copy(part, side):
        cut = pl.ds(part * half, half)
        n = 2 * part + side
        return remote(acts.at[0, cut, :], acts.at[1 + side, cut, :], act_s, act_r.at[act_wait[n]], (up, down)[side])

    def fwd_copy(part):
        cut = pl.ds(part * half, half)
        return remote(acts.at[1 + part, cut, :], acts.at[3, cut, :], fwd_s, fwd_r, (up, down)[part])

    def carried_step(t, waves):
        waves = tuple(pole * wave for pole, wave in zip(poles, waves))
        filt[row(t), :] = featq[row(t), :] * (filt[row(t), :] + tree_sum(list(waves)))
        return waves

    waves = tuple(res_rows[m * SUBS : (m + 1) * SUBS, :] * carry[m * SUBS : (m + 1) * SUBS, :] for m in range(MODES))
    for part in range(2):
        waves = steps(part * half, (part + 1) * half, carried_step, waves)
        for sub in range(SUBS):
            from_rows = pl.ds(part * half * SUBS + sub, half, stride=SUBS)
            acts[0, part * half : (part + 1) * half, sub * LANES : (sub + 1) * LANES] = filt[from_rows, :].astype(BF16)
        act_copy(part, part).start()
    act_copy(1, 0).start()
    act_copy(0, 1).start()

    @pl.when(early)
    def _():
        ring_next(2)
        sib_give(1)
        ring_last()

    pl.when(has_next)(halo_copy.wait_send)
    to_owner_all.wait_send()
    from_owner_all.wait_send()

    @pl.loop(1, NZ - z)
    def _(d):
        along_line(d).wait_send()

    sib_give(2)
    sib_give(3)
    own_all = remote(weight_hbm, own_weights, sib_s.at[0], sib_r.at[0], sibling)
    own_all.wait_send()
    own_all.wait_recv()
    for sent in range(3):
        shards_all(4, sent, 0).wait_send()
    res_all = remote(res_in, res_in, res_s, res_r, sibling)
    res_all.wait_send()
    res_all.wait_recv()
    for part in range(2):
        act_copy(part, part).wait_recv()
        fwd_copy(part).start()
    shards_wait(6, 9)
    twelve = weights.at[pl.ds(0, 12 * 32), :]
    sib_all = remote(twelve, twelve, sib_s.at[1], sib_r.at[1], sibling)
    sib_all.wait_recv()

    right, left = device(z, j, lax.rem(x + 1, NX)), device(z, j, lax.rem(x + 3, NX))
    sides = (right, left)

    def project(pair):
        rows = acts[2 * pair : 2 * pair + 2].reshape(2 * ROWS, CHANS)
        parts[pair] = lax.dot_general(weights[...], rows, (((1,), (1,)), ((), ())), preferred_element_type=F32)

    def band(pair, dx):
        first = lax.rem(x + dx, NX) * 4 + NZ - z
        slots = [lax.rem(first + i, NZ) for i in range(4)]
        return [parts[pair, shard_rows(slot, core), :] for slot in slots for core in range(2)]

    def far_copy(pair, side):
        n = 2 * pair + side
        return remote(far_out.at[n], far_in.at[n], far_s.at[pair], far_r.at[pair], sides[side])

    def near_copy(pair, side):
        n = 2 * pair + side
        return remote(near_out.at[n], near_in.at[n], near_s.at[pair], near_r.at[pair], sides[side])

    def far_all(pair):
        both = far_in.at[pl.ds(2 * pair, 2)]
        return remote(both, both, far_s.at[pair], far_r.at[pair], right)

    def near_all(pair):
        both = near_in.at[pl.ds(2 * pair, 2)]
        return remote(both, both, near_s.at[pair], near_r.at[pair], right)

    def begin(pair):
        project(pair)
        chunks = band(pair, 2)
        for side in range(2):
            for i in range(4):
                far_out[2 * pair + side, 32 * i : 32 * i + 32, :] = chunks[4 * side + i].astype(BF16)
            far_copy(pair, side).start()

    def middle(pair):
        far_all(pair).wait_recv()
        for side in range(2):
            n = 2 * pair + side
            for i, chunk in enumerate(band(pair, (1, 3)[side])):
                if i // 4 == side:
                    chunk = chunk + far_in[n, 32 * (i % 4) : 32 * (i % 4) + 32, :].astype(F32)
                near_out[n, 32 * i : 32 * i + 32, :] = chunk.astype(BF16)
            near_copy(pair, side).start()

    def fin_copy(block):
        return remote(back_rows.at[block - 1], final_in.at[y], fin_s, fin_r, beside(block))

    def stat_copy(block, dx):
        n = 4 * block + dx
        return remote(stat_out.at[block], stat_in.at[n], stat_s, stat_r, beside(block, dx))

    def finish(pair):
        near_all(pair).wait_recv()
        value = jnp.concatenate(band(pair, 0), axis=0)
        for side in range(2):
            value = value + near_in[2 * pair + side].astype(F32)
        for block in (2 * pair + 1, 2 * pair):
            lanes = slice(block % 2 * ROWS, (block % 2 + 1) * ROWS)
            if block == 0:
                part = value[:, lanes] + res_out[y].astype(F32)
                final_in[y] = part.astype(BF16)
            else:
                part = value[:, lanes] + res_in[block - 1].astype(F32)
                back_rows[block - 1] = part.astype(BF16)
                fin_copy(block).start()
            squares = jnp.sum(part * part, axis=0, keepdims=True)
            stat_out[block] = jnp.broadcast_to(squares, (SUBS, LANES))
            if block == 0:
                stat_in[0] = stat_out[0]
            for dx in range(NX):
                if (block, dx) != (0, 0):
                    stat_copy(block, dx).start()

    late_halves = remote(acts.at[1], acts.at[1], act_s, act_r.at[2], up)
    late_halves.wait_recv()
    begin(0)
    fwd_all = remote(acts.at[3], acts.at[3], fwd_s, fwd_r, up)
    fwd_all.wait_recv()
    begin(1)
    middle(0)
    middle(1)
    finish(0)
    finish(1)
    fin_all = remote(back_rows, final_in.at[pl.ds(0, NY - 1)], fin_s, fin_r, up)
    fin_all.wait_recv()

    for tile in range(SUBS):
        cut = slice(tile * LANES, (tile + 1) * LANES)
        from_rows = slice((tile // 2) * 64, (tile // 2) * 64 + 64)
        mixed = [final_in[2 * (tile % 2) + odd, from_rows, :].astype(F32) for odd in range(2)]
        value = jnp.concatenate(mixed, axis=0).T
        summed[:, cut] = value
        hidden_ref[:, cut] = value.astype(BF16)
    fifteen = stat_in.at[pl.ds(1, 15)]
    stat_all = remote(fifteen, fifteen, stat_s, stat_r, up)
    stat_all.wait_recv()
    total = tree_sum([stat_in[n] for n in range(16)])
    scale = lax.rsqrt(total * (1.0 / (NX * CHANS)) + 1e-05)
    scale = jnp.broadcast_to(scale[0:1, :], (ROWS, LANES)).T
    for tile in range(SUBS):
        cut = slice(tile * LANES, (tile + 1) * LANES)
        normed_ref[:, cut] = (summed[:, cut] * scale * gain_ref[tile : tile + 1, :]).astype(BF16)

    sib_all.wait_send()
    shards_all(6, 3, 0).wait_send()
    remote(acts.at[pl.ds(0, 2)], acts.at[pl.ds(0, 2)], act_s, act_r.at[2], up).wait_send()
    fwd_all.wait_send()
    for pair in range(2):
        far_all(pair).wait_send()
        near_all(pair).wait_send()
    fin_all.wait_send()
    stat_all.wait_send()


def shard_rows(slot, h):
    return pl.ds(pl.multiple_of(h * (NZ * 32) + slot * 32, 32), 32)


def tree_sum(terms):
    while len(terms) > 1:
        rest = [terms[-1]] if len(terms) % 2 else []
        terms = [a + b for a, b in zip(terms[0::2], terms[1::2])] + rest
    return terms[0]


def local(
    q_stream, k_stream, v_stream, short_filter, rates, residues, skip, prior_state, out_weight, residual, norm_gain
):
    vmem = pl.BlockSpec(memory_space=pltpu.VMEM)
    hbm = pl.BlockSpec(memory_space=pltpu.HBM)
    dma = pltpu.SemaphoreType.DMA
    wide = (ROWS * SUBS, LANES)
    params = (MODES * SUBS, LANES)
    pair = (2 * SUBS, LANES)
    rows = (ROWS, CHANS)
    scratch = [
        pltpu.VMEM(rows, BF16),
        pltpu.VMEM(rows, BF16),
        pltpu.VMEM(rows, BF16),
        pltpu.VMEM(short_filter.shape, F32),
        pltpu.VMEM((MODES, CHANS), F32),
        pltpu.VMEM((MODES, CHANS), F32),
        pltpu.VMEM((SUBS, LANES), F32),
        pltpu.VMEM((MODES, CHANS), F32),
        pltpu.VMEM(rows, BF16),
        pltpu.VMEM((SUBS, LANES), F32),
        pltpu.VMEM((3,) + wide, F32),
        pltpu.VMEM((3, 2 * SUBS, LANES), F32),
        pltpu.VMEM(wide, F32),
        pltpu.VMEM(wide, F32),
        pltpu.VMEM(wide, F32),
        pltpu.VMEM((9 * SUBS, LANES), F32),
        pltpu.VMEM(params, F32),
        pltpu.VMEM(params, F32),
        pltpu.VMEM(params, F32),
        pltpu.VMEM(params, F32),
        pltpu.VMEM(params, F32),
        pltpu.VMEM(params, F32),
        pltpu.VMEM(params, F32),
        pltpu.VMEM((NJ,) + pair, F32),
        pltpu.VMEM((NZ,) + pair, F32),
        pltpu.VMEM(pair, F32),
        pltpu.VMEM((NJ,) + pair, F32),
        pltpu.VMEM(params, F32),
        pltpu.VMEM((CHANS, CHANS), BF16),
        pltpu.VMEM((NY, ROWS, CHANS), BF16),
        pltpu.VMEM((4, LANES, 2 * ROWS), BF16),
        pltpu.VMEM((4, LANES, 2 * ROWS), BF16),
        pltpu.VMEM((4, BAND, 2 * ROWS), BF16),
        pltpu.VMEM((4, BAND, 2 * ROWS), BF16),
        pltpu.VMEM((2, CHANS, 2 * ROWS), F32),
        pltpu.VMEM((NY - 1, BAND, ROWS), BF16),
        pltpu.VMEM((NY, BAND, ROWS), BF16),
        pltpu.VMEM((NY, BAND, ROWS), BF16),
        pltpu.VMEM((NY - 1, BAND, ROWS), BF16),
        pltpu.VMEM((ROWS, CHANS), F32),
        pltpu.VMEM((NY, SUBS, LANES), F32),
        pltpu.VMEM((16, SUBS, LANES), F32),
    ]
    sems = [dma((11,))]
    for sent, got in (
        (0, 0), (0, 0), (NZ, NZ), (0, 0), (4, 10), (2, 2), (0, 3), (0, 0), (2, 2), (2, 2), (0, 0), (0, 0), (0, 0)
    ):
        sems += [dma((n,)) if n else dma(()) for n in (sent, got)]
    return pl.pallas_call(
        kernel,
        out_shape=(jax.ShapeDtypeStruct((ROWS, CHANS), BF16), jax.ShapeDtypeStruct((ROWS, CHANS), BF16)),
        in_specs=[hbm] * 11,
        out_specs=(vmem, vmem),
        scratch_shapes=scratch + sems,
        compiler_params=pltpu.CompilerParams(
            collective_id=0, has_side_effects=True, vmem_limit_bytes=63 * 1024 * 1024
        ),
        name="mixer",
    )(
        q_stream, k_stream, v_stream, short_filter, rates, residues, skip.reshape(SUBS, LANES), prior_state,
        out_weight.T, residual, norm_gain.reshape(SUBS, LANES),
    )


def solution(mesh):
    placed = (
        P("seq", "ch"),
        P("seq", "ch"),
        P("seq", "ch"),
        P(None, None, "ch"),
        P(None, "ch"),
        P(None, "ch"),
        P("ch"),
        P(None, "ch"),
        P("ch", "seq"),
        P("seq", "ch"),
        P("ch"),
    )
    return jax.shard_map(
        local,
        mesh=mesh,
        in_specs=placed,
        out_specs=(P("seq", "ch"), P("seq", "ch")),
        check_vma=False,
    )
```

```python
import functools

import jax
import jax.numpy as jnp
from jax import lax
from jax.experimental import pallas as pl
from jax.experimental.pallas import tpu as pltpu
from jax.sharding import PartitionSpec as P

MESH = pl.DeviceIdType.MESH
F32 = jnp.float32
BF16 = jnp.bfloat16
NX, NY, NZ, NH = 4, 4, 16, 2
NJ = NY * NH
ROWS = 128
CHANS = 1024
LANES = 128
SUBS = 8
MODES = 16
BAND = CHANS // NX


def one_minus_exp(x):
    series = jnp.full_like(x, 1.0 / 8.0)
    for n in (7.0, 6.0, 5.0, 4.0, 3.0, 2.0):
        series = (1.0 - x * series) * (1.0 / n)
    return jnp.where(x < 0.25, x * (1.0 - x * series), 1.0 - jnp.exp(-x))


def kernel(
    q_hbm, k_hbm, v_hbm, taps_hbm, rates_hbm, residues_hbm, skip_hbm, prior_hbm, weight_hbm, residual_hbm, gain_hbm,
    hidden_ref, normed_ref,
    q_ref, k_ref, v_ref, taps_ref, rates_ref, residues_ref, skip_ref, prior_ref, residual_ref, gain_ref,
    streams, halo, gated, featq, filt, tap_rows, rate_rows, res_rows, prior_rows, pole_rows, inres_rows, inflow_rows,
    ends, plane_in, line_in, line_out, back_out, carry,
    weights, acts, far_out, far_in, near_out, near_in, parts, back_rows, final_in,
    res_out, res_in, summed, stat_out, stat_in,
    input_s, halo_s, halo_r, s1_s, s1_r, s2_s, s2_r, s3_s, s3_r, ring_s, ring_r, sib_s, sib_r,
    act_s, act_r, fwd_s, fwd_r, far_s, far_r, near_s, near_r,
    fin_s, fin_r, res_s, res_r, stat_s, stat_r,
):
    seq, x = lax.axis_index("seq"), lax.axis_index("ch")
    z, j = lax.div(seq, NJ), lax.rem(seq, NJ)
    y, h = lax.div(j, NH), lax.rem(j, NH)

    def device(z_, j_, x_):
        return (z_ * NJ + j_, x_)

    def remote(src, dst, send, recv, target):
        return pltpu.make_async_remote_copy(
            src_ref=src, dst_ref=dst, send_sem=send, recv_sem=recv, device_id=target, device_id_type=MESH
        )

    def row(t):
        return pl.ds(pl.multiple_of(t * SUBS, SUBS), SUBS)

    own_weights = weights.at[shard_rows(0, h), :]
    inputs = [
        pltpu.make_async_copy(src, dst, input_s.at[n])
        for n, (src, dst) in enumerate((
            (k_hbm, k_ref), (v_hbm, v_ref), (q_hbm, q_ref), (weight_hbm, own_weights), (rates_hbm, rates_ref),
            (taps_hbm, taps_ref), (residues_hbm, residues_ref), (prior_hbm, prior_ref), (skip_hbm, skip_ref),
            (residual_hbm, residual_ref), (gain_hbm, gain_ref),
        ))
    ]
    for copy in inputs[:4]:
        copy.start()

    barrier = pltpu.get_barrier_semaphore()

    def greet(target):
        pl.semaphore_signal(barrier, inc=1, device_id=target, device_id_type=MESH)

    sibling = device(z, y * NH + 1 - h, x)

    def along(hops, core):
        return device(lax.rem(z + hops + NZ, NZ), y * NH + core, x)

    for d in range(1, NZ):
        greet(along(d, h))
    for d in (1, -1, 2 - 4 * h):
        greet(along(d, 1 - h))
    for d in range(1, NJ):
        greet(device(z, lax.rem(j + d, NJ), x))
    for d in range(1, NX):
        for e in range(NY):
            greet(device(z, lax.rem(y + e, NY) * NH + h, lax.rem(x + d, NX)))

    has_next, has_prev = seq < NZ * NJ - 1, seq > 0
    first_j, last_j = j == 0, j == NJ - 1

    @pl.when(last_j)
    def _():
        greet(device(lax.rem(z + 1, NZ), 0, x))

    @pl.when(first_j)
    def _():
        greet(device(lax.rem(z + NZ - 1, NZ), NJ - 1, x))

    for copy in inputs[4:]:
        copy.start()

    def shard(slot):
        return weights.at[shard_rows(slot, h), :]

    def ring_copy(src, hops, slot, sent, got, core=None):
        to = along(hops, h if core is None else core)
        return remote(src, shard(slot), ring_s.at[sent], ring_r.at[got], to)

    def ring_first():
        for d in (2, 1):
            ring_copy(weight_hbm, d, NZ - d, 0, 0 if d == 2 else 2).start()
            ring_copy(weight_hbm, -d, d, 0, 1 if d == 2 else 2).start()
        remote(weight_hbm, own_weights, sib_s.at[0], sib_r.at[0], sibling).start()

    def shards_all(count, sent, got):
        some = weights.at[pl.ds(0, count * 32), :]
        return remote(some, some, ring_s.at[sent], ring_r.at[got], sibling)

    def shards_wait(count, got):
        shards_all(count, 0, got).wait_recv()

    def ring_next(step):
        far, got = 2 * step, 3 * step
        shards_wait(1, got - 3)
        for d in (2, 1):
            ring_copy(shard(NZ - far), d, NZ - far - d, step, got if d == 2 else got + 2).start()
        shards_wait(1, got - 2)
        for d in (2, 1):
            ring_copy(shard(far), -d, far + d, step, got + 1 if d == 2 else got + 2).start()

    def ring_last():
        shards_wait(1, 6)
        shards_wait(1, 7)
        for core in (h, 1 - h):
            ring_copy(shard(NZ - 6 - 4 * h), 2 - 4 * h, 8, 3, 9, core).start()
        for core in (h, 1 - h):
            ring_copy(shard(NZ - 6), 1, NZ - 7, 3, 9, core).start()
            ring_copy(shard(6), -1, 7, 3, 9, core).start()

    def sib_copy(slot):
        two = weights.at[pl.ds(pl.multiple_of(h * (NZ * 32) + slot * 32, 32), 2 * 32), :]
        return remote(two, two, sib_s.at[1], sib_r.at[1], sibling)

    def sib_give(step):
        shards_wait(2, 3 * step - 1)
        sib_copy(NZ - 2 * step).start()
        sib_copy(2 * step - 1).start()

    peers = NJ - 1 + (NX - 1) * NY + NZ - 1 + 3
    edge = jnp.logical_or(first_j, last_j)
    early = z < 7

    def convert(stream, ref, begin, end):
        for part in range(SUBS):
            to = pl.ds(begin * SUBS + part, end - begin, stride=SUBS)
            streams[stream, to, :] = ref[begin:end, part * LANES : (part + 1) * LANES].astype(F32)

    for n in range(3):
        inputs[n].wait()
    for stream, ref in enumerate((q_ref, k_ref, v_ref)):
        convert(stream, ref, ROWS - 16, ROWS)
    last = (ROWS - 2) * SUBS
    halo_copy = remote(
        streams.at[:, pl.ds(last, 2 * SUBS), :], halo, halo_s, halo_r, (lax.rem(seq + 1, NZ * NJ), x)
    )
    convert(1, k_ref, 0, ROWS - 16)
    convert(2, v_ref, 0, ROWS - 16)
    for n in range(3, len(inputs)):
        inputs[n].wait()

    for part in range(SUBS):
        cut = slice(part * LANES, (part + 1) * LANES)
        to = pl.ds(part, MODES, stride=SUBS)
        rate_rows[to, :] = rates_ref[:, cut]
        res_rows[to, :] = residues_ref[:, cut]
        prior_rows[to, :] = prior_ref[:, cut]
        for stream in range(3):
            for tap in range(3):
                n = (3 * stream + tap) * SUBS + part
                tap_rows[n : n + 1, :] = taps_ref[stream, tap : tap + 1, cut]
    rates = rate_rows[...]
    inflow = jnp.sqrt(one_minus_exp(2.0 * rates))
    pole_rows[...] = jnp.exp(-rates)
    inflow_rows[...] = inflow
    inres_rows[...] = res_rows[...] * inflow

    def modes_of(ref):
        return [ref[m * SUBS : (m + 1) * SUBS, :] for m in range(MODES)]

    taps = [tap_rows[n * SUBS : (n + 1) * SUBS, :] for n in range(9)]
    poles = modes_of(pole_rows)
    skip = skip_ref[...]

    def feature(stream, now, back1, back2):
        return taps[3 * stream] * now + taps[3 * stream + 1] * back1 + taps[3 * stream + 2] * back2

    def gate(t, history):
        later, feats = [], []
        for stream, (back1, back2) in zip((1, 2), history):
            now = streams[stream, row(t), :]
            feats.append(feature(stream, now, back1, back2))
            later.append((now, back1))
        value = feats[0] * feats[1]
        gated[row(t), :] = value
        return value, tuple(later)

    def steps(begin, end, step, carried):
        def eight(block, carried):
            for t in range(8):
                carried = step(block * 8 + t, carried)
            return carried

        return lax.fori_loop(begin // 8, end // 8, eight, carried)

    def advance(states, value):
        return tuple(pole * state + value for pole, state in zip(poles, states))

    history = tuple((streams[s, SUBS : 2 * SUBS, :], streams[s, 0:SUBS, :]) for s in (1, 2))
    states = tuple(jnp.zeros((SUBS, LANES), F32) for _ in range(MODES))

    def scan_step(t, carried):
        states, history = carried
        value, history = gate(t, history)
        return advance(states, value), history

    scan = (states, history)
    for t in range(2, 8):
        scan = scan_step(t, scan)
    states, history = steps(8, ROWS, scan_step, scan)

    @pl.when(edge)
    def _():
        pl.semaphore_wait(barrier, peers + 1)

    @pl.when(jnp.logical_not(edge))
    def _():
        pl.semaphore_wait(barrier, peers)

    pl.when(has_next)(halo_copy.start)
    ring_first()

    for tile in range(SUBS):
        turned = residual_ref[:, tile * LANES : (tile + 1) * LANES].astype(F32).T.astype(BF16)
        to_rows = slice((tile // 2) * 64, (tile // 2) * 64 + 64)
        for odd in range(2):
            res_out[2 * (tile % 2) + odd, to_rows, :] = turned[64 * odd : 64 * odd + 64, :]

    def beside(block, dx=0):
        return device(z, lax.rem(y + (0, 3, 1, 2)[block], NY) * NH + h, x if dx == 0 else lax.rem(x + dx, NX))

    def res_copy(block):
        to = lax.rem(y + (0, 1, 3, 2)[block], NY)
        return remote(res_out.at[to], res_in.at[block - 1], res_s, res_r, device(z, to * NH + h, x))

    for block in range(1, 4):
        res_copy(block).start()
    convert(0, q_ref, 0, ROWS - 16)

    @pl.when(has_prev)
    def _():
        halo_copy.wait_recv()

    @pl.when(jnp.logical_not(has_prev))
    def _():
        halo[...] = jnp.zeros_like(halo)

    def halo_rows(s):
        return halo[s, SUBS : 2 * SUBS, :], halo[s, 0:SUBS, :]

    first, history = gate(0, (halo_rows(1), halo_rows(2)))
    second, history = gate(1, history)
    for m in range(MODES):
        at = slice(m * SUBS, (m + 1) * SUBS)
        late = jnp.exp(-(ROWS - 2.0) * rate_rows[at, :])
        ends[at, :] = inflow_rows[at, :] * (states[m] + late * (poles[m] * first + second))

    pair = 2 * SUBS

    def pair_rows(n):
        return pl.ds(pl.multiple_of(n * pair, pair), pair)

    def to_owner(d):
        to = lax.rem(j + d, NJ)
        return remote(ends.at[pair_rows(to), :], plane_in.at[j], s1_s, s1_r, device(z, to, x))

    def along_line(d):
        return remote(line_out, line_in.at[z], s2_s.at[d], s2_r.at[d], along(d, h))

    def from_owner(d):
        to = lax.rem(j + d, NJ)
        return remote(back_out.at[to], carry.at[pair_rows(j), :], s3_s, s3_r, device(z, to, x))

    for d in range(1, NJ):
        to_owner(d).start()

    plane_in[j] = ends[pair_rows(j), :]

    inres = modes_of(inres_rows)

    def output_step(t, carried):
        states, (back1, back2) = carried
        now = streams[0, row(t), :]
        featq[row(t), :] = feature(0, now, back1, back2)
        value = gated[row(t), :]
        states = advance(states, value)
        terms = [r * s for r, s in zip(inres, states)] + [skip * value]
        filt[row(t), :] = tree_sum(terms)
        return states, (now, back1)

    states = tuple(jnp.zeros((SUBS, LANES), F32) for _ in range(MODES))
    outputs = steps(0, 64, output_step, (states, halo_rows(0)))
    ring_next(1)

    others = plane_in.at[pl.ds(0, NJ - 1)]
    to_owner_all = remote(others, others, s1_s, s1_r, sibling)
    to_owner_all.wait_recv()

    my_rates = rate_rows[pair_rows(j), :]
    block_decay = jnp.exp(-float(ROWS) * my_rates)
    plane_decay = jnp.exp(-float(ROWS * NJ) * my_rates)
    total = plane_in[0]
    for i in range(1, NJ):
        total = block_decay * total + plane_in[i]
    line_out[...] = total

    @pl.loop(1, NZ - z)
    def _(d):
        along_line(d).start()

    late = jnp.logical_not(early)

    @pl.when(late)
    def _():
        ring_next(2)
        sib_give(1)

    steps(64, ROWS, output_step, outputs)

    @pl.loop(1, z + 1)
    def _(d):
        along_line(d).wait_recv()

    incoming = lax.fori_loop(0, z, lambda i, s: plane_decay * s + line_in[i], prior_rows[pair_rows(j), :])
    for i in range(NJ):
        back_out[i] = incoming
        incoming = block_decay * incoming + plane_in[i]

    for d in range(1, NJ):
        from_owner(d).start()

    carry[pair_rows(j), :] = back_out[j]


    others = back_out.at[pl.ds(0, NJ - 1)]
    from_owner_all = remote(others, others, s3_s, s3_r, sibling)
    from_owner_all.wait_recv()

    half = ROWS // 2
    up = device(z, lax.rem(y + 1, NY) * NH + h, x)
    down = device(z, lax.rem(y + 3, NY) * NH + h, x)
    across = device(z, lax.rem(y + 2, NY) * NH + h, x)

    act_wait = (0, 2, 2, 1)

    def act_copy(part, side):
        cut = pl.ds(part * half, half)
        n = 2 * part + side
        return remote(acts.at[0, cut, :], acts.at[1 + side, cut, :], act_s, act_r.at[act_wait[n]], (up, down)[side])

    def fwd_copy(part):
        cut = pl.ds(part * half, half)
        return remote(acts.at[1 + part, cut, :], acts.at[3, cut, :], fwd_s, fwd_r, (up, down)[part])

    def carried_step(t, waves):
        waves = tuple(pole * wave for pole, wave in zip(poles, waves))
        filt[row(t), :] = featq[row(t), :] * (filt[row(t), :] + tree_sum(list(waves)))
        return waves

    waves = tuple(res_rows[m * SUBS : (m + 1) * SUBS, :] * carry[m * SUBS : (m + 1) * SUBS, :] for m in range(MODES))
    for part in range(2):
        waves = steps(part * half, (part + 1) * half, carried_step, waves)
        for sub in range(SUBS):
            from_rows = pl.ds(part * half * SUBS + sub, half, stride=SUBS)
            acts[0, part * half : (part + 1) * half, sub * LANES : (sub + 1) * LANES] = filt[from_rows, :].astype(BF16)
        act_copy(part, part).start()
    act_copy(1, 0).start()
    act_copy(0, 1).start()

    @pl.when(early)
    def _():
        ring_next(2)
        sib_give(1)

    ring_last()

    pl.when(has_next)(halo_copy.wait_send)
    to_owner_all.wait_send()
    from_owner_all.wait_send()

    @pl.loop(1, NZ - z)
    def _(d):
        along_line(d).wait_send()

    sib_give(2)
    sib_give(3)
    own_all = remote(weight_hbm, own_weights, sib_s.at[0], sib_r.at[0], sibling)
    own_all.wait_send()
    own_all.wait_recv()
    for sent in range(3):
        shards_all(4, sent, 0).wait_send()
    res_all = remote(res_in, res_in, res_s, res_r, sibling)
    res_all.wait_send()
    res_all.wait_recv()
    for part in range(2):
        act_copy(part, part).wait_recv()
        fwd_copy(part).start()
    shards_wait(6, 9)
    twelve = weights.at[pl.ds(0, 12 * 32), :]
    sib_all = remote(twelve, twelve, sib_s.at[1], sib_r.at[1], sibling)
    sib_all.wait_recv()

    right, left = device(z, j, lax.rem(x + 1, NX)), device(z, j, lax.rem(x + 3, NX))
    sides = (right, left)

    def project(pair):
        rows = acts[2 * pair : 2 * pair + 2].reshape(2 * ROWS, CHANS)
        parts[pair] = lax.dot_general(weights[...], rows, (((1,), (1,)), ((), ())), preferred_element_type=F32)

    def band(pair, dx):
        first = lax.rem(x + dx, NX) * 4 + NZ - z
        slots = [lax.rem(first + i, NZ) for i in range(4)]
        return [parts[pair, shard_rows(slot, core), :] for slot in slots for core in range(2)]

    def far_copy(pair, side):
        n = 2 * pair + side
        return remote(far_out.at[n], far_in.at[n], far_s.at[pair], far_r.at[pair], sides[side])

    def near_copy(pair, side):
        n = 2 * pair + side
        return remote(near_out.at[n], near_in.at[n], near_s.at[pair], near_r.at[pair], sides[side])

    def far_all(pair):
        both = far_in.at[pl.ds(2 * pair, 2)]
        return remote(both, both, far_s.at[pair], far_r.at[pair], right)

    def near_all(pair):
        both = near_in.at[pl.ds(2 * pair, 2)]
        return remote(both, both, near_s.at[pair], near_r.at[pair], right)

    def begin(pair):
        project(pair)
        chunks = band(pair, 2)
        for side in range(2):
            for i in range(4):
                far_out[2 * pair + side, 32 * i : 32 * i + 32, :] = chunks[4 * side + i].astype(BF16)
            far_copy(pair, side).start()

    def middle(pair):
        far_all(pair).wait_recv()
        for side in range(2):
            n = 2 * pair + side
            for i, chunk in enumerate(band(pair, (1, 3)[side])):
                if i // 4 == side:
                    chunk = chunk + far_in[n, 32 * (i % 4) : 32 * (i % 4) + 32, :].astype(F32)
                near_out[n, 32 * i : 32 * i + 32, :] = chunk.astype(BF16)
            near_copy(pair, side).start()

    def fin_copy(block):
        return remote(back_rows.at[block - 1], final_in.at[y], fin_s, fin_r, beside(block))

    def stat_copy(block, dx):
        n = 4 * block + dx
        return remote(stat_out.at[block], stat_in.at[n], stat_s, stat_r, beside(block, dx))

    def finish(pair):
        near_all(pair).wait_recv()
        value = jnp.concatenate(band(pair, 0), axis=0)
        for side in range(2):
            value = value + near_in[2 * pair + side].astype(F32)
        for block in (2 * pair + 1, 2 * pair):
            lanes = slice(block % 2 * ROWS, (block % 2 + 1) * ROWS)
            if block == 0:
                part = value[:, lanes] + res_out[y].astype(F32)
                final_in[y] = part.astype(BF16)
            else:
                part = value[:, lanes] + res_in[block - 1].astype(F32)
                back_rows[block - 1] = part.astype(BF16)
                fin_copy(block).start()
            squares = jnp.sum(part * part, axis=0, keepdims=True)
            stat_out[block] = jnp.broadcast_to(squares, (SUBS, LANES))
            if block == 0:
                stat_in[0] = stat_out[0]
            for dx in range(NX):
                if (block, dx) != (0, 0):
                    stat_copy(block, dx).start()

    late_halves = remote(acts.at[1], acts.at[1], act_s, act_r.at[2], up)
    late_halves.wait_recv()
    begin(0)
    fwd_all = remote(acts.at[3], acts.at[3], fwd_s, fwd_r, up)
    fwd_all.wait_recv()
    begin(1)
    middle(0)
    middle(1)
    finish(0)
    finish(1)
    fin_all = remote(back_rows, final_in.at[pl.ds(0, NY - 1)], fin_s, fin_r, up)
    fin_all.wait_recv()

    for tile in range(SUBS):
        cut = slice(tile * LANES, (tile + 1) * LANES)
        from_rows = slice((tile // 2) * 64, (tile // 2) * 64 + 64)
        mixed = [final_in[2 * (tile % 2) + odd, from_rows, :].astype(F32) for odd in range(2)]
        value = jnp.concatenate(mixed, axis=0).T
        summed[:, cut] = value
        hidden_ref[:, cut] = value.astype(BF16)
    fifteen = stat_in.at[pl.ds(1, 15)]
    stat_all = remote(fifteen, fifteen, stat_s, stat_r, up)
    stat_all.wait_recv()
    total = tree_sum([stat_in[n] for n in range(16)])
    scale = lax.rsqrt(total * (1.0 / (NX * CHANS)) + 1e-05)
    scale = jnp.broadcast_to(scale[0:1, :], (ROWS, LANES)).T
    for tile in range(SUBS):
        cut = slice(tile * LANES, (tile + 1) * LANES)
        normed_ref[:, cut] = (summed[:, cut] * scale * gain_ref[tile : tile + 1, :]).astype(BF16)

    sib_all.wait_send()
    shards_all(6, 3, 0).wait_send()
    remote(acts.at[pl.ds(0, 2)], acts.at[pl.ds(0, 2)], act_s, act_r.at[2], up).wait_send()
    fwd_all.wait_send()
    for pair in range(2):
        far_all(pair).wait_send()
        near_all(pair).wait_send()
    fin_all.wait_send()
    stat_all.wait_send()


def shard_rows(slot, h):
    return pl.ds(pl.multiple_of(h * (NZ * 32) + slot * 32, 32), 32)


def tree_sum(terms):
    while len(terms) > 1:
        rest = [terms[-1]] if len(terms) % 2 else []
        terms = [a + b for a, b in zip(terms[0::2], terms[1::2])] + rest
    return terms[0]


def local(
    q_stream, k_stream, v_stream, short_filter, rates, residues, skip, prior_state, out_weight, residual, norm_gain
):
    vmem = pl.BlockSpec(memory_space=pltpu.VMEM)
    hbm = pl.BlockSpec(memory_space=pltpu.HBM)
    dma = pltpu.SemaphoreType.DMA
    wide = (ROWS * SUBS, LANES)
    params = (MODES * SUBS, LANES)
    pair = (2 * SUBS, LANES)
    rows = (ROWS, CHANS)
    scratch = [
        pltpu.VMEM(rows, BF16),
        pltpu.VMEM(rows, BF16),
        pltpu.VMEM(rows, BF16),
        pltpu.VMEM(short_filter.shape, F32),
        pltpu.VMEM((MODES, CHANS), F32),
        pltpu.VMEM((MODES, CHANS), F32),
        pltpu.VMEM((SUBS, LANES), F32),
        pltpu.VMEM((MODES, CHANS), F32),
        pltpu.VMEM(rows, BF16),
        pltpu.VMEM((SUBS, LANES), F32),
        pltpu.VMEM((3,) + wide, F32),
        pltpu.VMEM((3, 2 * SUBS, LANES), F32),
        pltpu.VMEM(wide, F32),
        pltpu.VMEM(wide, F32),
        pltpu.VMEM(wide, F32),
        pltpu.VMEM((9 * SUBS, LANES), F32),
        pltpu.VMEM(params, F32),
        pltpu.VMEM(params, F32),
        pltpu.VMEM(params, F32),
        pltpu.VMEM(params, F32),
        pltpu.VMEM(params, F32),
        pltpu.VMEM(params, F32),
        pltpu.VMEM(params, F32),
        pltpu.VMEM((NJ,) + pair, F32),
        pltpu.VMEM((NZ,) + pair, F32),
        pltpu.VMEM(pair, F32),
        pltpu.VMEM((NJ,) + pair, F32),
        pltpu.VMEM(params, F32),
        pltpu.VMEM((CHANS, CHANS), BF16),
        pltpu.VMEM((NY, ROWS, CHANS), BF16),
        pltpu.VMEM((4, LANES, 2 * ROWS), BF16),
        pltpu.VMEM((4, LANES, 2 * ROWS), BF16),
        pltpu.VMEM((4, BAND, 2 * ROWS), BF16),
        pltpu.VMEM((4, BAND, 2 * ROWS), BF16),
        pltpu.VMEM((2, CHANS, 2 * ROWS), F32),
        pltpu.VMEM((NY - 1, BAND, ROWS), BF16),
        pltpu.VMEM((NY, BAND, ROWS), BF16),
        pltpu.VMEM((NY, BAND, ROWS), BF16),
        pltpu.VMEM((NY - 1, BAND, ROWS), BF16),
        pltpu.VMEM((ROWS, CHANS), F32),
        pltpu.VMEM((NY, SUBS, LANES), F32),
        pltpu.VMEM((16, SUBS, LANES), F32),
    ]
    sems = [dma((11,))]
    for sent, got in (
        (0, 0), (0, 0), (NZ, NZ), (0, 0), (4, 10), (2, 2), (0, 3), (0, 0), (2, 2), (2, 2), (0, 0), (0, 0), (0, 0)
    ):
        sems += [dma((n,)) if n else dma(()) for n in (sent, got)]
    return pl.pallas_call(
        kernel,
        out_shape=(jax.ShapeDtypeStruct((ROWS, CHANS), BF16), jax.ShapeDtypeStruct((ROWS, CHANS), BF16)),
        in_specs=[hbm] * 11,
        out_specs=(vmem, vmem),
        scratch_shapes=scratch + sems,
        compiler_params=pltpu.CompilerParams(
            collective_id=0, has_side_effects=True, vmem_limit_bytes=63 * 1024 * 1024
        ),
        name="mixer",
    )(
        q_stream, k_stream, v_stream, short_filter, rates, residues, skip.reshape(SUBS, LANES), prior_state,
        out_weight.T, residual, norm_gain.reshape(SUBS, LANES),
    )


def solution(mesh):
    placed = (
        P("seq", "ch"),
        P("seq", "ch"),
        P("seq", "ch"),
        P(None, None, "ch"),
        P(None, "ch"),
        P(None, "ch"),
        P("ch"),
        P(None, "ch"),
        P("ch", "seq"),
        P("seq", "ch"),
        P("ch"),
    )
    return jax.shard_map(
        local,
        mesh=mesh,
        in_specs=placed,
        out_specs=(P("seq", "ch"), P("seq", "ch")),
        check_vma=False,
    )
```

```python
import functools

import jax
import jax.numpy as jnp
from jax import lax
from jax.experimental import pallas as pl
from jax.experimental.pallas import tpu as pltpu
from jax.sharding import PartitionSpec as P

MESH = pl.DeviceIdType.MESH
F32 = jnp.float32
BF16 = jnp.bfloat16
NX, NY, NZ, NH = 4, 4, 16, 2
NJ = NY * NH
ROWS = 128
CHANS = 1024
LANES = 128
SUBS = 8
MODES = 16
BAND = CHANS // NX


def one_minus_exp(x):
    series = jnp.full_like(x, 1.0 / 8.0)
    for n in (7.0, 6.0, 5.0, 4.0, 3.0, 2.0):
        series = (1.0 - x * series) * (1.0 / n)
    return jnp.where(x < 0.25, x * (1.0 - x * series), 1.0 - jnp.exp(-x))


def kernel(
    q_hbm, k_hbm, v_hbm, taps_hbm, rates_hbm, residues_hbm, skip_hbm, prior_hbm, weight_hbm, residual_hbm, gain_hbm,
    hidden_ref, normed_ref,
    q_ref, k_ref, v_ref, taps_ref, rates_ref, residues_ref, skip_ref, prior_ref, residual_ref, gain_ref,
    streams, halo, gated, featq, filt, tap_rows, rate_rows, res_rows, prior_rows, pole_rows, inres_rows, inflow_rows,
    ends, plane_in, line_in, line_out, back_out, carry,
    weights, acts, far_out, far_in, near_out, near_in, parts, back_rows, final_in,
    res_out, res_in, summed, stat_out, stat_in,
    input_s, halo_s, halo_r, s1_s, s1_r, s2_s, s2_r, s3_s, s3_r, ring_s, ring_r, sib_s, sib_r,
    act_s, act_r, fwd_s, fwd_r, far_s, far_r, near_s, near_r,
    fin_s, fin_r, res_s, res_r, stat_s, stat_r,
):
    seq, x = lax.axis_index("seq"), lax.axis_index("ch")
    z, j = lax.div(seq, NJ), lax.rem(seq, NJ)
    y, h = lax.div(j, NH), lax.rem(j, NH)

    def device(z_, j_, x_):
        return (z_ * NJ + j_, x_)

    def remote(src, dst, send, recv, target):
        return pltpu.make_async_remote_copy(
            src_ref=src, dst_ref=dst, send_sem=send, recv_sem=recv, device_id=target, device_id_type=MESH
        )

    def row(t):
        return pl.ds(pl.multiple_of(t * SUBS, SUBS), SUBS)

    own_weights = weights.at[shard_rows(0, h), :]
    inputs = [
        pltpu.make_async_copy(src, dst, input_s.at[n])
        for n, (src, dst) in enumerate((
            (k_hbm, k_ref), (v_hbm, v_ref), (q_hbm, q_ref), (weight_hbm, own_weights), (rates_hbm, rates_ref),
            (taps_hbm, taps_ref), (residues_hbm, residues_ref), (prior_hbm, prior_ref), (skip_hbm, skip_ref),
            (residual_hbm, residual_ref), (gain_hbm, gain_ref),
        ))
    ]
    for copy in inputs[:4]:
        copy.start()

    barrier = pltpu.get_barrier_semaphore()

    def greet(target):
        pl.semaphore_signal(barrier, inc=1, device_id=target, device_id_type=MESH)

    sibling = device(z, y * NH + 1 - h, x)

    def along(hops, core):
        return device(lax.rem(z + hops + NZ, NZ), y * NH + core, x)

    for d in range(1, NZ):
        greet(along(d, h))
    for d in (1, -1, 2 - 4 * h):
        greet(along(d, 1 - h))
    for d in range(1, NJ):
        greet(device(z, lax.rem(j + d, NJ), x))
    for d in range(1, NX):
        for e in range(NY):
            greet(device(z, lax.rem(y + e, NY) * NH + h, lax.rem(x + d, NX)))

    has_next, has_prev = seq < NZ * NJ - 1, seq > 0
    first_j, last_j = j == 0, j == NJ - 1

    @pl.when(last_j)
    def _():
        greet(device(lax.rem(z + 1, NZ), 0, x))

    @pl.when(first_j)
    def _():
        greet(device(lax.rem(z + NZ - 1, NZ), NJ - 1, x))

    for copy in inputs[4:]:
        copy.start()

    def shard(slot):
        return weights.at[shard_rows(slot, h), :]

    def ring_copy(src, hops, slot, sent, got, core=None):
        to = along(hops, h if core is None else core)
        return remote(src, shard(slot), ring_s.at[sent], ring_r.at[got], to)

    def ring_first():
        for d in (2, 1):
            ring_copy(weight_hbm, d, NZ - d, 0, 0 if d == 2 else 2).start()
            ring_copy(weight_hbm, -d, d, 0, 1 if d == 2 else 2).start()
        remote(weight_hbm, own_weights, sib_s.at[0], sib_r.at[0], sibling).start()

    def shards_all(count, sent, got):
        some = weights.at[pl.ds(0, count * 32), :]
        return remote(some, some, ring_s.at[sent], ring_r.at[got], sibling)

    def shards_wait(count, got):
        shards_all(count, 0, got).wait_recv()

    def ring_next(step):
        far, got = 2 * step, 3 * step
        shards_wait(1, got - 3)
        for d in (2, 1):
            ring_copy(shard(NZ - far), d, NZ - far - d, step, got if d == 2 else got + 2).start()
        shards_wait(1, got - 2)
        for d in (2, 1):
            ring_copy(shard(far), -d, far + d, step, got + 1 if d == 2 else got + 2).start()

    def ring_last():
        shards_wait(1, 6)
        shards_wait(1, 7)
        for core in (h, 1 - h):
            ring_copy(shard(NZ - 6 - 4 * h), 2 - 4 * h, 8, 3, 9, core).start()
        for core in (h, 1 - h):
            ring_copy(shard(NZ - 6), 1, NZ - 7, 3, 9, core).start()
            ring_copy(shard(6), -1, 7, 3, 9, core).start()

    def sib_copy(slot):
        two = weights.at[pl.ds(pl.multiple_of(h * (NZ * 32) + slot * 32, 32), 2 * 32), :]
        return remote(two, two, sib_s.at[1], sib_r.at[1], sibling)

    def sib_give(step):
        shards_wait(2, 3 * step - 1)
        sib_copy(NZ - 2 * step).start()
        sib_copy(2 * step - 1).start()

    peers = NJ - 1 + (NX - 1) * NY + NZ - 1 + 3
    edge = jnp.logical_or(first_j, last_j)
    early = z < 7

    def convert(stream, ref, begin, end):
        for part in range(SUBS):
            to = pl.ds(begin * SUBS + part, end - begin, stride=SUBS)
            streams[stream, to, :] = ref[begin:end, part * LANES : (part + 1) * LANES].astype(F32)

    for n in range(3):
        inputs[n].wait()
    for stream, ref in enumerate((q_ref, k_ref, v_ref)):
        convert(stream, ref, ROWS - 16, ROWS)
    last = (ROWS - 2) * SUBS
    halo_copy = remote(
        streams.at[:, pl.ds(last, 2 * SUBS), :], halo, halo_s, halo_r, (lax.rem(seq + 1, NZ * NJ), x)
    )
    convert(1, k_ref, 0, ROWS - 16)
    convert(2, v_ref, 0, ROWS - 16)
    for n in range(3, len(inputs)):
        inputs[n].wait()

    for part in range(SUBS):
        cut = slice(part * LANES, (part + 1) * LANES)
        to = pl.ds(part, MODES, stride=SUBS)
        rate_rows[to, :] = rates_ref[:, cut]
        res_rows[to, :] = residues_ref[:, cut]
        prior_rows[to, :] = prior_ref[:, cut]
        for stream in range(3):
            for tap in range(3):
                n = (3 * stream + tap) * SUBS + part
                tap_rows[n : n + 1, :] = taps_ref[stream, tap : tap + 1, cut]
    rates = rate_rows[...]
    inflow = jnp.sqrt(one_minus_exp(2.0 * rates))
    pole_rows[...] = jnp.exp(-rates)
    inflow_rows[...] = inflow
    inres_rows[...] = res_rows[...] * inflow

    def modes_of(ref):
        return [ref[m * SUBS : (m + 1) * SUBS, :] for m in range(MODES)]

    taps = [tap_rows[n * SUBS : (n + 1) * SUBS, :] for n in range(9)]
    poles = modes_of(pole_rows)
    skip = skip_ref[...]

    def feature(stream, now, back1, back2):
        return taps[3 * stream] * now + taps[3 * stream + 1] * back1 + taps[3 * stream + 2] * back2

    def gate(t, history):
        later, feats = [], []
        for stream, (back1, back2) in zip((1, 2), history):
            now = streams[stream, row(t), :]
            feats.append(feature(stream, now, back1, back2))
            later.append((now, back1))
        value = feats[0] * feats[1]
        gated[row(t), :] = value
        return value, tuple(later)

    def steps(begin, end, step, carried):
        def eight(block, carried):
            for t in range(8):
                carried = step(block * 8 + t, carried)
            return carried

        return lax.fori_loop(begin // 8, end // 8, eight, carried)

    def advance(states, value):
        return tuple(pole * state + value for pole, state in zip(poles, states))

    history = tuple((streams[s, SUBS : 2 * SUBS, :], streams[s, 0:SUBS, :]) for s in (1, 2))
    states = tuple(jnp.zeros((SUBS, LANES), F32) for _ in range(MODES))

    def scan_step(t, carried):
        states, history = carried
        value, history = gate(t, history)
        return advance(states, value), history

    scan = (states, history)
    for t in range(2, 8):
        scan = scan_step(t, scan)
    states, history = steps(8, ROWS, scan_step, scan)

    @pl.when(edge)
    def _():
        pl.semaphore_wait(barrier, peers + 1)

    @pl.when(jnp.logical_not(edge))
    def _():
        pl.semaphore_wait(barrier, peers)

    pl.when(has_next)(halo_copy.start)
    ring_first()

    for tile in range(SUBS):
        turned = residual_ref[:, tile * LANES : (tile + 1) * LANES].astype(F32).T.astype(BF16)
        to_rows = slice((tile // 2) * 64, (tile // 2) * 64 + 64)
        for odd in range(2):
            res_out[2 * (tile % 2) + odd, to_rows, :] = turned[64 * odd : 64 * odd + 64, :]

    def beside(block, dx=0):
        return device(z, lax.rem(y + (0, 3, 1, 2)[block], NY) * NH + h, x if dx == 0 else lax.rem(x + dx, NX))

    def res_copy(block):
        to = lax.rem(y + (0, 1, 3, 2)[block], NY)
        return remote(res_out.at[to], res_in.at[block - 1], res_s, res_r, device(z, to * NH + h, x))

    for block in range(1, 4):
        res_copy(block).start()
    convert(0, q_ref, 0, ROWS - 16)

    @pl.when(has_prev)
    def _():
        halo_copy.wait_recv()

    @pl.when(jnp.logical_not(has_prev))
    def _():
        halo[...] = jnp.zeros_like(halo)

    def halo_rows(s):
        return halo[s, SUBS : 2 * SUBS, :], halo[s, 0:SUBS, :]

    first, history = gate(0, (halo_rows(1), halo_rows(2)))
    second, history = gate(1, history)
    for m in range(MODES):
        at = slice(m * SUBS, (m + 1) * SUBS)
        late = jnp.exp(-(ROWS - 2.0) * rate_rows[at, :])
        ends[at, :] = inflow_rows[at, :] * (states[m] + late * (poles[m] * first + second))

    pair = 2 * SUBS

    def pair_rows(n):
        return pl.ds(pl.multiple_of(n * pair, pair), pair)

    def to_owner(d):
        to = lax.rem(j + d, NJ)
        return remote(ends.at[pair_rows(to), :], plane_in.at[j], s1_s, s1_r, device(z, to, x))

    def along_line(d):
        return remote(line_out, line_in.at[z], s2_s.at[d], s2_r.at[d], along(d, h))

    def from_owner(d):
        to = lax.rem(j + d, NJ)
        return remote(back_out.at[to], carry.at[pair_rows(j), :], s3_s, s3_r, device(z, to, x))

    for d in range(1, NJ):
        to_owner(d).start()

    plane_in[j] = ends[pair_rows(j), :]

    inres = modes_of(inres_rows)

    def output_step(t, carried):
        states, (back1, back2) = carried
        now = streams[0, row(t), :]
        featq[row(t), :] = feature(0, now, back1, back2)
        value = gated[row(t), :]
        states = advance(states, value)
        terms = [r * s for r, s in zip(inres, states)] + [skip * value]
        filt[row(t), :] = tree_sum(terms)
        return states, (now, back1)

    states = tuple(jnp.zeros((SUBS, LANES), F32) for _ in range(MODES))
    outputs = steps(0, 64, output_step, (states, halo_rows(0)))
    ring_next(1)

    others = plane_in.at[pl.ds(0, NJ - 1)]
    to_owner_all = remote(others, others, s1_s, s1_r, sibling)
    to_owner_all.wait_recv()

    my_rates = rate_rows[pair_rows(j), :]
    block_decay = jnp.exp(-float(ROWS) * my_rates)
    plane_decay = jnp.exp(-float(ROWS * NJ) * my_rates)
    total = plane_in[0]
    for i in range(1, NJ):
        total = block_decay * total + plane_in[i]
    line_out[...] = total

    @pl.loop(1, NZ - z)
    def _(d):
        along_line(d).start()

    late = jnp.logical_not(early)

    @pl.when(late)
    def _():
        ring_next(2)
        sib_give(1)

    steps(64, ROWS, output_step, outputs)
    highest = z >= 12
    pl.when(highest)(ring_last)

    @pl.loop(1, z + 1)
    def _(d):
        along_line(d).wait_recv()

    incoming = lax.fori_loop(0, z, lambda i, s: plane_decay * s + line_in[i], prior_rows[pair_rows(j), :])
    for i in range(NJ):
        back_out[i] = incoming
        incoming = block_decay * incoming + plane_in[i]

    for d in range(1, NJ):
        from_owner(d).start()

    carry[pair_rows(j), :] = back_out[j]


    others = back_out.at[pl.ds(0, NJ - 1)]
    from_owner_all = remote(others, others, s3_s, s3_r, sibling)
    from_owner_all.wait_recv()

    half = ROWS // 2
    up = device(z, lax.rem(y + 1, NY) * NH + h, x)
    down = device(z, lax.rem(y + 3, NY) * NH + h, x)
    across = device(z, lax.rem(y + 2, NY) * NH + h, x)

    act_wait = (0, 2, 2, 1)

    def act_copy(part, side):
        cut = pl.ds(part * half, half)
        n = 2 * part + side
        return remote(acts.at[0, cut, :], acts.at[1 + side, cut, :], act_s, act_r.at[act_wait[n]], (up, down)[side])

    def fwd_copy(part):
        cut = pl.ds(part * half, half)
        return remote(acts.at[1 + part, cut, :], acts.at[3, cut, :], fwd_s, fwd_r, (up, down)[part])

    def carried_step(t, waves):
        waves = tuple(pole * wave for pole, wave in zip(poles, waves))
        filt[row(t), :] = featq[row(t), :] * (filt[row(t), :] + tree_sum(list(waves)))
        return waves

    waves = tuple(res_rows[m * SUBS : (m + 1) * SUBS, :] * carry[m * SUBS : (m + 1) * SUBS, :] for m in range(MODES))
    for part in range(2):
        waves = steps(part * half, (part + 1) * half, carried_step, waves)
        for sub in range(SUBS):
            from_rows = pl.ds(part * half * SUBS + sub, half, stride=SUBS)
            acts[0, part * half : (part + 1) * half, sub * LANES : (sub + 1) * LANES] = filt[from_rows, :].astype(BF16)
        act_copy(part, part).start()
    act_copy(1, 0).start()
    act_copy(0, 1).start()

    @pl.when(early)
    def _():
        ring_next(2)
        sib_give(1)

    pl.when(jnp.logical_not(highest))(ring_last)

    pl.when(has_next)(halo_copy.wait_send)
    to_owner_all.wait_send()
    from_owner_all.wait_send()

    @pl.loop(1, NZ - z)
    def _(d):
        along_line(d).wait_send()

    sib_give(2)
    sib_give(3)
    own_all = remote(weight_hbm, own_weights, sib_s.at[0], sib_r.at[0], sibling)
    own_all.wait_send()
    own_all.wait_recv()
    for sent in range(3):
        shards_all(4, sent, 0).wait_send()
    res_all = remote(res_in, res_in, res_s, res_r, sibling)
    res_all.wait_send()
    res_all.wait_recv()
    for part in range(2):
        act_copy(part, part).wait_recv()
        fwd_copy(part).start()
    shards_wait(6, 9)
    twelve = weights.at[pl.ds(0, 12 * 32), :]
    sib_all = remote(twelve, twelve, sib_s.at[1], sib_r.at[1], sibling)
    sib_all.wait_recv()

    right, left = device(z, j, lax.rem(x + 1, NX)), device(z, j, lax.rem(x + 3, NX))
    sides = (right, left)

    def project(pair):
        rows = acts[2 * pair : 2 * pair + 2].reshape(2 * ROWS, CHANS)
        parts[pair] = lax.dot_general(weights[...], rows, (((1,), (1,)), ((), ())), preferred_element_type=F32)

    def band(pair, dx):
        first = lax.rem(x + dx, NX) * 4 + NZ - z
        slots = [lax.rem(first + i, NZ) for i in range(4)]
        return [parts[pair, shard_rows(slot, core), :] for slot in slots for core in range(2)]

    def far_copy(pair, side):
        n = 2 * pair + side
        return remote(far_out.at[n], far_in.at[n], far_s.at[pair], far_r.at[pair], sides[side])

    def near_copy(pair, side):
        n = 2 * pair + side
        return remote(near_out.at[n], near_in.at[n], near_s.at[pair], near_r.at[pair], sides[side])

    def far_all(pair):
        both = far_in.at[pl.ds(2 * pair, 2)]
        return remote(both, both, far_s.at[pair], far_r.at[pair], right)

    def near_all(pair):
        both = near_in.at[pl.ds(2 * pair, 2)]
        return remote(both, both, near_s.at[pair], near_r.at[pair], right)

    def begin(pair):
        project(pair)
        chunks = band(pair, 2)
        for side in range(2):
            for i in range(4):
                far_out[2 * pair + side, 32 * i : 32 * i + 32, :] = chunks[4 * side + i].astype(BF16)
            far_copy(pair, side).start()

    def middle(pair):
        far_all(pair).wait_recv()
        for side in range(2):
            n = 2 * pair + side
            for i, chunk in enumerate(band(pair, (1, 3)[side])):
                if i // 4 == side:
                    chunk = chunk + far_in[n, 32 * (i % 4) : 32 * (i % 4) + 32, :].astype(F32)
                near_out[n, 32 * i : 32 * i + 32, :] = chunk.astype(BF16)
            near_copy(pair, side).start()

    def fin_copy(block):
        return remote(back_rows.at[block - 1], final_in.at[y], fin_s, fin_r, beside(block))

    def stat_copy(block, dx):
        n = 4 * block + dx
        return remote(stat_out.at[block], stat_in.at[n], stat_s, stat_r, beside(block, dx))

    def finish(pair):
        near_all(pair).wait_recv()
        value = jnp.concatenate(band(pair, 0), axis=0)
        for side in range(2):
            value = value + near_in[2 * pair + side].astype(F32)
        for block in (2 * pair + 1, 2 * pair):
            lanes = slice(block % 2 * ROWS, (block % 2 + 1) * ROWS)
            if block == 0:
                part = value[:, lanes] + res_out[y].astype(F32)
                final_in[y] = part.astype(BF16)
            else:
                part = value[:, lanes] + res_in[block - 1].astype(F32)
                back_rows[block - 1] = part.astype(BF16)
                fin_copy(block).start()
            squares = jnp.sum(part * part, axis=0, keepdims=True)
            stat_out[block] = jnp.broadcast_to(squares, (SUBS, LANES))
            if block == 0:
                stat_in[0] = stat_out[0]
            for dx in range(NX):
                if (block, dx) != (0, 0):
                    stat_copy(block, dx).start()

    late_halves = remote(acts.at[1], acts.at[1], act_s, act_r.at[2], up)
    late_halves.wait_recv()
    begin(0)
    fwd_all = remote(acts.at[3], acts.at[3], fwd_s, fwd_r, up)
    fwd_all.wait_recv()
    begin(1)
    middle(0)
    middle(1)
    finish(0)
    finish(1)
    fin_all = remote(back_rows, final_in.at[pl.ds(0, NY - 1)], fin_s, fin_r, up)
    fin_all.wait_recv()

    for tile in range(SUBS):
        cut = slice(tile * LANES, (tile + 1) * LANES)
        from_rows = slice((tile // 2) * 64, (tile // 2) * 64 + 64)
        mixed = [final_in[2 * (tile % 2) + odd, from_rows, :].astype(F32) for odd in range(2)]
        value = jnp.concatenate(mixed, axis=0).T
        summed[:, cut] = value
        hidden_ref[:, cut] = value.astype(BF16)
    fifteen = stat_in.at[pl.ds(1, 15)]
    stat_all = remote(fifteen, fifteen, stat_s, stat_r, up)
    stat_all.wait_recv()
    total = tree_sum([stat_in[n] for n in range(16)])
    scale = lax.rsqrt(total * (1.0 / (NX * CHANS)) + 1e-05)
    scale = jnp.broadcast_to(scale[0:1, :], (ROWS, LANES)).T
    for tile in range(SUBS):
        cut = slice(tile * LANES, (tile + 1) * LANES)
        normed_ref[:, cut] = (summed[:, cut] * scale * gain_ref[tile : tile + 1, :]).astype(BF16)

    sib_all.wait_send()
    shards_all(6, 3, 0).wait_send()
    remote(acts.at[pl.ds(0, 2)], acts.at[pl.ds(0, 2)], act_s, act_r.at[2], up).wait_send()
    fwd_all.wait_send()
    for pair in range(2):
        far_all(pair).wait_send()
        near_all(pair).wait_send()
    fin_all.wait_send()
    stat_all.wait_send()


def shard_rows(slot, h):
    return pl.ds(pl.multiple_of(h * (NZ * 32) + slot * 32, 32), 32)


def tree_sum(terms):
    while len(terms) > 1:
        rest = [terms[-1]] if len(terms) % 2 else []
        terms = [a + b for a, b in zip(terms[0::2], terms[1::2])] + rest
    return terms[0]


def local(
    q_stream, k_stream, v_stream, short_filter, rates, residues, skip, prior_state, out_weight, residual, norm_gain
):
    vmem = pl.BlockSpec(memory_space=pltpu.VMEM)
    hbm = pl.BlockSpec(memory_space=pltpu.HBM)
    dma = pltpu.SemaphoreType.DMA
    wide = (ROWS * SUBS, LANES)
    params = (MODES * SUBS, LANES)
    pair = (2 * SUBS, LANES)
    rows = (ROWS, CHANS)
    scratch = [
        pltpu.VMEM(rows, BF16),
        pltpu.VMEM(rows, BF16),
        pltpu.VMEM(rows, BF16),
        pltpu.VMEM(short_filter.shape, F32),
        pltpu.VMEM((MODES, CHANS), F32),
        pltpu.VMEM((MODES, CHANS), F32),
        pltpu.VMEM((SUBS, LANES), F32),
        pltpu.VMEM((MODES, CHANS), F32),
        pltpu.VMEM(rows, BF16),
        pltpu.VMEM((SUBS, LANES), F32),
        pltpu.VMEM((3,) + wide, F32),
        pltpu.VMEM((3, 2 * SUBS, LANES), F32),
        pltpu.VMEM(wide, F32),
        pltpu.VMEM(wide, F32),
        pltpu.VMEM(wide, F32),
        pltpu.VMEM((9 * SUBS, LANES), F32),
        pltpu.VMEM(params, F32),
        pltpu.VMEM(params, F32),
        pltpu.VMEM(params, F32),
        pltpu.VMEM(params, F32),
        pltpu.VMEM(params, F32),
        pltpu.VMEM(params, F32),
        pltpu.VMEM(params, F32),
        pltpu.VMEM((NJ,) + pair, F32),
        pltpu.VMEM((NZ,) + pair, F32),
        pltpu.VMEM(pair, F32),
        pltpu.VMEM((NJ,) + pair, F32),
        pltpu.VMEM(params, F32),
        pltpu.VMEM((CHANS, CHANS), BF16),
        pltpu.VMEM((NY, ROWS, CHANS), BF16),
        pltpu.VMEM((4, LANES, 2 * ROWS), BF16),
        pltpu.VMEM((4, LANES, 2 * ROWS), BF16),
        pltpu.VMEM((4, BAND, 2 * ROWS), BF16),
        pltpu.VMEM((4, BAND, 2 * ROWS), BF16),
        pltpu.VMEM((2, CHANS, 2 * ROWS), F32),
        pltpu.VMEM((NY - 1, BAND, ROWS), BF16),
        pltpu.VMEM((NY, BAND, ROWS), BF16),
        pltpu.VMEM((NY, BAND, ROWS), BF16),
        pltpu.VMEM((NY - 1, BAND, ROWS), BF16),
        pltpu.VMEM((ROWS, CHANS), F32),
        pltpu.VMEM((NY, SUBS, LANES), F32),
        pltpu.VMEM((16, SUBS, LANES), F32),
    ]
    sems = [dma((11,))]
    for sent, got in (
        (0, 0), (0, 0), (NZ, NZ), (0, 0), (4, 10), (2, 2), (0, 3), (0, 0), (2, 2), (2, 2), (0, 0), (0, 0), (0, 0)
    ):
        sems += [dma((n,)) if n else dma(()) for n in (sent, got)]
    return pl.pallas_call(
        kernel,
        out_shape=(jax.ShapeDtypeStruct((ROWS, CHANS), BF16), jax.ShapeDtypeStruct((ROWS, CHANS), BF16)),
        in_specs=[hbm] * 11,
        out_specs=(vmem, vmem),
        scratch_shapes=scratch + sems,
        compiler_params=pltpu.CompilerParams(
            collective_id=0, has_side_effects=True, vmem_limit_bytes=63 * 1024 * 1024
        ),
        name="mixer",
    )(
        q_stream, k_stream, v_stream, short_filter, rates, residues, skip.reshape(SUBS, LANES), prior_state,
        out_weight.T, residual, norm_gain.reshape(SUBS, LANES),
    )


def solution(mesh):
    placed = (
        P("seq", "ch"),
        P("seq", "ch"),
        P("seq", "ch"),
        P(None, None, "ch"),
        P(None, "ch"),
        P(None, "ch"),
        P("ch"),
        P(None, "ch"),
        P("ch", "seq"),
        P("seq", "ch"),
        P("ch"),
    )
    return jax.shard_map(
        local,
        mesh=mesh,
        in_specs=placed,
        out_specs=(P("seq", "ch"), P("seq", "ch")),
        check_vma=False,
    )
```

```python
import functools

import jax
import jax.numpy as jnp
from jax import lax
from jax.experimental import pallas as pl
from jax.experimental.pallas import tpu as pltpu
from jax.sharding import PartitionSpec as P

MESH = pl.DeviceIdType.MESH
F32 = jnp.float32
BF16 = jnp.bfloat16
NX, NY, NZ, NH = 4, 4, 16, 2
NJ = NY * NH
ROWS = 128
CHANS = 1024
LANES = 128
SUBS = 8
MODES = 16
BAND = CHANS // NX


def one_minus_exp(x):
    series = jnp.full_like(x, 1.0 / 8.0)
    for n in (7.0, 6.0, 5.0, 4.0, 3.0, 2.0):
        series = (1.0 - x * series) * (1.0 / n)
    return jnp.where(x < 0.25, x * (1.0 - x * series), 1.0 - jnp.exp(-x))


def kernel(
    q_hbm, k_hbm, v_hbm, taps_hbm, rates_hbm, residues_hbm, skip_hbm, prior_hbm, weight_hbm, residual_hbm, gain_hbm,
    hidden_ref, normed_ref,
    q_ref, k_ref, v_ref, taps_ref, rates_ref, residues_ref, skip_ref, prior_ref, residual_ref, gain_ref,
    streams, halo, gated, featq, filt, tap_rows, rate_rows, res_rows, prior_rows, pole_rows, inres_rows, inflow_rows,
    ends, plane_in, line_in, line_out, back_out, carry,
    weights, acts, far_out, far_in, near_out, near_in, parts, back_rows, final_in,
    res_out, res_in, summed, stat_out, stat_in,
    input_s, halo_s, halo_r, s1_s, s1_r, s2_s, s2_r, s3_s, s3_r, ring_s, ring_r, sib_s, sib_r,
    act_s, act_r, fwd_s, fwd_r, far_s, far_r, near_s, near_r,
    fin_s, fin_r, res_s, res_r, stat_s, stat_r,
):
    seq, x = lax.axis_index("seq"), lax.axis_index("ch")
    z, j = lax.div(seq, NJ), lax.rem(seq, NJ)
    y, h = lax.div(j, NH), lax.rem(j, NH)

    def device(z_, j_, x_):
        return (z_ * NJ + j_, x_)

    def remote(src, dst, send, recv, target):
        return pltpu.make_async_remote_copy(
            src_ref=src, dst_ref=dst, send_sem=send, recv_sem=recv, device_id=target, device_id_type=MESH
        )

    def row(t):
        return pl.ds(pl.multiple_of(t * SUBS, SUBS), SUBS)

    own_weights = weights.at[shard_rows(0, h), :]
    inputs = [
        pltpu.make_async_copy(src, dst, input_s.at[n])
        for n, (src, dst) in enumerate((
            (k_hbm, k_ref), (v_hbm, v_ref), (q_hbm, q_ref), (weight_hbm, own_weights), (rates_hbm, rates_ref),
            (taps_hbm, taps_ref), (residues_hbm, residues_ref), (prior_hbm, prior_ref), (skip_hbm, skip_ref),
            (residual_hbm, residual_ref), (gain_hbm, gain_ref),
        ))
    ]
    for copy in inputs[:4]:
        copy.start()

    barrier = pltpu.get_barrier_semaphore()

    def greet(target):
        pl.semaphore_signal(barrier, inc=1, device_id=target, device_id_type=MESH)

    sibling = device(z, y * NH + 1 - h, x)

    def along(hops, core):
        return device(lax.rem(z + hops + NZ, NZ), y * NH + core, x)

    for d in range(1, NZ):
        greet(along(d, h))
    for d in (1, -1, 2 - 4 * h):
        greet(along(d, 1 - h))
    for d in range(1, NJ):
        greet(device(z, lax.rem(j + d, NJ), x))
    for d in range(1, NX):
        for e in range(NY):
            greet(device(z, lax.rem(y + e, NY) * NH + h, lax.rem(x + d, NX)))

    has_next, has_prev = seq < NZ * NJ - 1, seq > 0
    first_j, last_j = j == 0, j == NJ - 1

    @pl.when(last_j)
    def _():
        greet(device(lax.rem(z + 1, NZ), 0, x))

    @pl.when(first_j)
    def _():
        greet(device(lax.rem(z + NZ - 1, NZ), NJ - 1, x))

    for copy in inputs[4:]:
        copy.start()

    def shard(slot):
        return weights.at[shard_rows(slot, h), :]

    def ring_copy(src, hops, slot, sent, got, core=None):
        to = along(hops, h if core is None else core)
        return remote(src, shard(slot), ring_s.at[sent], ring_r.at[got], to)

    def ring_first():
        for d in (2, 1):
            ring_copy(weight_hbm, d, NZ - d, 0, 0 if d == 2 else 2).start()
            ring_copy(weight_hbm, -d, d, 0, 1 if d == 2 else 2).start()
        remote(weight_hbm, own_weights, sib_s.at[0], sib_r.at[0], sibling).start()

    def shards_all(count, sent, got):
        some = weights.at[pl.ds(0, count * 32), :]
        return remote(some, some, ring_s.at[sent], ring_r.at[got], sibling)

    def shards_wait(count, got):
        shards_all(count, 0, got).wait_recv()

    def ring_next(step):
        far, got = 2 * step, 3 * step
        shards_wait(1, got - 3)
        for d in (2, 1):
            ring_copy(shard(NZ - far), d, NZ - far - d, step, got if d == 2 else got + 2).start()
        shards_wait(1, got - 2)
        for d in (2, 1):
            ring_copy(shard(far), -d, far + d, step, got + 1 if d == 2 else got + 2).start()

    def ring_last():
        shards_wait(1, 6)
        shards_wait(1, 7)
        for core in (h, 1 - h):
            ring_copy(shard(NZ - 6 - 4 * h), 2 - 4 * h, 8, 3, 9, core).start()
        for core in (h, 1 - h):
            ring_copy(shard(NZ - 6), 1, NZ - 7, 3, 9, core).start()
            ring_copy(shard(6), -1, 7, 3, 9, core).start()

    def sib_copy(slot):
        two = weights.at[pl.ds(pl.multiple_of(h * (NZ * 32) + slot * 32, 32), 2 * 32), :]
        return remote(two, two, sib_s.at[1], sib_r.at[1], sibling)

    def sib_give(step):
        shards_wait(2, 3 * step - 1)
        sib_copy(NZ - 2 * step).start()
        sib_copy(2 * step - 1).start()

    peers = NJ - 1 + (NX - 1) * NY + NZ - 1 + 3
    edge = jnp.logical_or(first_j, last_j)
    early = z < 7

    def convert(stream, ref, begin, end):
        for part in range(SUBS):
            to = pl.ds(begin * SUBS + part, end - begin, stride=SUBS)
            streams[stream, to, :] = ref[begin:end, part * LANES : (part + 1) * LANES].astype(F32)

    for n in range(3):
        inputs[n].wait()
    for stream, ref in enumerate((q_ref, k_ref, v_ref)):
        convert(stream, ref, ROWS - 16, ROWS)
    last = (ROWS - 2) * SUBS
    halo_copy = remote(
        streams.at[:, pl.ds(last, 2 * SUBS), :], halo, halo_s, halo_r, (lax.rem(seq + 1, NZ * NJ), x)
    )
    convert(1, k_ref, 0, ROWS - 16)
    convert(2, v_ref, 0, ROWS - 16)
    for n in range(3, len(inputs)):
        inputs[n].wait()

    for part in range(SUBS):
        cut = slice(part * LANES, (part + 1) * LANES)
        to = pl.ds(part, MODES, stride=SUBS)
        rate_rows[to, :] = rates_ref[:, cut]
        res_rows[to, :] = residues_ref[:, cut]
        prior_rows[to, :] = prior_ref[:, cut]
        for stream in range(3):
            for tap in range(3):
                n = (3 * stream + tap) * SUBS + part
                tap_rows[n : n + 1, :] = taps_ref[stream, tap : tap + 1, cut]
    rates = rate_rows[...]
    inflow = jnp.sqrt(one_minus_exp(2.0 * rates))
    pole_rows[...] = jnp.exp(-rates)
    inflow_rows[...] = inflow
    inres_rows[...] = res_rows[...] * inflow

    def modes_of(ref):
        return [ref[m * SUBS : (m + 1) * SUBS, :] for m in range(MODES)]

    taps = [tap_rows[n * SUBS : (n + 1) * SUBS, :] for n in range(9)]
    poles = modes_of(pole_rows)
    skip = skip_ref[...]

    def feature(stream, now, back1, back2):
        return taps[3 * stream] * now + taps[3 * stream + 1] * back1 + taps[3 * stream + 2] * back2

    def gate(t, history):
        later, feats = [], []
        for stream, (back1, back2) in zip((1, 2), history):
            now = streams[stream, row(t), :]
            feats.append(feature(stream, now, back1, back2))
            later.append((now, back1))
        value = feats[0] * feats[1]
        gated[row(t), :] = value
        return value, tuple(later)

    def steps(begin, end, step, carried):
        def eight(block, carried):
            for t in range(8):
                carried = step(block * 8 + t, carried)
            return carried

        return lax.fori_loop(begin // 8, end // 8, eight, carried)

    def advance(states, value):
        return tuple(pole * state + value for pole, state in zip(poles, states))

    history = tuple((streams[s, SUBS : 2 * SUBS, :], streams[s, 0:SUBS, :]) for s in (1, 2))
    states = tuple(jnp.zeros((SUBS, LANES), F32) for _ in range(MODES))

    def scan_step(t, carried):
        states, history = carried
        value, history = gate(t, history)
        return advance(states, value), history

    scan = (states, history)
    for t in range(2, 8):
        scan = scan_step(t, scan)
    states, history = steps(8, ROWS, scan_step, scan)

    @pl.when(edge)
    def _():
        pl.semaphore_wait(barrier, peers + 1)

    @pl.when(jnp.logical_not(edge))
    def _():
        pl.semaphore_wait(barrier, peers)

    pl.when(has_next)(halo_copy.start)
    ring_first()

    for tile in range(SUBS):
        turned = residual_ref[:, tile * LANES : (tile + 1) * LANES].astype(F32).T.astype(BF16)
        to_rows = slice((tile // 2) * 64, (tile // 2) * 64 + 64)
        for odd in range(2):
            res_out[2 * (tile % 2) + odd, to_rows, :] = turned[64 * odd : 64 * odd + 64, :]

    def beside(block, dx=0):
        return device(z, lax.rem(y + (0, 3, 1, 2)[block], NY) * NH + h, x if dx == 0 else lax.rem(x + dx, NX))

    def res_copy(block):
        to = lax.rem(y + (0, 1, 3, 2)[block], NY)
        return remote(res_out.at[to], res_in.at[block - 1], res_s, res_r, device(z, to * NH + h, x))

    for block in range(1, 4):
        res_copy(block).start()
    convert(0, q_ref, 0, ROWS - 16)

    @pl.when(has_prev)
    def _():
        halo_copy.wait_recv()

    @pl.when(jnp.logical_not(has_prev))
    def _():
        halo[...] = jnp.zeros_like(halo)

    def halo_rows(s):
        return halo[s, SUBS : 2 * SUBS, :], halo[s, 0:SUBS, :]

    first, history = gate(0, (halo_rows(1), halo_rows(2)))
    second, history = gate(1, history)
    for m in range(MODES):
        at = slice(m * SUBS, (m + 1) * SUBS)
        late = jnp.exp(-(ROWS - 2.0) * rate_rows[at, :])
        ends[at, :] = inflow_rows[at, :] * (states[m] + late * (poles[m] * first + second))

    pair = 2 * SUBS

    def pair_rows(n):
        return pl.ds(pl.multiple_of(n * pair, pair), pair)

    def to_owner(d):
        to = lax.rem(j + d, NJ)
        return remote(ends.at[pair_rows(to), :], plane_in.at[j], s1_s, s1_r, device(z, to, x))

    def along_line(d):
        return remote(line_out, line_in.at[z], s2_s.at[d], s2_r.at[d], along(d, h))

    def from_owner(d):
        to = lax.rem(j + d, NJ)
        return remote(back_out.at[to], carry.at[pair_rows(j), :], s3_s, s3_r, device(z, to, x))

    for d in range(1, NJ):
        to_owner(d).start()

    plane_in[j] = ends[pair_rows(j), :]

    inres = modes_of(inres_rows)

    def output_step(t, carried):
        states, (back1, back2) = carried
        now = streams[0, row(t), :]
        featq[row(t), :] = feature(0, now, back1, back2)
        value = gated[row(t), :]
        states = advance(states, value)
        terms = [r * s for r, s in zip(inres, states)] + [skip * value]
        filt[row(t), :] = tree_sum(terms)
        return states, (now, back1)

    states = tuple(jnp.zeros((SUBS, LANES), F32) for _ in range(MODES))
    outputs = steps(0, 64, output_step, (states, halo_rows(0)))
    ring_next(1)

    others = plane_in.at[pl.ds(0, NJ - 1)]
    to_owner_all = remote(others, others, s1_s, s1_r, sibling)
    to_owner_all.wait_recv()

    my_rates = rate_rows[pair_rows(j), :]
    block_decay = jnp.exp(-float(ROWS) * my_rates)
    plane_decay = jnp.exp(-float(ROWS * NJ) * my_rates)
    total = plane_in[0]
    for i in range(1, NJ):
        total = block_decay * total + plane_in[i]
    line_out[...] = total

    @pl.loop(1, NZ - z)
    def _(d):
        along_line(d).start()

    late = jnp.logical_not(early)

    @pl.when(late)
    def _():
        ring_next(2)
        sib_give(1)

    steps(64, ROWS, output_step, outputs)
    highest = z >= 12
    pl.when(highest)(ring_last)

    @pl.loop(1, z + 1)
    def _(d):
        along_line(d).wait_recv()

    incoming = lax.fori_loop(0, z, lambda i, s: plane_decay * s + line_in[i], prior_rows[pair_rows(j), :])
    for i in range(NJ):
        back_out[i] = incoming
        incoming = block_decay * incoming + plane_in[i]

    for d in range(1, NJ):
        from_owner(d).start()

    carry[pair_rows(j), :] = back_out[j]


    others = back_out.at[pl.ds(0, NJ - 1)]
    from_owner_all = remote(others, others, s3_s, s3_r, sibling)
    from_owner_all.wait_recv()

    half = ROWS // 2
    up = device(z, lax.rem(y + 1, NY) * NH + h, x)
    down = device(z, lax.rem(y + 3, NY) * NH + h, x)
    across = device(z, lax.rem(y + 2, NY) * NH + h, x)

    act_wait = (0, 2, 2, 1)

    def act_copy(part, side):
        cut = pl.ds(part * half, half)
        n = 2 * part + side
        return remote(acts.at[0, cut, :], acts.at[1 + side, cut, :], act_s, act_r.at[act_wait[n]], (up, down)[side])

    def fwd_copy(part):
        cut = pl.ds(part * half, half)
        return remote(acts.at[1 + part, cut, :], acts.at[3, cut, :], fwd_s, fwd_r, (up, down)[part])

    def carried_step(t, waves):
        waves = tuple(pole * wave for pole, wave in zip(poles, waves))
        filt[row(t), :] = featq[row(t), :] * (filt[row(t), :] + tree_sum(list(waves)))
        return waves

    waves = tuple(res_rows[m * SUBS : (m + 1) * SUBS, :] * carry[m * SUBS : (m + 1) * SUBS, :] for m in range(MODES))
    for part in range(2):
        waves = steps(part * half, (part + 1) * half, carried_step, waves)
        for sub in range(SUBS):
            from_rows = pl.ds(part * half * SUBS + sub, half, stride=SUBS)
            acts[0, part * half : (part + 1) * half, sub * LANES : (sub + 1) * LANES] = filt[from_rows, :].astype(BF16)
        act_copy(part, part).start()
    act_copy(1, 0).start()
    act_copy(0, 1).start()

    @pl.when(early)
    def _():
        ring_next(2)
        sib_give(1)

    pl.when(jnp.logical_not(highest))(ring_last)

    pl.when(has_next)(halo_copy.wait_send)
    to_owner_all.wait_send()
    from_owner_all.wait_send()

    @pl.loop(1, NZ - z)
    def _(d):
        along_line(d).wait_send()

    sib_give(2)
    sib_give(3)
    own_all = remote(weight_hbm, own_weights, sib_s.at[0], sib_r.at[0], sibling)
    own_all.wait_send()
    own_all.wait_recv()
    for sent in range(3):
        shards_all(4, sent, 0).wait_send()
    res_all = remote(res_in, res_in, res_s, res_r, sibling)
    res_all.wait_send()
    res_all.wait_recv()
    for part in range(2):
        act_copy(part, part).wait_recv()
        fwd_copy(part).start()
    twelve = weights.at[pl.ds(0, 12 * 32), :]
    sib_all = remote(twelve, twelve, sib_s.at[1], sib_r.at[1], sibling)
    sib_all.wait_recv()

    right, left = device(z, j, lax.rem(x + 1, NX)), device(z, j, lax.rem(x + 3, NX))
    sides = (right, left)

    def project(rows, weight):
        return lax.dot_general(weight, rows, (((1,), (1,)), ((), ())), preferred_element_type=F32)

    last_slots = [(core * NZ * 32 + 7 * 32, 3 * 32) for core in range(2)]
    other_slots = ((0, 224), (320, 416), (832, 192))

    def project_others(pair):
        rows = acts[2 * pair : 2 * pair + 2].reshape(2 * ROWS, CHANS)
        for at, count in other_slots:
            parts[pair, at : at + count, :] = project(rows, weights[at : at + count, :])

    def project_last():
        rows = acts[...].reshape(NY * ROWS, CHANS)
        some = jnp.concatenate([weights[at : at + count, :] for at, count in last_slots], axis=0)
        value = project(rows, some)
        for pair in range(2):
            for n, (at, count) in enumerate(last_slots):
                parts[pair, at : at + count, :] = value[n * count : (n + 1) * count, 2 * pair * ROWS : 2 * (pair + 1) * ROWS]

    def band(pair, dx):
        first = lax.rem(x + dx, NX) * 4 + NZ - z
        slots = [lax.rem(first + i, NZ) for i in range(4)]
        return [parts[pair, shard_rows(slot, core), :] for slot in slots for core in range(2)]

    def far_copy(pair, side):
        n = 2 * pair + side
        return remote(far_out.at[n], far_in.at[n], far_s.at[pair], far_r.at[pair], sides[side])

    def near_copy(pair, side):
        n = 2 * pair + side
        return remote(near_out.at[n], near_in.at[n], near_s.at[pair], near_r.at[pair], sides[side])

    def far_all(pair):
        both = far_in.at[pl.ds(2 * pair, 2)]
        return remote(both, both, far_s.at[pair], far_r.at[pair], right)

    def near_all(pair):
        both = near_in.at[pl.ds(2 * pair, 2)]
        return remote(both, both, near_s.at[pair], near_r.at[pair], right)

    def begin(pair):
        chunks = band(pair, 2)
        for side in range(2):
            for i in range(4):
                far_out[2 * pair + side, 32 * i : 32 * i + 32, :] = chunks[4 * side + i].astype(BF16)
            far_copy(pair, side).start()

    def middle(pair):
        far_all(pair).wait_recv()
        for side in range(2):
            n = 2 * pair + side
            for i, chunk in enumerate(band(pair, (1, 3)[side])):
                if i // 4 == side:
                    chunk = chunk + far_in[n, 32 * (i % 4) : 32 * (i % 4) + 32, :].astype(F32)
                near_out[n, 32 * i : 32 * i + 32, :] = chunk.astype(BF16)
            near_copy(pair, side).start()

    def fin_copy(block):
        return remote(back_rows.at[block - 1], final_in.at[y], fin_s, fin_r, beside(block))

    def stat_copy(block, dx):
        n = 4 * block + dx
        return remote(stat_out.at[block], stat_in.at[n], stat_s, stat_r, beside(block, dx))

    def finish(pair):
        near_all(pair).wait_recv()
        value = jnp.concatenate(band(pair, 0), axis=0)
        for side in range(2):
            value = value + near_in[2 * pair + side].astype(F32)
        for block in (2 * pair + 1, 2 * pair):
            lanes = slice(block % 2 * ROWS, (block % 2 + 1) * ROWS)
            if block == 0:
                part = value[:, lanes] + res_out[y].astype(F32)
                final_in[y] = part.astype(BF16)
            else:
                part = value[:, lanes] + res_in[block - 1].astype(F32)
                back_rows[block - 1] = part.astype(BF16)
                fin_copy(block).start()
            squares = jnp.sum(part * part, axis=0, keepdims=True)
            stat_out[block] = jnp.broadcast_to(squares, (SUBS, LANES))
            if block == 0:
                stat_in[0] = stat_out[0]
            for dx in range(NX):
                if (block, dx) != (0, 0):
                    stat_copy(block, dx).start()

    late_halves = remote(acts.at[1], acts.at[1], act_s, act_r.at[2], up)
    late_halves.wait_recv()
    project_others(0)
    fwd_all = remote(acts.at[3], acts.at[3], fwd_s, fwd_r, up)
    fwd_all.wait_recv()
    project_others(1)
    shards_wait(6, 9)
    project_last()
    begin(0)
    begin(1)
    middle(0)
    middle(1)
    finish(0)
    finish(1)
    fin_all = remote(back_rows, final_in.at[pl.ds(0, NY - 1)], fin_s, fin_r, up)
    fin_all.wait_recv()

    for tile in range(SUBS):
        cut = slice(tile * LANES, (tile + 1) * LANES)
        from_rows = slice((tile // 2) * 64, (tile // 2) * 64 + 64)
        mixed = [final_in[2 * (tile % 2) + odd, from_rows, :].astype(F32) for odd in range(2)]
        value = jnp.concatenate(mixed, axis=0).T
        summed[:, cut] = value
        hidden_ref[:, cut] = value.astype(BF16)
    sib_all.wait_send()
    shards_all(6, 3, 0).wait_send()
    remote(acts.at[pl.ds(0, 2)], acts.at[pl.ds(0, 2)], act_s, act_r.at[2], up).wait_send()
    fwd_all.wait_send()
    for pair in range(2):
        far_all(pair).wait_send()
        near_all(pair).wait_send()
    fin_all.wait_send()

    fifteen = stat_in.at[pl.ds(1, 15)]
    stat_all = remote(fifteen, fifteen, stat_s, stat_r, up)
    stat_all.wait_recv()
    total = tree_sum([stat_in[n] for n in range(16)])
    scale = lax.rsqrt(total * (1.0 / (NX * CHANS)) + 1e-05)
    scale = jnp.broadcast_to(scale[0:1, :], (ROWS, LANES)).T
    for tile in range(SUBS):
        cut = slice(tile * LANES, (tile + 1) * LANES)
        normed_ref[:, cut] = (summed[:, cut] * scale * gain_ref[tile : tile + 1, :]).astype(BF16)
    stat_all.wait_send()


def shard_rows(slot, h):
    return pl.ds(pl.multiple_of(h * (NZ * 32) + slot * 32, 32), 32)


def tree_sum(terms):
    while len(terms) > 1:
        rest = [terms[-1]] if len(terms) % 2 else []
        terms = [a + b for a, b in zip(terms[0::2], terms[1::2])] + rest
    return terms[0]


def local(
    q_stream, k_stream, v_stream, short_filter, rates, residues, skip, prior_state, out_weight, residual, norm_gain
):
    vmem = pl.BlockSpec(memory_space=pltpu.VMEM)
    hbm = pl.BlockSpec(memory_space=pltpu.HBM)
    dma = pltpu.SemaphoreType.DMA
    wide = (ROWS * SUBS, LANES)
    params = (MODES * SUBS, LANES)
    pair = (2 * SUBS, LANES)
    rows = (ROWS, CHANS)
    scratch = [
        pltpu.VMEM(rows, BF16),
        pltpu.VMEM(rows, BF16),
        pltpu.VMEM(rows, BF16),
        pltpu.VMEM(short_filter.shape, F32),
        pltpu.VMEM((MODES, CHANS), F32),
        pltpu.VMEM((MODES, CHANS), F32),
        pltpu.VMEM((SUBS, LANES), F32),
        pltpu.VMEM((MODES, CHANS), F32),
        pltpu.VMEM(rows, BF16),
        pltpu.VMEM((SUBS, LANES), F32),
        pltpu.VMEM((3,) + wide, F32),
        pltpu.VMEM((3, 2 * SUBS, LANES), F32),
        pltpu.VMEM(wide, F32),
        pltpu.VMEM(wide, F32),
        pltpu.VMEM(wide, F32),
        pltpu.VMEM((9 * SUBS, LANES), F32),
        pltpu.VMEM(params, F32),
        pltpu.VMEM(params, F32),
        pltpu.VMEM(params, F32),
        pltpu.VMEM(params, F32),
        pltpu.VMEM(params, F32),
        pltpu.VMEM(params, F32),
        pltpu.VMEM(params, F32),
        pltpu.VMEM((NJ,) + pair, F32),
        pltpu.VMEM((NZ,) + pair, F32),
        pltpu.VMEM(pair, F32),
        pltpu.VMEM((NJ,) + pair, F32),
        pltpu.VMEM(params, F32),
        pltpu.VMEM((CHANS, CHANS), BF16),
        pltpu.VMEM((NY, ROWS, CHANS), BF16),
        pltpu.VMEM((4, LANES, 2 * ROWS), BF16),
        pltpu.VMEM((4, LANES, 2 * ROWS), BF16),
        pltpu.VMEM((4, BAND, 2 * ROWS), BF16),
        pltpu.VMEM((4, BAND, 2 * ROWS), BF16),
        pltpu.VMEM((2, CHANS, 2 * ROWS), F32),
        pltpu.VMEM((NY - 1, BAND, ROWS), BF16),
        pltpu.VMEM((NY, BAND, ROWS), BF16),
        pltpu.VMEM((NY, BAND, ROWS), BF16),
        pltpu.VMEM((NY - 1, BAND, ROWS), BF16),
        pltpu.VMEM((ROWS, CHANS), F32),
        pltpu.VMEM((NY, SUBS, LANES), F32),
        pltpu.VMEM((16, SUBS, LANES), F32),
    ]
    sems = [dma((11,))]
    for sent, got in (
        (0, 0), (0, 0), (NZ, NZ), (0, 0), (4, 10), (2, 2), (0, 3), (0, 0), (2, 2), (2, 2), (0, 0), (0, 0), (0, 0)
    ):
        sems += [dma((n,)) if n else dma(()) for n in (sent, got)]
    return pl.pallas_call(
        kernel,
        out_shape=(jax.ShapeDtypeStruct((ROWS, CHANS), BF16), jax.ShapeDtypeStruct((ROWS, CHANS), BF16)),
        in_specs=[hbm] * 11,
        out_specs=(vmem, vmem),
        scratch_shapes=scratch + sems,
        compiler_params=pltpu.CompilerParams(
            collective_id=0, has_side_effects=True, vmem_limit_bytes=63 * 1024 * 1024
        ),
        name="mixer",
    )(
        q_stream, k_stream, v_stream, short_filter, rates, residues, skip.reshape(SUBS, LANES), prior_state,
        out_weight.T, residual, norm_gain.reshape(SUBS, LANES),
    )


def solution(mesh):
    placed = (
        P("seq", "ch"),
        P("seq", "ch"),
        P("seq", "ch"),
        P(None, None, "ch"),
        P(None, "ch"),
        P(None, "ch"),
        P("ch"),
        P(None, "ch"),
        P("ch", "seq"),
        P("seq", "ch"),
        P("ch"),
    )
    return jax.shard_map(
        local,
        mesh=mesh,
        in_specs=placed,
        out_specs=(P("seq", "ch"), P("seq", "ch")),
        check_vma=False,
    )
```

```python
import functools

import jax
import jax.numpy as jnp
from jax import lax
from jax.experimental import pallas as pl
from jax.experimental.pallas import tpu as pltpu
from jax.sharding import PartitionSpec as P

MESH = pl.DeviceIdType.MESH
F32 = jnp.float32
BF16 = jnp.bfloat16
NX, NY, NZ, NH = 4, 4, 16, 2
NJ = NY * NH
ROWS = 128
CHANS = 1024
LANES = 128
SUBS = 8
MODES = 16
BAND = CHANS // NX


def one_minus_exp(x):
    series = jnp.full_like(x, 1.0 / 8.0)
    for n in (7.0, 6.0, 5.0, 4.0, 3.0, 2.0):
        series = (1.0 - x * series) * (1.0 / n)
    return jnp.where(x < 0.25, x * (1.0 - x * series), 1.0 - jnp.exp(-x))


def kernel(
    q_hbm, k_hbm, v_hbm, taps_hbm, rates_hbm, residues_hbm, skip_hbm, prior_hbm, weight_hbm, residual_hbm, gain_hbm,
    hidden_ref, normed_ref,
    q_ref, k_ref, v_ref, taps_ref, rates_ref, residues_ref, skip_ref, prior_ref, residual_ref, gain_ref,
    streams, halo, gated, featq, filt, tap_rows, rate_rows, res_rows, prior_rows, pole_rows, inres_rows, inflow_rows,
    ends, plane_in, line_in, line_out, back_out, carry,
    weights, acts, far_out, far_in, near_out, near_in, parts, back_rows, final_in,
    res_out, res_in, summed, stat_out, stat_in,
    input_s, halo_s, halo_r, s1_s, s1_r, s2_s, s2_r, s3_s, s3_r, ring_s, ring_r, sib_s, sib_r,
    act_s, act_r, fwd_s, fwd_r, far_s, far_r, near_s, near_r,
    fin_s, fin_r, res_s, res_r, stat_s, stat_r,
):
    seq, x = lax.axis_index("seq"), lax.axis_index("ch")
    z, j = lax.div(seq, NJ), lax.rem(seq, NJ)
    y, h = lax.div(j, NH), lax.rem(j, NH)

    def device(z_, j_, x_):
        return (z_ * NJ + j_, x_)

    def remote(src, dst, send, recv, target):
        return pltpu.make_async_remote_copy(
            src_ref=src, dst_ref=dst, send_sem=send, recv_sem=recv, device_id=target, device_id_type=MESH
        )

    def row(t):
        return pl.ds(pl.multiple_of(t * SUBS, SUBS), SUBS)

    own_weights = weights.at[shard_rows(0, h), :]
    inputs = [
        pltpu.make_async_copy(src, dst, input_s.at[n])
        for n, (src, dst) in enumerate((
            (k_hbm, k_ref), (v_hbm, v_ref), (q_hbm, q_ref), (weight_hbm, own_weights), (rates_hbm, rates_ref),
            (taps_hbm, taps_ref), (residues_hbm, residues_ref), (prior_hbm, prior_ref), (skip_hbm, skip_ref),
            (residual_hbm, residual_ref), (gain_hbm, gain_ref),
        ))
    ]
    for copy in inputs[:4]:
        copy.start()

    barrier = pltpu.get_barrier_semaphore()

    def greet(target):
        pl.semaphore_signal(barrier, inc=1, device_id=target, device_id_type=MESH)

    sibling = device(z, y * NH + 1 - h, x)

    def along(hops, core):
        return device(lax.rem(z + hops + NZ, NZ), y * NH + core, x)

    for d in range(1, NZ):
        greet(along(d, h))
    for d in (1, -1, 2 - 4 * h):
        greet(along(d, 1 - h))
    for d in range(1, NJ):
        greet(device(z, lax.rem(j + d, NJ), x))
    for d in range(1, NX):
        for e in range(NY):
            greet(device(z, lax.rem(y + e, NY) * NH + h, lax.rem(x + d, NX)))

    has_next, has_prev = seq < NZ * NJ - 1, seq > 0
    first_j, last_j = j == 0, j == NJ - 1

    @pl.when(last_j)
    def _():
        greet(device(lax.rem(z + 1, NZ), 0, x))

    @pl.when(first_j)
    def _():
        greet(device(lax.rem(z + NZ - 1, NZ), NJ - 1, x))

    for copy in inputs[4:]:
        copy.start()

    def shard(slot):
        return weights.at[shard_rows(slot, h), :]

    def ring_copy(src, hops, slot, sent, got, core=None):
        to = along(hops, h if core is None else core)
        return remote(src, shard(slot), ring_s.at[sent], ring_r.at[got], to)

    def ring_first():
        for d in (2, 1):
            ring_copy(weight_hbm, d, NZ - d, 0, 0 if d == 2 else 2).start()
            ring_copy(weight_hbm, -d, d, 0, 1 if d == 2 else 2).start()
        remote(weight_hbm, own_weights, sib_s.at[0], sib_r.at[0], sibling).start()

    def shards_all(count, sent, got):
        some = weights.at[pl.ds(0, count * 32), :]
        return remote(some, some, ring_s.at[sent], ring_r.at[got], sibling)

    def shards_wait(count, got):
        shards_all(count, 0, got).wait_recv()

    def ring_next(step):
        far, got = 2 * step, 3 * step
        shards_wait(1, got - 3)
        for d in (2, 1):
            ring_copy(shard(NZ - far), d, NZ - far - d, step, got if d == 2 else got + 2).start()
        shards_wait(1, got - 2)
        for d in (2, 1):
            ring_copy(shard(far), -d, far + d, step, got + 1 if d == 2 else got + 2).start()

    def ring_last(side):
        shards_wait(1, 6 + side)
        src, hops, slot = ((shard(NZ - 6), 1, NZ - 7), (shard(6), -1, 7))[side]

        @pl.when(h == side)
        def _():
            for core in (h, 1 - h):
                ring_copy(src, 2 * hops, 8, 3, 9, core).start()

        for core in (h, 1 - h):
            ring_copy(src, hops, slot, 3, 9, core).start()

    def sib_copy(slot):
        two = weights.at[pl.ds(pl.multiple_of(h * (NZ * 32) + slot * 32, 32), 2 * 32), :]
        return remote(two, two, sib_s.at[1], sib_r.at[1], sibling)

    def sib_give(step):
        shards_wait(2, 3 * step - 1)
        sib_copy(NZ - 2 * step).start()
        sib_copy(2 * step - 1).start()

    peers = NJ - 1 + (NX - 1) * NY + NZ - 1 + 3
    edge = jnp.logical_or(first_j, last_j)
    early = z < 7

    def convert(stream, ref, begin, end):
        for part in range(SUBS):
            to = pl.ds(begin * SUBS + part, end - begin, stride=SUBS)
            streams[stream, to, :] = ref[begin:end, part * LANES : (part + 1) * LANES].astype(F32)

    for n in range(3):
        inputs[n].wait()
    for stream, ref in enumerate((q_ref, k_ref, v_ref)):
        convert(stream, ref, ROWS - 16, ROWS)
    last = (ROWS - 2) * SUBS
    halo_copy = remote(
        streams.at[:, pl.ds(last, 2 * SUBS), :], halo, halo_s, halo_r, (lax.rem(seq + 1, NZ * NJ), x)
    )
    convert(1, k_ref, 0, ROWS - 16)
    convert(2, v_ref, 0, ROWS - 16)
    for n in range(3, len(inputs)):
        inputs[n].wait()

    for part in range(SUBS):
        cut = slice(part * LANES, (part + 1) * LANES)
        to = pl.ds(part, MODES, stride=SUBS)
        rate_rows[to, :] = rates_ref[:, cut]
        res_rows[to, :] = residues_ref[:, cut]
        prior_rows[to, :] = prior_ref[:, cut]
        for stream in range(3):
            for tap in range(3):
                n = (3 * stream + tap) * SUBS + part
                tap_rows[n : n + 1, :] = taps_ref[stream, tap : tap + 1, cut]
    rates = rate_rows[...]
    inflow = jnp.sqrt(one_minus_exp(2.0 * rates))
    pole_rows[...] = jnp.exp(-rates)
    inflow_rows[...] = inflow
    inres_rows[...] = res_rows[...] * inflow

    def modes_of(ref):
        return [ref[m * SUBS : (m + 1) * SUBS, :] for m in range(MODES)]

    taps = [tap_rows[n * SUBS : (n + 1) * SUBS, :] for n in range(9)]
    poles = modes_of(pole_rows)
    skip = skip_ref[...]

    def feature(stream, now, back1, back2):
        return taps[3 * stream] * now + taps[3 * stream + 1] * back1 + taps[3 * stream + 2] * back2

    def gate(t, history):
        later, feats = [], []
        for stream, (back1, back2) in zip((1, 2), history):
            now = streams[stream, row(t), :]
            feats.append(feature(stream, now, back1, back2))
            later.append((now, back1))
        value = feats[0] * feats[1]
        gated[row(t), :] = value
        return value, tuple(later)

    def steps(begin, end, step, carried):
        def eight(block, carried):
            for t in range(8):
                carried = step(block * 8 + t, carried)
            return carried

        return lax.fori_loop(begin // 8, end // 8, eight, carried)

    def advance(states, value):
        return tuple(pole * state + value for pole, state in zip(poles, states))

    history = tuple((streams[s, SUBS : 2 * SUBS, :], streams[s, 0:SUBS, :]) for s in (1, 2))
    states = tuple(jnp.zeros((SUBS, LANES), F32) for _ in range(MODES))

    def scan_step(t, carried):
        states, history = carried
        value, history = gate(t, history)
        return advance(states, value), history

    scan = (states, history)
    for t in range(2, 8):
        scan = scan_step(t, scan)
    states, history = steps(8, ROWS, scan_step, scan)

    @pl.when(edge)
    def _():
        pl.semaphore_wait(barrier, peers + 1)

    @pl.when(jnp.logical_not(edge))
    def _():
        pl.semaphore_wait(barrier, peers)

    pl.when(has_next)(halo_copy.start)
    ring_first()

    for tile in range(SUBS):
        turned = residual_ref[:, tile * LANES : (tile + 1) * LANES].astype(F32).T.astype(BF16)
        to_rows = slice((tile // 2) * 64, (tile // 2) * 64 + 64)
        for odd in range(2):
            res_out[2 * (tile % 2) + odd, to_rows, :] = turned[64 * odd : 64 * odd + 64, :]

    def beside(block, dx=0):
        return device(z, lax.rem(y + (0, 3, 1, 2)[block], NY) * NH + h, x if dx == 0 else lax.rem(x + dx, NX))

    def res_copy(block):
        to = lax.rem(y + (0, 1, 3, 2)[block], NY)
        return remote(res_out.at[to], res_in.at[block - 1], res_s, res_r, device(z, to * NH + h, x))

    for block in range(1, 4):
        res_copy(block).start()
    convert(0, q_ref, 0, ROWS - 16)

    @pl.when(has_prev)
    def _():
        halo_copy.wait_recv()

    @pl.when(jnp.logical_not(has_prev))
    def _():
        halo[...] = jnp.zeros_like(halo)

    def halo_rows(s):
        return halo[s, SUBS : 2 * SUBS, :], halo[s, 0:SUBS, :]

    first, history = gate(0, (halo_rows(1), halo_rows(2)))
    second, history = gate(1, history)
    for m in range(MODES):
        at = slice(m * SUBS, (m + 1) * SUBS)
        late = jnp.exp(-(ROWS - 2.0) * rate_rows[at, :])
        ends[at, :] = inflow_rows[at, :] * (states[m] + late * (poles[m] * first + second))

    pair = 2 * SUBS

    def pair_rows(n):
        return pl.ds(pl.multiple_of(n * pair, pair), pair)

    def to_owner(d):
        to = lax.rem(j + d, NJ)
        return remote(ends.at[pair_rows(to), :], plane_in.at[j], s1_s, s1_r, device(z, to, x))

    def along_line(d):
        return remote(line_out, line_in.at[z], s2_s.at[d], s2_r.at[d], along(d, h))

    def from_owner(d):
        to = lax.rem(j + d, NJ)
        return remote(back_out.at[to], carry.at[pair_rows(j), :], s3_s, s3_r, device(z, to, x))

    for d in range(1, NJ):
        to_owner(d).start()

    plane_in[j] = ends[pair_rows(j), :]

    inres = modes_of(inres_rows)

    def output_step(t, carried):
        states, (back1, back2) = carried
        now = streams[0, row(t), :]
        featq[row(t), :] = feature(0, now, back1, back2)
        value = gated[row(t), :]
        states = advance(states, value)
        terms = [r * s for r, s in zip(inres, states)] + [skip * value]
        filt[row(t), :] = tree_sum(terms)
        return states, (now, back1)

    states = tuple(jnp.zeros((SUBS, LANES), F32) for _ in range(MODES))
    outputs = steps(0, 64, output_step, (states, halo_rows(0)))
    ring_next(1)

    others = plane_in.at[pl.ds(0, NJ - 1)]
    to_owner_all = remote(others, others, s1_s, s1_r, sibling)
    to_owner_all.wait_recv()

    my_rates = rate_rows[pair_rows(j), :]
    block_decay = jnp.exp(-float(ROWS) * my_rates)
    plane_decay = jnp.exp(-float(ROWS * NJ) * my_rates)
    total = plane_in[0]
    for i in range(1, NJ):
        total = block_decay * total + plane_in[i]
    line_out[...] = total

    @pl.loop(1, NZ - z)
    def _(d):
        along_line(d).start()

    late = jnp.logical_not(early)

    @pl.when(late)
    def _():
        ring_next(2)
        sib_give(1)

    steps(64, ROWS, output_step, outputs)
    highest = z >= 14

    @pl.when(highest)
    def _():
        ring_last(0)

    @pl.loop(1, z + 1)
    def _(d):
        along_line(d).wait_recv()

    incoming = lax.fori_loop(0, z, lambda i, s: plane_decay * s + line_in[i], prior_rows[pair_rows(j), :])
    for i in range(NJ):
        back_out[i] = incoming
        incoming = block_decay * incoming + plane_in[i]

    for d in range(1, NJ):
        from_owner(d).start()

    carry[pair_rows(j), :] = back_out[j]


    others = back_out.at[pl.ds(0, NJ - 1)]
    from_owner_all = remote(others, others, s3_s, s3_r, sibling)
    from_owner_all.wait_recv()

    half = ROWS // 2
    up = device(z, lax.rem(y + 1, NY) * NH + h, x)
    down = device(z, lax.rem(y + 3, NY) * NH + h, x)
    across = device(z, lax.rem(y + 2, NY) * NH + h, x)

    act_wait = (0, 2, 2, 1)

    def act_copy(part, side):
        cut = pl.ds(part * half, half)
        n = 2 * part + side
        return remote(acts.at[0, cut, :], acts.at[1 + side, cut, :], act_s, act_r.at[act_wait[n]], (up, down)[side])

    def fwd_copy(part):
        cut = pl.ds(part * half, half)
        return remote(acts.at[1 + part, cut, :], acts.at[3, cut, :], fwd_s, fwd_r, (up, down)[part])

    def carried_step(t, waves):
        waves = tuple(pole * wave for pole, wave in zip(poles, waves))
        filt[row(t), :] = featq[row(t), :] * (filt[row(t), :] + tree_sum(list(waves)))
        return waves

    waves = tuple(res_rows[m * SUBS : (m + 1) * SUBS, :] * carry[m * SUBS : (m + 1) * SUBS, :] for m in range(MODES))
    for part in range(2):
        waves = steps(part * half, (part + 1) * half, carried_step, waves)
        for sub in range(SUBS):
            from_rows = pl.ds(part * half * SUBS + sub, half, stride=SUBS)
            acts[0, part * half : (part + 1) * half, sub * LANES : (sub + 1) * LANES] = filt[from_rows, :].astype(BF16)
        act_copy(part, part).start()
    act_copy(1, 0).start()
    act_copy(0, 1).start()

    @pl.when(early)
    def _():
        ring_next(2)
        sib_give(1)

    @pl.when(jnp.logical_not(highest))
    def _():
        ring_last(0)

    ring_last(1)

    pl.when(has_next)(halo_copy.wait_send)
    to_owner_all.wait_send()
    from_owner_all.wait_send()

    @pl.loop(1, NZ - z)
    def _(d):
        along_line(d).wait_send()

    sib_give(2)
    sib_give(3)
    own_all = remote(weight_hbm, own_weights, sib_s.at[0], sib_r.at[0], sibling)
    own_all.wait_send()
    own_all.wait_recv()
    for sent in range(3):
        shards_all(4, sent, 0).wait_send()
    res_all = remote(res_in, res_in, res_s, res_r, sibling)
    res_all.wait_send()
    res_all.wait_recv()
    for part in range(2):
        act_copy(part, part).wait_recv()
        fwd_copy(part).start()
    twelve = weights.at[pl.ds(0, 12 * 32), :]
    sib_all = remote(twelve, twelve, sib_s.at[1], sib_r.at[1], sibling)
    sib_all.wait_recv()

    right, left = device(z, j, lax.rem(x + 1, NX)), device(z, j, lax.rem(x + 3, NX))
    sides = (right, left)

    def project(rows, weight):
        return lax.dot_general(weight, rows, (((1,), (1,)), ((), ())), preferred_element_type=F32)

    last_slots = [(core * NZ * 32 + 7 * 32, 3 * 32) for core in range(2)]
    other_slots = ((0, 224), (320, 416), (832, 192))

    def project_others(pair):
        rows = acts[2 * pair : 2 * pair + 2].reshape(2 * ROWS, CHANS)
        for at, count in other_slots:
            parts[pair, at : at + count, :] = project(rows, weights[at : at + count, :])

    def project_last():
        rows = acts[...].reshape(NY * ROWS, CHANS)
        some = jnp.concatenate([weights[at : at + count, :] for at, count in last_slots], axis=0)
        value = project(rows, some)
        for pair in range(2):
            for n, (at, count) in enumerate(last_slots):
                parts[pair, at : at + count, :] = value[n * count : (n + 1) * count, 2 * pair * ROWS : 2 * (pair + 1) * ROWS]

    def band(pair, dx):
        first = lax.rem(x + dx, NX) * 4 + NZ - z
        slots = [lax.rem(first + i, NZ) for i in range(4)]
        return [parts[pair, shard_rows(slot, core), :] for slot in slots for core in range(2)]

    def far_copy(pair, side):
        n = 2 * pair + side
        return remote(far_out.at[n], far_in.at[n], far_s.at[pair], far_r.at[pair], sides[side])

    def near_copy(pair, side):
        n = 2 * pair + side
        return remote(near_out.at[n], near_in.at[n], near_s.at[pair], near_r.at[pair], sides[side])

    def far_all(pair):
        both = far_in.at[pl.ds(2 * pair, 2)]
        return remote(both, both, far_s.at[pair], far_r.at[pair], right)

    def near_all(pair):
        both = near_in.at[pl.ds(2 * pair, 2)]
        return remote(both, both, near_s.at[pair], near_r.at[pair], right)

    def begin(pair):
        chunks = band(pair, 2)
        for side in range(2):
            for i in range(4):
                far_out[2 * pair + side, 32 * i : 32 * i + 32, :] = chunks[4 * side + i].astype(BF16)
            far_copy(pair, side).start()

    def middle(pair):
        far_all(pair).wait_recv()
        for side in range(2):
            n = 2 * pair + side
            for i, chunk in enumerate(band(pair, (1, 3)[side])):
                if i // 4 == side:
                    chunk = chunk + far_in[n, 32 * (i % 4) : 32 * (i % 4) + 32, :].astype(F32)
                near_out[n, 32 * i : 32 * i + 32, :] = chunk.astype(BF16)
            near_copy(pair, side).start()

    def fin_copy(block):
        return remote(back_rows.at[block - 1], final_in.at[y], fin_s, fin_r, beside(block))

    def stat_copy(block, dx):
        n = 4 * block + dx
        return remote(stat_out.at[block], stat_in.at[n], stat_s, stat_r, beside(block, dx))

    def finish(pair):
        near_all(pair).wait_recv()
        value = jnp.concatenate(band(pair, 0), axis=0)
        for side in range(2):
            value = value + near_in[2 * pair + side].astype(F32)
        for block in (2 * pair + 1, 2 * pair):
            lanes = slice(block % 2 * ROWS, (block % 2 + 1) * ROWS)
            if block == 0:
                part = value[:, lanes] + res_out[y].astype(F32)
                final_in[y] = part.astype(BF16)
            else:
                part = value[:, lanes] + res_in[block - 1].astype(F32)
                back_rows[block - 1] = part.astype(BF16)
                fin_copy(block).start()
            squares = jnp.sum(part * part, axis=0, keepdims=True)
            stat_out[block] = jnp.broadcast_to(squares, (SUBS, LANES))
            if block == 0:
                stat_in[0] = stat_out[0]
            for dx in range(NX):
                if (block, dx) != (0, 0):
                    stat_copy(block, dx).start()

    late_halves = remote(acts.at[1], acts.at[1], act_s, act_r.at[2], up)
    late_halves.wait_recv()
    project_others(0)
    fwd_all = remote(acts.at[3], acts.at[3], fwd_s, fwd_r, up)
    fwd_all.wait_recv()
    project_others(1)
    shards_wait(6, 9)
    project_last()
    begin(0)
    begin(1)
    middle(0)
    middle(1)
    finish(0)
    finish(1)
    fin_all = remote(back_rows, final_in.at[pl.ds(0, NY - 1)], fin_s, fin_r, up)
    fin_all.wait_recv()

    for tile in range(SUBS):
        cut = slice(tile * LANES, (tile + 1) * LANES)
        from_rows = slice((tile // 2) * 64, (tile // 2) * 64 + 64)
        mixed = [final_in[2 * (tile % 2) + odd, from_rows, :].astype(F32) for odd in range(2)]
        value = jnp.concatenate(mixed, axis=0).T
        summed[:, cut] = value
        hidden_ref[:, cut] = value.astype(BF16)
    sib_all.wait_send()
    shards_all(6, 3, 0).wait_send()
    remote(acts.at[pl.ds(0, 2)], acts.at[pl.ds(0, 2)], act_s, act_r.at[2], up).wait_send()
    fwd_all.wait_send()
    for pair in range(2):
        far_all(pair).wait_send()
        near_all(pair).wait_send()
    fin_all.wait_send()

    fifteen = stat_in.at[pl.ds(1, 15)]
    stat_all = remote(fifteen, fifteen, stat_s, stat_r, up)
    stat_all.wait_recv()
    total = tree_sum([stat_in[n] for n in range(16)])
    scale = lax.rsqrt(total * (1.0 / (NX * CHANS)) + 1e-05)
    scale = jnp.broadcast_to(scale[0:1, :], (ROWS, LANES)).T
    for tile in range(SUBS):
        cut = slice(tile * LANES, (tile + 1) * LANES)
        normed_ref[:, cut] = (summed[:, cut] * scale * gain_ref[tile : tile + 1, :]).astype(BF16)
    stat_all.wait_send()


def shard_rows(slot, h):
    return pl.ds(pl.multiple_of(h * (NZ * 32) + slot * 32, 32), 32)


def tree_sum(terms):
    while len(terms) > 1:
        rest = [terms[-1]] if len(terms) % 2 else []
        terms = [a + b for a, b in zip(terms[0::2], terms[1::2])] + rest
    return terms[0]


def local(
    q_stream, k_stream, v_stream, short_filter, rates, residues, skip, prior_state, out_weight, residual, norm_gain
):
    vmem = pl.BlockSpec(memory_space=pltpu.VMEM)
    hbm = pl.BlockSpec(memory_space=pltpu.HBM)
    dma = pltpu.SemaphoreType.DMA
    wide = (ROWS * SUBS, LANES)
    params = (MODES * SUBS, LANES)
    pair = (2 * SUBS, LANES)
    rows = (ROWS, CHANS)
    scratch = [
        pltpu.VMEM(rows, BF16),
        pltpu.VMEM(rows, BF16),
        pltpu.VMEM(rows, BF16),
        pltpu.VMEM(short_filter.shape, F32),
        pltpu.VMEM((MODES, CHANS), F32),
        pltpu.VMEM((MODES, CHANS), F32),
        pltpu.VMEM((SUBS, LANES), F32),
        pltpu.VMEM((MODES, CHANS), F32),
        pltpu.VMEM(rows, BF16),
        pltpu.VMEM((SUBS, LANES), F32),
        pltpu.VMEM((3,) + wide, F32),
        pltpu.VMEM((3, 2 * SUBS, LANES), F32),
        pltpu.VMEM(wide, F32),
        pltpu.VMEM(wide, F32),
        pltpu.VMEM(wide, F32),
        pltpu.VMEM((9 * SUBS, LANES), F32),
        pltpu.VMEM(params, F32),
        pltpu.VMEM(params, F32),
        pltpu.VMEM(params, F32),
        pltpu.VMEM(params, F32),
        pltpu.VMEM(params, F32),
        pltpu.VMEM(params, F32),
        pltpu.VMEM(params, F32),
        pltpu.VMEM((NJ,) + pair, F32),
        pltpu.VMEM((NZ,) + pair, F32),
        pltpu.VMEM(pair, F32),
        pltpu.VMEM((NJ,) + pair, F32),
        pltpu.VMEM(params, F32),
        pltpu.VMEM((CHANS, CHANS), BF16),
        pltpu.VMEM((NY, ROWS, CHANS), BF16),
        pltpu.VMEM((4, LANES, 2 * ROWS), BF16),
        pltpu.VMEM((4, LANES, 2 * ROWS), BF16),
        pltpu.VMEM((4, BAND, 2 * ROWS), BF16),
        pltpu.VMEM((4, BAND, 2 * ROWS), BF16),
        pltpu.VMEM((2, CHANS, 2 * ROWS), F32),
        pltpu.VMEM((NY - 1, BAND, ROWS), BF16),
        pltpu.VMEM((NY, BAND, ROWS), BF16),
        pltpu.VMEM((NY, BAND, ROWS), BF16),
        pltpu.VMEM((NY - 1, BAND, ROWS), BF16),
        pltpu.VMEM((ROWS, CHANS), F32),
        pltpu.VMEM((NY, SUBS, LANES), F32),
        pltpu.VMEM((16, SUBS, LANES), F32),
    ]
    sems = [dma((11,))]
    for sent, got in (
        (0, 0), (0, 0), (NZ, NZ), (0, 0), (4, 10), (2, 2), (0, 3), (0, 0), (2, 2), (2, 2), (0, 0), (0, 0), (0, 0)
    ):
        sems += [dma((n,)) if n else dma(()) for n in (sent, got)]
    return pl.pallas_call(
        kernel,
        out_shape=(jax.ShapeDtypeStruct((ROWS, CHANS), BF16), jax.ShapeDtypeStruct((ROWS, CHANS), BF16)),
        in_specs=[hbm] * 11,
        out_specs=(vmem, vmem),
        scratch_shapes=scratch + sems,
        compiler_params=pltpu.CompilerParams(
            collective_id=0, has_side_effects=True, vmem_limit_bytes=63 * 1024 * 1024
        ),
        name="mixer",
    )(
        q_stream, k_stream, v_stream, short_filter, rates, residues, skip.reshape(SUBS, LANES), prior_state,
        out_weight.T, residual, norm_gain.reshape(SUBS, LANES),
    )


def solution(mesh):
    placed = (
        P("seq", "ch"),
        P("seq", "ch"),
        P("seq", "ch"),
        P(None, None, "ch"),
        P(None, "ch"),
        P(None, "ch"),
        P("ch"),
        P(None, "ch"),
        P("ch", "seq"),
        P("seq", "ch"),
        P("ch"),
    )
    return jax.shard_map(
        local,
        mesh=mesh,
        in_specs=placed,
        out_specs=(P("seq", "ch"), P("seq", "ch")),
        check_vma=False,
    )
```

```python
import functools

import jax
import jax.numpy as jnp
from jax import lax
from jax.experimental import pallas as pl
from jax.experimental.pallas import tpu as pltpu
from jax.sharding import PartitionSpec as P

MESH = pl.DeviceIdType.MESH
F32 = jnp.float32
BF16 = jnp.bfloat16
NX, NY, NZ, NH = 4, 4, 16, 2
NJ = NY * NH
ROWS = 128
CHANS = 1024
LANES = 128
SUBS = 8
MODES = 16
BAND = CHANS // NX


def one_minus_exp(x):
    series = jnp.full_like(x, 1.0 / 8.0)
    for n in (7.0, 6.0, 5.0, 4.0, 3.0, 2.0):
        series = (1.0 - x * series) * (1.0 / n)
    return jnp.where(x < 0.25, x * (1.0 - x * series), 1.0 - jnp.exp(-x))


def kernel(
    q_hbm, k_hbm, v_hbm, taps_hbm, rates_hbm, residues_hbm, skip_hbm, prior_hbm, weight_hbm, residual_hbm, gain_hbm,
    hidden_ref, normed_ref,
    q_ref, k_ref, v_ref, taps_ref, rates_ref, residues_ref, skip_ref, prior_ref, residual_ref, gain_ref,
    streams, halo, gated, featq, filt, tap_rows, rate_rows, res_rows, prior_rows, pole_rows, inres_rows, inflow_rows,
    ends, plane_in, line_in, line_out, back_out, carry,
    weights, acts, far_out, far_in, near_out, near_in, parts, back_rows, final_in,
    res_out, res_in, summed, stat_out, stat_in,
    input_s, halo_s, halo_r, s1_s, s1_r, s2_s, s2_r, s3_s, s3_r, ring_s, ring_r, sib_s, sib_r,
    act_s, act_r, fwd_s, fwd_r, far_s, far_r, near_s, near_r,
    fin_s, fin_r, res_s, res_r, stat_s, stat_r,
):
    seq, x = lax.axis_index("seq"), lax.axis_index("ch")
    z, j = lax.div(seq, NJ), lax.rem(seq, NJ)
    y, h = lax.div(j, NH), lax.rem(j, NH)

    def device(z_, j_, x_):
        return (z_ * NJ + j_, x_)

    def remote(src, dst, send, recv, target):
        return pltpu.make_async_remote_copy(
            src_ref=src, dst_ref=dst, send_sem=send, recv_sem=recv, device_id=target, device_id_type=MESH
        )

    def row(t):
        return pl.ds(pl.multiple_of(t * SUBS, SUBS), SUBS)

    own_weights = weights.at[shard_rows(0, h), :]
    inputs = [
        pltpu.make_async_copy(src, dst, input_s.at[n])
        for n, (src, dst) in enumerate((
            (k_hbm, k_ref), (v_hbm, v_ref), (q_hbm, q_ref), (weight_hbm, own_weights), (rates_hbm, rates_ref),
            (taps_hbm, taps_ref), (residues_hbm, residues_ref), (prior_hbm, prior_ref), (skip_hbm, skip_ref),
            (residual_hbm, residual_ref), (gain_hbm, gain_ref),
        ))
    ]
    for copy in inputs[:4]:
        copy.start()

    barrier = pltpu.get_barrier_semaphore()

    def greet(target):
        pl.semaphore_signal(barrier, inc=1, device_id=target, device_id_type=MESH)

    sibling = device(z, y * NH + 1 - h, x)

    def along(hops, core):
        return device(lax.rem(z + hops + NZ, NZ), y * NH + core, x)

    for d in range(1, NZ):
        greet(along(d, h))
    for d in (1, -1, 2 - 4 * h):
        greet(along(d, 1 - h))
    for d in range(1, NJ):
        greet(device(z, lax.rem(j + d, NJ), x))
    for d in range(1, NX):
        for e in range(NY):
            greet(device(z, lax.rem(y + e, NY) * NH + h, lax.rem(x + d, NX)))

    has_next, has_prev = seq < NZ * NJ - 1, seq > 0
    first_j, last_j = j == 0, j == NJ - 1

    @pl.when(last_j)
    def _():
        greet(device(lax.rem(z + 1, NZ), 0, x))

    @pl.when(first_j)
    def _():
        greet(device(lax.rem(z + NZ - 1, NZ), NJ - 1, x))

    for copy in inputs[4:]:
        copy.start()

    def shard(slot):
        return weights.at[shard_rows(slot, h), :]

    def ring_copy(src, hops, slot, sent, got, core=None):
        to = along(hops, h if core is None else core)
        return remote(src, shard(slot), ring_s.at[sent], ring_r.at[got], to)

    def ring_first():
        for d in (2, 1):
            ring_copy(weight_hbm, d, NZ - d, 0, 0 if d == 2 else 2).start()
            ring_copy(weight_hbm, -d, d, 0, 1 if d == 2 else 2).start()
        remote(weight_hbm, own_weights, sib_s.at[0], sib_r.at[0], sibling).start()

    def shards_all(count, sent, got):
        some = weights.at[pl.ds(0, count * 32), :]
        return remote(some, some, ring_s.at[sent], ring_r.at[got], sibling)

    def shards_wait(count, got):
        shards_all(count, 0, got).wait_recv()

    def ring_next(step):
        far, got = 2 * step, 3 * step
        shards_wait(1, got - 3)
        for d in (2, 1):
            ring_copy(shard(NZ - far), d, NZ - far - d, step, got if d == 2 else got + 2).start()
        shards_wait(1, got - 2)
        for d in (2, 1):
            ring_copy(shard(far), -d, far + d, step, got + 1 if d == 2 else got + 2).start()

    def ring_last(side):
        shards_wait(1, 6 + side)
        src, hops, slot = ((shard(NZ - 6), 1, NZ - 7), (shard(6), -1, 7))[side]

        @pl.when(h == side)
        def _():
            for core in (h, 1 - h):
                ring_copy(src, 2 * hops, 8, 3, 9, core).start()

        for core in (h, 1 - h):
            ring_copy(src, hops, slot, 3, 9, core).start()

    def sib_copy(slot):
        two = weights.at[pl.ds(pl.multiple_of(h * (NZ * 32) + slot * 32, 32), 2 * 32), :]
        return remote(two, two, sib_s.at[1], sib_r.at[1], sibling)

    def sib_give(step):
        shards_wait(2, 3 * step - 1)
        sib_copy(NZ - 2 * step).start()
        sib_copy(2 * step - 1).start()

    peers = NJ - 1 + (NX - 1) * NY + NZ - 1 + 3
    edge = jnp.logical_or(first_j, last_j)
    early = z < 7

    def convert(stream, ref, begin, end):
        for part in range(SUBS):
            to = pl.ds(begin * SUBS + part, end - begin, stride=SUBS)
            streams[stream, to, :] = ref[begin:end, part * LANES : (part + 1) * LANES].astype(F32)

    for n in range(3):
        inputs[n].wait()
    for stream, ref in enumerate((q_ref, k_ref, v_ref)):
        convert(stream, ref, ROWS - 16, ROWS)
    last = (ROWS - 2) * SUBS
    halo_copy = remote(
        streams.at[:, pl.ds(last, 2 * SUBS), :], halo, halo_s, halo_r, (lax.rem(seq + 1, NZ * NJ), x)
    )
    convert(1, k_ref, 0, ROWS - 16)
    convert(2, v_ref, 0, ROWS - 16)
    for n in range(3, len(inputs)):
        inputs[n].wait()

    for part in range(SUBS):
        cut = slice(part * LANES, (part + 1) * LANES)
        to = pl.ds(part, MODES, stride=SUBS)
        rate_rows[to, :] = rates_ref[:, cut]
        res_rows[to, :] = residues_ref[:, cut]
        prior_rows[to, :] = prior_ref[:, cut]
        for stream in range(3):
            for tap in range(3):
                n = (3 * stream + tap) * SUBS + part
                tap_rows[n : n + 1, :] = taps_ref[stream, tap : tap + 1, cut]
    rates = rate_rows[...]
    inflow = jnp.sqrt(one_minus_exp(2.0 * rates))
    pole_rows[...] = jnp.exp(-rates)
    inflow_rows[...] = inflow
    inres_rows[...] = res_rows[...] * inflow

    def modes_of(ref):
        return [ref[m * SUBS : (m + 1) * SUBS, :] for m in range(MODES)]

    taps = [tap_rows[n * SUBS : (n + 1) * SUBS, :] for n in range(9)]
    poles = modes_of(pole_rows)
    skip = skip_ref[...]

    def feature(stream, now, back1, back2):
        return taps[3 * stream] * now + taps[3 * stream + 1] * back1 + taps[3 * stream + 2] * back2

    def gate(t, history):
        later, feats = [], []
        for stream, (back1, back2) in zip((1, 2), history):
            now = streams[stream, row(t), :]
            feats.append(feature(stream, now, back1, back2))
            later.append((now, back1))
        value = feats[0] * feats[1]
        gated[row(t), :] = value
        return value, tuple(later)

    def steps(begin, end, step, carried):
        def eight(block, carried):
            for t in range(8):
                carried = step(block * 8 + t, carried)
            return carried

        return lax.fori_loop(begin // 8, end // 8, eight, carried)

    def advance(states, value):
        return tuple(pole * state + value for pole, state in zip(poles, states))

    history = tuple((streams[s, SUBS : 2 * SUBS, :], streams[s, 0:SUBS, :]) for s in (1, 2))
    states = tuple(jnp.zeros((SUBS, LANES), F32) for _ in range(MODES))

    def scan_step(t, carried):
        states, history = carried
        value, history = gate(t, history)
        return advance(states, value), history

    scan = (states, history)
    for t in range(2, 8):
        scan = scan_step(t, scan)
    states, history = steps(8, ROWS, scan_step, scan)

    @pl.when(edge)
    def _():
        pl.semaphore_wait(barrier, peers + 1)

    @pl.when(jnp.logical_not(edge))
    def _():
        pl.semaphore_wait(barrier, peers)

    pl.when(has_next)(halo_copy.start)
    ring_first()

    for tile in range(SUBS):
        turned = residual_ref[:, tile * LANES : (tile + 1) * LANES].astype(F32).T.astype(BF16)
        to_rows = slice((tile // 2) * 64, (tile // 2) * 64 + 64)
        for odd in range(2):
            res_out[2 * (tile % 2) + odd, to_rows, :] = turned[64 * odd : 64 * odd + 64, :]

    def beside(block, dx=0):
        return device(z, lax.rem(y + (0, 3, 1, 2)[block], NY) * NH + h, x if dx == 0 else lax.rem(x + dx, NX))

    def res_copy(block):
        to = lax.rem(y + (0, 1, 3, 2)[block], NY)
        return remote(res_out.at[to], res_in.at[block - 1], res_s, res_r, device(z, to * NH + h, x))

    for block in range(1, 4):
        res_copy(block).start()
    convert(0, q_ref, 0, ROWS - 16)

    @pl.when(has_prev)
    def _():
        halo_copy.wait_recv()

    @pl.when(jnp.logical_not(has_prev))
    def _():
        halo[...] = jnp.zeros_like(halo)

    def halo_rows(s):
        return halo[s, SUBS : 2 * SUBS, :], halo[s, 0:SUBS, :]

    first, history = gate(0, (halo_rows(1), halo_rows(2)))
    second, history = gate(1, history)
    for m in range(MODES):
        at = slice(m * SUBS, (m + 1) * SUBS)
        late = jnp.exp(-(ROWS - 2.0) * rate_rows[at, :])
        ends[at, :] = inflow_rows[at, :] * (states[m] + late * (poles[m] * first + second))

    pair = 2 * SUBS

    def pair_rows(n):
        return pl.ds(pl.multiple_of(n * pair, pair), pair)

    def to_owner(d):
        to = lax.rem(j + d, NJ)
        return remote(ends.at[pair_rows(to), :], plane_in.at[j], s1_s, s1_r, device(z, to, x))

    def along_line(d):
        return remote(line_out, line_in.at[z], s2_s.at[d], s2_r.at[d], along(d, h))

    def from_owner(d):
        to = lax.rem(j + d, NJ)
        return remote(back_out.at[to], carry.at[pair_rows(j), :], s3_s, s3_r, device(z, to, x))

    for d in range(1, NJ):
        to_owner(d).start()

    plane_in[j] = ends[pair_rows(j), :]

    inres = modes_of(inres_rows)

    def output_step(t, carried):
        states, (back1, back2) = carried
        now = streams[0, row(t), :]
        featq[row(t), :] = feature(0, now, back1, back2)
        value = gated[row(t), :]
        states = advance(states, value)
        terms = [r * s for r, s in zip(inres, states)] + [skip * value]
        filt[row(t), :] = tree_sum(terms)
        return states, (now, back1)

    states = tuple(jnp.zeros((SUBS, LANES), F32) for _ in range(MODES))
    outputs = steps(0, 64, output_step, (states, halo_rows(0)))
    ring_next(1)

    others = plane_in.at[pl.ds(0, NJ - 1)]
    to_owner_all = remote(others, others, s1_s, s1_r, sibling)
    to_owner_all.wait_recv()

    my_rates = rate_rows[pair_rows(j), :]
    block_decay = jnp.exp(-float(ROWS) * my_rates)
    plane_decay = jnp.exp(-float(ROWS * NJ) * my_rates)
    total = plane_in[0]
    for i in range(1, NJ):
        total = block_decay * total + plane_in[i]
    line_out[...] = total

    @pl.loop(1, NZ - z)
    def _(d):
        along_line(d).start()

    late = jnp.logical_not(early)

    @pl.when(late)
    def _():
        ring_next(2)
        sib_give(1)

    steps(64, ROWS, output_step, outputs)
    highest = z >= 14

    @pl.when(highest)
    def _():
        ring_last(0)

    @pl.loop(1, z + 1)
    def _(d):
        along_line(d).wait_recv()

    incoming = lax.fori_loop(0, z, lambda i, s: plane_decay * s + line_in[i], prior_rows[pair_rows(j), :])
    for i in range(NJ):
        back_out[i] = incoming
        incoming = block_decay * incoming + plane_in[i]

    for d in range(1, NJ):
        from_owner(d).start()

    carry[pair_rows(j), :] = back_out[j]


    others = back_out.at[pl.ds(0, NJ - 1)]
    from_owner_all = remote(others, others, s3_s, s3_r, sibling)
    from_owner_all.wait_recv()

    half = ROWS // 2
    up = device(z, lax.rem(y + 1, NY) * NH + h, x)
    down = device(z, lax.rem(y + 3, NY) * NH + h, x)
    across = device(z, lax.rem(y + 2, NY) * NH + h, x)

    act_wait = (0, 2, 2, 1)

    def act_copy(part, side):
        cut = pl.ds(part * half, half)
        n = 2 * part + side
        return remote(acts.at[0, cut, :], acts.at[1 + side, cut, :], act_s, act_r.at[act_wait[n]], (up, down)[side])

    def fwd_copy(part):
        cut = pl.ds(part * half, half)
        return remote(acts.at[1 + part, cut, :], acts.at[3, cut, :], fwd_s, fwd_r, (up, down)[part])

    def carried_step(t, waves):
        waves = tuple(pole * wave for pole, wave in zip(poles, waves))
        filt[row(t), :] = featq[row(t), :] * (filt[row(t), :] + tree_sum(list(waves)))
        return waves

    waves = tuple(res_rows[m * SUBS : (m + 1) * SUBS, :] * carry[m * SUBS : (m + 1) * SUBS, :] for m in range(MODES))
    for part in range(2):
        waves = steps(part * half, (part + 1) * half, carried_step, waves)
        for sub in range(SUBS):
            from_rows = pl.ds(part * half * SUBS + sub, half, stride=SUBS)
            acts[0, part * half : (part + 1) * half, sub * LANES : (sub + 1) * LANES] = filt[from_rows, :].astype(BF16)
        act_copy(part, part).start()
    act_copy(1, 0).start()
    act_copy(0, 1).start()

    @pl.when(early)
    def _():
        ring_next(2)
        sib_give(1)

    def forward(part):
        act_copy(part, part).wait_recv()
        fwd_copy(part).start()

    forward(0)

    @pl.when(jnp.logical_not(highest))
    def _():
        ring_last(0)

    forward(1)
    ring_last(1)

    pl.when(has_next)(halo_copy.wait_send)
    to_owner_all.wait_send()
    from_owner_all.wait_send()

    @pl.loop(1, NZ - z)
    def _(d):
        along_line(d).wait_send()

    sib_give(2)
    sib_give(3)
    own_all = remote(weight_hbm, own_weights, sib_s.at[0], sib_r.at[0], sibling)
    own_all.wait_send()
    own_all.wait_recv()
    for sent in range(3):
        shards_all(4, sent, 0).wait_send()
    res_all = remote(res_in, res_in, res_s, res_r, sibling)
    res_all.wait_send()
    res_all.wait_recv()
    twelve = weights.at[pl.ds(0, 12 * 32), :]
    sib_all = remote(twelve, twelve, sib_s.at[1], sib_r.at[1], sibling)
    sib_all.wait_recv()

    right, left = device(z, j, lax.rem(x + 1, NX)), device(z, j, lax.rem(x + 3, NX))
    sides = (right, left)

    def project(rows, weight):
        return lax.dot_general(weight, rows, (((1,), (1,)), ((), ())), preferred_element_type=F32)

    last_slots = [(core * NZ * 32 + 7 * 32, 3 * 32) for core in range(2)]
    other_slots = ((0, 224), (320, 416), (832, 192))

    def project_others(pair):
        rows = acts[2 * pair : 2 * pair + 2].reshape(2 * ROWS, CHANS)
        for at, count in other_slots:
            parts[pair, at : at + count, :] = project(rows, weights[at : at + count, :])

    def project_last(pair):
        rows = acts[2 * pair : 2 * pair + 2].reshape(2 * ROWS, CHANS)
        some = jnp.concatenate([weights[at : at + count, :] for at, count in last_slots], axis=0)
        value = project(rows, some)
        for n, (at, count) in enumerate(last_slots):
            parts[pair, at : at + count, :] = value[n * count : (n + 1) * count, :]

    def band(pair, dx):
        first = lax.rem(x + dx, NX) * 4 + NZ - z
        slots = [lax.rem(first + i, NZ) for i in range(4)]
        return [parts[pair, shard_rows(slot, core), :] for slot in slots for core in range(2)]

    def far_copy(pair, side):
        n = 2 * pair + side
        return remote(far_out.at[n], far_in.at[n], far_s.at[pair], far_r.at[pair], sides[side])

    def near_copy(pair, side):
        n = 2 * pair + side
        return remote(near_out.at[n], near_in.at[n], near_s.at[pair], near_r.at[pair], sides[side])

    def far_all(pair):
        both = far_in.at[pl.ds(2 * pair, 2)]
        return remote(both, both, far_s.at[pair], far_r.at[pair], right)

    def near_all(pair):
        both = near_in.at[pl.ds(2 * pair, 2)]
        return remote(both, both, near_s.at[pair], near_r.at[pair], right)

    def begin(pair):
        chunks = band(pair, 2)
        for side in range(2):
            for i in range(4):
                far_out[2 * pair + side, 32 * i : 32 * i + 32, :] = chunks[4 * side + i].astype(BF16)
            far_copy(pair, side).start()

    def middle(pair):
        far_all(pair).wait_recv()
        for side in range(2):
            n = 2 * pair + side
            for i, chunk in enumerate(band(pair, (1, 3)[side])):
                if i // 4 == side:
                    chunk = chunk + far_in[n, 32 * (i % 4) : 32 * (i % 4) + 32, :].astype(F32)
                near_out[n, 32 * i : 32 * i + 32, :] = chunk.astype(BF16)
            near_copy(pair, side).start()

    def fin_copy(block):
        return remote(back_rows.at[block - 1], final_in.at[y], fin_s, fin_r, beside(block))

    def stat_copy(block, dx):
        n = 4 * block + dx
        return remote(stat_out.at[block], stat_in.at[n], stat_s, stat_r, beside(block, dx))

    def finish(pair):
        near_all(pair).wait_recv()
        value = jnp.concatenate(band(pair, 0), axis=0)
        for side in range(2):
            value = value + near_in[2 * pair + side].astype(F32)
        for block in (2 * pair + 1, 2 * pair):
            lanes = slice(block % 2 * ROWS, (block % 2 + 1) * ROWS)
            if block == 0:
                part = value[:, lanes] + res_out[y].astype(F32)
                final_in[y] = part.astype(BF16)
            else:
                part = value[:, lanes] + res_in[block - 1].astype(F32)
                back_rows[block - 1] = part.astype(BF16)
                fin_copy(block).start()
            squares = jnp.sum(part * part, axis=0, keepdims=True)
            stat_out[block] = jnp.broadcast_to(squares, (SUBS, LANES))
            if block == 0:
                stat_in[0] = stat_out[0]
            for dx in range(NX):
                if (block, dx) != (0, 0):
                    stat_copy(block, dx).start()

    late_halves = remote(acts.at[1], acts.at[1], act_s, act_r.at[2], up)
    late_halves.wait_recv()
    project_others(0)
    shards_wait(6, 9)
    project_last(0)
    begin(0)
    fwd_all = remote(acts.at[3], acts.at[3], fwd_s, fwd_r, up)
    fwd_all.wait_recv()
    project_others(1)
    project_last(1)
    begin(1)
    middle(0)
    middle(1)
    finish(0)
    finish(1)
    fin_all = remote(back_rows, final_in.at[pl.ds(0, NY - 1)], fin_s, fin_r, up)
    fin_all.wait_recv()

    for tile in range(SUBS):
        cut = slice(tile * LANES, (tile + 1) * LANES)
        from_rows = slice((tile // 2) * 64, (tile // 2) * 64 + 64)
        mixed = [final_in[2 * (tile % 2) + odd, from_rows, :].astype(F32) for odd in range(2)]
        value = jnp.concatenate(mixed, axis=0).T
        summed[:, cut] = value
        hidden_ref[:, cut] = value.astype(BF16)
    sib_all.wait_send()
    shards_all(6, 3, 0).wait_send()
    remote(acts.at[pl.ds(0, 2)], acts.at[pl.ds(0, 2)], act_s, act_r.at[2], up).wait_send()
    fwd_all.wait_send()
    for pair in range(2):
        far_all(pair).wait_send()
        near_all(pair).wait_send()
    fin_all.wait_send()

    fifteen = stat_in.at[pl.ds(1, 15)]
    stat_all = remote(fifteen, fifteen, stat_s, stat_r, up)
    stat_all.wait_recv()
    total = tree_sum([stat_in[n] for n in range(16)])
    scale = lax.rsqrt(total * (1.0 / (NX * CHANS)) + 1e-05)
    scale = jnp.broadcast_to(scale[0:1, :], (ROWS, LANES)).T
    for tile in range(SUBS):
        cut = slice(tile * LANES, (tile + 1) * LANES)
        normed_ref[:, cut] = (summed[:, cut] * scale * gain_ref[tile : tile + 1, :]).astype(BF16)
    stat_all.wait_send()


def shard_rows(slot, h):
    return pl.ds(pl.multiple_of(h * (NZ * 32) + slot * 32, 32), 32)


def tree_sum(terms):
    while len(terms) > 1:
        rest = [terms[-1]] if len(terms) % 2 else []
        terms = [a + b for a, b in zip(terms[0::2], terms[1::2])] + rest
    return terms[0]


def local(
    q_stream, k_stream, v_stream, short_filter, rates, residues, skip, prior_state, out_weight, residual, norm_gain
):
    vmem = pl.BlockSpec(memory_space=pltpu.VMEM)
    hbm = pl.BlockSpec(memory_space=pltpu.HBM)
    dma = pltpu.SemaphoreType.DMA
    wide = (ROWS * SUBS, LANES)
    params = (MODES * SUBS, LANES)
    pair = (2 * SUBS, LANES)
    rows = (ROWS, CHANS)
    scratch = [
        pltpu.VMEM(rows, BF16),
        pltpu.VMEM(rows, BF16),
        pltpu.VMEM(rows, BF16),
        pltpu.VMEM(short_filter.shape, F32),
        pltpu.VMEM((MODES, CHANS), F32),
        pltpu.VMEM((MODES, CHANS), F32),
        pltpu.VMEM((SUBS, LANES), F32),
        pltpu.VMEM((MODES, CHANS), F32),
        pltpu.VMEM(rows, BF16),
        pltpu.VMEM((SUBS, LANES), F32),
        pltpu.VMEM((3,) + wide, F32),
        pltpu.VMEM((3, 2 * SUBS, LANES), F32),
        pltpu.VMEM(wide, F32),
        pltpu.VMEM(wide, F32),
        pltpu.VMEM(wide, F32),
        pltpu.VMEM((9 * SUBS, LANES), F32),
        pltpu.VMEM(params, F32),
        pltpu.VMEM(params, F32),
        pltpu.VMEM(params, F32),
        pltpu.VMEM(params, F32),
        pltpu.VMEM(params, F32),
        pltpu.VMEM(params, F32),
        pltpu.VMEM(params, F32),
        pltpu.VMEM((NJ,) + pair, F32),
        pltpu.VMEM((NZ,) + pair, F32),
        pltpu.VMEM(pair, F32),
        pltpu.VMEM((NJ,) + pair, F32),
        pltpu.VMEM(params, F32),
        pltpu.VMEM((CHANS, CHANS), BF16),
        pltpu.VMEM((NY, ROWS, CHANS), BF16),
        pltpu.VMEM((4, LANES, 2 * ROWS), BF16),
        pltpu.VMEM((4, LANES, 2 * ROWS), BF16),
        pltpu.VMEM((4, BAND, 2 * ROWS), BF16),
        pltpu.VMEM((4, BAND, 2 * ROWS), BF16),
        pltpu.VMEM((2, CHANS, 2 * ROWS), F32),
        pltpu.VMEM((NY - 1, BAND, ROWS), BF16),
        pltpu.VMEM((NY, BAND, ROWS), BF16),
        pltpu.VMEM((NY, BAND, ROWS), BF16),
        pltpu.VMEM((NY - 1, BAND, ROWS), BF16),
        pltpu.VMEM((ROWS, CHANS), F32),
        pltpu.VMEM((NY, SUBS, LANES), F32),
        pltpu.VMEM((16, SUBS, LANES), F32),
    ]
    sems = [dma((11,))]
    for sent, got in (
        (0, 0), (0, 0), (NZ, NZ), (0, 0), (4, 10), (2, 2), (0, 3), (0, 0), (2, 2), (2, 2), (0, 0), (0, 0), (0, 0)
    ):
        sems += [dma((n,)) if n else dma(()) for n in (sent, got)]
    return pl.pallas_call(
        kernel,
        out_shape=(jax.ShapeDtypeStruct((ROWS, CHANS), BF16), jax.ShapeDtypeStruct((ROWS, CHANS), BF16)),
        in_specs=[hbm] * 11,
        out_specs=(vmem, vmem),
        scratch_shapes=scratch + sems,
        compiler_params=pltpu.CompilerParams(
            collective_id=0, has_side_effects=True, vmem_limit_bytes=63 * 1024 * 1024
        ),
        name="mixer",
    )(
        q_stream, k_stream, v_stream, short_filter, rates, residues, skip.reshape(SUBS, LANES), prior_state,
        out_weight.T, residual, norm_gain.reshape(SUBS, LANES),
    )


def solution(mesh):
    placed = (
        P("seq", "ch"),
        P("seq", "ch"),
        P("seq", "ch"),
        P(None, None, "ch"),
        P(None, "ch"),
        P(None, "ch"),
        P("ch"),
        P(None, "ch"),
        P("ch", "seq"),
        P("seq", "ch"),
        P("ch"),
    )
    return jax.shard_map(
        local,
        mesh=mesh,
        in_specs=placed,
        out_specs=(P("seq", "ch"), P("seq", "ch")),
        check_vma=False,
    )
```

```python
import functools

import jax
import jax.numpy as jnp
from jax import lax
from jax.experimental import pallas as pl
from jax.experimental.pallas import tpu as pltpu
from jax.sharding import PartitionSpec as P

MESH = pl.DeviceIdType.MESH
F32 = jnp.float32
BF16 = jnp.bfloat16
NX, NY, NZ, NH = 4, 4, 16, 2
NJ = NY * NH
ROWS = 128
CHANS = 1024
LANES = 128
SUBS = 8
MODES = 16
BAND = CHANS // NX


def one_minus_exp(x):
    series = jnp.full_like(x, 1.0 / 8.0)
    for n in (7.0, 6.0, 5.0, 4.0, 3.0, 2.0):
        series = (1.0 - x * series) * (1.0 / n)
    return jnp.where(x < 0.25, x * (1.0 - x * series), 1.0 - jnp.exp(-x))


def kernel(
    q_hbm, k_hbm, v_hbm, taps_hbm, rates_hbm, residues_hbm, skip_hbm, prior_hbm, weight_hbm, residual_hbm, gain_hbm,
    hidden_ref, normed_ref,
    q_ref, k_ref, v_ref, taps_ref, rates_ref, residues_ref, skip_ref, prior_ref, residual_ref, gain_ref,
    streams, halo, gated, featq, filt, tap_rows, rate_rows, res_rows, prior_rows, pole_rows, inres_rows, inflow_rows,
    ends, plane_in, line_in, line_out, back_out, carry,
    weights, acts, far_out, far_in, near_out, near_in, parts, back_rows, final_in,
    res_out, res_in, summed, stat_out, stat_in,
    input_s, halo_s, halo_r, s1_s, s1_r, s2_s, s2_r, s3_s, s3_r, ring_s, ring_r, sib_s, sib_r,
    act_s, act_r, fwd_s, fwd_r, far_s, far_r, near_s, near_r,
    fin_s, fin_r, res_s, res_r, stat_s, stat_r,
):
    seq, x = lax.axis_index("seq"), lax.axis_index("ch")
    z, j = lax.div(seq, NJ), lax.rem(seq, NJ)
    y, h = lax.div(j, NH), lax.rem(j, NH)

    def device(z_, j_, x_):
        return (z_ * NJ + j_, x_)

    def remote(src, dst, send, recv, target):
        return pltpu.make_async_remote_copy(
            src_ref=src, dst_ref=dst, send_sem=send, recv_sem=recv, device_id=target, device_id_type=MESH
        )

    def row(t):
        return pl.ds(pl.multiple_of(t * SUBS, SUBS), SUBS)

    own_weights = weights.at[shard_rows(0, h), :]
    inputs = [
        pltpu.make_async_copy(src, dst, input_s.at[n])
        for n, (src, dst) in enumerate((
            (k_hbm, k_ref), (v_hbm, v_ref), (q_hbm, q_ref), (weight_hbm, own_weights), (rates_hbm, rates_ref),
            (taps_hbm, taps_ref), (residues_hbm, residues_ref), (prior_hbm, prior_ref), (skip_hbm, skip_ref),
            (residual_hbm, residual_ref), (gain_hbm, gain_ref),
        ))
    ]
    for copy in inputs[:4]:
        copy.start()

    barrier = pltpu.get_barrier_semaphore()

    def greet(target):
        pl.semaphore_signal(barrier, inc=1, device_id=target, device_id_type=MESH)

    sibling = device(z, y * NH + 1 - h, x)

    def along(hops, core):
        return device(lax.rem(z + hops + NZ, NZ), y * NH + core, x)

    for d in range(1, NZ):
        greet(along(d, h))
    for d in (1, -1, 2 - 4 * h):
        greet(along(d, 1 - h))
    for d in range(1, NJ):
        greet(device(z, lax.rem(j + d, NJ), x))
    for d in range(1, NX):
        for e in range(NY):
            greet(device(z, lax.rem(y + e, NY) * NH + h, lax.rem(x + d, NX)))

    has_next, has_prev = seq < NZ * NJ - 1, seq > 0
    first_j, last_j = j == 0, j == NJ - 1

    @pl.when(last_j)
    def _():
        greet(device(lax.rem(z + 1, NZ), 0, x))

    @pl.when(first_j)
    def _():
        greet(device(lax.rem(z + NZ - 1, NZ), NJ - 1, x))

    for copy in inputs[4:]:
        copy.start()

    def shard(slot):
        return weights.at[shard_rows(slot, h), :]

    def ring_copy(src, hops, slot, sent, got, core=None):
        to = along(hops, h if core is None else core)
        return remote(src, shard(slot), ring_s.at[sent], ring_r.at[got], to)

    def ring_first():
        for d in (2, 1):
            ring_copy(weight_hbm, d, NZ - d, 0, 0 if d == 2 else 2).start()
            ring_copy(weight_hbm, -d, d, 0, 1 if d == 2 else 2).start()
        remote(weight_hbm, own_weights, sib_s.at[0], sib_r.at[0], sibling).start()

    def shards_all(count, sent, got):
        some = weights.at[pl.ds(0, count * 32), :]
        return remote(some, some, ring_s.at[sent], ring_r.at[got], sibling)

    def shards_wait(count, got):
        shards_all(count, 0, got).wait_recv()

    def ring_next(step):
        far, got = 2 * step, 3 * step
        shards_wait(1, got - 3)
        for d in (2, 1):
            ring_copy(shard(NZ - far), d, NZ - far - d, step, got if d == 2 else got + 2).start()
        shards_wait(1, got - 2)
        for d in (2, 1):
            ring_copy(shard(far), -d, far + d, step, got + 1 if d == 2 else got + 2).start()

    def ring_last(side):
        shards_wait(1, 6 + side)
        src, hops, slot = ((shard(NZ - 6), 1, NZ - 7), (shard(6), -1, 7))[side]

        @pl.when(h == side)
        def _():
            for core in (h, 1 - h):
                ring_copy(src, 2 * hops, 8, 3, 9, core).start()

        for core in (h, 1 - h):
            ring_copy(src, hops, slot, 3, 9, core).start()

    def sib_copy(slot):
        two = weights.at[pl.ds(pl.multiple_of(h * (NZ * 32) + slot * 32, 32), 2 * 32), :]
        return remote(two, two, sib_s.at[1], sib_r.at[1], sibling)

    def sib_give(step):
        shards_wait(2, 3 * step - 1)
        sib_copy(NZ - 2 * step).start()
        sib_copy(2 * step - 1).start()

    peers = NJ - 1 + (NX - 1) * NY + NZ - 1 + 3
    edge = jnp.logical_or(first_j, last_j)
    early = z < 7

    def convert(stream, ref, begin, end):
        for part in range(SUBS):
            to = pl.ds(begin * SUBS + part, end - begin, stride=SUBS)
            streams[stream, to, :] = ref[begin:end, part * LANES : (part + 1) * LANES].astype(F32)

    for n in range(3):
        inputs[n].wait()
    for stream, ref in enumerate((q_ref, k_ref, v_ref)):
        convert(stream, ref, ROWS - 16, ROWS)
    last = (ROWS - 2) * SUBS
    halo_copy = remote(
        streams.at[:, pl.ds(last, 2 * SUBS), :], halo, halo_s, halo_r, (lax.rem(seq + 1, NZ * NJ), x)
    )
    convert(1, k_ref, 0, ROWS - 16)
    convert(2, v_ref, 0, ROWS - 16)
    for n in range(3, len(inputs)):
        inputs[n].wait()

    for part in range(SUBS):
        cut = slice(part * LANES, (part + 1) * LANES)
        to = pl.ds(part, MODES, stride=SUBS)
        rate_rows[to, :] = rates_ref[:, cut]
        res_rows[to, :] = residues_ref[:, cut]
        prior_rows[to, :] = prior_ref[:, cut]
        for stream in range(3):
            for tap in range(3):
                n = (3 * stream + tap) * SUBS + part
                tap_rows[n : n + 1, :] = taps_ref[stream, tap : tap + 1, cut]
    rates = rate_rows[...]
    inflow = jnp.sqrt(one_minus_exp(2.0 * rates))
    pole_rows[...] = jnp.exp(-rates)
    inflow_rows[...] = inflow
    inres_rows[...] = res_rows[...] * inflow

    def modes_of(ref):
        return [ref[m * SUBS : (m + 1) * SUBS, :] for m in range(MODES)]

    taps = [tap_rows[n * SUBS : (n + 1) * SUBS, :] for n in range(9)]
    poles = modes_of(pole_rows)
    skip = skip_ref[...]

    def feature(stream, now, back1, back2):
        return taps[3 * stream] * now + taps[3 * stream + 1] * back1 + taps[3 * stream + 2] * back2

    def gate(t, history):
        later, feats = [], []
        for stream, (back1, back2) in zip((1, 2), history):
            now = streams[stream, row(t), :]
            feats.append(feature(stream, now, back1, back2))
            later.append((now, back1))
        value = feats[0] * feats[1]
        gated[row(t), :] = value
        return value, tuple(later)

    def steps(begin, end, step, carried):
        def eight(block, carried):
            for t in range(8):
                carried = step(block * 8 + t, carried)
            return carried

        return lax.fori_loop(begin // 8, end // 8, eight, carried)

    def advance(states, value):
        return tuple(pole * state + value for pole, state in zip(poles, states))

    history = tuple((streams[s, SUBS : 2 * SUBS, :], streams[s, 0:SUBS, :]) for s in (1, 2))
    states = tuple(jnp.zeros((SUBS, LANES), F32) for _ in range(MODES))

    def scan_step(t, carried):
        states, history = carried
        value, history = gate(t, history)
        return advance(states, value), history

    scan = (states, history)
    for t in range(2, 8):
        scan = scan_step(t, scan)
    states, history = steps(8, ROWS, scan_step, scan)

    @pl.when(edge)
    def _():
        pl.semaphore_wait(barrier, peers + 1)

    @pl.when(jnp.logical_not(edge))
    def _():
        pl.semaphore_wait(barrier, peers)

    pl.when(has_next)(halo_copy.start)
    ring_first()

    for tile in range(SUBS):
        turned = residual_ref[:, tile * LANES : (tile + 1) * LANES].astype(F32).T.astype(BF16)
        to_rows = slice((tile // 2) * 64, (tile // 2) * 64 + 64)
        for odd in range(2):
            res_out[2 * (tile % 2) + odd, to_rows, :] = turned[64 * odd : 64 * odd + 64, :]

    def beside(block, dx=0):
        return device(z, lax.rem(y + (0, 3, 1, 2)[block], NY) * NH + h, x if dx == 0 else lax.rem(x + dx, NX))

    def res_copy(block):
        to = lax.rem(y + (0, 1, 3, 2)[block], NY)
        return remote(res_out.at[to], res_in.at[block - 1], res_s, res_r, device(z, to * NH + h, x))

    for block in range(1, 4):
        res_copy(block).start()
    convert(0, q_ref, 0, ROWS - 16)

    @pl.when(has_prev)
    def _():
        halo_copy.wait_recv()

    @pl.when(jnp.logical_not(has_prev))
    def _():
        halo[...] = jnp.zeros_like(halo)

    def halo_rows(s):
        return halo[s, SUBS : 2 * SUBS, :], halo[s, 0:SUBS, :]

    first, history = gate(0, (halo_rows(1), halo_rows(2)))
    second, history = gate(1, history)
    for m in range(MODES):
        at = slice(m * SUBS, (m + 1) * SUBS)
        late = jnp.exp(-(ROWS - 2.0) * rate_rows[at, :])
        ends[at, :] = inflow_rows[at, :] * (states[m] + late * (poles[m] * first + second))

    pair = 2 * SUBS

    def pair_rows(n):
        return pl.ds(pl.multiple_of(n * pair, pair), pair)

    def to_owner(d):
        to = lax.rem(j + d, NJ)
        return remote(ends.at[pair_rows(to), :], plane_in.at[j], s1_s, s1_r, device(z, to, x))

    def along_line(d):
        return remote(line_out, line_in.at[z], s2_s.at[d], s2_r.at[d], along(d, h))

    def from_owner(d):
        to = lax.rem(j + d, NJ)
        return remote(back_out.at[to], carry.at[pair_rows(j), :], s3_s, s3_r, device(z, to, x))

    for d in range(1, NJ):
        to_owner(d).start()

    plane_in[j] = ends[pair_rows(j), :]

    inres = modes_of(inres_rows)

    def output_step(t, carried):
        states, (back1, back2) = carried
        now = streams[0, row(t), :]
        featq[row(t), :] = feature(0, now, back1, back2)
        value = gated[row(t), :]
        states = advance(states, value)
        terms = [r * s for r, s in zip(inres, states)] + [skip * value]
        filt[row(t), :] = tree_sum(terms)
        return states, (now, back1)

    states = tuple(jnp.zeros((SUBS, LANES), F32) for _ in range(MODES))
    outputs = steps(0, 64, output_step, (states, halo_rows(0)))
    ring_next(1)

    others = plane_in.at[pl.ds(0, NJ - 1)]
    to_owner_all = remote(others, others, s1_s, s1_r, sibling)
    to_owner_all.wait_recv()

    my_rates = rate_rows[pair_rows(j), :]
    block_decay = jnp.exp(-float(ROWS) * my_rates)
    plane_decay = jnp.exp(-float(ROWS * NJ) * my_rates)
    total = plane_in[0]
    for i in range(1, NJ):
        total = block_decay * total + plane_in[i]
    line_out[...] = total

    @pl.loop(1, NZ - z)
    def _(d):
        along_line(d).start()

    late = jnp.logical_not(early)

    @pl.when(late)
    def _():
        ring_next(2)
        sib_give(1)

    steps(64, ROWS, output_step, outputs)
    highest = z >= 14

    @pl.when(highest)
    def _():
        ring_last(0)

    @pl.loop(1, z + 1)
    def _(d):
        along_line(d).wait_recv()

    incoming = lax.fori_loop(0, z, lambda i, s: plane_decay * s + line_in[i], prior_rows[pair_rows(j), :])
    for i in range(NJ):
        back_out[i] = incoming
        incoming = block_decay * incoming + plane_in[i]

    for d in range(1, NJ):
        from_owner(d).start()

    carry[pair_rows(j), :] = back_out[j]


    others = back_out.at[pl.ds(0, NJ - 1)]
    from_owner_all = remote(others, others, s3_s, s3_r, sibling)
    from_owner_all.wait_recv()

    half = ROWS // 2
    up = device(z, lax.rem(y + 1, NY) * NH + h, x)
    down = device(z, lax.rem(y + 3, NY) * NH + h, x)
    across = device(z, lax.rem(y + 2, NY) * NH + h, x)

    act_wait = (0, 2, 2, 1)

    def act_copy(part, side):
        cut = pl.ds(part * half, half)
        n = 2 * part + side
        return remote(acts.at[0, cut, :], acts.at[1 + side, cut, :], act_s, act_r.at[act_wait[n]], (up, down)[side])

    def fwd_copy(part):
        cut = pl.ds(part * half, half)
        return remote(acts.at[1 + part, cut, :], acts.at[3, cut, :], fwd_s, fwd_r, (up, down)[part])

    def carried_step(t, waves):
        waves = tuple(pole * wave for pole, wave in zip(poles, waves))
        filt[row(t), :] = featq[row(t), :] * (filt[row(t), :] + tree_sum(list(waves)))
        return waves

    waves = tuple(res_rows[m * SUBS : (m + 1) * SUBS, :] * carry[m * SUBS : (m + 1) * SUBS, :] for m in range(MODES))
    for part in range(2):
        waves = steps(part * half, (part + 1) * half, carried_step, waves)
        for sub in range(SUBS):
            from_rows = pl.ds(part * half * SUBS + sub, half, stride=SUBS)
            acts[0, part * half : (part + 1) * half, sub * LANES : (sub + 1) * LANES] = filt[from_rows, :].astype(BF16)
        act_copy(part, part).start()
    act_copy(1, 0).start()
    act_copy(0, 1).start()

    @pl.when(early)
    def _():
        ring_next(2)
        sib_give(1)

    def forward(part):
        act_copy(part, part).wait_recv()
        fwd_copy(part).start()

    @pl.when(jnp.logical_not(highest))
    def _():
        ring_last(0)

    ring_last(1)

    pl.when(has_next)(halo_copy.wait_send)
    to_owner_all.wait_send()
    from_owner_all.wait_send()

    @pl.loop(1, NZ - z)
    def _(d):
        along_line(d).wait_send()

    forward(0)
    forward(1)
    sib_give(2)
    sib_give(3)
    own_all = remote(weight_hbm, own_weights, sib_s.at[0], sib_r.at[0], sibling)
    own_all.wait_send()
    own_all.wait_recv()
    for sent in range(3):
        shards_all(4, sent, 0).wait_send()
    res_all = remote(res_in, res_in, res_s, res_r, sibling)
    res_all.wait_send()
    res_all.wait_recv()
    twelve = weights.at[pl.ds(0, 12 * 32), :]
    sib_all = remote(twelve, twelve, sib_s.at[1], sib_r.at[1], sibling)
    sib_all.wait_recv()

    right, left = device(z, j, lax.rem(x + 1, NX)), device(z, j, lax.rem(x + 3, NX))
    sides = (right, left)

    def project(rows, weight):
        return lax.dot_general(weight, rows, (((1,), (1,)), ((), ())), preferred_element_type=F32)

    last_slots = [(core * NZ * 32 + 7 * 32, 3 * 32) for core in range(2)]
    other_slots = ((0, 224), (320, 416), (832, 192))

    def project_others(pair):
        rows = acts[2 * pair : 2 * pair + 2].reshape(2 * ROWS, CHANS)
        for at, count in other_slots:
            parts[pair, at : at + count, :] = project(rows, weights[at : at + count, :])

    def project_last(pair):
        rows = acts[2 * pair : 2 * pair + 2].reshape(2 * ROWS, CHANS)
        some = jnp.concatenate([weights[at : at + count, :] for at, count in last_slots], axis=0)
        value = project(rows, some)
        for n, (at, count) in enumerate(last_slots):
            parts[pair, at : at + count, :] = value[n * count : (n + 1) * count, :]

    def band(pair, dx):
        first = lax.rem(x + dx, NX) * 4 + NZ - z
        slots = [lax.rem(first + i, NZ) for i in range(4)]
        return [parts[pair, shard_rows(slot, core), :] for slot in slots for core in range(2)]

    def far_copy(pair, side):
        n = 2 * pair + side
        return remote(far_out.at[n], far_in.at[n], far_s.at[pair], far_r.at[pair], sides[side])

    def near_copy(pair, side):
        n = 2 * pair + side
        return remote(near_out.at[n], near_in.at[n], near_s.at[pair], near_r.at[pair], sides[side])

    def far_all(pair):
        both = far_in.at[pl.ds(2 * pair, 2)]
        return remote(both, both, far_s.at[pair], far_r.at[pair], right)

    def near_all(pair):
        both = near_in.at[pl.ds(2 * pair, 2)]
        return remote(both, both, near_s.at[pair], near_r.at[pair], right)

    def begin(pair):
        chunks = band(pair, 2)
        for side in range(2):
            for i in range(4):
                far_out[2 * pair + side, 32 * i : 32 * i + 32, :] = chunks[4 * side + i].astype(BF16)
            far_copy(pair, side).start()

    def middle(pair):
        far_all(pair).wait_recv()
        for side in range(2):
            n = 2 * pair + side
            for i, chunk in enumerate(band(pair, (1, 3)[side])):
                if i // 4 == side:
                    chunk = chunk + far_in[n, 32 * (i % 4) : 32 * (i % 4) + 32, :].astype(F32)
                near_out[n, 32 * i : 32 * i + 32, :] = chunk.astype(BF16)
            near_copy(pair, side).start()

    def fin_copy(block):
        return remote(back_rows.at[block - 1], final_in.at[y], fin_s, fin_r, beside(block))

    def stat_copy(block, dx):
        n = 4 * block + dx
        return remote(stat_out.at[block], stat_in.at[n], stat_s, stat_r, beside(block, dx))

    def finish(pair):
        near_all(pair).wait_recv()
        value = jnp.concatenate(band(pair, 0), axis=0)
        for side in range(2):
            value = value + near_in[2 * pair + side].astype(F32)
        for block in (2 * pair + 1, 2 * pair):
            lanes = slice(block % 2 * ROWS, (block % 2 + 1) * ROWS)
            if block == 0:
                part = value[:, lanes] + res_out[y].astype(F32)
                final_in[y] = part.astype(BF16)
            else:
                part = value[:, lanes] + res_in[block - 1].astype(F32)
                back_rows[block - 1] = part.astype(BF16)
                fin_copy(block).start()
            squares = jnp.sum(part * part, axis=0, keepdims=True)
            stat_out[block] = jnp.broadcast_to(squares, (SUBS, LANES))
            if block == 0:
                stat_in[0] = stat_out[0]
            for dx in range(NX):
                if (block, dx) != (0, 0):
                    stat_copy(block, dx).start()

    late_halves = remote(acts.at[1], acts.at[1], act_s, act_r.at[2], up)
    late_halves.wait_recv()
    project_others(0)
    shards_wait(6, 9)
    project_last(0)
    begin(0)
    fwd_all = remote(acts.at[3], acts.at[3], fwd_s, fwd_r, up)
    fwd_all.wait_recv()
    project_others(1)
    project_last(1)
    begin(1)
    middle(0)
    middle(1)
    finish(0)
    finish(1)
    fin_all = remote(back_rows, final_in.at[pl.ds(0, NY - 1)], fin_s, fin_r, up)
    fin_all.wait_recv()

    for tile in range(SUBS):
        cut = slice(tile * LANES, (tile + 1) * LANES)
        from_rows = slice((tile // 2) * 64, (tile // 2) * 64 + 64)
        mixed = [final_in[2 * (tile % 2) + odd, from_rows, :].astype(F32) for odd in range(2)]
        value = jnp.concatenate(mixed, axis=0).T
        summed[:, cut] = value
        hidden_ref[:, cut] = value.astype(BF16)
    sib_all.wait_send()
    shards_all(6, 3, 0).wait_send()
    remote(acts.at[pl.ds(0, 2)], acts.at[pl.ds(0, 2)], act_s, act_r.at[2], up).wait_send()
    fwd_all.wait_send()
    for pair in range(2):
        far_all(pair).wait_send()
        near_all(pair).wait_send()
    fin_all.wait_send()

    fifteen = stat_in.at[pl.ds(1, 15)]
    stat_all = remote(fifteen, fifteen, stat_s, stat_r, up)
    stat_all.wait_recv()
    total = tree_sum([stat_in[n] for n in range(16)])
    scale = lax.rsqrt(total * (1.0 / (NX * CHANS)) + 1e-05)
    scale = jnp.broadcast_to(scale[0:1, :], (ROWS, LANES)).T
    for tile in range(SUBS):
        cut = slice(tile * LANES, (tile + 1) * LANES)
        normed_ref[:, cut] = (summed[:, cut] * scale * gain_ref[tile : tile + 1, :]).astype(BF16)
    stat_all.wait_send()


def shard_rows(slot, h):
    return pl.ds(pl.multiple_of(h * (NZ * 32) + slot * 32, 32), 32)


def tree_sum(terms):
    while len(terms) > 1:
        rest = [terms[-1]] if len(terms) % 2 else []
        terms = [a + b for a, b in zip(terms[0::2], terms[1::2])] + rest
    return terms[0]


def local(
    q_stream, k_stream, v_stream, short_filter, rates, residues, skip, prior_state, out_weight, residual, norm_gain
):
    vmem = pl.BlockSpec(memory_space=pltpu.VMEM)
    hbm = pl.BlockSpec(memory_space=pltpu.HBM)
    dma = pltpu.SemaphoreType.DMA
    wide = (ROWS * SUBS, LANES)
    params = (MODES * SUBS, LANES)
    pair = (2 * SUBS, LANES)
    rows = (ROWS, CHANS)
    scratch = [
        pltpu.VMEM(rows, BF16),
        pltpu.VMEM(rows, BF16),
        pltpu.VMEM(rows, BF16),
        pltpu.VMEM(short_filter.shape, F32),
        pltpu.VMEM((MODES, CHANS), F32),
        pltpu.VMEM((MODES, CHANS), F32),
        pltpu.VMEM((SUBS, LANES), F32),
        pltpu.VMEM((MODES, CHANS), F32),
        pltpu.VMEM(rows, BF16),
        pltpu.VMEM((SUBS, LANES), F32),
        pltpu.VMEM((3,) + wide, F32),
        pltpu.VMEM((3, 2 * SUBS, LANES), F32),
        pltpu.VMEM(wide, F32),
        pltpu.VMEM(wide, F32),
        pltpu.VMEM(wide, F32),
        pltpu.VMEM((9 * SUBS, LANES), F32),
        pltpu.VMEM(params, F32),
        pltpu.VMEM(params, F32),
        pltpu.VMEM(params, F32),
        pltpu.VMEM(params, F32),
        pltpu.VMEM(params, F32),
        pltpu.VMEM(params, F32),
        pltpu.VMEM(params, F32),
        pltpu.VMEM((NJ,) + pair, F32),
        pltpu.VMEM((NZ,) + pair, F32),
        pltpu.VMEM(pair, F32),
        pltpu.VMEM((NJ,) + pair, F32),
        pltpu.VMEM(params, F32),
        pltpu.VMEM((CHANS, CHANS), BF16),
        pltpu.VMEM((NY, ROWS, CHANS), BF16),
        pltpu.VMEM((4, LANES, 2 * ROWS), BF16),
        pltpu.VMEM((4, LANES, 2 * ROWS), BF16),
        pltpu.VMEM((4, BAND, 2 * ROWS), BF16),
        pltpu.VMEM((4, BAND, 2 * ROWS), BF16),
        pltpu.VMEM((2, CHANS, 2 * ROWS), F32),
        pltpu.VMEM((NY - 1, BAND, ROWS), BF16),
        pltpu.VMEM((NY, BAND, ROWS), BF16),
        pltpu.VMEM((NY, BAND, ROWS), BF16),
        pltpu.VMEM((NY - 1, BAND, ROWS), BF16),
        pltpu.VMEM((ROWS, CHANS), F32),
        pltpu.VMEM((NY, SUBS, LANES), F32),
        pltpu.VMEM((16, SUBS, LANES), F32),
    ]
    sems = [dma((11,))]
    for sent, got in (
        (0, 0), (0, 0), (NZ, NZ), (0, 0), (4, 10), (2, 2), (0, 3), (0, 0), (2, 2), (2, 2), (0, 0), (0, 0), (0, 0)
    ):
        sems += [dma((n,)) if n else dma(()) for n in (sent, got)]
    return pl.pallas_call(
        kernel,
        out_shape=(jax.ShapeDtypeStruct((ROWS, CHANS), BF16), jax.ShapeDtypeStruct((ROWS, CHANS), BF16)),
        in_specs=[hbm] * 11,
        out_specs=(vmem, vmem),
        scratch_shapes=scratch + sems,
        compiler_params=pltpu.CompilerParams(
            collective_id=0, has_side_effects=True, vmem_limit_bytes=63 * 1024 * 1024
        ),
        name="mixer",
    )(
        q_stream, k_stream, v_stream, short_filter, rates, residues, skip.reshape(SUBS, LANES), prior_state,
        out_weight.T, residual, norm_gain.reshape(SUBS, LANES),
    )


def solution(mesh):
    placed = (
        P("seq", "ch"),
        P("seq", "ch"),
        P("seq", "ch"),
        P(None, None, "ch"),
        P(None, "ch"),
        P(None, "ch"),
        P("ch"),
        P(None, "ch"),
        P("ch", "seq"),
        P("seq", "ch"),
        P("ch"),
    )
    return jax.shard_map(
        local,
        mesh=mesh,
        in_specs=placed,
        out_specs=(P("seq", "ch"), P("seq", "ch")),
        check_vma=False,
    )
```
